32 devices in a mesh: dp: 4 (over y, core), fsdp: 8 (over z, x).
Axes of the slice: x: 2, y: 2, z: 4, core: 2. Of those that a mesh axis runs over, the one named last changes fastest.
Arguments:
- frames: bfloat16 [32, 160, 512], P(('dp', 'fsdp')), may hold values from -6 to 6
- lengths: int32 [32], P(('dp', 'fsdp')), may hold values from 10 to 160, as said below
- cotangent: bfloat16 [32, 160, 512], P(('dp', 'fsdp')), may hold values from -6 to 6
- params: float32 [8210944], P(('dp', 'fsdp')), as said below
- first_moment: float32 [8210944], P(('dp', 'fsdp'))
- second_moment: float32 [8210944], P(('dp', 'fsdp')), as said below
Outputs:
- out: bfloat16 [32, 160, 512], P(('dp', 'fsdp'))
- frames_grad: bfloat16 [32, 160, 512], P(('dp', 'fsdp'))
- new_params: float32 [8210944], P(('dp', 'fsdp'))
- new_first: float32 [8210944], P(('dp', 'fsdp'))
- new_second: float32 [8210944], P(('dp', 'fsdp'))
- weight_norms: float32 [12], replicated
- update_norms: float32 [12], replicated
- trust_ratios: float32 [12], replicated
- gain_grads: float32 [4096], replicated
The draws below stay inside these ranges and needn't reach their ends.
Inputs may be any that keep to these rules, and one draw needn't show every extreme that they name: `lengths`: in every draw some utterance has exactly 160 valid frames. `params`: the gains are positive. `second_moment`: every entry is positive.
All inputs are finite; a program needn't handle non-finite values.
Results may differ from the reference program's by a relative error of at most 0.02.
Values may be sent and summed in bfloat16 or wider, within the bound.
No kernel may reach another device: no remote copies, remote signals or barrier semaphores. Data moves between devices by JAX's collectives and lax.ppermute only.
A program may use at most 256 MiB of HBM per device.

```python
import math
import jax
import jax.numpy as jnp
from jax import lax

D = 512
H = 8
HS = 64
FF = 2048
CG = 3072
KER = 31
RELW = 128
NMAT = 12
STEP = 8
LMAX = 160
UTTS = 32
NPARAM = 8210944


def segment_table():
    gate_width = CG // 2
    grad_base = math.sqrt(UTTS * LMAX / 2.0)
    matrix_grad = 0.3 * grad_base
    return [(D * FF, D ** (-0.5), matrix_grad, 0.0), (FF * D, FF ** (-0.5), matrix_grad, 0.0), (D * 3 * D, D ** (-0.5), matrix_grad, 0.0), (D * D, 3.0 * D ** (-0.5), matrix_grad, 0.0), (D * CG, D ** (-0.5), matrix_grad, 0.0), (gate_width * D, gate_width ** (-0.5), matrix_grad, 0.0), (2 * D * D, (2 * D) ** (-0.5), matrix_grad, 0.0), (D * FF, D ** (-0.5), matrix_grad, 0.0), (FF * D, FF ** (-0.5), matrix_grad, 0.0), (5 * D + gate_width, 0.1, grad_base, 1.0), (KER * (gate_width + 2 * D), KER ** (-0.5), matrix_grad, 0.0), (RELW * H, 1.0, 2.0 * math.sqrt(UTTS / LMAX), 0.0)]


def spread_vector(column, low_end, high_end):
    pieces = []
    for segment in segment_table():
        entries = segment[0]
        rising = low_end + (high_end - low_end) * jnp.arange(entries, dtype=jnp.float32) / entries
        pieces.append(segment[column] * rising)
    return jnp.concatenate(pieces)


def draw_params(key, part):
    key = jax.random.fold_in(key, 11)
    normal_draw = jnp.clip(jax.random.normal(key, (NPARAM,), jnp.float32), -4.0, 4.0)
    return spread_vector(3, 0.6, 1.8) + spread_vector(1, 0.6, 1.8) * normal_draw


def draw_first_moment(key, part):
    key = jax.random.fold_in(key, 23)
    normal_draw = jnp.clip(jax.random.normal(key, (NPARAM,), jnp.float32), -4.0, 4.0)
    return spread_vector(2, 0.5, 1.5) * normal_draw


def draw_second_moment(key, part):
    key = jax.random.fold_in(key, 37)
    factor = jnp.exp(jax.random.uniform(key, (NPARAM,), jnp.float32, 0.0, math.log(4.0)))
    scale_vector = spread_vector(2, 1.0, 1.0)
    return scale_vector * scale_vector * factor


def draw_lengths(key, part):
    key = jax.random.fold_in(key, 5)
    first_key, second_key = jax.random.split(key)
    order = jnp.arange(UTTS, dtype=jnp.int32)
    shortest = max(1, LMAX // 15)
    floor_rise = shortest + (LMAX // 3 - shortest) * order // (UTTS - 1)
    top_rise = LMAX // 3 + (LMAX - LMAX // 3) * order // (UTTS - 1)
    drawn = jax.random.randint(first_key, (UTTS,), floor_rise, top_rise + 1)
    chosen = jax.random.randint(second_key, (), 0, UTTS)
    return jnp.where(order == chosen, LMAX, drawn).astype(jnp.int32)


def block_scale(own_key, dims, cuts, least, largest):
    def one(axis_at, shards_of):
        steps = jax.random.uniform(jax.random.fold_in(jax.random.fold_in(own_key, 6), axis_at), (shards_of,), jnp.float32, least / len(cuts), largest / len(cuts))
        return jnp.repeat(jnp.exp(steps), dims[axis_at] // shards_of).reshape((-1,) + (1,) * (len(dims) - axis_at - 1))

    level = one(*cuts[0])
    for cut in cuts[1:]:
        level = level * one(*cut)
    return level


def normal_values(own_key, dims, scale, reach, cuts=(), kind=jnp.bfloat16):
    values = scale * jax.random.normal(own_key, dims, jnp.float32)
    if cuts:
        values = values * block_scale(own_key, dims, cuts, -0.22, 0.18)
    return jnp.clip(values, -reach, reach).astype(kind)


def setup_inputs(seed: int = 0) -> dict:
    seeds = jax.random.split(jax.random.key(seed), 7)
    return {
        "frames": normal_values(seeds[0], (UTTS, LMAX, D), 1.0, 6.0, ((0, 32),)),
        "lengths": draw_lengths(jax.random.fold_in(seeds[6], 71), 0),
        "cotangent": normal_values(seeds[2], (UTTS, LMAX, D), 1.0, 6.0, ((0, 32),)),
        "params": draw_params(jax.random.fold_in(seeds[6], 71), 0),
        "first_moment": draw_first_moment(jax.random.fold_in(seeds[6], 71), 0),
        "second_moment": draw_second_moment(jax.random.fold_in(seeds[6], 71), 0),
    }


@jax.custom_vjp
def low(v):
    return lax.optimization_barrier(v.astype(jnp.bfloat16)).astype(jnp.float32)

@jax.custom_vjp
def low_back(v):
    return v

def low_keep(v):
    return (low(v), None)

def low_pass(kept, grad):
    return (grad,)

def back_keep(v):
    return (v, None)

def back_low(kept, grad):
    return (low(grad),)
low.defvjp(low_keep, low_pass)
low_back.defvjp(back_keep, back_low)
NORM_EPS = 1e-05
ADAM_EPS = 1e-06
MASK_FILL = -1000000000.0

def segment_shapes():
    gate_width = CG // 2
    return [(D, FF), (FF, D), (D, 3 * D), (D, D), (D, CG), (gate_width, D), (2 * D, D), (D, FF), (FF, D), (5 * D + gate_width,), (KER, gate_width + 2 * D), (RELW, H)]

def unpack(flat):
    pieces = []
    offset = 0
    for extent in segment_shapes():
        entries = math.prod(extent)
        pieces.append(flat[offset:offset + entries].reshape(extent))
        offset = offset + entries
    return pieces

def product(left, right):
    return jnp.dot(left, right, precision=lax.Precision.HIGHEST, preferred_element_type=jnp.float32)

def layer_norm(values, gain):
    centered = values - lax.optimization_barrier(jnp.mean(values, axis=-1, keepdims=True))
    variance = lax.optimization_barrier(jnp.mean(centered * centered, axis=-1, keepdims=True))
    return centered * lax.rsqrt(variance + NORM_EPS) * gain

def depthwise(values, kernel):
    taps = kernel.shape[0]
    margin = taps // 2
    frame_slots = values.shape[-2]
    padding = [(0, 0)] * (values.ndim - 2) + [(margin, margin), (0, 0)]
    padded = jnp.pad(values, padding)
    result = jnp.zeros_like(values)
    for offset in range(taps):
        result = result + kernel[offset] * lax.slice_in_dim(padded, offset, offset + frame_slots, axis=values.ndim - 2)
    return result

def feed_forward(values, gain, w_in, w_out):
    normed = low(layer_norm(values, gain))
    hidden = low_back(product(normed, w_in))
    active = low(jax.nn.silu(hidden))
    return low_back(product(active, w_out))

def attend(packed, rel_table, valid_row):
    frame_slots = packed.shape[0]
    heads_first = packed.reshape(frame_slots, 3, H, HS).transpose(1, 2, 0, 3)
    span = lax.iota(jnp.int32, frame_slots)
    buckets = jnp.clip(span[None, :] - span[:, None], -(RELW // 2), RELW // 2 - 1) + RELW // 2

    @jax.checkpoint
    def one_head(operands):
        queries, key_rows, value_rows, column = operands
        scores = product(queries, key_rows.T) * HS ** (-0.5) + column[buckets]
        scores = low_back(scores)
        scores = jnp.where(valid_row[None, :] > 0, scores, MASK_FILL)
        attention = jax.nn.softmax(scores, axis=-1)
        return product(low(attention), value_rows)
    context = lax.map(one_head, (heads_first[0], heads_first[1], heads_first[2], rel_table.T))
    context = context.transpose(1, 0, 2).reshape(frame_slots, D)
    return low_back(low(context))

def block_forward(frame_rows, valid_row, flat):
    ffa_in, ffa_out, att_qkv, att_out, cg_in, cg_out, merge_out, ffb_in, ffb_out, gains, kernels, rel_table = unpack(low(flat))
    gate_width = CG // 2
    valid_col = valid_row[:, None]
    x_one = frame_rows + 0.5 * feed_forward(frame_rows, gains[0:D], ffa_in, ffa_out)
    packed = low_back(low(product(low(layer_norm(x_one, gains[D:2 * D])), att_qkv)))
    context = attend(packed, rel_table, valid_row)
    att_output = low_back(product(context, att_out))
    hidden = low_back(product(low(layer_norm(x_one, gains[2 * D:3 * D])), cg_in))
    activated = jax.nn.gelu(hidden, approximate=False)
    conv_gate = depthwise(layer_norm(activated[:, gate_width:], gains[5 * D:]) * valid_col, kernels[:, :gate_width])
    cg_output = low_back(product(low(activated[:, :gate_width] * conv_gate), cg_out))
    joined = jnp.concatenate([att_output, cg_output], axis=1)
    mixed = low(joined + depthwise(joined * valid_col, kernels[:, gate_width:]))
    x_two = x_one + low_back(product(mixed, merge_out))
    x_three = x_two + 0.5 * feed_forward(x_two, gains[3 * D:4 * D], ffb_in, ffb_out)
    return layer_norm(x_three, gains[4 * D:5 * D]) * valid_col

def reference(frames, lengths, cotangent, params, first_moment, second_moment):
    span = lax.iota(jnp.int32, LMAX)

    def one_utterance(grad_total, operands):
        frame_rows, length_value, cot_rows = operands
        valid_row = (span < length_value).astype(jnp.float32)
        result, pullback = jax.vjp(lambda rows_in, flat: block_forward(rows_in, valid_row, flat), frame_rows.astype(jnp.float32), params)
        rows_grad, flat_grad = pullback(cot_rows.astype(jnp.float32))
        return (grad_total + flat_grad, (result.astype(jnp.bfloat16), rows_grad.astype(jnp.bfloat16)))
    grad, (outputs, frames_grad) = lax.scan(one_utterance, jnp.zeros((NPARAM,), jnp.float32), (frames, lengths, cotangent))
    gain_grads = unpack(grad)[9]
    labels = jnp.concatenate([jnp.full((math.prod(extent),), segment_index, jnp.int32) for segment_index, extent in enumerate(segment_shapes())])
    new_first = 0.5 * first_moment + 0.5 * grad
    new_second = 0.5 * second_moment + 0.5 * grad * grad
    first_hat = new_first / (1.0 - 0.5 ** STEP)
    second_hat = new_second / (1.0 - 0.5 ** STEP)
    update = first_hat / (jnp.sqrt(second_hat) + ADAM_EPS) + 0.01 * params
    weight_norms = jnp.sqrt(jax.ops.segment_sum(params * params, labels, num_segments=NMAT))
    update_norms = jnp.sqrt(jax.ops.segment_sum(update * update, labels, num_segments=NMAT))
    trust_ratios = weight_norms / (update_norms + ADAM_EPS)
    new_params = params - 0.5 * trust_ratios[labels] * update
    return (outputs, frames_grad, new_params, new_first, new_second, weight_norms, update_norms, trust_ratios, gain_grads)
```

```python
import math

import jax
import jax.numpy as jnp
from jax import lax
from jax.experimental import pallas as pl
from jax.experimental.pallas import tpu as pltpu
from jax.sharding import PartitionSpec as P

STEP = 8
BETA_FIRST = 0.5
BETA_SECOND = 0.5
LEARN_RATE = 0.5
WEIGHT_DECAY = 0.01
ADAM_EPS = 1e-06
AXES = ("dp", "fsdp")


def segment_shapes():
    gate_width = CG // 2
    return [
        (D, FF),
        (FF, D),
        (D, 3 * D),
        (D, D),
        (D, CG),
        (gate_width, D),
        (2 * D, D),
        (D, FF),
        (FF, D),
        (5 * D + gate_width,),
        (KER, gate_width + 2 * D),
        (RELW, H),
    ]


D = 512
H = 8
HS = 64
FF = 2048
CG = 3072
KER = 31
RELW = 128
NORM_EPS = 1e-05
MASK_FILL = -1000000000.0
ROW = 512
SLOTS = 160
KEYS = 256
PAD = 16
PADDED = SLOTS + 2 * PAD
GATE = CG // 2
BLOCK = {
    "ffa_in": 0,
    "ffa_out": 4,
    "qkv": 8,
    "att_out": 11,
    "cg_in": 12,
    "cg_out": 18,
    "merge": 21,
    "ffb_in": 23,
    "ffb_out": 27,
    "small": 31,
}
TAPS_AT = 8
REL_AT = 8 + 5 * KER
SMALL = 176
F32, BF16 = jnp.float32, jnp.bfloat16


def dot(left, right):
    return lax.dot_general(left, right, (((1,), (0,)), ((), ())), preferred_element_type=F32)


def dot_t(left, right):
    return lax.dot_general(left, right, (((1,), (1,)), ((), ())), preferred_element_type=F32)


def t_dot(left, right):
    return lax.dot_general(left, right, (((0,), (0,)), ((), ())), preferred_element_type=F32)


def low(values):
    return values.astype(BF16)


def each(count, body):
    def step(at, carry):
        body(at)
        return carry

    lax.fori_loop(0, count, step, 0)


def part(at, size):
    return pl.ds(pl.multiple_of(at * size, size), size)


def normed(values):
    centered = values - jnp.mean(values, axis=-1, keepdims=True)
    variance = jnp.mean(centered * centered, axis=-1, keepdims=True)
    scale = lax.rsqrt(variance + NORM_EPS)
    return centered * scale, scale


def valid_rows(at, size, length):
    return (at * size + lax.broadcasted_iota(jnp.int32, (size, 1), 0) < length).astype(F32)


def norm_back(values, gain, grad):
    hat, scale = normed(values)
    inner = grad * gain
    moved = jnp.mean(inner, axis=-1, keepdims=True) + hat * jnp.mean(inner * hat, axis=-1, keepdims=True)
    return scale * (inner - moved), grad * hat


def erf(values):
    at = jnp.clip(values, -4.0, 4.0)
    square = at * at
    top = jnp.full_like(at, -2.72614225801306e-10)
    for factor in (
        2.77068142495902e-08,
        -2.10102402082508e-06,
        -5.69250639462346e-05,
        -7.34990630326855e-04,
        -2.95459980854025e-03,
        -1.60960333262415e-02,
    ):
        top = top * square + factor
    under = jnp.full_like(at, -1.45660718464996e-05)
    for factor in (
        -2.13374055278905e-04,
        -1.68282697438203e-03,
        -7.37332916720468e-03,
        -1.42647390514189e-02,
    ):
        under = under * square + factor
    return at * top / under


def source_block(coords, at):
    y, c, z, x = coords[0], coords[1], coords[2], coords[3]
    yy, cc, xx, zz = y ^ ((at // 8) % 2), c ^ (at // 16), x ^ ((at // 4) % 2), (z + 4 - at % 4) & 3
    return ((yy * 2 + cc) * 4 + zz) * 2 + xx


def gradient_slot(coords, block):
    y, c, x = coords[0], coords[1], coords[3]
    yy, cc, zz, xx = block // 16, (block // 8) % 2, (block // 2) % 4, block % 2
    return 16 * (c ^ cc) + 8 * (y ^ yy) + 4 * (x ^ xx) + zz


class Loads:
    def __init__(self, coords, sources, wanted, sems):
        self.wanted = wanted
        self.sources = sources
        self.sems = sems
        for at, source in enumerate(sources):
            block = source_block(coords, at)
            first = 0
            for low_block, count, target, rows in wanted:
                here = block - low_block

                @pl.when((here >= 0) & (here < count))
                def _(source=source, target=target, rows=rows, here=here, first=first):
                    pltpu.make_async_copy(
                        source.at[0:rows], target.at[part(here, ROW)] if rows == ROW else target, sems.at[first + here]
                    ).start()

                first = first + count

    def wait(self, which):
        first = sum(count for _, count, _, _ in self.wanted[:which])
        _, count, target, rows = self.wanted[which]
        for at in range(count):
            place = target.at[ROW * at : ROW * at + rows]
            pltpu.make_async_copy(self.sources[0].at[0:rows], place, self.sems.at[first + at]).wait()


class Emits:
    def __init__(self, coords, target, sems):
        self.coords, self.target, self.sems = coords, target, sems
        self.pending = []

    def put(self, block, values):
        copy = pltpu.make_async_copy(
            values, self.target.at[gradient_slot(self.coords, block)], self.sems.at[len(self.pending)]
        )
        copy.start()
        self.pending.append(copy)

    def wait(self):
        for copy in self.pending:
            copy.wait()


def split_columns(raw, target, wide, stage):
    def chunk(k):
        rows = part(k, 128 * wide)
        for lane in range(4):
            stage[lane, 0 : 128 * wide, :] = raw[rows, lane * 128 : lane * 128 + 128].astype(F32)
        for c in range(wide):
            for lane in range(4):
                place = ROW * c + lane * 128
                target[part(k, 128), place : place + 128] = low(stage[lane, pl.ds(c, 128, stride=wide), :])

    each(4, chunk)


def weight_columns(left, grads, wide, stage, target):
    def chunk(k):
        lhs = left[:, part(k, 128)]
        for at in range(2 * wide):
            value = t_dot(lhs, grads[:, 256 * at : 256 * at + 256])
            for half in range(2):
                lane = (at % 2) * 2 + half
                stage[lane, pl.ds(at // 2, 128, stride=wide), :] = value[:, 128 * half : 128 * half + 128]
        rows = part(k, 128 * wide)
        for lane in range(4):
            target[rows, lane * 128 : lane * 128 + 128] = low(stage[lane, 0 : 128 * wide, :])

    each(4, chunk)


def weight_rows(left, grads, count, target):
    def chunk(k):
        lhs = left[:, part(k, 256)]
        for at in range(2):
            target[part(k, 256), 256 * at : 256 * at + 256] = low(t_dot(lhs, grads[:, 256 * at : 256 * at + 256]))

    each(count, chunk)


def norm_rows(source, gain, target):
    def chunk(k):
        hat, _ = normed(source[part(k, 32), :].astype(F32))
        target[part(k, 32), :] = low(hat * gain)

    each(5, chunk)


def norm_rows_back(values, gain, grad, total, add):
    total[...] = jnp.zeros_like(total)

    def chunk(k):
        rows = part(k, 32)
        back, products = norm_back(values[rows, :].astype(F32), gain, grad[rows, :])
        total[...] += jnp.sum(products.reshape(4, 8, products.shape[-1]), axis=0)
        add(rows, back)

    each(5, chunk)
    return jnp.sum(total[...], axis=0, keepdims=True)


def feed_forward(inputs, gain, w_in, w_out, nrm, act, slope, result):
    norm_rows(inputs, gain, nrm)

    def up(j):
        at = part(j, 256)
        hidden = dot(nrm[...], w_in[:, at])
        sig = jax.nn.sigmoid(hidden)
        active = hidden * sig
        act[:, at] = low(active)
        slope[:, at] = low(sig + active * (1.0 - sig))

    each(FF // 256, up)

    def down(j):
        at = part(j, 256)
        result[:, at] = inputs[:, at].astype(F32) + 0.5 * dot(act[...], w_out[:, at])

    each(2, down)


def feed_back(dout, w_in, w_out, nrm, act, slope, dhid, dnrm, stage, g_in, g_out):
    def up(j):
        at = part(j, 256)
        grad = dot_t(dout[...], w_out[at, :])
        dhid[:, at] = low(grad * slope[:, at].astype(F32))

    each(FF // 256, up)
    weight_rows(act, dout, 8, g_out)

    def down(j):
        at = part(j, 256)
        dnrm[:, at] = dot_t(dhid[...], w_in[at, :])

    each(2, down)
    weight_columns(nrm, dhid, 4, stage, g_in)


def first_kernel(coords, frames, *refs):
    sources, refs = refs[:32], refs[32:]
    x1, nrm, act, slope, w_in_out, w_out_out, small, taps, raw, w_in, w_out, stage, low_small, sems, out_sems = refs
    loads = Loads(
        coords,
        sources,
        [(BLOCK["small"], 1, low_small, SMALL), (BLOCK["ffa_in"], 4, raw, ROW), (BLOCK["ffa_out"], 4, w_out, ROW)],
        sems,
    )
    loads.wait(0)
    small[...] = low_small[...].astype(F32)
    taps[...] = jnp.zeros_like(taps)
    for tap in range(KER):
        for c in range(5):
            taps[tap : tap + 1, ROW * c : ROW * c + ROW] = small[TAPS_AT + 5 * tap + c : TAPS_AT + 5 * tap + c + 1, :]
    loads.wait(1)
    split_columns(raw, w_in, 4, stage)
    keep_in = pltpu.make_async_copy(w_in, w_in_out, out_sems.at[0])
    keep_in.start()
    loads.wait(2)
    keep_out = pltpu.make_async_copy(w_out, w_out_out, out_sems.at[1])
    keep_out.start()
    feed_forward(frames, small[0:1, :], w_in, w_out, nrm, act, slope, x1)
    keep_in.wait()
    keep_out.wait()


def bucket_map():
    entry = lax.broadcasted_iota(jnp.int32, (2 * ROW, ROW), 0) // H
    far = lax.broadcasted_iota(jnp.int32, (2 * ROW, ROW), 1)
    far = jnp.where(far >= ROW // 2, far - ROW, far)
    bucket = jnp.clip(far, -(RELW // 2), RELW // 2 - 1) + RELW // 2
    return (entry == bucket).astype(F32)


def own_entries(flat):
    entry = lax.broadcasted_iota(jnp.int32, (H, 2 * ROW), 1)
    head = lax.broadcasted_iota(jnp.int32, (H, 2 * ROW), 0)
    return jnp.where(lax.rem(entry, H) == head, flat, 0.0)


def attention_kernel(coords, length, x1, small, *refs):
    sources, refs = refs[:32], refs[32:]
    a_out, nrm, qkv, probs, ctx, w_qkv_out, w_att_out, raw, w_qkv, w_att, stage, bias, sems, out_sems = refs
    loads = Loads(coords, sources, [(BLOCK["qkv"], 3, raw, ROW), (BLOCK["att_out"], 1, w_att, ROW)], sems)
    norm_rows(x1, small[1:2, :], nrm)
    qkv[SLOTS:KEYS, :] = jnp.zeros((KEYS - SLOTS, 3 * D), BF16)
    flat = jnp.concatenate([small[REL_AT : REL_AT + 1, :], small[REL_AT + 1 : REL_AT + 2, :]], axis=1)
    bias[...] = dot(low(own_entries(jnp.broadcast_to(flat, (H, 2 * ROW)))), low(bucket_map()))
    loads.wait(0)
    split_columns(raw, w_qkv, 3, stage)
    keep_qkv = pltpu.make_async_copy(w_qkv, w_qkv_out, out_sems.at[0])
    keep_qkv.start()
    loads.wait(1)
    keep_att = pltpu.make_async_copy(w_att, w_att_out, out_sems.at[1])
    keep_att.start()

    def project(j):
        at = part(j, 256)
        qkv[0:SLOTS, at] = low(dot(nrm[...], w_qkv[:, at]))

    each(3 * D // 256, project)
    valid = lax.broadcasted_iota(jnp.int32, (1, KEYS), 1) < length[0]
    first_half = lax.broadcasted_iota(jnp.int32, (1, 128), 1) < HS

    def heads(pair):
        queries = qkv[0:SLOTS, part(pair, 128)]
        keys = qkv[:, part(pair + 4, 128)]
        values = qkv[:, part(pair + 8, 128)]
        outs = []
        for odd in range(2):
            head = 2 * pair + odd
            mine = jnp.where(first_half if odd == 0 else jnp.logical_not(first_half), queries, jnp.zeros_like(queries))
            spread = jnp.broadcast_to(bias[pl.ds(head, 1), :], (SLOTS, ROW))
            spread = pltpu.roll(spread, 0, 1, stride=1, stride_axis=0)[:, 0:KEYS]
            scores = jnp.where(valid, dot_t(mine, keys) * HS ** (-0.5) + spread, MASK_FILL)
            shifted = jnp.exp(scores - jnp.max(scores, axis=-1, keepdims=True))
            chances = low(shifted / jnp.sum(shifted, axis=-1, keepdims=True))
            probs[head] = chances
            outs.append(dot(chances, values))
        ctx[:, part(pair, 128)] = low(jnp.where(first_half, outs[0], outs[1]))

    each(H // 2, heads)

    def project_out(j):
        at = part(j, 256)
        a_out[:, at] = dot(ctx[...], w_att[:, at])

    each(2, project_out)
    keep_qkv.wait()
    keep_att.wait()


def convolve(padded, taps, tap_lane, width, finish):
    def chunk(j):
        at = part(j, 128)
        total = jnp.zeros((SLOTS, 128), F32)
        for tap in range(KER):
            total = total + taps[tap : tap + 1, part(j + tap_lane // 128, 128)] * padded[tap + 1 : tap + 1 + SLOTS, at]
        finish(at, total)

    each(width // 128, chunk)


def convolve_back(grads, padded, taps, tap_lane, width, dtaps, finish):
    def chunk(j):
        at = part(j, 128)
        lane = part(j + tap_lane // 128, 128)
        total = jnp.zeros((SLOTS, 128), F32)
        for tap in range(KER):
            total = total + taps[tap : tap + 1, lane] * grads[KER - tap : KER - tap + SLOTS, at]
        finish(at, total)
        own = grads[PAD : PAD + SLOTS, at]
        for tap in range(KER):
            product = own * padded[tap + 1 : tap + 1 + SLOTS, at]
            dtaps[tap : tap + 1, lane] = jnp.sum(product, axis=0, keepdims=True)

    each(width // 128, chunk)


def clear_margins(padded):
    padded[0:PAD, :] = jnp.zeros((PAD, padded.shape[1]), F32)
    padded[PAD + SLOTS : PADDED, :] = jnp.zeros((PAD, padded.shape[1]), F32)


def gating_kernel(coords, length, x1, small, taps, *refs):
    sources, refs = refs[:32], refs[32:]
    c_out, nrm, ug, slope, gpad, cv, gated, w_cg_out, w_co_out, raw, w_cg, w_co, stage, hid, sems, out_sems = refs
    loads = Loads(coords, sources, [(BLOCK["cg_in"], 6, raw, ROW), (BLOCK["cg_out"], 3, w_co, ROW)], sems)
    norm_rows(x1, small[2:3, :], nrm)
    clear_margins(gpad)
    loads.wait(0)
    split_columns(raw, w_cg, 6, stage)
    keep_cg = pltpu.make_async_copy(w_cg, w_cg_out, out_sems.at[0])
    keep_cg.start()

    def up(j):
        at = part(j, 256)
        hid[...] = dot(nrm[...], w_cg[:, at])

        def rows(k):
            row = part(k, 32)
            hidden = hid[row, :]
            half = 0.5 + 0.5 * erf(hidden * (2.0**-0.5))
            ug[row, at] = hidden * half
            slope[row, at] = low(half + hidden * jnp.exp(-0.5 * hidden * hidden) * ((2.0 * math.pi) ** -0.5))

        each(5, rows)

    each(CG // 256, up)

    def gate(k):
        hat, _ = normed(ug[part(k, 16), GATE:])
        valid = valid_rows(k, 16, length[0])
        for c in range(3):
            at = slice(ROW * c, ROW * c + ROW)
            gpad[part(k + 1, 16), at] = hat[:, at] * small[5 + c : 6 + c, :] * valid

    each(SLOTS // 16, gate)

    def finish(at, total):
        cv[:, at] = low(total)
        gated[:, at] = low(ug[:, at] * total)

    convolve(gpad, taps, 0, GATE, finish)
    loads.wait(1)
    keep_co = pltpu.make_async_copy(w_co, w_co_out, out_sems.at[1])
    keep_co.start()

    def down(j):
        at = part(j, 256)
        c_out[:, at] = dot(gated[...], w_co[:, at])

    each(2, down)
    keep_cg.wait()
    keep_co.wait()


def last_kernel(coords, length, a_out, c_out, x1, cot, small, taps, *refs):
    sources, refs = refs[:32], refs[32:]
    out, dx, mixed, mpad, w_merge_out, sgrad, grads = refs[:7]
    (
        raw, w_merge, w_in, w_out, stage, x2, x3, nrm, act, slope, dout, dhid, dnrm, total, g_in, g_out,
        sems, out_sems,
    ) = refs[7:]
    loads = Loads(
        coords,
        sources,
        [(BLOCK["merge"], 2, w_merge, ROW), (BLOCK["ffb_in"], 4, raw, ROW), (BLOCK["ffb_out"], 4, w_out, ROW)],
        sems,
    )
    clear_margins(mpad)

    def join(k):
        row = part(k, 32)
        valid = valid_rows(k, 32, length[0])
        padded = pl.ds(pl.multiple_of(k * 32 + PAD, 16), 32)
        mpad[padded, 0:D] = a_out[row, :] * valid
        mpad[padded, D:] = c_out[row, :] * valid

    each(5, join)

    def finish_with(source, shift):
        def finish(at, value):
            mixed[:, at] = low(source[:, part_of(at, shift)] + value)

        return finish

    def part_of(at, shift):
        return pl.ds(pl.multiple_of(at.start - shift, 128), 128)

    def chunk(j):
        at = part(j, 128)
        value = jnp.zeros((SLOTS, 128), F32)
        for tap in range(KER):
            value = value + taps[tap : tap + 1, part(j + GATE // 128, 128)] * mpad[tap + 1 : tap + 1 + SLOTS, at]

        @pl.when(j < 4)
        def _():
            mixed[:, at] = low(a_out[:, at] + value)

        @pl.when(j >= 4)
        def _():
            mixed[:, at] = low(c_out[:, part(j - 4, 128)] + value)

    each(2 * D // 128, chunk)
    loads.wait(0)
    keep = pltpu.make_async_copy(w_merge, w_merge_out, out_sems.at[8])
    keep.start()

    def merge(j):
        at = part(j, 256)
        x2[:, at] = x1[:, at] + dot(mixed[...], w_merge[:, at])

    each(2, merge)
    loads.wait(1)
    split_columns(raw, w_in, 4, stage)
    loads.wait(2)
    feed_forward(x2, small[3:4, :], w_in, w_out, nrm, act, slope, x3)
    sgrad[...] = jnp.zeros_like(sgrad)
    total[...] = jnp.zeros_like(total)
    gain = small[4:5, :]

    def final(k):
        row = part(k, 32)
        valid = valid_rows(k, 32, length[0])
        values = x3[row, :]
        hat, _ = normed(values)
        out[row, :] = low(hat * gain * valid)
        back, products = norm_back(values, gain, cot[row, :].astype(F32) * valid)
        total[...] += jnp.sum(products.reshape(4, 8, D), axis=0)
        dx[row, :] = back
        dout[row, :] = low(0.5 * back)

    each(5, final)
    sgrad[4:5, :] = jnp.sum(total[...], axis=0, keepdims=True)
    feed_back(dout, w_in, w_out, nrm, act, slope, dhid, dnrm, stage, g_in, g_out)
    emits = Emits(coords, grads, out_sems)
    for at in range(4):
        emits.put(BLOCK["ffb_out"] + at, g_out.at[ROW * at : ROW * at + ROW])
    for at in range(4):
        emits.put(BLOCK["ffb_in"] + at, g_in.at[ROW * at : ROW * at + ROW])

    def add(rows, back):
        dx[rows, :] += back

    sgrad[3:4, :] = norm_rows_back(x2, small[3:4, :], dnrm, total, add)
    keep.wait()
    emits.wait()


def back_gating_kernel(
    coords, length, dx_in, mixed, mpad, x1, nrm, ug, slope, gpad, cv, gated, small, taps, sgrad_in, w_merge, w_co, w_cg,
    grads_in, *refs
):
    dx, datt, sgrad, grads = refs[:4]
    dgrad, djoin, dpad, dgate, dhid, dnrm, dtaps, total, total_gate, stage, g_merge, g_co, g_cg, out_sems = refs[4:]
    emits = Emits(coords, grads, out_sems)
    sgrad[...] = sgrad_in[...]
    clear_margins(dpad)

    def lower(k):
        dgrad[part(k, 32), :] = low(dx_in[part(k, 32), :])

    each(5, lower)

    def merge(j):
        at = part(j, 256)
        dpad[PAD : PAD + SLOTS, at] = dot_t(dgrad[...], w_merge[at, :])

    each(2 * D // 256, merge)
    weight_rows(mixed, dgrad, 4, g_merge)
    for at in range(2):
        emits.put(BLOCK["merge"] + at, g_merge.at[ROW * at : ROW * at + ROW])

    def finish(at, value):
        row_valid = valid_rows(0, SLOTS, length[0])
        djoin[:, at] = low(dpad[PAD : PAD + SLOTS, at] + value * row_valid)

    convolve_back(dpad, mpad, taps, GATE, 2 * D, dtaps, finish)
    datt[...] = djoin[:, 0:D]

    def gate(j):
        at = part(j, 256)
        value = dot_t(djoin[:, D:], w_co[at, :])
        dhid[:, at] = low(value * cv[:, at].astype(F32) * slope[:, at].astype(F32))
        dpad[PAD : PAD + SLOTS, at] = value * ug[:, at]

    each(GATE // 256, gate)

    def co_rows(k):
        lhs = gated[:, part(k, 256)]
        for at in range(2):
            place = slice(256 * at, 256 * at + 256)
            g_co[part(k, 256), place] = low(t_dot(lhs, djoin[:, D + 256 * at : D + 256 * at + 256]))

    each(6, co_rows)
    for at in range(3):
        emits.put(BLOCK["cg_out"] + at, g_co.at[ROW * at : ROW * at + ROW])

    def finish_gate(at, value):
        dgate[:, at] = value * valid_rows(0, SLOTS, length[0])

    convolve_back(dpad, gpad, taps, 0, GATE, dtaps, finish_gate)
    gain = jnp.concatenate([small[5:6, :], small[6:7, :], small[7:8, :]], axis=1)
    total_gate[...] = jnp.zeros_like(total_gate)

    def gate_norm(k):
        row = part(k, 16)
        back, products = norm_back(ug[row, GATE:], gain, dgate[row, :])
        total_gate[...] += products[0:8, :] + products[8:16, :]
        dhid[row, GATE:] = low(back * slope[row, GATE:].astype(F32))

    each(SLOTS // 16, gate_norm)
    gain_grad = jnp.sum(total_gate[...], axis=0, keepdims=True)
    for c in range(3):
        sgrad[5 + c : 6 + c, :] = gain_grad[:, ROW * c : ROW * c + ROW]
    for tap in range(KER):
        for c in range(5):
            at = TAPS_AT + 5 * tap + c
            sgrad[at : at + 1, :] = dtaps[tap : tap + 1, ROW * c : ROW * c + ROW]

    def down(j):
        at = part(j, 256)
        dnrm[:, at] = dot_t(dhid[...], w_cg[at, :])

    each(2, down)
    weight_columns(nrm, dhid, 6, stage, g_cg)
    for at in range(6):
        emits.put(BLOCK["cg_in"] + at, g_cg.at[ROW * at : ROW * at + ROW])

    def add(rows, back):
        dx[rows, :] = dx_in[rows, :] + back

    sgrad[2:3, :] = norm_rows_back(x1, small[2:3, :], dnrm, total, add)
    emits.wait()


def back_attention_kernel(
    coords, dx_in, datt, x1, nrm, qkv, probs, ctx, small, sgrad_in, w_qkv, w_att, grads_in, *refs
):
    dx, sgrad, grads, dctx, dqkv, dnrm, total, stage, sums, g_qkv, g_att, out_sems = refs
    emits = Emits(coords, grads, out_sems)
    sgrad[...] = sgrad_in[...]

    def project(j):
        at = part(j, 256)
        dctx[:, at] = low(dot_t(datt[...], w_att[at, :]))

    each(2, project)
    weight_rows(ctx, datt, 2, g_att)
    emits.put(BLOCK["att_out"], g_att)
    first_half = lax.broadcasted_iota(jnp.int32, (1, 128), 1) < HS
    at_row = lax.broadcasted_iota(jnp.int32, (SLOTS, SLOTS), 0)
    at_column = lax.broadcasted_iota(jnp.int32, (SLOTS, SLOTS), 1)
    flip = low((at_row + at_column == SLOTS - 1).astype(F32))

    def heads(pair):
        queries = qkv[0:SLOTS, part(pair, 128)]
        keys = qkv[:, part(pair + 4, 128)]
        values = qkv[:, part(pair + 8, 128)]
        context = dctx[:, part(pair, 128)]
        q_parts, k_parts, v_parts = [], [], []
        for odd in range(2):
            head = 2 * pair + odd
            half = first_half if odd == 0 else jnp.logical_not(first_half)
            chances = probs[head]
            v_parts.append(t_dot(chances, context)[0:SLOTS])
            wide_chances = chances.astype(F32)
            chance_grad = dot_t(jnp.where(half, context, jnp.zeros_like(context)), values)
            inner = jnp.sum(wide_chances * chance_grad, axis=-1, keepdims=True)
            score_grad = low(wide_chances * (chance_grad - inner))
            q_parts.append(dot(score_grad, keys))
            k_parts.append(t_dot(score_grad, queries)[0:SLOTS])
            wide = jnp.concatenate([dot(flip, score_grad), jnp.zeros((SLOTS, ROW - KEYS), F32)], axis=1)
            wide = pltpu.roll(wide, ROW - SLOTS + 1, 1, stride=1, stride_axis=0)
            sums[pl.ds(head, 1), :] = jnp.sum(wide, axis=0, keepdims=True)
        scale = HS ** (-0.5)
        dqkv[:, part(pair, 128)] = low(jnp.where(first_half, q_parts[0], q_parts[1]) * scale)
        dqkv[:, part(pair + 4, 128)] = low(jnp.where(first_half, k_parts[0], k_parts[1]) * scale)
        dqkv[:, part(pair + 8, 128)] = low(jnp.where(first_half, v_parts[0], v_parts[1]))

    each(H // 2, heads)

    def down(j):
        at = part(j, 256)
        dnrm[:, at] = dot_t(dqkv[...], w_qkv[at, :])

    each(2, down)
    weight_columns(nrm, dqkv, 3, stage, g_qkv)
    for at in range(3):
        emits.put(BLOCK["qkv"] + at, g_qkv.at[ROW * at : ROW * at + ROW])

    def add(rows, back):
        dx[rows, :] = dx_in[rows, :] + back

    sgrad[1:2, :] = norm_rows_back(x1, small[1:2, :], dnrm, total, add)
    by_entry = lax.dot_general(
        sums[...],
        bucket_map(),
        (((1,), (1,)), ((), ())),
        precision=lax.Precision.HIGHEST,
        preferred_element_type=F32,
    )
    flat = jnp.sum(own_entries(by_entry), axis=0, keepdims=True)
    sgrad[REL_AT : REL_AT + 1, :] = flat[:, 0:ROW]
    sgrad[REL_AT + 1 : REL_AT + 2, :] = flat[:, ROW:]
    emits.wait()


def back_first_kernel(coords, dx_in, frames, nrm, act, slope, small, sgrad_in, w_in, w_out, grads_in, *refs):
    fgrad, gains, grads, dout, dhid, dnrm, total, stage, g_in, g_out, g_small, out_sems = refs
    emits = Emits(coords, grads, out_sems)

    def lower(k):
        dout[part(k, 32), :] = low(0.5 * dx_in[part(k, 32), :])

    each(5, lower)
    feed_back(dout, w_in, w_out, nrm, act, slope, dhid, dnrm, stage, g_in, g_out)
    for at in range(4):
        emits.put(BLOCK["ffa_out"] + at, g_out.at[ROW * at : ROW * at + ROW])
    for at in range(4):
        emits.put(BLOCK["ffa_in"] + at, g_in.at[ROW * at : ROW * at + ROW])

    def add(rows, back):
        fgrad[rows, :] = low(dx_in[rows, :] + back)

    gain_grad = norm_rows_back(frames, small[0:1, :], dnrm, total, add)
    gains[...] = sgrad_in[0:8, :]
    gains[0:1, :] = gain_grad
    g_small[0:SMALL, :] = low(sgrad_in[...])
    g_small[0:16, :] = low(jnp.concatenate([gains[...], sgrad_in[8:16, :]], axis=0))
    g_small[SMALL:ROW, :] = jnp.zeros((ROW - SMALL, ROW), BF16)
    emits.put(BLOCK["small"], g_small)
    emits.wait()


VM = pl.BlockSpec(memory_space=pltpu.VMEM)
SM = pl.BlockSpec(memory_space=pltpu.SMEM)
ANY = pl.BlockSpec(memory_space=pl.ANY)
GRADS = ((32, ROW, ROW), BF16)


def call(kernel, name, ins, outs, scratch, aliases=None):
    return pl.pallas_call(
        kernel,
        name=name,
        in_specs=[space for space, _ in ins],
        out_specs=[space for space, _ in outs],
        out_shape=[jax.ShapeDtypeStruct(*kind) for _, kind in outs],
        scratch_shapes=[
            pltpu.SemaphoreType.DMA((each_one,)) if isinstance(each_one, int) else pltpu.VMEM(*each_one)
            for each_one in scratch
        ],
        input_output_aliases=aliases or {},
        compiler_params=pltpu.CompilerParams(vmem_limit_bytes=56 * 2**20),
    )(*[array for _, array in ins])


def layer(coords, length, frames, cot, blocks):
    sources = [(ANY, block) for block in blocks]
    place = (SM, coords)
    wide = ((SLOTS, D), F32)
    thin = ((SLOTS, D), BF16)
    ff = ((SLOTS, FF), BF16)
    x1, nrm_a, act_a, slope_a, w_ffa_in, w_ffa_out, small, taps = call(
        first_kernel,
        "ffa_forward",
        [place, (VM, frames)] + sources,
        [
            (VM, wide),
            (VM, thin),
            (VM, ff),
            (VM, ff),
            (ANY, ((D, FF), BF16)),
            (ANY, ((FF, D), BF16)),
            (VM, ((SMALL, ROW), F32)),
            (VM, ((32, 5 * ROW), F32)),
        ],
        [
            ((FF, D), BF16),
            ((D, FF), BF16),
            ((FF, D), BF16),
            ((4, 128 * 4, 128), F32),
            ((SMALL, ROW), BF16),
            9,
            2,
        ],
    )
    a_out, nrm_t, qkv, probs, ctx, w_qkv, w_att = call(
        attention_kernel,
        "attention_forward",
        [place, (SM, length), (VM, x1), (VM, small)] + sources,
        [
            (VM, wide),
            (VM, thin),
            (VM, ((KEYS, 3 * D), BF16)),
            (VM, ((H, SLOTS, KEYS), BF16)),
            (VM, thin),
            (ANY, ((D, 3 * D), BF16)),
            (ANY, ((D, D), BF16)),
        ],
        [
            ((3 * D, D), BF16),
            ((D, 3 * D), BF16),
            ((D, D), BF16),
            ((4, 128 * 3, 128), F32),
            ((H, ROW), F32),
            4,
            2,
        ],
    )
    c_out, nrm_c, ug, slope_c, gpad, cv, gated, w_cg, w_co = call(
        gating_kernel,
        "gating_forward",
        [place, (SM, length), (VM, x1), (VM, small), (VM, taps)] + sources,
        [
            (VM, wide),
            (VM, thin),
            (VM, ((SLOTS, CG), F32)),
            (VM, ((SLOTS, CG), BF16)),
            (VM, ((PADDED, GATE), F32)),
            (VM, ((SLOTS, GATE), BF16)),
            (VM, ((SLOTS, GATE), BF16)),
            (ANY, ((D, CG), BF16)),
            (ANY, ((GATE, D), BF16)),
        ],
        [
            ((CG, D), BF16),
            ((D, CG), BF16),
            ((GATE, D), BF16),
            ((4, 128 * 6, 128), F32),
            ((SLOTS, 256), F32),
            9,
            2,
        ],
    )
    out, dx2, mixed, mpad, w_merge, sgrad, grads = call(
        last_kernel,
        "merge_ffb",
        [place, (SM, length), (VM, a_out), (VM, c_out), (VM, x1), (VM, cot), (VM, small), (VM, taps)] + sources,
        [
            (VM, thin),
            (VM, wide),
            (VM, ((SLOTS, 2 * D), BF16)),
            (VM, ((PADDED, 2 * D), F32)),
            (ANY, ((2 * D, D), BF16)),
            (VM, ((SMALL, ROW), F32)),
            (ANY, GRADS),
        ],
        [
            ((FF, D), BF16),
            ((2 * D, D), BF16),
            ((D, FF), BF16),
            ((FF, D), BF16),
            ((4, 128 * 4, 128), F32),
            wide,
            wide,
            thin,
            ff,
            ff,
            thin,
            ff,
            wide,
            ((8, D), F32),
            ((FF, D), BF16),
            ((FF, D), BF16),
            10,
            9,
        ],
    )
    dx1, datt, sgrad, grads = call(
        back_gating_kernel,
        "gating_backward",
        [place, (SM, length)]
        + [(VM, a) for a in (dx2, mixed, mpad, x1, nrm_c, ug, slope_c, gpad, cv, gated, small, taps, sgrad)]
        + [(VM, w_merge), (VM, w_co), (VM, w_cg), (ANY, grads)],
        [(VM, wide), (VM, thin), (VM, ((SMALL, ROW), F32)), (ANY, GRADS)],
        [
            thin,
            ((SLOTS, 2 * D), BF16),
            ((PADDED, GATE), F32),
            ((SLOTS, GATE), F32),
            ((SLOTS, CG), BF16),
            wide,
            ((32, 5 * ROW), F32),
            ((8, D), F32),
            ((8, GATE), F32),
            ((4, 128 * 6, 128), F32),
            ((2 * D, D), BF16),
            ((GATE, D), BF16),
            ((CG, D), BF16),
            11,
        ],
        {18: 3},
    )
    dx1, sgrad, grads = call(
        back_attention_kernel,
        "attention_backward",
        [place]
        + [(VM, a) for a in (dx1, datt, x1, nrm_t, qkv, probs, ctx, small, sgrad)]
        + [(VM, w_qkv), (VM, w_att), (ANY, grads)],
        [(VM, wide), (VM, ((SMALL, ROW), F32)), (ANY, GRADS)],
        [
            thin,
            ((SLOTS, 3 * D), BF16),
            wide,
            ((8, D), F32),
            ((4, 128 * 3, 128), F32),
            ((H, ROW), F32),
            ((3 * D, D), BF16),
            ((D, D), BF16),
            4,
        ],
        {12: 2},
    )
    fgrad, gains, grads = call(
        back_first_kernel,
        "ffa_backward",
        [place]
        + [(VM, a) for a in (dx1, frames, nrm_a, act_a, slope_a, small, sgrad)]
        + [(VM, w_ffa_in), (VM, w_ffa_out), (ANY, grads)],
        [(VM, thin), (VM, ((8, ROW), F32)), (ANY, GRADS)],
        [
            thin,
            ff,
            wide,
            ((8, D), F32),
            ((4, 128 * 4, 128), F32),
            ((FF, D), BF16),
            ((FF, D), BF16),
            ((ROW, ROW), BF16),
            9,
        ],
        {10: 2},
    )
    return out, fgrad, gains, grads


def segment_bounds():
    bounds = [0]
    for extent in segment_shapes():
        bounds.append(bounds[-1] + math.prod(extent))
    return bounds


def block_rows(device_count):
    total_rows = -(-segment_bounds()[-1] // ROW)
    step = 16 * device_count
    return -(-total_rows // step) * 16


def align_shard(low_shard, shard_size, rows):
    devices = lax.axis_size("dp") * lax.axis_size("fsdp")
    me = lax.axis_index(AXES)
    block = rows * ROW
    lead = block - shard_size
    pieces = [low_shard]
    have = shard_size
    need = lead * (devices - 1) + block
    hop = 1
    while have < need:
        part = min(shard_size, need - have)
        pairs = [(i, i - hop) for i in range(hop, devices)]
        pieces.append(lax.ppermute(low_shard[:part], AXES, pairs))
        have = have + part
        hop = hop + 1
    return lax.dynamic_slice(jnp.concatenate(pieces), (me * lead,), (block,)).reshape(rows, ROW)


def unalign_block(block_sum, shard_size):
    devices = lax.axis_size("dp") * lax.axis_size("fsdp")
    me = lax.axis_index(AXES)
    rows = block_sum.shape[0]
    block = rows * ROW
    lead = block - shard_size
    flat = block_sum.reshape(-1)
    pieces = [flat]
    have = block
    need = lead * (devices - 1) + block
    hop = 1
    while have < need:
        part = min(block, need - have)
        pairs = [(i, i + hop) for i in range(devices - hop)]
        pieces.insert(0, lax.ppermute(flat[block - part :], AXES, pairs))
        have = have + part
        hop = hop + 1
    start = have - block - me * lead
    return lax.dynamic_slice(jnp.concatenate(pieces), (start,), (shard_size,))


def pair_lists():
    ring = [(i, (i + 2) % 8) for i in range(8)]
    across_x = [(i, i ^ 1) for i in range(8)]
    across_y = [(i, i ^ 2) for i in range(4)]
    across_core = [(i, i ^ 1) for i in range(4)]
    return ring, across_x, across_y, across_core


def fast_mesh():
    return lax.axis_size("dp") == 4 and lax.axis_size("fsdp") == 8


def gather_blocks(block):
    rows = block.shape[0]
    if not fast_mesh():
        whole = lax.all_gather(block, AXES, axis=0, tiled=True).reshape(32, ROW, ROW)
        order = [source_block((0, 0, 0, 0), at) for at in range(32)]
        return [whole[at] for at in order]
    ring, across_x, across_y, across_core = pair_lists()
    own = [block]
    for _ in range(3):
        own.append(lax.ppermute(own[-1], "fsdp", ring))
    by_x = [lax.ppermute(each_one, "fsdp", across_x) for each_one in own]
    by_y = [lax.ppermute(each_one, "dp", across_y) for each_one in own]
    both = [lax.ppermute(each_one, "fsdp", across_x) for each_one in by_y[:2]]
    both = both + [lax.ppermute(each_one, "dp", across_y) for each_one in by_x[2:]]
    near = own + by_x + by_y + both
    far = [lax.ppermute(each_one, "dp", across_core) for each_one in near]
    return near + far


def added(*parts):
    total = parts[0].astype(jnp.float32)
    for part in parts[1:]:
        total = total + part.astype(jnp.float32)
    return total


def scatter_blocks(grads, coords):
    if not fast_mesh():
        devices = lax.axis_size("dp") * lax.axis_size("fsdp")
        order = [gradient_slot((0, 0, 0, 0), block) for block in range(32)]
        rows = jnp.concatenate([grads[at] for at in order]).reshape(devices, -1, ROW)
        return lax.psum_scatter(rows, AXES, scatter_dimension=0).astype(F32)
    ring, across_x, across_y, across_core = pair_lists()
    z = coords[2]

    def core_sum(kind):
        theirs = lax.ppermute(grads[16 + 4 * kind : 20 + 4 * kind], "dp", across_core)
        return low(added(grads[4 * kind : 4 * kind + 4], theirs))

    diagonal = core_sum(3)
    to_x = core_sum(1)
    to_y = core_sum(2)
    mine = core_sum(0)
    from_x = lax.ppermute(diagonal[:2], "fsdp", across_x)
    from_y = lax.ppermute(diagonal[2:], "dp", across_y)
    to_y = jnp.concatenate([low(added(to_y[:2], from_x)), to_y[2:]])
    to_x = jnp.concatenate([to_x[:2], low(added(to_x[2:], from_y))])

    def at(array, back):
        return lax.dynamic_index_in_dim(array, lax.rem(z + 4 - back, 4), 0, keepdims=False)

    running = None
    for back in (1, 2, 3, 0):
        parts = [
            at(mine, back),
            lax.ppermute(at(to_x, back), "fsdp", across_x),
            lax.ppermute(at(to_y, back), "dp", across_y),
        ]
        if running is not None:
            parts.append(lax.ppermute(running, "fsdp", ring))
        running = added(*parts)
        if back:
            running = low(running)
    return running


def sum_everywhere(vector):
    if not fast_mesh():
        return lax.psum(vector, AXES)
    _, across_x, across_y, across_core = pair_lists()
    near_z = [(i, i ^ 2) for i in range(8)]
    far_z = [(i, i ^ 4) for i in range(8)]
    for axis, pairs in (
        ("dp", across_core),
        ("fsdp", across_x),
        ("dp", across_y),
        ("fsdp", near_z),
        ("fsdp", far_z),
    ):
        vector = vector + lax.ppermute(vector, axis, pairs)
    return vector


def most_segments(shard_size, devices):
    bounds = segment_bounds()
    most = 1
    for at in range(devices):
        low, high = at * shard_size, (at + 1) * shard_size
        most = max(most, sum(1 for b in bounds[1:-1] if low < b < high) + 1)
    return most


def shards(frames, lengths, cotangent, params, first_moment, second_moment):
    shard_size = params.shape[0]
    devices = lax.axis_size("dp") * lax.axis_size("fsdp")
    me = lax.axis_index(AXES)
    rows = block_rows(devices)
    if fast_mesh():
        dp, fsdp = lax.axis_index("dp"), lax.axis_index("fsdp")
        coords = jnp.stack([dp // 2, dp % 2, fsdp // 2, fsdp % 2]).astype(jnp.int32)
    else:
        coords = jnp.zeros((4,), jnp.int32)
    blocks = gather_blocks(align_shard(low(params), shard_size, rows))
    result, frames_grad, gains, grads = layer(coords, lengths, frames[0], cotangent[0], blocks)
    block_sum = scatter_blocks(grads, coords)
    grad_shard = unalign_block(low(block_sum), shard_size).astype(F32)
    new_first = BETA_FIRST * first_moment + (1.0 - BETA_FIRST) * grad_shard
    new_second = BETA_SECOND * second_moment + (1.0 - BETA_SECOND) * grad_shard * grad_shard
    first_hat = new_first / (1.0 - BETA_FIRST**STEP)
    second_hat = new_second / (1.0 - BETA_SECOND**STEP)
    update = first_hat / (jnp.sqrt(second_hat) + ADAM_EPS) + WEIGHT_DECAY * params
    count = len(segment_shapes())
    bounds = segment_bounds()
    spans = most_segments(shard_size, devices)
    shard_low = me * shard_size
    first_segment = sum((shard_low >= b).astype(jnp.int32) for b in bounds[1:-1])
    table = jnp.asarray(bounds[1:] + [bounds[-1]] * spans, jnp.int32)
    ends = lax.dynamic_slice(table, (first_segment,), (spans,)) - shard_low
    positions = lax.iota(jnp.int32, shard_size)

    def segment_sums(values):
        total = jnp.zeros((count + spans,), jnp.float32)
        sums = []
        low = jnp.int32(0)
        for at in range(spans):
            inside = (positions >= low) & (positions < ends[at])
            sums.append(jnp.sum(jnp.where(inside, values, 0.0)))
            low = ends[at]
        return lax.dynamic_update_slice(total, jnp.stack(sums), (first_segment,))[:count]

    parts = jnp.concatenate(
        [segment_sums(params * params), segment_sums(update * update), jnp.zeros((8,), jnp.float32)]
    )
    everywhere = sum_everywhere(jnp.concatenate([parts, gains.reshape(-1)]))
    weight_squares = everywhere[:count]
    update_squares = everywhere[count : 2 * count]
    gain_grads = everywhere[parts.shape[0] :]
    weight_norms = jnp.sqrt(weight_squares)
    update_norms = jnp.sqrt(update_squares)
    trust_ratios = weight_norms / (update_norms + ADAM_EPS)
    near_trust = lax.dynamic_slice(
        jnp.concatenate([trust_ratios, jnp.zeros((spans,), jnp.float32)]), (first_segment,), (spans,)
    )
    entry_trust = jnp.broadcast_to(near_trust[spans - 1], (shard_size,))
    for at in range(spans - 2, -1, -1):
        entry_trust = jnp.where(positions < ends[at], near_trust[at], entry_trust)
    new_params = params - LEARN_RATE * entry_trust * update
    return (
        result.reshape(frames.shape),
        frames_grad.reshape(frames.shape),
        new_params,
        new_first,
        new_second,
        weight_norms,
        update_norms,
        trust_ratios,
        gain_grads,
    )


def solution(mesh):
    placed = (
        P(("dp", "fsdp"), None, None),
        P(("dp", "fsdp")),
        P(("dp", "fsdp"), None, None),
        P(("dp", "fsdp")),
        P(("dp", "fsdp")),
        P(("dp", "fsdp")),
    )
    return jax.shard_map(
        shards,
        mesh=mesh,
        in_specs=placed,
        out_specs=(
            P(("dp", "fsdp"), None, None),
            P(("dp", "fsdp"), None, None),
            P(("dp", "fsdp")),
            P(("dp", "fsdp")),
            P(("dp", "fsdp")),
            P(),
            P(),
            P(),
            P(),
        ),
        check_vma=False,
    )
```

```python
import math

import jax
import jax.numpy as jnp
from jax import lax
from jax.experimental import pallas as pl
from jax.experimental.pallas import tpu as pltpu
from jax.sharding import PartitionSpec as P

STEP = 8
BETA_FIRST = 0.5
BETA_SECOND = 0.5
LEARN_RATE = 0.5
WEIGHT_DECAY = 0.01
ADAM_EPS = 1e-06
AXES = ("dp", "fsdp")


def segment_shapes():
    gate_width = CG // 2
    return [
        (D, FF),
        (FF, D),
        (D, 3 * D),
        (D, D),
        (D, CG),
        (gate_width, D),
        (2 * D, D),
        (D, FF),
        (FF, D),
        (5 * D + gate_width,),
        (KER, gate_width + 2 * D),
        (RELW, H),
    ]


D = 512
H = 8
HS = 64
FF = 2048
CG = 3072
KER = 31
RELW = 128
NORM_EPS = 1e-05
MASK_FILL = -1000000000.0
ROW = 512
HALF = ROW // 2
SLOTS = 160
KEYS = 256
PAD = 16
PADDED = SLOTS + 2 * PAD
GATE = CG // 2
BLOCK = {
    "ffa_in": 0,
    "ffa_out": 4,
    "qkv": 8,
    "att_out": 11,
    "cg_in": 12,
    "cg_out": 18,
    "merge": 21,
    "ffb_in": 23,
    "ffb_out": 27,
    "small": 31,
}
TAPS_AT = 8
REL_AT = 8 + 5 * KER
SMALL = 176
F32, BF16 = jnp.float32, jnp.bfloat16


def dot(left, right):
    return lax.dot_general(left, right, (((1,), (0,)), ((), ())), preferred_element_type=F32)


def dot_t(left, right):
    return lax.dot_general(left, right, (((1,), (1,)), ((), ())), preferred_element_type=F32)


def t_dot(left, right):
    return lax.dot_general(left, right, (((0,), (0,)), ((), ())), preferred_element_type=F32)


def low(values):
    return values.astype(BF16)


def each(count, body):
    def step(at, carry):
        body(at)
        return carry

    lax.fori_loop(0, count, step, 0)


def part(at, size):
    return pl.ds(pl.multiple_of(at * size, size), size)


def normed(values):
    centered = values - jnp.mean(values, axis=-1, keepdims=True)
    variance = jnp.mean(centered * centered, axis=-1, keepdims=True)
    scale = lax.rsqrt(variance + NORM_EPS)
    return centered * scale, scale


def valid_rows(at, size, length):
    return (at * size + lax.broadcasted_iota(jnp.int32, (size, 1), 0) < length).astype(F32)


def norm_back(values, gain, grad):
    hat, scale = normed(values)
    inner = grad * gain
    moved = jnp.mean(inner, axis=-1, keepdims=True) + hat * jnp.mean(inner * hat, axis=-1, keepdims=True)
    return scale * (inner - moved), grad * hat


def erf(values):
    at = jnp.clip(values, -4.0, 4.0)
    square = at * at
    top = jnp.full_like(at, -2.72614225801306e-10)
    for factor in (
        2.77068142495902e-08,
        -2.10102402082508e-06,
        -5.69250639462346e-05,
        -7.34990630326855e-04,
        -2.95459980854025e-03,
        -1.60960333262415e-02,
    ):
        top = top * square + factor
    under = jnp.full_like(at, -1.45660718464996e-05)
    for factor in (
        -2.13374055278905e-04,
        -1.68282697438203e-03,
        -7.37332916720468e-03,
        -1.42647390514189e-02,
    ):
        under = under * square + factor
    return at * top / under


PIECES = []
for far_core in range(2):
    for kind in ((0, 0), (0, 1), (1, 0)):
        PIECES += [(far_core, *kind, back, 0, ROW) for back in range(4)]
    for first_row in (0, ROW // 2):
        PIECES += [(far_core, 1, 1, back, first_row, ROW // 2) for back in range(4)]


def source_block(coords, piece):
    y, c, z, x = coords[0], coords[1], coords[2], coords[3]
    yy, cc, xx, zz = y ^ piece[1], c ^ piece[0], x ^ piece[2], (z + 4 - piece[3]) & 3
    return ((yy * 2 + cc) * 4 + zz) * 2 + xx


def gradient_slot(coords, block):
    y, c, x = coords[0], coords[1], coords[3]
    yy, cc, zz, xx = block // 16, (block // 8) % 2, (block // 2) % 4, block % 2
    return 16 * (c ^ cc) + 8 * (y ^ yy) + 4 * (x ^ xx) + zz


class Loads:
    def __init__(self, coords, sources, wanted, sems):
        self.wanted = wanted
        self.source = sources[0]
        self.sems = sems
        for piece, source in zip(PIECES, sources):
            block = source_block(coords, piece)
            first = 0
            for low_block, count, target, rows in wanted:
                here = block - low_block

                @pl.when((here >= 0) & (here < count))
                def _(piece=piece, source=source, target=target, rows=rows, here=here, first=first):
                    for half in range(2):
                        inside = HALF * half - piece[4]
                        size = min(HALF, rows - HALF * half)
                        if 0 <= inside < piece[5] and size > 0:
                            place = pl.ds(pl.multiple_of(here * ROW + HALF * half, 16), size)
                            pltpu.make_async_copy(
                                source.at[inside : inside + size], target.at[place], sems.at[first + 2 * here + half]
                            ).start()

                first = first + 2 * count

    def wait(self, which):
        first = 2 * sum(count for _, count, _, _ in self.wanted[:which])
        _, count, target, rows = self.wanted[which]
        for at in range(count):
            for half in range(2):
                size = min(HALF, rows - HALF * half)
                if size > 0:
                    start = ROW * at + HALF * half
                    pltpu.make_async_copy(
                        self.source.at[0:size], target.at[start : start + size], self.sems.at[first + 2 * at + half]
                    ).wait()


class Emits:
    def __init__(self, coords, target, sems):
        self.coords, self.target, self.sems = coords, target, sems
        self.pending = []

    def put(self, block, values):
        copy = pltpu.make_async_copy(
            values, self.target.at[gradient_slot(self.coords, block)], self.sems.at[len(self.pending)]
        )
        copy.start()
        self.pending.append(copy)

    def wait(self):
        for copy in self.pending:
            copy.wait()


def split_columns(raw, target, wide, stage):
    def chunk(k):
        rows = part(k, 128 * wide)
        for lane in range(4):
            stage[lane, 0 : 128 * wide, :] = raw[rows, lane * 128 : lane * 128 + 128].astype(F32)
        for c in range(wide):
            for lane in range(4):
                place = ROW * c + lane * 128
                target[part(k, 128), place : place + 128] = low(stage[lane, pl.ds(c, 128, stride=wide), :])

    each(4, chunk)


def weight_columns(left, grads, wide, stage, target):
    def chunk(k):
        lhs = left[:, part(k, 128)]
        for at in range(2 * wide):
            value = t_dot(lhs, grads[:, 256 * at : 256 * at + 256])
            for half in range(2):
                lane = (at % 2) * 2 + half
                stage[lane, pl.ds(at // 2, 128, stride=wide), :] = value[:, 128 * half : 128 * half + 128]
        rows = part(k, 128 * wide)
        for lane in range(4):
            target[rows, lane * 128 : lane * 128 + 128] = low(stage[lane, 0 : 128 * wide, :])

    each(4, chunk)


def weight_rows(left, grads, count, target):
    def chunk(k):
        lhs = left[:, part(k, 256)]
        for at in range(2):
            target[part(k, 256), 256 * at : 256 * at + 256] = low(t_dot(lhs, grads[:, 256 * at : 256 * at + 256]))

    each(count, chunk)


def norm_rows(source, gain, target):
    def chunk(k):
        hat, _ = normed(source[part(k, 32), :].astype(F32))
        target[part(k, 32), :] = low(hat * gain)

    each(5, chunk)


def norm_rows_back(values, gain, grad, total, add):
    total[...] = jnp.zeros_like(total)

    def chunk(k):
        rows = part(k, 32)
        back, products = norm_back(values[rows, :].astype(F32), gain, grad[rows, :])
        total[...] += jnp.sum(products.reshape(4, 8, products.shape[-1]), axis=0)
        add(rows, back)

    each(5, chunk)
    return jnp.sum(total[...], axis=0, keepdims=True)


def feed_forward(inputs, gain, w_in, w_out, nrm, act, slope, result):
    norm_rows(inputs, gain, nrm)

    def up(j):
        at = part(j, 256)
        hidden = dot(nrm[...], w_in[:, at])
        sig = jax.nn.sigmoid(hidden)
        active = hidden * sig
        act[:, at] = low(active)
        slope[:, at] = low(sig + active * (1.0 - sig))

    each(FF // 256, up)

    def down(j):
        at = part(j, 256)
        result[:, at] = inputs[:, at].astype(F32) + 0.5 * dot(act[...], w_out[:, at])

    each(2, down)


def feed_back(dout, w_in, w_out, nrm, act, slope, dhid, dnrm, stage, g_in, g_out):
    def up(j):
        at = part(j, 256)
        grad = dot_t(dout[...], w_out[at, :])
        dhid[:, at] = low(grad * slope[:, at].astype(F32))

    each(FF // 256, up)
    weight_rows(act, dout, 8, g_out)

    def down(j):
        at = part(j, 256)
        dnrm[:, at] = dot_t(dhid[...], w_in[at, :])

    each(2, down)
    weight_columns(nrm, dhid, 4, stage, g_in)


def first_kernel(coords, frames, *refs):
    sources, refs = refs[: len(PIECES)], refs[len(PIECES) :]
    x1, nrm, act, slope, w_in_out, w_out_out, small, taps, raw, w_in, w_out, stage, low_small, sems, out_sems = refs
    loads = Loads(
        coords,
        sources,
        [(BLOCK["small"], 1, low_small, SMALL), (BLOCK["ffa_in"], 4, raw, ROW), (BLOCK["ffa_out"], 4, w_out, ROW)],
        sems,
    )
    loads.wait(0)
    small[...] = low_small[...].astype(F32)
    taps[...] = jnp.zeros_like(taps)
    for tap in range(KER):
        for c in range(5):
            taps[tap : tap + 1, ROW * c : ROW * c + ROW] = small[TAPS_AT + 5 * tap + c : TAPS_AT + 5 * tap + c + 1, :]
    loads.wait(1)
    split_columns(raw, w_in, 4, stage)
    keep_in = pltpu.make_async_copy(w_in, w_in_out, out_sems.at[0])
    keep_in.start()
    loads.wait(2)
    keep_out = pltpu.make_async_copy(w_out, w_out_out, out_sems.at[1])
    keep_out.start()
    feed_forward(frames, small[0:1, :], w_in, w_out, nrm, act, slope, x1)
    keep_in.wait()
    keep_out.wait()


def bucket_map():
    entry = lax.broadcasted_iota(jnp.int32, (2 * ROW, ROW), 0) // H
    far = lax.broadcasted_iota(jnp.int32, (2 * ROW, ROW), 1)
    far = jnp.where(far >= ROW // 2, far - ROW, far)
    bucket = jnp.clip(far, -(RELW // 2), RELW // 2 - 1) + RELW // 2
    return (entry == bucket).astype(F32)


def own_entries(flat):
    entry = lax.broadcasted_iota(jnp.int32, (H, 2 * ROW), 1)
    head = lax.broadcasted_iota(jnp.int32, (H, 2 * ROW), 0)
    return jnp.where(lax.rem(entry, H) == head, flat, 0.0)


def attention_kernel(coords, length, x1, small, *refs):
    sources, refs = refs[: len(PIECES)], refs[len(PIECES) :]
    a_out, nrm, qkv, probs, ctx, w_qkv_out, w_att_out, raw, w_qkv, w_att, stage, bias, sems, out_sems = refs
    loads = Loads(coords, sources, [(BLOCK["qkv"], 3, raw, ROW), (BLOCK["att_out"], 1, w_att, ROW)], sems)
    norm_rows(x1, small[1:2, :], nrm)
    qkv[SLOTS:KEYS, :] = jnp.zeros((KEYS - SLOTS, 3 * D), BF16)
    flat = jnp.concatenate([small[REL_AT : REL_AT + 1, :], small[REL_AT + 1 : REL_AT + 2, :]], axis=1)
    bias[...] = dot(low(own_entries(jnp.broadcast_to(flat, (H, 2 * ROW)))), low(bucket_map()))
    loads.wait(0)
    split_columns(raw, w_qkv, 3, stage)
    keep_qkv = pltpu.make_async_copy(w_qkv, w_qkv_out, out_sems.at[0])
    keep_qkv.start()
    loads.wait(1)
    keep_att = pltpu.make_async_copy(w_att, w_att_out, out_sems.at[1])
    keep_att.start()

    def project(j):
        at = part(j, 256)
        qkv[0:SLOTS, at] = low(dot(nrm[...], w_qkv[:, at]))

    each(3 * D // 256, project)
    valid = lax.broadcasted_iota(jnp.int32, (1, KEYS), 1) < length[0]
    first_half = lax.broadcasted_iota(jnp.int32, (1, 128), 1) < HS

    def heads(pair):
        queries = qkv[0:SLOTS, part(pair, 128)]
        keys = qkv[:, part(pair + 4, 128)]
        values = qkv[:, part(pair + 8, 128)]
        outs = []
        for odd in range(2):
            head = 2 * pair + odd
            mine = jnp.where(first_half if odd == 0 else jnp.logical_not(first_half), queries, jnp.zeros_like(queries))
            spread = jnp.broadcast_to(bias[pl.ds(head, 1), :], (SLOTS, ROW))
            spread = pltpu.roll(spread, 0, 1, stride=1, stride_axis=0)[:, 0:KEYS]
            scores = jnp.where(valid, dot_t(mine, keys) * HS ** (-0.5) + spread, MASK_FILL)
            shifted = jnp.exp(scores - jnp.max(scores, axis=-1, keepdims=True))
            chances = low(shifted / jnp.sum(shifted, axis=-1, keepdims=True))
            probs[head] = chances
            outs.append(dot(chances, values))
        ctx[:, part(pair, 128)] = low(jnp.where(first_half, outs[0], outs[1]))

    each(H // 2, heads)

    def project_out(j):
        at = part(j, 256)
        a_out[:, at] = dot(ctx[...], w_att[:, at])

    each(2, project_out)
    keep_qkv.wait()
    keep_att.wait()


def convolve(padded, taps, tap_lane, width, finish):
    def chunk(j):
        at = part(j, 128)
        total = jnp.zeros((SLOTS, 128), F32)
        for tap in range(KER):
            total = total + taps[tap : tap + 1, part(j + tap_lane // 128, 128)] * padded[tap + 1 : tap + 1 + SLOTS, at]
        finish(at, total)

    each(width // 128, chunk)


def convolve_back(grads, padded, taps, tap_lane, width, dtaps, finish):
    def chunk(j):
        at = part(j, 128)
        lane = part(j + tap_lane // 128, 128)
        total = jnp.zeros((SLOTS, 128), F32)
        for tap in range(KER):
            total = total + taps[tap : tap + 1, lane] * grads[KER - tap : KER - tap + SLOTS, at]
        finish(at, total)
        own = grads[PAD : PAD + SLOTS, at]
        for tap in range(KER):
            product = own * padded[tap + 1 : tap + 1 + SLOTS, at]
            dtaps[tap : tap + 1, lane] = jnp.sum(product, axis=0, keepdims=True)

    each(width // 128, chunk)


def clear_margins(padded):
    padded[0:PAD, :] = jnp.zeros((PAD, padded.shape[1]), F32)
    padded[PAD + SLOTS : PADDED, :] = jnp.zeros((PAD, padded.shape[1]), F32)


def gating_kernel(coords, length, x1, small, taps, *refs):
    sources, refs = refs[: len(PIECES)], refs[len(PIECES) :]
    c_out, nrm, ug, slope, gpad, cv, gated, w_cg_out, w_co_out, raw, w_cg, w_co, stage, hid, sems, out_sems = refs
    loads = Loads(coords, sources, [(BLOCK["cg_in"], 6, raw, ROW), (BLOCK["cg_out"], 3, w_co, ROW)], sems)
    norm_rows(x1, small[2:3, :], nrm)
    clear_margins(gpad)
    loads.wait(0)
    split_columns(raw, w_cg, 6, stage)
    keep_cg = pltpu.make_async_copy(w_cg, w_cg_out, out_sems.at[0])
    keep_cg.start()

    def up(j):
        at = part(j, 256)
        hid[...] = dot(nrm[...], w_cg[:, at])

        def rows(k):
            row = part(k, 32)
            hidden = hid[row, :]
            half = 0.5 + 0.5 * erf(hidden * (2.0**-0.5))
            ug[row, at] = hidden * half
            slope[row, at] = low(half + hidden * jnp.exp(-0.5 * hidden * hidden) * ((2.0 * math.pi) ** -0.5))

        each(5, rows)

    each(CG // 256, up)

    def gate(k):
        hat, _ = normed(ug[part(k, 16), GATE:])
        valid = valid_rows(k, 16, length[0])
        for c in range(3):
            at = slice(ROW * c, ROW * c + ROW)
            gpad[part(k + 1, 16), at] = hat[:, at] * small[5 + c : 6 + c, :] * valid

    each(SLOTS // 16, gate)

    def finish(at, total):
        cv[:, at] = low(total)
        gated[:, at] = low(ug[:, at] * total)

    convolve(gpad, taps, 0, GATE, finish)
    loads.wait(1)
    keep_co = pltpu.make_async_copy(w_co, w_co_out, out_sems.at[1])
    keep_co.start()

    def down(j):
        at = part(j, 256)
        c_out[:, at] = dot(gated[...], w_co[:, at])

    each(2, down)
    keep_cg.wait()
    keep_co.wait()


def last_kernel(coords, length, a_out, c_out, x1, cot, small, taps, *refs):
    sources, refs = refs[: len(PIECES)], refs[len(PIECES) :]
    out, dx, mixed, mpad, w_merge_out, sgrad, grads = refs[:7]
    (
        raw, w_merge, w_in, w_out, stage, x2, x3, nrm, act, slope, dout, dhid, dnrm, total, g_in, g_out,
        sems, out_sems,
    ) = refs[7:]
    loads = Loads(
        coords,
        sources,
        [(BLOCK["merge"], 2, w_merge, ROW), (BLOCK["ffb_in"], 4, raw, ROW), (BLOCK["ffb_out"], 4, w_out, ROW)],
        sems,
    )
    clear_margins(mpad)

    def join(k):
        row = part(k, 32)
        valid = valid_rows(k, 32, length[0])
        padded = pl.ds(pl.multiple_of(k * 32 + PAD, 16), 32)
        mpad[padded, 0:D] = a_out[row, :] * valid
        mpad[padded, D:] = c_out[row, :] * valid

    each(5, join)

    def finish_with(source, shift):
        def finish(at, value):
            mixed[:, at] = low(source[:, part_of(at, shift)] + value)

        return finish

    def part_of(at, shift):
        return pl.ds(pl.multiple_of(at.start - shift, 128), 128)

    def chunk(j):
        at = part(j, 128)
        value = jnp.zeros((SLOTS, 128), F32)
        for tap in range(KER):
            value = value + taps[tap : tap + 1, part(j + GATE // 128, 128)] * mpad[tap + 1 : tap + 1 + SLOTS, at]

        @pl.when(j < 4)
        def _():
            mixed[:, at] = low(a_out[:, at] + value)

        @pl.when(j >= 4)
        def _():
            mixed[:, at] = low(c_out[:, part(j - 4, 128)] + value)

    each(2 * D // 128, chunk)
    loads.wait(0)
    keep = pltpu.make_async_copy(w_merge, w_merge_out, out_sems.at[8])
    keep.start()

    def merge(j):
        at = part(j, 256)
        x2[:, at] = x1[:, at] + dot(mixed[...], w_merge[:, at])

    each(2, merge)
    loads.wait(1)
    split_columns(raw, w_in, 4, stage)
    loads.wait(2)
    feed_forward(x2, small[3:4, :], w_in, w_out, nrm, act, slope, x3)
    sgrad[...] = jnp.zeros_like(sgrad)
    total[...] = jnp.zeros_like(total)
    gain = small[4:5, :]

    def final(k):
        row = part(k, 32)
        valid = valid_rows(k, 32, length[0])
        values = x3[row, :]
        hat, _ = normed(values)
        out[row, :] = low(hat * gain * valid)
        back, products = norm_back(values, gain, cot[row, :].astype(F32) * valid)
        total[...] += jnp.sum(products.reshape(4, 8, D), axis=0)
        dx[row, :] = back
        dout[row, :] = low(0.5 * back)

    each(5, final)
    sgrad[4:5, :] = jnp.sum(total[...], axis=0, keepdims=True)
    feed_back(dout, w_in, w_out, nrm, act, slope, dhid, dnrm, stage, g_in, g_out)
    emits = Emits(coords, grads, out_sems)
    for at in range(4):
        emits.put(BLOCK["ffb_out"] + at, g_out.at[ROW * at : ROW * at + ROW])
    for at in range(4):
        emits.put(BLOCK["ffb_in"] + at, g_in.at[ROW * at : ROW * at + ROW])

    def add(rows, back):
        dx[rows, :] += back

    sgrad[3:4, :] = norm_rows_back(x2, small[3:4, :], dnrm, total, add)
    keep.wait()
    emits.wait()


def back_gating_kernel(
    coords, length, dx_in, mixed, mpad, x1, nrm, ug, slope, gpad, cv, gated, small, taps, sgrad_in, w_merge, w_co, w_cg,
    grads_in, *refs
):
    dx, datt, sgrad, grads = refs[:4]
    dgrad, djoin, dpad, dgate, dhid, dnrm, dtaps, total, total_gate, stage, g_merge, g_co, g_cg, out_sems = refs[4:]
    emits = Emits(coords, grads, out_sems)
    sgrad[...] = sgrad_in[...]
    clear_margins(dpad)

    def lower(k):
        dgrad[part(k, 32), :] = low(dx_in[part(k, 32), :])

    each(5, lower)

    def merge(j):
        at = part(j, 256)
        dpad[PAD : PAD + SLOTS, at] = dot_t(dgrad[...], w_merge[at, :])

    each(2 * D // 256, merge)
    weight_rows(mixed, dgrad, 4, g_merge)
    for at in range(2):
        emits.put(BLOCK["merge"] + at, g_merge.at[ROW * at : ROW * at + ROW])

    def finish(at, value):
        row_valid = valid_rows(0, SLOTS, length[0])
        djoin[:, at] = low(dpad[PAD : PAD + SLOTS, at] + value * row_valid)

    convolve_back(dpad, mpad, taps, GATE, 2 * D, dtaps, finish)
    datt[...] = djoin[:, 0:D]

    def gate(j):
        at = part(j, 256)
        value = dot_t(djoin[:, D:], w_co[at, :])
        dhid[:, at] = low(value * cv[:, at].astype(F32) * slope[:, at].astype(F32))
        dpad[PAD : PAD + SLOTS, at] = value * ug[:, at]

    each(GATE // 256, gate)

    def co_rows(k):
        lhs = gated[:, part(k, 256)]
        for at in range(2):
            place = slice(256 * at, 256 * at + 256)
            g_co[part(k, 256), place] = low(t_dot(lhs, djoin[:, D + 256 * at : D + 256 * at + 256]))

    each(6, co_rows)
    for at in range(3):
        emits.put(BLOCK["cg_out"] + at, g_co.at[ROW * at : ROW * at + ROW])

    def finish_gate(at, value):
        dgate[:, at] = value * valid_rows(0, SLOTS, length[0])

    convolve_back(dpad, gpad, taps, 0, GATE, dtaps, finish_gate)
    gain = jnp.concatenate([small[5:6, :], small[6:7, :], small[7:8, :]], axis=1)
    total_gate[...] = jnp.zeros_like(total_gate)

    def gate_norm(k):
        row = part(k, 16)
        back, products = norm_back(ug[row, GATE:], gain, dgate[row, :])
        total_gate[...] += products[0:8, :] + products[8:16, :]
        dhid[row, GATE:] = low(back * slope[row, GATE:].astype(F32))

    each(SLOTS // 16, gate_norm)
    gain_grad = jnp.sum(total_gate[...], axis=0, keepdims=True)
    for c in range(3):
        sgrad[5 + c : 6 + c, :] = gain_grad[:, ROW * c : ROW * c + ROW]
    for tap in range(KER):
        for c in range(5):
            at = TAPS_AT + 5 * tap + c
            sgrad[at : at + 1, :] = dtaps[tap : tap + 1, ROW * c : ROW * c + ROW]

    def down(j):
        at = part(j, 256)
        dnrm[:, at] = dot_t(dhid[...], w_cg[at, :])

    each(2, down)
    weight_columns(nrm, dhid, 6, stage, g_cg)
    for at in range(6):
        emits.put(BLOCK["cg_in"] + at, g_cg.at[ROW * at : ROW * at + ROW])

    def add(rows, back):
        dx[rows, :] = dx_in[rows, :] + back

    sgrad[2:3, :] = norm_rows_back(x1, small[2:3, :], dnrm, total, add)
    emits.wait()


def back_attention_kernel(
    coords, dx_in, datt, x1, nrm, qkv, probs, ctx, small, sgrad_in, w_qkv, w_att, grads_in, *refs
):
    dx, sgrad, grads, dctx, dqkv, dnrm, total, stage, sums, g_qkv, g_att, out_sems = refs
    emits = Emits(coords, grads, out_sems)
    sgrad[...] = sgrad_in[...]

    def project(j):
        at = part(j, 256)
        dctx[:, at] = low(dot_t(datt[...], w_att[at, :]))

    each(2, project)
    weight_rows(ctx, datt, 2, g_att)
    emits.put(BLOCK["att_out"], g_att)
    first_half = lax.broadcasted_iota(jnp.int32, (1, 128), 1) < HS
    at_row = lax.broadcasted_iota(jnp.int32, (SLOTS, SLOTS), 0)
    at_column = lax.broadcasted_iota(jnp.int32, (SLOTS, SLOTS), 1)
    flip = low((at_row + at_column == SLOTS - 1).astype(F32))

    def heads(pair):
        queries = qkv[0:SLOTS, part(pair, 128)]
        keys = qkv[:, part(pair + 4, 128)]
        values = qkv[:, part(pair + 8, 128)]
        context = dctx[:, part(pair, 128)]
        q_parts, k_parts, v_parts = [], [], []
        for odd in range(2):
            head = 2 * pair + odd
            half = first_half if odd == 0 else jnp.logical_not(first_half)
            chances = probs[head]
            v_parts.append(t_dot(chances, context)[0:SLOTS])
            wide_chances = chances.astype(F32)
            chance_grad = dot_t(jnp.where(half, context, jnp.zeros_like(context)), values)
            inner = jnp.sum(wide_chances * chance_grad, axis=-1, keepdims=True)
            score_grad = low(wide_chances * (chance_grad - inner))
            q_parts.append(dot(score_grad, keys))
            k_parts.append(t_dot(score_grad, queries)[0:SLOTS])
            wide = jnp.concatenate([dot(flip, score_grad), jnp.zeros((SLOTS, ROW - KEYS), F32)], axis=1)
            wide = pltpu.roll(wide, ROW - SLOTS + 1, 1, stride=1, stride_axis=0)
            sums[pl.ds(head, 1), :] = jnp.sum(wide, axis=0, keepdims=True)
        scale = HS ** (-0.5)
        dqkv[:, part(pair, 128)] = low(jnp.where(first_half, q_parts[0], q_parts[1]) * scale)
        dqkv[:, part(pair + 4, 128)] = low(jnp.where(first_half, k_parts[0], k_parts[1]) * scale)
        dqkv[:, part(pair + 8, 128)] = low(jnp.where(first_half, v_parts[0], v_parts[1]))

    each(H // 2, heads)

    def down(j):
        at = part(j, 256)
        dnrm[:, at] = dot_t(dqkv[...], w_qkv[at, :])

    each(2, down)
    weight_columns(nrm, dqkv, 3, stage, g_qkv)
    for at in range(3):
        emits.put(BLOCK["qkv"] + at, g_qkv.at[ROW * at : ROW * at + ROW])

    def add(rows, back):
        dx[rows, :] = dx_in[rows, :] + back

    sgrad[1:2, :] = norm_rows_back(x1, small[1:2, :], dnrm, total, add)
    by_entry = lax.dot_general(
        sums[...],
        bucket_map(),
        (((1,), (1,)), ((), ())),
        precision=lax.Precision.HIGHEST,
        preferred_element_type=F32,
    )
    flat = jnp.sum(own_entries(by_entry), axis=0, keepdims=True)
    sgrad[REL_AT : REL_AT + 1, :] = flat[:, 0:ROW]
    sgrad[REL_AT + 1 : REL_AT + 2, :] = flat[:, ROW:]
    emits.wait()


def back_first_kernel(coords, dx_in, frames, nrm, act, slope, small, sgrad_in, w_in, w_out, grads_in, *refs):
    fgrad, gains, grads, dout, dhid, dnrm, total, stage, g_in, g_out, g_small, out_sems = refs
    emits = Emits(coords, grads, out_sems)

    def lower(k):
        dout[part(k, 32), :] = low(0.5 * dx_in[part(k, 32), :])

    each(5, lower)
    feed_back(dout, w_in, w_out, nrm, act, slope, dhid, dnrm, stage, g_in, g_out)
    for at in range(4):
        emits.put(BLOCK["ffa_out"] + at, g_out.at[ROW * at : ROW * at + ROW])
    for at in range(4):
        emits.put(BLOCK["ffa_in"] + at, g_in.at[ROW * at : ROW * at + ROW])

    def add(rows, back):
        fgrad[rows, :] = low(dx_in[rows, :] + back)

    gain_grad = norm_rows_back(frames, small[0:1, :], dnrm, total, add)
    gains[...] = sgrad_in[0:8, :]
    gains[0:1, :] = gain_grad
    g_small[0:SMALL, :] = low(sgrad_in[...])
    g_small[0:16, :] = low(jnp.concatenate([gains[...], sgrad_in[8:16, :]], axis=0))
    g_small[SMALL:ROW, :] = jnp.zeros((ROW - SMALL, ROW), BF16)
    emits.put(BLOCK["small"], g_small)
    emits.wait()


VM = pl.BlockSpec(memory_space=pltpu.VMEM)
SM = pl.BlockSpec(memory_space=pltpu.SMEM)
ANY = pl.BlockSpec(memory_space=pl.ANY)
GRADS = ((32, ROW, ROW), BF16)


def call(kernel, name, ins, outs, scratch, aliases=None):
    return pl.pallas_call(
        kernel,
        name=name,
        in_specs=[space for space, _ in ins],
        out_specs=[space for space, _ in outs],
        out_shape=[jax.ShapeDtypeStruct(*kind) for _, kind in outs],
        scratch_shapes=[
            pltpu.SemaphoreType.DMA((each_one,)) if isinstance(each_one, int) else pltpu.VMEM(*each_one)
            for each_one in scratch
        ],
        input_output_aliases=aliases or {},
        compiler_params=pltpu.CompilerParams(vmem_limit_bytes=56 * 2**20),
    )(*[array for _, array in ins])


def layer(coords, length, frames, cot, blocks):
    sources = [(ANY, block) for block in blocks]
    place = (SM, coords)
    wide = ((SLOTS, D), F32)
    thin = ((SLOTS, D), BF16)
    ff = ((SLOTS, FF), BF16)
    x1, nrm_a, act_a, slope_a, w_ffa_in, w_ffa_out, small, taps = call(
        first_kernel,
        "ffa_forward",
        [place, (VM, frames)] + sources,
        [
            (VM, wide),
            (VM, thin),
            (VM, ff),
            (VM, ff),
            (ANY, ((D, FF), BF16)),
            (ANY, ((FF, D), BF16)),
            (VM, ((SMALL, ROW), F32)),
            (VM, ((32, 5 * ROW), F32)),
        ],
        [
            ((FF, D), BF16),
            ((D, FF), BF16),
            ((FF, D), BF16),
            ((4, 128 * 4, 128), F32),
            ((SMALL, ROW), BF16),
            18,
            2,
        ],
    )
    a_out, nrm_t, qkv, probs, ctx, w_qkv, w_att = call(
        attention_kernel,
        "attention_forward",
        [place, (SM, length), (VM, x1), (VM, small)] + sources,
        [
            (VM, wide),
            (VM, thin),
            (VM, ((KEYS, 3 * D), BF16)),
            (VM, ((H, SLOTS, KEYS), BF16)),
            (VM, thin),
            (ANY, ((D, 3 * D), BF16)),
            (ANY, ((D, D), BF16)),
        ],
        [
            ((3 * D, D), BF16),
            ((D, 3 * D), BF16),
            ((D, D), BF16),
            ((4, 128 * 3, 128), F32),
            ((H, ROW), F32),
            8,
            2,
        ],
    )
    c_out, nrm_c, ug, slope_c, gpad, cv, gated, w_cg, w_co = call(
        gating_kernel,
        "gating_forward",
        [place, (SM, length), (VM, x1), (VM, small), (VM, taps)] + sources,
        [
            (VM, wide),
            (VM, thin),
            (VM, ((SLOTS, CG), F32)),
            (VM, ((SLOTS, CG), BF16)),
            (VM, ((PADDED, GATE), F32)),
            (VM, ((SLOTS, GATE), BF16)),
            (VM, ((SLOTS, GATE), BF16)),
            (ANY, ((D, CG), BF16)),
            (ANY, ((GATE, D), BF16)),
        ],
        [
            ((CG, D), BF16),
            ((D, CG), BF16),
            ((GATE, D), BF16),
            ((4, 128 * 6, 128), F32),
            ((SLOTS, 256), F32),
            18,
            2,
        ],
    )
    out, dx2, mixed, mpad, w_merge, sgrad, grads = call(
        last_kernel,
        "merge_ffb",
        [place, (SM, length), (VM, a_out), (VM, c_out), (VM, x1), (VM, cot), (VM, small), (VM, taps)] + sources,
        [
            (VM, thin),
            (VM, wide),
            (VM, ((SLOTS, 2 * D), BF16)),
            (VM, ((PADDED, 2 * D), F32)),
            (ANY, ((2 * D, D), BF16)),
            (VM, ((SMALL, ROW), F32)),
            (ANY, GRADS),
        ],
        [
            ((FF, D), BF16),
            ((2 * D, D), BF16),
            ((D, FF), BF16),
            ((FF, D), BF16),
            ((4, 128 * 4, 128), F32),
            wide,
            wide,
            thin,
            ff,
            ff,
            thin,
            ff,
            wide,
            ((8, D), F32),
            ((FF, D), BF16),
            ((FF, D), BF16),
            20,
            9,
        ],
    )
    dx1, datt, sgrad, grads = call(
        back_gating_kernel,
        "gating_backward",
        [place, (SM, length)]
        + [(VM, a) for a in (dx2, mixed, mpad, x1, nrm_c, ug, slope_c, gpad, cv, gated, small, taps, sgrad)]
        + [(VM, w_merge), (VM, w_co), (VM, w_cg), (ANY, grads)],
        [(VM, wide), (VM, thin), (VM, ((SMALL, ROW), F32)), (ANY, GRADS)],
        [
            thin,
            ((SLOTS, 2 * D), BF16),
            ((PADDED, GATE), F32),
            ((SLOTS, GATE), F32),
            ((SLOTS, CG), BF16),
            wide,
            ((32, 5 * ROW), F32),
            ((8, D), F32),
            ((8, GATE), F32),
            ((4, 128 * 6, 128), F32),
            ((2 * D, D), BF16),
            ((GATE, D), BF16),
            ((CG, D), BF16),
            11,
        ],
        {18: 3},
    )
    dx1, sgrad, grads = call(
        back_attention_kernel,
        "attention_backward",
        [place]
        + [(VM, a) for a in (dx1, datt, x1, nrm_t, qkv, probs, ctx, small, sgrad)]
        + [(VM, w_qkv), (VM, w_att), (ANY, grads)],
        [(VM, wide), (VM, ((SMALL, ROW), F32)), (ANY, GRADS)],
        [
            thin,
            ((SLOTS, 3 * D), BF16),
            wide,
            ((8, D), F32),
            ((4, 128 * 3, 128), F32),
            ((H, ROW), F32),
            ((3 * D, D), BF16),
            ((D, D), BF16),
            4,
        ],
        {12: 2},
    )
    fgrad, gains, grads = call(
        back_first_kernel,
        "ffa_backward",
        [place]
        + [(VM, a) for a in (dx1, frames, nrm_a, act_a, slope_a, small, sgrad)]
        + [(VM, w_ffa_in), (VM, w_ffa_out), (ANY, grads)],
        [(VM, thin), (VM, ((8, ROW), F32)), (ANY, GRADS)],
        [
            thin,
            ff,
            wide,
            ((8, D), F32),
            ((4, 128 * 4, 128), F32),
            ((FF, D), BF16),
            ((FF, D), BF16),
            ((ROW, ROW), BF16),
            9,
        ],
        {10: 2},
    )
    return out, fgrad, gains, grads


def segment_bounds():
    bounds = [0]
    for extent in segment_shapes():
        bounds.append(bounds[-1] + math.prod(extent))
    return bounds


def block_rows(device_count):
    total_rows = -(-segment_bounds()[-1] // ROW)
    step = 16 * device_count
    return -(-total_rows // step) * 16


def align_shard(low_shard, shard_size, rows):
    devices = lax.axis_size("dp") * lax.axis_size("fsdp")
    me = lax.axis_index(AXES)
    block = rows * ROW
    lead = block - shard_size
    pieces = [low_shard]
    have = shard_size
    need = lead * (devices - 1) + block
    hop = 1
    while have < need:
        part = min(shard_size, need - have)
        pairs = [(i, i - hop) for i in range(hop, devices)]
        pieces.append(lax.ppermute(low_shard[:part], AXES, pairs))
        have = have + part
        hop = hop + 1
    return lax.dynamic_slice(jnp.concatenate(pieces), (me * lead,), (block,)).reshape(rows, ROW)


def unalign_block(block_sum, shard_size, padded):
    devices = lax.axis_size("dp") * lax.axis_size("fsdp")
    me = lax.axis_index(AXES)
    rows = block_sum.shape[0]
    block = rows * ROW
    lead = block - shard_size
    flat = block_sum.reshape(-1)
    pieces = [flat]
    have = block
    need = lead * (devices - 1) + block
    hop = 1
    while have < need:
        part = min(block, need - have)
        pairs = [(i, i + hop) for i in range(devices - hop)]
        pieces.insert(0, lax.ppermute(flat[block - part :], AXES, pairs))
        have = have + part
        hop = hop + 1
    start = have - block - me * lead
    pieces.append(jnp.zeros((max(0, padded - block),), flat.dtype))
    return lax.dynamic_slice(jnp.concatenate(pieces), (start,), (padded,))


def pair_lists():
    ring = [(i, (i + 2) % 8) for i in range(8)]
    across_x = [(i, i ^ 1) for i in range(8)]
    across_y = [(i, i ^ 2) for i in range(4)]
    across_core = [(i, i ^ 1) for i in range(4)]
    return ring, across_x, across_y, across_core


def fast_mesh():
    return lax.axis_size("dp") == 4 and lax.axis_size("fsdp") == 8


def gather_blocks(block):
    if not fast_mesh():
        whole = lax.all_gather(block, AXES, axis=0, tiled=True).reshape(32, ROW, ROW)
        return [whole[source_block((0, 0, 0, 0), piece)][piece[4] : piece[4] + piece[5]] for piece in PIECES]
    ring, across_x, across_y, across_core = pair_lists()
    own = [block]
    for _ in range(3):
        own.append(lax.ppermute(own[-1], "fsdp", ring))
    by_x = [lax.ppermute(each_one, "fsdp", across_x) for each_one in own]
    by_y = [lax.ppermute(each_one, "dp", across_y) for each_one in own]
    top = [lax.ppermute(each_one[:HALF], "fsdp", across_x) for each_one in by_y]
    bottom = [lax.ppermute(each_one[HALF:], "dp", across_y) for each_one in by_x]
    near = own + by_x + by_y + top + bottom
    far = [lax.ppermute(each_one, "dp", across_core) for each_one in near]
    return near + far


def added(*parts):
    total = parts[0].astype(jnp.float32)
    for part in parts[1:]:
        total = total + part.astype(jnp.float32)
    return total


def scatter_blocks(grads, coords):
    if not fast_mesh():
        devices = lax.axis_size("dp") * lax.axis_size("fsdp")
        order = [gradient_slot((0, 0, 0, 0), block) for block in range(32)]
        rows = jnp.concatenate([grads[at] for at in order]).reshape(devices, -1, ROW)
        return lax.psum_scatter(rows, AXES, scatter_dimension=0).astype(F32)
    ring, across_x, across_y, across_core = pair_lists()
    z = coords[2]

    def core_sum(kind):
        theirs = lax.ppermute(grads[16 + 4 * kind : 20 + 4 * kind], "dp", across_core)
        return low(added(grads[4 * kind : 4 * kind + 4], theirs))

    diagonal = core_sum(3)
    to_x = core_sum(1)
    to_y = core_sum(2)
    mine = core_sum(0)
    from_x = lax.ppermute(diagonal[:2], "fsdp", across_x)
    from_y = lax.ppermute(diagonal[2:], "dp", across_y)
    to_y = jnp.concatenate([low(added(to_y[:2], from_x)), to_y[2:]])
    to_x = jnp.concatenate([to_x[:2], low(added(to_x[2:], from_y))])

    def at(array, back):
        return lax.dynamic_index_in_dim(array, lax.rem(z + 4 - back, 4), 0, keepdims=False)

    running = None
    for back in (1, 2, 3, 0):
        parts = [
            at(mine, back),
            lax.ppermute(at(to_x, back), "fsdp", across_x),
            lax.ppermute(at(to_y, back), "dp", across_y),
        ]
        if running is not None:
            parts.append(lax.ppermute(running, "fsdp", ring))
        running = added(*parts)
        if back:
            running = low(running)
    return running


def sum_everywhere(vector):
    if not fast_mesh():
        return lax.psum(vector, AXES)
    _, across_x, across_y, across_core = pair_lists()
    near_z = [(i, i ^ 2) for i in range(8)]
    far_z = [(i, i ^ 4) for i in range(8)]
    for axis, pairs in (
        ("dp", across_core),
        ("fsdp", across_x),
        ("dp", across_y),
        ("fsdp", near_z),
        ("fsdp", far_z),
    ):
        vector = vector + lax.ppermute(vector, axis, pairs)
    return vector


def most_segments(shard_size, devices):
    bounds = segment_bounds()
    most = 1
    for at in range(devices):
        low_end, high_end = at * shard_size, (at + 1) * shard_size
        most = max(most, sum(1 for b in bounds[1:-1] if low_end < b < high_end) + 1)
    return most


LANES = 128
CHUNK = 256


def entry_places(step):
    row = step * CHUNK + lax.broadcasted_iota(jnp.int32, (CHUNK, LANES), 0)
    return row * LANES + lax.broadcasted_iota(jnp.int32, (CHUNK, LANES), 1)


def update_kernel(segments, params, first, second, grad, new_first, new_second, update, sums):
    step = pl.program_id(0)
    spans = segments.shape[0] - 2

    @pl.when(step == 0)
    def _():
        sums[...] = jnp.zeros_like(sums)

    grads = grad[...]
    firsts = BETA_FIRST * first[...] + (1.0 - BETA_FIRST) * grads
    seconds = BETA_SECOND * second[...] + (1.0 - BETA_SECOND) * grads * grads
    new_first[...] = firsts
    new_second[...] = seconds
    first_hat = firsts * (1.0 / (1.0 - BETA_FIRST**STEP))
    second_hat = seconds * (1.0 / (1.0 - BETA_SECOND**STEP))
    values = params[...]
    change = first_hat / (jnp.sqrt(second_hat) + ADAM_EPS) + WEIGHT_DECAY * values
    update[...] = change
    places = entry_places(step)
    lane = lax.broadcasted_iota(jnp.int32, (1, LANES), 1)
    for at in range(spans):
        inside = (places >= segments[1 + at]) & (places < segments[2 + at])
        mine = lane == segments[0] + at
        for row, entries in enumerate((values, change)):
            squares = jnp.where(inside, entries * entries, 0.0)
            total = jnp.sum(jnp.sum(squares, axis=0, keepdims=True), axis=1, keepdims=True)
            sums[row : row + 1, :] += jnp.where(mine, total, 0.0)


def apply_kernel(segments, sums, params, update, new_params, norms):
    step = pl.program_id(0)
    spans = segments.shape[0] - 2
    roots = jnp.sqrt(sums[0:2, :])
    trust = roots[0:1, :] / (roots[1:2, :] + ADAM_EPS)
    norms[0:2, :] = roots
    norms[2:3, :] = trust
    places = entry_places(step)
    lane = lax.broadcasted_iota(jnp.int32, (1, LANES), 1)
    scale = jnp.zeros((CHUNK, LANES), F32)
    for at in range(spans):
        own = jnp.sum(jnp.where(lane == segments[0] + at, trust, 0.0), axis=1, keepdims=True)
        scale = jnp.where(places >= segments[1 + at], own, scale)
    new_params[...] = params[...] - LEARN_RATE * scale * update[...]


def shards(frames, lengths, cotangent, params, first_moment, second_moment):
    shard_size = params.shape[0]
    devices = lax.axis_size("dp") * lax.axis_size("fsdp")
    me = lax.axis_index(AXES)
    rows = block_rows(devices)
    if fast_mesh():
        dp, fsdp = lax.axis_index("dp"), lax.axis_index("fsdp")
        coords = jnp.stack([dp // 2, dp % 2, fsdp // 2, fsdp % 2]).astype(jnp.int32)
    else:
        coords = jnp.zeros((4,), jnp.int32)
    blocks = gather_blocks(align_shard(low(params), shard_size, rows))
    result, frames_grad, gains, grads = layer(coords, lengths, frames[0], cotangent[0], blocks)
    block_sum = scatter_blocks(grads, coords)
    steps = -(-shard_size // (LANES * CHUNK))
    padded = steps * LANES * CHUNK
    grad_shard = unalign_block(low(block_sum), shard_size, padded).astype(F32)

    def square(flat):
        return jnp.pad(flat, (0, padded - flat.shape[0])).reshape(-1, LANES)

    bounds = segment_bounds()
    spans = most_segments(shard_size, devices)
    shard_low = me * shard_size
    first_segment = sum((shard_low >= b).astype(jnp.int32) for b in bounds[1:-1])
    table = jnp.asarray(bounds[1:] + [bounds[-1]] * spans, jnp.int32)
    ends = jnp.clip(lax.dynamic_slice(table, (first_segment,), (spans,)) - shard_low, 0, shard_size)
    segments = jnp.concatenate([first_segment[None], jnp.zeros((1,), jnp.int32), ends]).astype(jnp.int32)
    grid = pl.BlockSpec((CHUNK, LANES), lambda step: (step, 0))
    whole = pl.BlockSpec((8, LANES), lambda step: (0, 0))
    flat_kind = jax.ShapeDtypeStruct((padded // LANES, LANES), F32)
    tile_kind = jax.ShapeDtypeStruct((8, LANES), F32)
    params_square = square(params)
    new_first, new_second, update, sums = pl.pallas_call(
        update_kernel,
        name="update",
        grid=(steps,),
        in_specs=[SM] + [grid] * 4,
        out_specs=[grid] * 3 + [whole],
        out_shape=[flat_kind] * 3 + [tile_kind],
    )(segments, params_square, square(first_moment), square(second_moment), grad_shard.reshape(-1, LANES))
    gain_grads = sum_everywhere(gains).reshape(-1)
    sums = sum_everywhere(sums)
    new_params, norms = pl.pallas_call(
        apply_kernel,
        name="apply",
        grid=(steps,),
        in_specs=[SM, whole, grid, grid],
        out_specs=[grid, whole],
        out_shape=[flat_kind, tile_kind],
    )(segments, sums, params_square, update)
    count = len(segment_shapes())
    return (
        result.reshape(frames.shape),
        frames_grad.reshape(frames.shape),
        new_params.reshape(-1)[:shard_size],
        new_first.reshape(-1)[:shard_size],
        new_second.reshape(-1)[:shard_size],
        norms[0, :count],
        norms[1, :count],
        norms[2, :count],
        gain_grads,
    )


def solution(mesh):
    placed = (
        P(("dp", "fsdp"), None, None),
        P(("dp", "fsdp")),
        P(("dp", "fsdp"), None, None),
        P(("dp", "fsdp")),
        P(("dp", "fsdp")),
        P(("dp", "fsdp")),
    )
    return jax.shard_map(
        shards,
        mesh=mesh,
        in_specs=placed,
        out_specs=(
            P(("dp", "fsdp"), None, None),
            P(("dp", "fsdp"), None, None),
            P(("dp", "fsdp")),
            P(("dp", "fsdp")),
            P(("dp", "fsdp")),
            P(),
            P(),
            P(),
            P(),
        ),
        check_vma=False,
    )
```

```python
import math
from types import SimpleNamespace

import jax
import jax.numpy as jnp
from jax import lax
from jax.experimental import pallas as pl
from jax.experimental.pallas import tpu as pltpu
from jax.sharding import PartitionSpec as P

STEP = 8
BETA_FIRST = 0.5
BETA_SECOND = 0.5
LEARN_RATE = 0.5
WEIGHT_DECAY = 0.01
ADAM_EPS = 1e-06
AXES = ("dp", "fsdp")


def segment_shapes():
    gate_width = CG // 2
    return [
        (D, FF),
        (FF, D),
        (D, 3 * D),
        (D, D),
        (D, CG),
        (gate_width, D),
        (2 * D, D),
        (D, FF),
        (FF, D),
        (5 * D + gate_width,),
        (KER, gate_width + 2 * D),
        (RELW, H),
    ]


D = 512
H = 8
HS = 64
FF = 2048
CG = 3072
KER = 31
RELW = 128
NORM_EPS = 1e-05
MASK_FILL = -1000000000.0
ROW = 512
HALF = ROW // 2
SLOTS = 160
KEYS = 256
PAD = 16
PADDED = SLOTS + 2 * PAD
GATE = CG // 2
BLOCK = {
    "ffa_in": (0, 4),
    "ffa_out": (4, 4),
    "qkv": (8, 3),
    "att_out": (11, 1),
    "cg_in": (12, 6),
    "cg_out": (18, 3),
    "merge": (21, 2),
    "ffb_in": (23, 4),
    "ffb_out": (27, 4),
    "small": (31, 1),
}
TAPS_AT = 8
REL_AT = 8 + 5 * KER
SMALL = 176
F32, BF16 = jnp.float32, jnp.bfloat16


def dot(left, right):
    return lax.dot_general(left, right, (((1,), (0,)), ((), ())), preferred_element_type=F32)


def dot_t(left, right):
    return lax.dot_general(left, right, (((1,), (1,)), ((), ())), preferred_element_type=F32)


def t_dot(left, right):
    return lax.dot_general(left, right, (((0,), (0,)), ((), ())), preferred_element_type=F32)


def low(values):
    return values.astype(BF16)


def each(count, body):
    def step(at, carry):
        body(at)
        return carry

    lax.fori_loop(0, count, step, 0)


def part(at, size):
    if isinstance(at, int):
        return slice(at * size, at * size + size)
    return pl.ds(pl.multiple_of(at * size, size), size)


def rows_of(name):
    first, count = BLOCK[name]
    return slice(ROW * first, ROW * (first + count))


def lane_mean(values, width):
    return jnp.sum(values, axis=-1, keepdims=True) * (1.0 / width)


def normed(values):
    centered = values - lane_mean(values, values.shape[-1])
    scale = lax.rsqrt(lane_mean(centered * centered, values.shape[-1]) + NORM_EPS)
    return centered * scale, scale


def valid_rows(length):
    return (lax.broadcasted_iota(jnp.int32, (SLOTS, 1), 0) < length).astype(F32)


def fold_rows(values):
    return jnp.sum(values, axis=0, keepdims=True)


def norm_rows(source, gain, target):
    for k in range(2):
        hat, _ = normed(source[part(k, 80), :].astype(F32))
        target[part(k, 80), :] = low(hat * gain)


def norm_rows_back(values, gain, grad, add):
    total = jnp.zeros((1, values.shape[1]), F32)
    for k in range(2):
        rows = part(k, 80)
        hat, scale = normed(values[rows, :].astype(F32))
        mine = grad[rows, :]
        total = total + fold_rows(mine * hat)
        inner = mine * gain
        width = values.shape[1]
        moved = lane_mean(inner, width) + hat * lane_mean(inner * hat, width)
        add(rows, scale * (inner - moved))
    return total


PIECES = []
for far_core in range(2):
    for kind in ((0, 0), (0, 1), (1, 0)):
        PIECES += [(far_core, *kind, back, 0, ROW) for back in range(4)]
    for first_row in (0, HALF):
        PIECES += [(far_core, 1, 1, back, first_row, HALF) for back in range(4)]


def source_block(coords, piece):
    y, c, z, x = coords[0], coords[1], coords[2], coords[3]
    yy, cc, xx, zz = y ^ piece[1], c ^ piece[0], x ^ piece[2], (z + 4 - piece[3]) & 3
    return ((yy * 2 + cc) * 4 + zz) * 2 + xx


class Loads:
    def __init__(self, coords, sources, target, sems):
        self.source, self.target, self.sems = sources[0], target, sems
        for piece, source in zip(PIECES, sources):
            block = source_block(coords, piece)
            for half in range(2):
                inside = HALF * half - piece[4]
                if 0 <= inside < piece[5]:
                    place = pl.ds(pl.multiple_of(block * ROW + HALF * half, HALF), HALF)
                    pltpu.make_async_copy(
                        source.at[inside : inside + HALF], target.at[place], sems.at[2 * block + half]
                    ).start()

    def wait(self, name):
        first, count = BLOCK[name]
        for at in range(2 * first, 2 * (first + count)):
            pltpu.make_async_copy(
                self.source.at[0:HALF], self.target.at[HALF * at : HALF * at + HALF], self.sems.at[at]
            ).wait()


class Emits:
    def __init__(self, coords, kept, sent, sems):
        self.coords, self.kept, self.sent, self.sems = coords, kept, sent, sems
        self.pending = []

    def put(self, block, values):
        core, z, x = (block // 8) % 2, (block // 2) % 4, block % 2
        slot = 4 * (self.coords[3] ^ x) + ((self.coords[2] + 3 - z) & 3)
        sem = self.sems.at[len(self.pending)]


        @pl.when(self.coords[1] == core)
        def _():
            pltpu.make_async_copy(values, self.kept.at[slot], sem).start()

        @pl.when(self.coords[1] != core)
        def _():
            pltpu.make_async_copy(values, self.sent.at[slot], sem).start()

        self.pending.append(pltpu.make_async_copy(values, self.kept.at[slot], sem))

    def put_tensor(self, name, rows):
        first, count = BLOCK[name]
        for at in range(count):
            self.put(first + at, rows.at[ROW * at : ROW * at + ROW])

    def wait(self):
        for copy in self.pending:
            copy.wait()


def split_columns(raw, target, wide, stage):
    def chunk(k):
        rows = part(k, 128 * wide)
        for lane in range(4):
            stage[lane, 0 : 128 * wide, :] = raw[rows, lane * 128 : lane * 128 + 128].astype(F32)
        for c in range(wide):
            for lane in range(4):
                place = ROW * c + lane * 128
                target[part(k, 128), place : place + 128] = low(stage[lane, pl.ds(c, 128, stride=wide), :])

    each(4, chunk)


def weight_columns(left, grads, wide, stage, left_t, target):
    left_t[...] = left[...].T

    def chunk(j):
        value = dot(left_t[...], grads[:, part(j, 256)])
        c, pair = j // 2, (j % 2) * 2
        for half in range(2):
            stage[pair + half, pl.ds(c, ROW, stride=wide), :] = value[:, 128 * half : 128 * half + 128]

    each(2 * wide, chunk)

    def lower(k):
        rows = part(k, ROW)
        for lane in range(4):
            target[rows, lane * 128 : lane * 128 + 128] = low(stage[lane, rows, :])

    each(wide, lower)


def weight_rows(left, grads, count, left_t, target):
    def chunk(k):
        left_t[...] = left[:, part(k, ROW)].T
        for at in range(2):
            target[part(k, ROW), 256 * at : 256 * at + 256] = low(dot(left_t[...], grads[:, 256 * at : 256 * at + 256]))

    each(count, chunk)


def feed_forward(inputs, gain, w_in, w_out, nrm, act, slope, result):
    norm_rows(inputs, gain, nrm)

    def up(j):
        at = part(j, 256)
        hidden = dot(nrm[...], w_in[:, at])
        sig = jax.nn.sigmoid(hidden)
        active = hidden * sig
        act[:, at] = low(active)
        slope[:, at] = low(sig + active * (1.0 - sig))

    each(FF // 256, up)

    def down(j):
        at = part(j, 256)
        result[:, at] = inputs[:, at].astype(F32) + 0.5 * dot(act[...], w_out[:, at])

    each(2, down)


def feed_back(dout, w_in, w_out, nrm, act, slope, dhid, dnrm, stage, left_t, g_in, g_out, emits, name):
    def up(j):
        at = part(j, 256)
        grad = dot_t(dout[...], w_out[at, :])
        dhid[:, at] = low(grad * slope[:, at].astype(F32))

    each(FF // 256, up)
    weight_rows(act, dout, 4, left_t, g_out)
    emits.put_tensor(name + "_out", g_out)

    def down(j):
        at = part(j, 256)
        dnrm[:, at] = dot_t(dhid[:, 0:FF], w_in[at, :])

    each(2, down)
    weight_columns(nrm, dhid, 4, stage, left_t, g_in)
    emits.put_tensor(name + "_in", g_in)


def bucket_map():
    entry = lax.broadcasted_iota(jnp.int32, (2 * ROW, ROW), 0) // H
    far = lax.broadcasted_iota(jnp.int32, (2 * ROW, ROW), 1)
    far = jnp.where(far >= ROW // 2, far - ROW, far)
    bucket = jnp.clip(far, -(RELW // 2), RELW // 2 - 1) + RELW // 2
    return (entry == bucket).astype(F32)


def own_entries(flat):
    entry = lax.broadcasted_iota(jnp.int32, (H, 2 * ROW), 1)
    head = lax.broadcasted_iota(jnp.int32, (H, 2 * ROW), 0)
    return jnp.where(lax.rem(entry, H) == head, flat, 0.0)


def tap_row(small, tap, row, lane):
    return small[lane, pl.ds(TAPS_AT + 5 * tap + row, 1), :]


def shifted_sum(padded, at, factor):
    total = None
    for low_part in range(8):
        slab = padded[low_part : low_part + SLOTS + 24, at]
        inner = None
        for high_part in range(4):
            offset = 8 * high_part + low_part
            if offset:
                term = factor(offset) * slab[8 * high_part : 8 * high_part + SLOTS]
                inner = term if inner is None else inner + term
        total = inner if total is None else total + inner
    return total


def convolve(padded, small, first_row, width, finish):

    def chunk(j):
        at = part(j, 128)
        row, lane = first_row + j // 4, j % 4
        finish(j, at, shifted_sum(padded, at, lambda offset: tap_row(small, offset - 1, row, lane)))

    each(width // 128, chunk)


def convolve_back(grads, padded, small, first_row, width, sgrad, finish):

    def chunk(j):
        at = part(j, 128)
        row, lane = first_row + j // 4, j % 4
        finish(j, at, shifted_sum(grads, at, lambda offset: tap_row(small, KER - offset, row, lane)))
        own = grads[PAD : PAD + SLOTS, at]
        for low_part in range(8):
            slab = padded[low_part : low_part + SLOTS + 24, at]
            for high_part in range(4):
                offset = 8 * high_part + low_part
                if offset:
                    tile = slab[8 * high_part : 8 * high_part + SLOTS]
                    sgrad[lane, pl.ds(TAPS_AT + 5 * (offset - 1) + row, 1), :] = fold_rows(own * tile)

    each(width // 128, chunk)


def clear_margins(padded):
    padded[0:PAD, :] = jnp.zeros((PAD, padded.shape[1]), F32)
    padded[PAD + SLOTS : PADDED, :] = jnp.zeros((PAD, padded.shape[1]), F32)


def gelu_parts(hidden):
    bell = jnp.exp(-0.5 * hidden * hidden)
    spread = 1.0 + (0.3275911 * 2.0**-0.5) * jnp.abs(hidden)
    near = pl.reciprocal(spread, approx=True)
    near = near * (2.0 - spread * near)
    tail = jnp.full_like(near, 0.5 * 1.061405429)
    for factor in (-1.453152027, 1.421413741, -0.284496736, 0.254829592):
        tail = tail * near + 0.5 * factor
    tail = tail * near * bell
    below = jnp.where(hidden >= 0.0, 1.0 - tail, tail)
    return hidden * below, below + hidden * bell * ((2.0 * math.pi) ** -0.5)


def attention_forward(r, length):
    norm_rows(r.x1, r.small[1:2, :], r.nrm_t)
    r.qkv[SLOTS:KEYS, :] = jnp.zeros((KEYS - SLOTS, 3 * D), BF16)
    flat = jnp.concatenate([r.small[REL_AT : REL_AT + 1, :], r.small[REL_AT + 1 : REL_AT + 2, :]], axis=1)
    r.bias[...] = dot(low(own_entries(jnp.broadcast_to(flat, (H, 2 * ROW)))), low(bucket_map()))

    def project(j):
        at = part(j, 256)
        r.qkv[0:SLOTS, at] = low(dot(r.nrm_t[...], r.w_qkv[:, at]))

    each(3 * D // 256, project)
    valid = lax.broadcasted_iota(jnp.int32, (1, KEYS), 1) < length
    first_half = lax.broadcasted_iota(jnp.int32, (1, 128), 1) < HS

    def heads(pair):
        queries = r.qkv[0:SLOTS, part(pair, 128)]
        keys = r.qkv[:, part(pair + 4, 128)]
        values = r.qkv[:, part(pair + 8, 128)]
        outs = []
        for odd in range(2):
            head = 2 * pair + odd
            half = first_half if odd == 0 else jnp.logical_not(first_half)
            mine = jnp.where(half, queries, jnp.zeros_like(queries))
            spread = jnp.broadcast_to(r.bias[pl.ds(head, 1), :], (SLOTS, ROW))
            spread = pltpu.roll(spread, 0, 1, stride=1, stride_axis=0)[:, 0:KEYS]
            scores = jnp.where(valid, dot_t(mine, keys) * HS ** (-0.5) + spread, MASK_FILL)
            shifted = jnp.exp(scores - jnp.max(scores, axis=-1, keepdims=True))
            chances = low(shifted / jnp.sum(shifted, axis=-1, keepdims=True))
            r.probs[head] = chances
            outs.append(dot(chances, values))
        r.ctx[:, part(pair, 128)] = low(jnp.where(first_half, outs[0], outs[1]))

    each(H // 2, heads)

    def project_out(j):
        at = part(j, 256)
        r.cat[:, at] = dot(r.ctx[...], r.w[rows_of("att_out"), at])

    each(2, project_out)


def gating_forward(r, length):
    norm_rows(r.x1, r.small[2:3, :], r.nrm_c)

    def up(j):
        at = part(j, 256)
        r.hid[...] = dot(r.nrm_c[...], r.w_cg[:, at])
        for k in range(5):
            rows = part(k, 32)
            active, slope = gelu_parts(r.hid[rows, :])
            r.ug[rows, at] = active
            r.slope_c[rows, at] = low(slope)

    each(CG // 256, up)
    tiles = [slice(GATE + 128 * j, GATE + 128 * j + 128) for j in range(GATE // 128)]
    total = jnp.zeros((SLOTS, 128), F32)
    for at in tiles:
        total = total + r.ug[:, at]
    mean = lane_mean(total, GATE)
    total = jnp.zeros((SLOTS, 128), F32)
    for at in tiles:
        centered = r.ug[:, at] - mean
        total = total + centered * centered
    scale = lax.rsqrt(lane_mean(total, GATE) + NORM_EPS)
    r.gmean[...] = jnp.broadcast_to(mean, (SLOTS, 128))
    r.gscale[...] = jnp.broadcast_to(scale, (SLOTS, 128))
    scale = scale * valid_rows(length)
    for j, at in enumerate(tiles):
        gain = r.small[5 + j // 4 : 6 + j // 4, part(j % 4, 128)]
        r.gpad[PAD : PAD + SLOTS, part(j, 128)] = (r.ug[:, at] - mean) * scale * gain

    def finish(j, at, value):
        r.cv[:, at] = low(value)
        r.gated[:, at] = low(r.ug[:, at] * value)

    convolve(r.gpad, r.tiles, 0, GATE, finish)

    def down(j):
        r.cat[:, part(j + 2, 256)] = dot(r.gated[...], r.w[rows_of("cg_out"), part(j, 256)])

    each(2, down)


def merge_forward(r, length):
    valid = valid_rows(length)
    for j in range(8):
        at = part(j, 128)
        r.mpad[PAD : PAD + SLOTS, at] = r.cat[:, at] * valid

    def finish(j, at, value):
        r.mixed[:, at] = low(r.cat[:, at] + value)

    convolve(r.mpad, r.tiles, 3, 2 * D, finish)

    def merge(j):
        at = part(j, 256)
        r.x2[:, at] = r.x1[:, at] + dot(r.mixed[...], r.w[rows_of("merge"), at])

    each(2, merge)


def final_norm(r, length):
    gain = r.small[4:5, :]
    valid = valid_rows(length)
    total = jnp.zeros((1, D), F32)
    for k in range(2):
        rows = part(k, 80)
        hat, scale = normed(r.x3[rows, :])
        r.out[rows, :] = low(hat * gain * valid[80 * k : 80 * k + 80])
        mine = r.cot[rows, :].astype(F32) * valid[80 * k : 80 * k + 80]
        total = total + fold_rows(mine * hat)
        inner = mine * gain
        back = scale * (inner - (lane_mean(inner, D) + hat * lane_mean(inner * hat, D)))
        r.dx[rows, :] = back
        r.dout[rows, :] = low(0.5 * back)
    r.gains[4:5, :] = total


def merge_back(r, length, emits):
    for k in range(2):
        r.dout[part(k, 80), :] = low(r.dx[part(k, 80), :])
    w_merge = r.w.at[rows_of("merge")]

    def merge(j):
        at = part(j, 256)
        r.dpad[PAD : PAD + SLOTS, at] = dot_t(r.dout[...], w_merge[at, :])

    each(2 * D // 256, merge)
    weight_rows(r.mixed, r.dout, 2, r.left_t, w_merge)
    emits.put_tensor("merge", w_merge)

    def finish(j, at, value):
        r.djoin[:, at] = low(r.dpad[PAD : PAD + SLOTS, at] + value * valid_rows(length))

    convolve_back(r.dpad, r.mpad, r.tiles, 3, 2 * D, r.tgrad, finish)


def gating_back(r, length, emits):
    w_co = r.w.at[rows_of("cg_out")]

    def gate(j):
        at = part(j, 256)
        value = dot_t(r.djoin[:, D:], w_co[at, :])
        r.dhid[:, at] = low(value * r.cv[:, at].astype(F32) * r.slope_c[:, at].astype(F32))
        r.dpad[PAD : PAD + SLOTS, at] = value * r.ug[:, at]

    each(GATE // 256, gate)
    r.dout[...] = r.djoin[:, D:]
    weight_rows(r.gated, r.dout, 3, r.left_t, w_co)
    emits.put_tensor("cg_out", w_co)

    def finish(j, at, value):
        r.dgate[:, at] = value * valid_rows(length)

    convolve_back(r.dpad, r.gpad, r.tiles, 0, GATE, r.tgrad, finish)
    r.sum_inner[...] = jnp.zeros_like(r.sum_inner)
    r.sum_hat[...] = jnp.zeros_like(r.sum_hat)

    def gate_sums(j):
        row, lane = 5 + j // 4, j % 4
        hat = (r.ug[:, part(j + GATE // 128, 128)] - r.gmean[...]) * r.gscale[...]
        grad = r.dgate[:, part(j, 128)]
        r.tgrad[lane, pl.ds(row, 1), :] = fold_rows(grad * hat)
        inner = grad * r.tiles[lane, pl.ds(row, 1), :]
        r.sum_inner[...] += inner
        r.sum_hat[...] += inner * hat

    def gate_back(j):
        row, lane = 5 + j // 4, j % 4
        far = part(j + GATE // 128, 128)
        hat = (r.ug[:, far] - r.gmean[...]) * r.gscale[...]
        inner = r.dgate[:, part(j, 128)] * r.tiles[lane, pl.ds(row, 1), :]
        back = r.gscale[...] * (inner - r.sum_inner[...] - hat * r.sum_hat[...])
        r.dhid[:, far] = low(back * r.slope_c[:, far].astype(F32))

    each(GATE // 128, gate_sums)
    for sums in (r.sum_inner, r.sum_hat):
        sums[...] = jnp.broadcast_to(lane_mean(sums[...], GATE), (SLOTS, 128))
    each(GATE // 128, gate_back)

    def down(j):
        at = part(j, 256)
        r.dnrm[:, at] = dot_t(r.dhid[...], r.w_cg[at, :])

    each(2, down)
    g_cg = r.w.at[rows_of("cg_in")]
    weight_columns(r.nrm_c, r.dhid, 6, r.stage, r.left_t, g_cg)
    emits.put_tensor("cg_in", g_cg)

    def add(rows, back):
        r.dx[rows, :] += back

    r.gains[2:3, :] = norm_rows_back(r.x1, r.small[2:3, :], r.dnrm, add)


def forward_kernel(names, coords, length_ref, frames, cot, *refs):
    sources, refs = refs[: len(PIECES)], refs[len(PIECES) :]
    r = SimpleNamespace(**dict(zip(names, refs)))
    r.cot = cot
    length = length_ref[0]
    loads = Loads(coords, sources, r.w, r.load_sems)
    kept = []

    def keep(source, target):
        copy = pltpu.make_async_copy(source, target, r.keep_sems.at[len(kept)])
        copy.start()
        kept.append(copy)

    for padded in (r.gpad, r.mpad, r.dpad):
        clear_margins(padded)
    r.tgrad[...] = jnp.zeros_like(r.tgrad)
    r.gains[...] = jnp.zeros_like(r.gains)
    loads.wait("small")
    r.small[...] = r.w[ROW * 31 : ROW * 31 + SMALL, :].astype(F32)
    for lane in range(4):
        r.tiles[lane] = r.small[:, part(lane, 128)]
    loads.wait("ffa_in")
    split_columns(r.w.at[rows_of("ffa_in")], r.w_ffa_in, 4, r.stage)
    keep(r.w_ffa_in, r.keep_ffa_in)
    loads.wait("ffa_out")
    keep(r.w.at[rows_of("ffa_out")], r.keep_ffa_out)
    feed_forward(frames, r.small[0:1, :], r.w_ffa_in, r.w.at[rows_of("ffa_out")], r.nrm, r.act, r.slope, r.x1)
    keep(r.nrm, r.keep_nrm)
    keep(r.act, r.keep_act)
    keep(r.slope, r.keep_slope)
    keep(r.x1, r.keep_x1)
    loads.wait("qkv")
    split_columns(r.w.at[rows_of("qkv")], r.w_qkv, 3, r.stage)
    keep(r.w_qkv, r.keep_qkv)
    loads.wait("att_out")
    keep(r.w.at[rows_of("att_out")], r.keep_att)
    attention_forward(r, length)
    keep(r.nrm_t, r.keep_nrm_t)
    keep(r.qkv, r.keep_heads)
    keep(r.probs, r.keep_probs)
    keep(r.ctx, r.keep_ctx)
    loads.wait("cg_in")
    split_columns(r.w.at[rows_of("cg_in")], r.w_cg, 6, r.stage)
    loads.wait("cg_out")
    gating_forward(r, length)
    loads.wait("merge")
    merge_forward(r, length)
    loads.wait("ffb_in")
    split_columns(r.w.at[rows_of("ffb_in")], r.w_ffb_in, 4, r.stage)
    loads.wait("ffb_out")
    w_out = r.w.at[rows_of("ffb_out")]
    feed_forward(r.x2, r.small[3:4, :], r.w_ffb_in, w_out, r.nrm_b, r.act_b, r.slope_b, r.x3)
    final_norm(r, length)
    high = Emits(coords, r.high_kept, r.high_sent, r.high_sems)
    every = Emits(coords, r.low_kept, r.low_sent, r.low_sems)

    def put(block, values):
        (high if block >= 16 else every).put(block, values)

    emits = SimpleNamespace(
        put_tensor=lambda name, rows: [
            put(BLOCK[name][0] + at, rows.at[ROW * at : ROW * at + ROW]) for at in range(BLOCK[name][1])
        ]
    )
    feed_back(
        r.dout, r.w_ffb_in, w_out, r.nrm_b, r.act_b, r.slope_b, r.dhid, r.dnrm, r.stage, r.left_t,
        r.w.at[rows_of("ffb_in")], w_out, emits, "ffb",
    )

    def add(rows, back):
        r.dx[rows, :] += back

    r.gains[3:4, :] = norm_rows_back(r.x2, r.small[3:4, :], r.dnrm, add)
    merge_back(r, length, emits)
    keep(r.djoin, r.keep_djoin)
    gating_back(r, length, emits)
    keep(r.dx, r.keep_dx)
    for lane in range(4):
        at = part(lane, 128)
        r.gains[5:8, at] = r.tgrad[lane, 5:8, :]
        r.w[ROW * 31 : ROW * 31 + SMALL, at] = low(r.tgrad[lane])
    r.w[ROW * 31 : ROW * 31 + 16, :] = low(
        jnp.concatenate(
            [
                jnp.zeros((8, ROW), F32),
                jnp.concatenate([r.tgrad[lane, 8:16, :] for lane in range(4)], axis=1),
            ],
            axis=0,
        )
    )
    r.w[ROW * 31 + SMALL : ROW * 32, :] = jnp.zeros((ROW - SMALL, ROW), BF16)
    put(31, r.w.at[ROW * 31 : ROW * 32])
    for copy in kept:
        copy.wait()
    high.wait()
    every.wait()


def attention_back(r, emits):
    def project(j):
        at = part(j, 256)
        r.dctx[:, at] = low(dot_t(r.datt[...], r.w_att[at, :]))

    each(2, project)
    weight_rows(r.ctx, r.datt, 1, r.left_t, r.w_att)
    emits.put_tensor("att_out", r.w_att)
    first_half = lax.broadcasted_iota(jnp.int32, (1, 128), 1) < HS
    at_row = lax.broadcasted_iota(jnp.int32, (SLOTS, SLOTS), 0)
    at_column = lax.broadcasted_iota(jnp.int32, (SLOTS, SLOTS), 1)
    flip = low((at_row + at_column == SLOTS - 1).astype(F32))

    def heads(pair):
        queries = r.qkv[0:SLOTS, part(pair, 128)]
        keys = r.qkv[:, part(pair + 4, 128)]
        values = r.qkv[:, part(pair + 8, 128)]
        context = r.dctx[:, part(pair, 128)]
        q_parts, k_parts, v_parts = [], [], []
        for odd in range(2):
            head = 2 * pair + odd
            half = first_half if odd == 0 else jnp.logical_not(first_half)
            chances = r.probs[head]
            v_parts.append(t_dot(chances, context)[0:SLOTS])
            wide_chances = chances.astype(F32)
            chance_grad = dot_t(jnp.where(half, context, jnp.zeros_like(context)), values)
            inner = jnp.sum(wide_chances * chance_grad, axis=-1, keepdims=True)
            score_grad = low(wide_chances * (chance_grad - inner))
            q_parts.append(dot(score_grad, keys))
            k_parts.append(t_dot(score_grad, queries)[0:SLOTS])
            wide = jnp.concatenate([dot(flip, score_grad), jnp.zeros((SLOTS, ROW - KEYS), F32)], axis=1)
            wide = pltpu.roll(wide, ROW - SLOTS + 1, 1, stride=1, stride_axis=0)
            r.sums[pl.ds(head, 1), :] = fold_rows(wide)
        scale = HS ** (-0.5)
        r.dhid[:, part(pair, 128)] = low(jnp.where(first_half, q_parts[0], q_parts[1]) * scale)
        r.dhid[:, part(pair + 4, 128)] = low(jnp.where(first_half, k_parts[0], k_parts[1]) * scale)
        r.dhid[:, part(pair + 8, 128)] = low(jnp.where(first_half, v_parts[0], v_parts[1]))

    each(H // 2, heads)

    def down(j):
        at = part(j, 256)
        r.dnrm[:, at] = dot_t(r.dhid[:, 0 : 3 * D], r.w_qkv[at, :])

    each(2, down)

    def add(rows, back):
        r.dx[rows, :] += back
        r.dout[rows, :] = low(0.5 * r.dx[rows, :])

    r.late[1:2, :] = norm_rows_back(r.x1, r.gain_rows[1:2, :], r.dnrm, add)


def attention_weights_back(r, emits):
    weight_columns(r.nrm_t, r.dhid, 3, r.stage, r.left_t, r.g_qkv)
    emits.put_tensor("qkv", r.g_qkv)
    by_entry = lax.dot_general(
        r.sums[...],
        bucket_map(),
        (((1,), (1,)), ((), ())),
        precision=lax.Precision.HIGHEST,
        preferred_element_type=F32,
    )
    flat = fold_rows(own_entries(by_entry))
    r.late[8:9, :] = flat[:, 0:ROW]
    r.late[9:10, :] = flat[:, ROW:]


def backward_kernel(names, coords, frames, gains, gain_rows, *refs):
    r = SimpleNamespace(**dict(zip(names, refs)))
    r.gain_rows = gain_rows
    waits = {}
    for at, (name, source, target) in enumerate(
        (
            ("att", r.in_att, r.w_att),
            ("djoin", r.in_djoin.at[:, 0:D], r.datt),
            ("ctx", r.in_ctx, r.ctx),
            ("heads", r.in_heads, r.qkv),
            ("probs", r.in_probs, r.probs),
            ("qkv", r.in_qkv, r.w_qkv),
            ("x1", r.in_x1, r.x1),
            ("dx", r.in_dx, r.dx),
            ("nrm_t", r.in_nrm_t, r.nrm_t),
            ("ffa_out", r.in_ffa_out, r.w_ffa_out),
            ("slope", r.in_slope, r.slope),
            ("act", r.in_act, r.act),
            ("ffa_in", r.in_ffa_in, r.w_ffa_in),
            ("nrm", r.in_nrm, r.nrm),
        )
    ):
        waits[name] = pltpu.make_async_copy(source, target, r.load_sems.at[at])
        waits[name].start()
    r.late[...] = jnp.zeros_like(r.late)
    emits = Emits(coords, r.low_kept, r.low_sent, r.low_sems)
    for name in ("att", "djoin", "ctx", "heads", "probs", "qkv", "x1", "dx"):
        waits[name].wait()
    attention_back(r, emits)
    waits["nrm_t"].wait()
    attention_weights_back(r, emits)
    for name in ("ffa_out", "slope", "act", "ffa_in", "nrm"):
        waits[name].wait()
    feed_back(
        r.dout, r.w_ffa_in, r.w_ffa_out, r.nrm, r.act, r.slope, r.dhid, r.dnrm, r.stage, r.left_t, r.g_ffa_in,
        r.w_ffa_out, emits, "ffa",
    )

    def add(rows, back):
        r.fgrad[rows, :] = low(r.dx[rows, :] + back)

    r.late[0:1, :] = norm_rows_back(frames, gain_rows[0:1, :], r.dnrm, add)
    r.late[2:8, :] = gains[2:8, :]
    emits.wait()


VM = pl.BlockSpec(memory_space=pltpu.VMEM)
SM = pl.BlockSpec(memory_space=pltpu.SMEM)
ANY = pl.BlockSpec(memory_space=pl.ANY)
WIDE, THIN = ((SLOTS, D), F32), ((SLOTS, D), BF16)
FULL = ((SLOTS, FF), BF16)
HALF_GRADS = ((8, ROW, ROW), BF16)

FORWARD_OUT = {
    "out": (VM, THIN),
    "gains": (VM, ((8, ROW), F32)),
    "small": (VM, ((SMALL, ROW), F32)),
    "high_kept": (ANY, HALF_GRADS),
    "high_sent": (ANY, HALF_GRADS),
    "low_kept": (ANY, HALF_GRADS),
    "low_sent": (ANY, HALF_GRADS),
    "keep_ffa_in": (ANY, ((D, FF), BF16)),
    "keep_ffa_out": (ANY, ((FF, D), BF16)),
    "keep_qkv": (ANY, ((D, 3 * D), BF16)),
    "keep_att": (ANY, ((D, D), BF16)),
    "keep_nrm": (ANY, THIN),
    "keep_act": (ANY, FULL),
    "keep_slope": (ANY, FULL),
    "keep_x1": (ANY, WIDE),
    "keep_nrm_t": (ANY, THIN),
    "keep_heads": (ANY, ((KEYS, 3 * D), BF16)),
    "keep_probs": (ANY, ((H, SLOTS, KEYS), BF16)),
    "keep_ctx": (ANY, THIN),
    "keep_djoin": (ANY, ((SLOTS, 2 * D), BF16)),
    "keep_dx": (ANY, WIDE),
}
FORWARD_SCRATCH = {
    "w": ((32 * ROW, ROW), BF16),
    "w_ffa_in": ((D, FF), BF16),
    "w_qkv": ((D, 3 * D), BF16),
    "w_cg": ((D, CG), BF16),
    "w_ffb_in": ((D, FF), BF16),
    "stage": ((4, 6 * ROW, 128), F32),
    "left_t": ((ROW, SLOTS), BF16),
    "tiles": ((4, SMALL, 128), F32),
    "tgrad": ((4, SMALL, 128), F32),
    "bias": ((H, ROW), F32),
    "nrm": THIN,
    "act": FULL,
    "slope": FULL,
    "nrm_t": THIN,
    "qkv": ((KEYS, 3 * D), BF16),
    "probs": ((H, SLOTS, KEYS), BF16),
    "ctx": THIN,
    "nrm_c": THIN,
    "hid": ((SLOTS, 256), F32),
    "ug": ((SLOTS, CG), F32),
    "slope_c": ((SLOTS, CG), BF16),
    "gmean": ((SLOTS, 128), F32),
    "gscale": ((SLOTS, 128), F32),
    "sum_inner": ((SLOTS, 128), F32),
    "sum_hat": ((SLOTS, 128), F32),
    "gpad": ((PADDED, GATE), F32),
    "cv": ((SLOTS, GATE), BF16),
    "gated": ((SLOTS, GATE), BF16),
    "cat": ((SLOTS, 2 * D), F32),
    "mpad": ((PADDED, 2 * D), F32),
    "mixed": ((SLOTS, 2 * D), BF16),
    "nrm_b": THIN,
    "act_b": FULL,
    "slope_b": FULL,
    "dpad": ((PADDED, GATE), F32),
    "djoin": ((SLOTS, 2 * D), BF16),
    "dgate": ((SLOTS, GATE), F32),
    "dhid": ((SLOTS, CG), BF16),
    "dnrm": WIDE,
    "dout": THIN,
    "dx": WIDE,
    "x1": WIDE,
    "x2": WIDE,
    "x3": WIDE,
    "load_sems": 64,
    "keep_sems": 16,
    "high_sems": 16,
    "low_sems": 4,
}
BACKWARD_IN = (
    "ffa_in", "ffa_out", "qkv", "att", "nrm", "act", "slope", "x1", "nrm_t", "heads", "probs", "ctx", "djoin", "dx",
)
BACKWARD_OUT = {
    "fgrad": (VM, THIN),
    "late": (VM, ((16, ROW), F32)),
    "low_kept": (ANY, HALF_GRADS),
    "low_sent": (ANY, HALF_GRADS),
}
BACKWARD_SCRATCH = {
    "w_ffa_in": ((D, FF), BF16),
    "w_ffa_out": ((FF, D), BF16),
    "w_qkv": ((D, 3 * D), BF16),
    "w_att": ((D, D), BF16),
    "g_ffa_in": ((FF, D), BF16),
    "g_qkv": ((3 * D, D), BF16),
    "stage": ((4, 4 * ROW, 128), F32),
    "left_t": ((ROW, SLOTS), BF16),
    "sums": ((H, ROW), F32),
    "nrm": THIN,
    "act": FULL,
    "slope": FULL,
    "nrm_t": THIN,
    "qkv": ((KEYS, 3 * D), BF16),
    "probs": ((H, SLOTS, KEYS), BF16),
    "ctx": THIN,
    "datt": THIN,
    "dctx": THIN,
    "dhid": FULL,
    "dnrm": WIDE,
    "dout": THIN,
    "dx": WIDE,
    "x1": WIDE,
    "load_sems": 14,
    "low_sems": 12,
}


def call(kernel, name, ins, outs, scratch, limit, aliases=None):
    return pl.pallas_call(
        kernel,
        name=name,
        in_specs=[space for space, _ in ins],
        out_specs=[space for space, _ in outs],
        out_shape=[jax.ShapeDtypeStruct(*kind) for _, kind in outs],
        scratch_shapes=[
            pltpu.SemaphoreType.DMA((each_one,)) if isinstance(each_one, int) else pltpu.VMEM(*each_one)
            for each_one in scratch
        ],
        input_output_aliases=aliases or {},
        compiler_params=pltpu.CompilerParams(vmem_limit_bytes=limit * 2**20),
    )(*[array for _, array in ins])


def forward(coords, length, frames, cot, blocks):
    def kernel(*refs):
        forward_kernel([*FORWARD_OUT, *FORWARD_SCRATCH], *refs)

    outs = call(
        kernel,
        "forward",
        [(SM, coords), (SM, length), (VM, frames), (VM, cot)] + [(ANY, block) for block in blocks],
        list(FORWARD_OUT.values()),
        list(FORWARD_SCRATCH.values()),
        58,
    )
    return dict(zip(FORWARD_OUT, outs))


def backward(coords, frames, state):
    def kernel(*refs):
        names = ["in_" + name for name in BACKWARD_IN] + ["in_low_kept", "in_low_sent"]
        backward_kernel([*names, *BACKWARD_OUT, *BACKWARD_SCRATCH], *refs)

    ins = [(SM, coords), (VM, frames), (VM, state["gains"]), (VM, state["small"])]
    ins += [(ANY, state["keep_" + name]) for name in BACKWARD_IN]
    ins += [(ANY, state["low_kept"]), (ANY, state["low_sent"])]
    outs = call(
        kernel,
        "backward",
        ins,
        list(BACKWARD_OUT.values()),
        list(BACKWARD_SCRATCH.values()),
        58,
        {len(ins) - 2: 2, len(ins) - 1: 3},
    )
    return dict(zip(BACKWARD_OUT, outs))


def segment_bounds():
    bounds = [0]
    for extent in segment_shapes():
        bounds.append(bounds[-1] + math.prod(extent))
    return bounds


def block_rows(device_count):
    total_rows = -(-segment_bounds()[-1] // ROW)
    step = 16 * device_count
    return -(-total_rows // step) * 16


def align_shard(low_shard, shard_size, rows):
    devices = lax.axis_size("dp") * lax.axis_size("fsdp")
    me = lax.axis_index(AXES)
    block = rows * ROW
    lead = block - shard_size
    pieces = [low_shard]
    have = shard_size
    need = lead * (devices - 1) + block
    hop = 1
    while have < need:
        part = min(shard_size, need - have)
        pairs = [(i, i - hop) for i in range(hop, devices)]
        pieces.append(lax.ppermute(low_shard[:part], AXES, pairs))
        have = have + part
        hop = hop + 1
    return lax.dynamic_slice(jnp.concatenate(pieces), (me * lead,), (block,)).reshape(rows, ROW)


def unalign_block(block_sum, shard_size, padded):
    devices = lax.axis_size("dp") * lax.axis_size("fsdp")
    me = lax.axis_index(AXES)
    rows = block_sum.shape[0]
    block = rows * ROW
    lead = block - shard_size
    flat = block_sum.reshape(-1)
    pieces = [flat]
    have = block
    need = lead * (devices - 1) + block
    hop = 1
    while have < need:
        part = min(block, need - have)
        pairs = [(i, i + hop) for i in range(devices - hop)]
        pieces.insert(0, lax.ppermute(flat[block - part :], AXES, pairs))
        have = have + part
        hop = hop + 1
    start = have - block - me * lead
    pieces.append(jnp.zeros((max(0, padded - block),), flat.dtype))
    return lax.dynamic_slice(jnp.concatenate(pieces), (start,), (padded,))


def pair_lists():
    ring = [(i, (i + 2) % 8) for i in range(8)]
    across_x = [(i, i ^ 1) for i in range(8)]
    across_y = [(i, i ^ 2) for i in range(4)]
    across_core = [(i, i ^ 1) for i in range(4)]
    return ring, across_x, across_y, across_core


def fast_mesh():
    return lax.axis_size("dp") == 4 and lax.axis_size("fsdp") == 8


def after(value, *others):
    return lax.optimization_barrier((value, *others))[0]


def gather_blocks(block):
    if not fast_mesh():
        whole = lax.all_gather(block, AXES, axis=0, tiled=True).reshape(32, ROW, ROW)
        return [whole[source_block((0, 0, 0, 0), piece)][piece[4] : piece[4] + piece[5]] for piece in PIECES]
    ring, across_x, across_y, across_core = pair_lists()

    def over_x(value):
        return lax.ppermute(value, "fsdp", across_x)

    def over_y(value):
        return lax.ppermute(value, "dp", across_y)

    def over_core(value, *others):
        return lax.ppermute(after(value, *others), "dp", across_core)

    own = [block]
    for _ in range(3):
        own.append(lax.ppermute(own[-1], "fsdp", ring))
    by_x = [over_x(each_one) for each_one in own]
    by_y = [over_y(each_one) for each_one in own]
    top = [over_x(each_one[:HALF]) for each_one in by_y]
    bottom = [over_y(each_one[HALF:]) for each_one in by_x]
    near = own + by_x + by_y + top + bottom
    later = [own[2], own[3], by_x[3], by_y[3]]
    far = [over_core(each_one) for each_one in own]
    far += [over_core(by_x[at], later[at]) for at in range(3)] + [over_core(by_x[3])]
    far += [over_core(by_y[at], later[at]) for at in range(3)] + [over_core(by_y[3])]
    ends = [own[3], by_x[2], by_x[3], top[3]]
    far += [over_core(top[at], ends[at]) for at in range(3)] + [over_core(top[3])]
    far += [over_core(bottom[at], ends[at]) for at in range(3)] + [over_core(bottom[3])]
    return near + far


def added(*parts):
    total = parts[0].astype(F32)
    for each_one in parts[1:]:
        total = total + each_one.astype(F32)
    return total


def placed_late(late, rows, me):
    block = jnp.concatenate(
        [
            jnp.zeros((rows, ROW), F32),
            late[0:8],
            jnp.zeros((REL_AT - 8, ROW), F32),
            late[8:10],
            jnp.zeros((ROW - REL_AT - 2 + rows, ROW), F32),
        ]
    )
    start = jnp.clip(me * rows - ROW * BLOCK["small"][0] + rows, 0, ROW + rows)
    return lax.dynamic_slice(block, (start, 0), (rows, ROW))


def scatter_blocks(state, back, coords, rows, me):
    late = back["late"]
    if not fast_mesh():
        late = lax.psum(late, AXES)
        blocks = []
        for half in ((back["low_kept"], back["low_sent"]), (state["high_kept"], state["high_sent"])):
            for core in half:
                blocks += [core[4 * x + (3 - z) % 4] for z in range(4) for x in range(2)]
        own = lax.psum_scatter(jnp.concatenate(blocks), AXES, scatter_dimension=0, tiled=True)
        return own.astype(F32) + placed_late(late, rows, me), late[0:8]
    ring, across_x, across_y, across_core = pair_lists()
    high = coords[0] == 1
    high_kept, low_kept = state["high_kept"], back["low_kept"]
    high_got = lax.ppermute(state["high_sent"], "dp", across_core)
    low_got = [lax.ppermute(back["low_sent"][4:], "dp", across_core)]
    low_got.insert(0, lax.ppermute(back["low_sent"][:4], "dp", across_core))

    def chip_sum(own_half, x, first, last):
        here = slice(4 * x + first, 4 * x + last)
        of_high = added(high_kept[here], high_got[here])
        of_low = added(low_kept[here], low_got[x][first:last])
        return low(jnp.where(high == own_half, of_high, of_low))

    def over_x(value):
        return lax.ppermute(value, "fsdp", across_x)

    def over_y(value):
        return lax.ppermute(value, "dp", across_y)

    from_y = over_y(chip_sum(False, 1, 0, 2))
    from_x = over_x(chip_sum(False, 1, 2, 4))
    to_y = chip_sum(False, 0, 0, 2)
    to_x_late = chip_sum(True, 1, 2, 4)
    sent_y = [over_y(to_y[0]), over_y(to_y[1])]
    to_x = low(added(chip_sum(True, 1, 0, 2), from_y))
    sent_x = [over_x(to_x[0]), over_x(to_x[1])]
    to_y_late = low(added(chip_sum(False, 0, 2, 4), from_x))
    sent_x += [over_x(to_x_late[0]), over_x(to_x_late[1])]
    sent_y += [over_y(to_y_late[0]), over_y(to_y_late[1])]
    mine = chip_sum(True, 0, 0, 4)
    late = late + lax.ppermute(late, "dp", across_core)
    late = late + over_x(late)
    late = late + over_y(late)
    running = low(added(mine[0], sent_x[0], sent_y[0]))
    running = low(added(mine[1], sent_x[1], sent_y[1], lax.ppermute(running, "fsdp", ring)))
    late = late + lax.ppermute(late, "fsdp", [(i, i ^ 2) for i in range(8)])
    running = low(added(mine[2], sent_x[2], sent_y[2], lax.ppermute(running, "fsdp", ring)))
    late = late + lax.ppermute(after(late, running), "fsdp", [(i, i ^ 4) for i in range(8)])
    total = added(mine[3], sent_x[3], sent_y[3], lax.ppermute(after(running, late), "fsdp", ring))
    return total + placed_late(late, rows, me), late[0:8]


def sum_everywhere(vector):
    if not fast_mesh():
        return lax.psum(vector, AXES)
    _, across_x, across_y, across_core = pair_lists()
    near_z = [(i, i ^ 2) for i in range(8)]
    far_z = [(i, i ^ 4) for i in range(8)]
    for axis, pairs in (
        ("dp", across_core),
        ("fsdp", across_x),
        ("dp", across_y),
        ("fsdp", near_z),
        ("fsdp", far_z),
    ):
        vector = vector + lax.ppermute(vector, axis, pairs)
    return vector


def most_segments(shard_size, devices):
    bounds = segment_bounds()
    most = 1
    for at in range(devices):
        low_end, high_end = at * shard_size, (at + 1) * shard_size
        most = max(most, sum(1 for b in bounds[1:-1] if low_end < b < high_end) + 1)
    return most


LANES = 128
CHUNK = 256


def entry_places(step):
    row = step * CHUNK + lax.broadcasted_iota(jnp.int32, (CHUNK, LANES), 0)
    return row * LANES + lax.broadcasted_iota(jnp.int32, (CHUNK, LANES), 1)


def update_kernel(segments, params, first, second, grad, new_first, new_second, update, sums):
    step = pl.program_id(0)
    spans = segments.shape[0] - 2

    @pl.when(step == 0)
    def _():
        sums[...] = jnp.zeros_like(sums)

    grads = grad[...]
    firsts = BETA_FIRST * first[...] + (1.0 - BETA_FIRST) * grads
    seconds = BETA_SECOND * second[...] + (1.0 - BETA_SECOND) * grads * grads
    new_first[...] = firsts
    new_second[...] = seconds
    first_hat = firsts * (1.0 / (1.0 - BETA_FIRST**STEP))
    second_hat = seconds * (1.0 / (1.0 - BETA_SECOND**STEP))
    values = params[...]
    change = first_hat / (jnp.sqrt(second_hat) + ADAM_EPS) + WEIGHT_DECAY * values
    update[...] = change
    places = entry_places(step)
    lane = lax.broadcasted_iota(jnp.int32, (1, LANES), 1)
    for at in range(spans):
        inside = (places >= segments[1 + at]) & (places < segments[2 + at])
        mine = lane == segments[0] + at
        for row, entries in enumerate((values, change)):
            squares = jnp.where(inside, entries * entries, 0.0)
            total = jnp.sum(jnp.sum(squares, axis=0, keepdims=True), axis=1, keepdims=True)
            sums[row : row + 1, :] += jnp.where(mine, total, 0.0)


def apply_kernel(segments, sums, params, update, new_params, norms):
    step = pl.program_id(0)
    spans = segments.shape[0] - 2
    roots = jnp.sqrt(sums[0:2, :])
    trust = roots[0:1, :] / (roots[1:2, :] + ADAM_EPS)
    norms[0:2, :] = roots
    norms[2:3, :] = trust
    places = entry_places(step)
    lane = lax.broadcasted_iota(jnp.int32, (1, LANES), 1)
    scale = jnp.zeros((CHUNK, LANES), F32)
    for at in range(spans):
        own = jnp.sum(jnp.where(lane == segments[0] + at, trust, 0.0), axis=1, keepdims=True)
        scale = jnp.where(places >= segments[1 + at], own, scale)
    new_params[...] = params[...] - LEARN_RATE * scale * update[...]


def shards(frames, lengths, cotangent, params, first_moment, second_moment):
    shard_size = params.shape[0]
    devices = lax.axis_size("dp") * lax.axis_size("fsdp")
    me = lax.axis_index(AXES)
    rows = block_rows(devices)
    if fast_mesh():
        dp, fsdp = lax.axis_index("dp"), lax.axis_index("fsdp")
        coords = jnp.stack([dp // 2, dp % 2, fsdp // 2, fsdp % 2]).astype(jnp.int32)
    else:
        coords = jnp.zeros((4,), jnp.int32)
    blocks = gather_blocks(align_shard(low(params), shard_size, rows))
    state = forward(coords, lengths, frames[0], cotangent[0], blocks)
    back = backward(coords, frames[0], state)
    block_sum, gain_grads = scatter_blocks(state, back, coords, rows, me)
    steps = -(-shard_size // (LANES * CHUNK))
    padded = steps * LANES * CHUNK
    grad_shard = unalign_block(low(block_sum), shard_size, padded).astype(F32)

    def square(flat):
        return jnp.pad(flat, (0, padded - flat.shape[0])).reshape(-1, LANES)

    bounds = segment_bounds()
    spans = most_segments(shard_size, devices)
    shard_low = me * shard_size
    first_segment = sum((shard_low >= b).astype(jnp.int32) for b in bounds[1:-1])
    table = jnp.asarray(bounds[1:] + [bounds[-1]] * spans, jnp.int32)
    ends = jnp.clip(lax.dynamic_slice(table, (first_segment,), (spans,)) - shard_low, 0, shard_size)
    segments = jnp.concatenate([first_segment[None], jnp.zeros((1,), jnp.int32), ends]).astype(jnp.int32)
    grid = pl.BlockSpec((CHUNK, LANES), lambda step: (step, 0))
    whole = pl.BlockSpec((8, LANES), lambda step: (0, 0))
    flat_kind = jax.ShapeDtypeStruct((padded // LANES, LANES), F32)
    tile_kind = jax.ShapeDtypeStruct((8, LANES), F32)
    params_square = square(params)
    new_first, new_second, update, sums = pl.pallas_call(
        update_kernel,
        name="update",
        grid=(steps,),
        in_specs=[SM] + [grid] * 4,
        out_specs=[grid] * 3 + [whole],
        out_shape=[flat_kind] * 3 + [tile_kind],
    )(segments, params_square, square(first_moment), square(second_moment), grad_shard.reshape(-1, LANES))
    sums = sum_everywhere(sums)
    new_params, norms = pl.pallas_call(
        apply_kernel,
        name="apply",
        grid=(steps,),
        in_specs=[SM, whole, grid, grid],
        out_specs=[grid, whole],
        out_shape=[flat_kind, tile_kind],
    )(segments, sums, params_square, update)
    count = len(segment_shapes())
    return (
        state["out"].reshape(frames.shape),
        back["fgrad"].reshape(frames.shape),
        new_params.reshape(-1)[:shard_size],
        new_first.reshape(-1)[:shard_size],
        new_second.reshape(-1)[:shard_size],
        norms[0, :count],
        norms[1, :count],
        norms[2, :count],
        gain_grads.reshape(-1),
    )


def solution(mesh):
    placed = (
        P(("dp", "fsdp"), None, None),
        P(("dp", "fsdp")),
        P(("dp", "fsdp"), None, None),
        P(("dp", "fsdp")),
        P(("dp", "fsdp")),
        P(("dp", "fsdp")),
    )
    return jax.shard_map(
        shards,
        mesh=mesh,
        in_specs=placed,
        out_specs=(
            P(("dp", "fsdp"), None, None),
            P(("dp", "fsdp"), None, None),
            P(("dp", "fsdp")),
            P(("dp", "fsdp")),
            P(("dp", "fsdp")),
            P(),
            P(),
            P(),
            P(),
        ),
        check_vma=False,
    )
```

```python
import math
from types import SimpleNamespace

import jax
import jax.numpy as jnp
from jax import lax
from jax.experimental import pallas as pl
from jax.experimental.pallas import tpu as pltpu
from jax.sharding import PartitionSpec as P

STEP = 8
BETA_FIRST = 0.5
BETA_SECOND = 0.5
LEARN_RATE = 0.5
WEIGHT_DECAY = 0.01
ADAM_EPS = 1e-06
AXES = ("dp", "fsdp")


def segment_shapes():
    gate_width = CG // 2
    return [
        (D, FF),
        (FF, D),
        (D, 3 * D),
        (D, D),
        (D, CG),
        (gate_width, D),
        (2 * D, D),
        (D, FF),
        (FF, D),
        (5 * D + gate_width,),
        (KER, gate_width + 2 * D),
        (RELW, H),
    ]


D = 512
H = 8
HS = 64
FF = 2048
CG = 3072
KER = 31
RELW = 128
NORM_EPS = 1e-05
MASK_FILL = -1000000000.0
ROW = 512
HALF = ROW // 2
SLOTS = 160
KEYS = 256
PAD = 16
PADDED = SLOTS + 2 * PAD
GATE = CG // 2
BLOCK = {
    "ffa_in": (0, 4),
    "ffa_out": (4, 4),
    "qkv": (8, 3),
    "att_out": (11, 1),
    "cg_in": (12, 6),
    "cg_out": (18, 3),
    "merge": (21, 2),
    "ffb_in": (23, 4),
    "ffb_out": (27, 4),
    "small": (31, 1),
}
TAPS_AT = 8
REL_AT = 8 + 5 * KER
SMALL = 176
F32, BF16 = jnp.float32, jnp.bfloat16


def dot(left, right):
    return lax.dot_general(left, right, (((1,), (0,)), ((), ())), preferred_element_type=F32)


def dot_t(left, right):
    return lax.dot_general(left, right, (((1,), (1,)), ((), ())), preferred_element_type=F32)


def t_dot(left, right):
    return lax.dot_general(left, right, (((0,), (0,)), ((), ())), preferred_element_type=F32)


def low(values):
    return values.astype(BF16)


def each(count, body):
    def step(at, carry):
        body(at)
        return carry

    lax.fori_loop(0, count, step, 0)


def part(at, size):
    if isinstance(at, int):
        return slice(at * size, at * size + size)
    return pl.ds(pl.multiple_of(at * size, size), size)


def rows_of(name):
    first, count = BLOCK[name]
    return slice(ROW * first, ROW * (first + count))


def lane_mean(values, width):
    return jnp.sum(values, axis=-1, keepdims=True) * (1.0 / width)


def normed(values):
    centered = values - lane_mean(values, values.shape[-1])
    scale = lax.rsqrt(lane_mean(centered * centered, values.shape[-1]) + NORM_EPS)
    return centered * scale, scale


def valid_rows(length):
    return (lax.broadcasted_iota(jnp.int32, (SLOTS, 1), 0) < length).astype(F32)


def fold_rows(values):
    return jnp.sum(values, axis=0, keepdims=True)


def norm_rows(source, gain, target):
    for k in range(2):
        hat, _ = normed(source[part(k, 80), :].astype(F32))
        target[part(k, 80), :] = low(hat * gain)


def norm_rows_back(values, gain, grad, add):
    total = jnp.zeros((1, values.shape[1]), F32)
    for k in range(2):
        rows = part(k, 80)
        hat, scale = normed(values[rows, :].astype(F32))
        mine = grad[rows, :]
        total = total + fold_rows(mine * hat)
        inner = mine * gain
        width = values.shape[1]
        moved = lane_mean(inner, width) + hat * lane_mean(inner * hat, width)
        add(rows, scale * (inner - moved))
    return total


TOTAL_ROWS = 16037
PARTS = 32
TILE = 16
SPAN = 528
STARTS = [TILE * (TOTAL_ROWS * d // (PARTS * TILE)) for d in range(PARTS + 1)]
SHORTEST = min(high - first for first, high in zip(STARTS, STARTS[1:]))


def start_of(d):
    return ((TOTAL_ROWS * d) >> 9) * TILE


def gathered_layout():
    layout = []
    for core in range(2):
        layout += [[(core, 0, 0, back, 0, SPAN, 0)] for back in range(4)]
        for y, x, first, last in ((0, 1, 0, HALF), (1, 0, HALF, SPAN)):
            whole = [(core, y, x, back, 0, SPAN, 0) for back in range(4)]
            diagonal = [(core, 1, 1, back, first, last) for back in range(4)]
            layout += [[whole[0]], [whole[1]]]
            layout += [[whole[2], (*diagonal[0], SPAN)], [whole[3], (*diagonal[1], SPAN)]]
            layout += [[(*diagonal[2], 0)], [(*diagonal[3], 0)]]
    return layout


LAYOUT = gathered_layout()


def source_part(coords, piece):
    y, c, z, x = coords[0], coords[1], coords[2], coords[3]
    yy, cc, xx, zz = y ^ piece[1], c ^ piece[0], x ^ piece[2], (z + 4 - piece[3]) & 3
    return ((yy * 2 + cc) * 4 + zz) * 2 + xx


class Loads:
    def __init__(self, coords, sources, target, seams, sems):
        self.source, self.target, self.seams, self.sems = sources[0], target, seams, sems
        self.here, self.joined = set(), set()
        seams[0, 0] = jnp.zeros((TILE, ROW), BF16)
        seams[PARTS, 1] = jnp.zeros((TILE, ROW), BF16)

        def rows(at, size):
            return pl.ds(pl.multiple_of(at, TILE), size)

        for pieces, source in zip(LAYOUT, sources):
            for piece in pieces:
                first, last, offset = piece[4:]
                offset = offset - first
                d = source_part(coords, piece)
                start = start_of(d)
                length = start_of(d + 1) - start
                inner, outer = max(first, TILE), min(last, SHORTEST)
                sem = sems.at[d]
                pltpu.make_async_copy(
                    source.at[offset + inner : offset + outer], target.at[rows(start + inner, outer - inner)], sem
                ).start()
                if first == 0:
                    pltpu.make_async_copy(source.at[offset : offset + TILE], seams.at[d, 1], sem).start()
                if last == SPAN:

                    @pl.when(length > SHORTEST)
                    def _(source=source, offset=offset, start=start, sem=sem):
                        pltpu.make_async_copy(
                            source.at[offset + SHORTEST : offset + SHORTEST + TILE],
                            target.at[rows(start + SHORTEST, TILE)],
                            sem,
                        ).start()

                    pltpu.make_async_copy(source.at[rows(offset + length, TILE)], seams.at[d + 1, 0], sem).start()

    def wait_part(self, d):
        if d in self.here or not 0 <= d < PARTS:
            return
        self.here.add(d)
        size = STARTS[d + 1] - STARTS[d] + TILE
        pltpu.make_async_copy(self.source.at[0:size], self.target.at[0:size], self.sems.at[d]).wait()

    def wait(self, name):
        rows = rows_of(name)
        last = min(rows.stop, STARTS[-1] + TILE)
        for d in range(PARTS + 1):
            if STARTS[d] < last and STARTS[d] + TILE > rows.start and d not in self.joined:
                self.wait_part(d - 1)
                self.wait_part(d)
                self.joined.add(d)
                self.target[STARTS[d] : STARTS[d] + TILE, :] = self.seams[d, 0] + self.seams[d, 1]
            if d < PARTS and STARTS[d] + TILE < last and STARTS[d + 1] > rows.start:
                self.wait_part(d)


class Emits:
    def __init__(self, coords, halves, sems):
        self.coords, self.halves, self.sems = coords, halves, sems
        self.pending = []

    def put(self, d, values, rows):
        core, z, x = (d // 8) % 2, (d // 2) % 4, d % 2
        kept, sent = self.halves[d // 16]
        far_x = self.coords[3] ^ x
        place = (self.coords[2] + 3 - z) & 3
        sem = self.sems.at[len(self.pending)]

        @pl.when(self.coords[1] == core)
        def _():
            pltpu.make_async_copy(values, kept.at[4 * far_x + place, rows], sem).start()

        @pl.when((self.coords[1] != core) & (far_x == 0))
        def _():
            pltpu.make_async_copy(values, sent[0].at[place, rows], sem).start()

        @pl.when((self.coords[1] != core) & (far_x == 1))
        def _():
            pltpu.make_async_copy(values, sent[1].at[place, rows], sem).start()

        self.pending.append(pltpu.make_async_copy(values, kept.at[0, rows], sem))

    def put_tensor(self, name, values):
        rows = rows_of(name)
        for d in range(PARTS):
            first, last = max(rows.start, STARTS[d]), min(rows.stop, STARTS[d] + SPAN)
            if first < last:
                self.put(d, values.at[first - rows.start : last - rows.start], slice(first - STARTS[d], last - STARTS[d]))

    def wait(self):
        for copy in self.pending:
            copy.wait()


def split_columns(raw, target, wide, stage):
    def chunk(k):
        rows = part(k, 128 * wide)
        for lane in range(4):
            stage[lane, 0 : 128 * wide, :] = raw[rows, lane * 128 : lane * 128 + 128].astype(F32)
        for c in range(wide):
            for lane in range(4):
                place = ROW * c + lane * 128
                target[part(k, 128), place : place + 128] = low(stage[lane, pl.ds(c, 128, stride=wide), :])

    each(4, chunk)


def weight_columns(left, grads, wide, stage, left_t, target):
    left_t[...] = left[...].T

    def chunk(j):
        value = dot(left_t[...], grads[:, part(j, 256)])
        c, pair = j // 2, (j % 2) * 2
        for half in range(2):
            stage[pair + half, pl.ds(c, ROW, stride=wide), :] = value[:, 128 * half : 128 * half + 128]

    each(2 * wide, chunk)

    def lower(k):
        rows = part(k, ROW)
        for lane in range(4):
            target[rows, lane * 128 : lane * 128 + 128] = low(stage[lane, rows, :])

    each(wide, lower)


def weight_rows(left, grads, count, left_t, target):
    def chunk(k):
        left_t[...] = left[:, part(k, ROW)].T
        for at in range(2):
            target[part(k, ROW), 256 * at : 256 * at + 256] = low(dot(left_t[...], grads[:, 256 * at : 256 * at + 256]))

    each(count, chunk)


def feed_forward(inputs, gain, w_in, w_out, nrm, act, slope, result):
    norm_rows(inputs, gain, nrm)

    def up(j):
        at = part(j, 256)
        hidden = dot(nrm[...], w_in[:, at])
        sig = jax.nn.sigmoid(hidden)
        active = hidden * sig
        act[:, at] = low(active)
        slope[:, at] = low(sig + active * (1.0 - sig))

    each(FF // 256, up)

    def down(j):
        at = part(j, 256)
        result[:, at] = inputs[:, at].astype(F32) + 0.5 * dot(act[...], w_out[:, at])

    each(2, down)


def feed_back(dout, w_in, w_out, nrm, act, slope, dhid, dnrm, stage, left_t, g_in, g_out, emits, name):
    def up(j):
        at = part(j, 256)
        grad = dot_t(dout[...], w_out[at, :])
        dhid[:, at] = low(grad * slope[:, at].astype(F32))

    each(FF // 256, up)
    weight_rows(act, dout, 4, left_t, g_out)
    emits.put_tensor(name + "_out", g_out)

    def down(j):
        at = part(j, 256)
        dnrm[:, at] = dot_t(dhid[:, 0:FF], w_in[at, :])

    each(2, down)
    weight_columns(nrm, dhid, 4, stage, left_t, g_in)
    emits.put_tensor(name + "_in", g_in)


def bucket_map():
    entry = lax.broadcasted_iota(jnp.int32, (2 * ROW, ROW), 0) // H
    far = lax.broadcasted_iota(jnp.int32, (2 * ROW, ROW), 1)
    far = jnp.where(far >= ROW // 2, far - ROW, far)
    bucket = jnp.clip(far, -(RELW // 2), RELW // 2 - 1) + RELW // 2
    return (entry == bucket).astype(F32)


def own_entries(flat):
    entry = lax.broadcasted_iota(jnp.int32, (H, 2 * ROW), 1)
    head = lax.broadcasted_iota(jnp.int32, (H, 2 * ROW), 0)
    return jnp.where(lax.rem(entry, H) == head, flat, 0.0)


def tap_row(small, tap, row, lane):
    return small[lane, pl.ds(TAPS_AT + 5 * tap + row, 1), :]


def shifted_sum(padded, at, factor):
    total = None
    for low_part in range(8):
        slab = padded[low_part : low_part + SLOTS + 24, at]
        inner = None
        for high_part in range(4):
            offset = 8 * high_part + low_part
            if offset:
                term = factor(offset) * slab[8 * high_part : 8 * high_part + SLOTS]
                inner = term if inner is None else inner + term
        total = inner if total is None else total + inner
    return total


def convolve(padded, small, first_row, width, finish):

    def chunk(j):
        at = part(j, 128)
        row, lane = first_row + j // 4, j % 4
        finish(j, at, shifted_sum(padded, at, lambda offset: tap_row(small, offset - 1, row, lane)))

    each(width // 128, chunk)


def convolve_back(grads, padded, small, first_row, width, sgrad, finish):

    def chunk(j):
        at = part(j, 128)
        row, lane = first_row + j // 4, j % 4
        finish(j, at, shifted_sum(grads, at, lambda offset: tap_row(small, KER - offset, row, lane)))
        own = grads[PAD : PAD + SLOTS, at]
        for low_part in range(8):
            slab = padded[low_part : low_part + SLOTS + 24, at]
            for high_part in range(4):
                offset = 8 * high_part + low_part
                if offset:
                    tile = slab[8 * high_part : 8 * high_part + SLOTS]
                    sgrad[lane, pl.ds(TAPS_AT + 5 * (offset - 1) + row, 1), :] = fold_rows(own * tile)

    each(width // 128, chunk)


def clear_margins(padded):
    padded[0:PAD, :] = jnp.zeros((PAD, padded.shape[1]), F32)
    padded[PAD + SLOTS : PADDED, :] = jnp.zeros((PAD, padded.shape[1]), F32)


def gelu_parts(hidden):
    bell = jnp.exp(-0.5 * hidden * hidden)
    spread = 1.0 + (0.3275911 * 2.0**-0.5) * jnp.abs(hidden)
    near = pl.reciprocal(spread, approx=True)
    near = near * (2.0 - spread * near)
    tail = jnp.full_like(near, 0.5 * 1.061405429)
    for factor in (-1.453152027, 1.421413741, -0.284496736, 0.254829592):
        tail = tail * near + 0.5 * factor
    tail = tail * near * bell
    below = jnp.where(hidden >= 0.0, 1.0 - tail, tail)
    return hidden * below, below + hidden * bell * ((2.0 * math.pi) ** -0.5)


def attention_forward(r, length):
    norm_rows(r.x1, r.small[1:2, :], r.nrm_t)
    r.qkv[SLOTS:KEYS, :] = jnp.zeros((KEYS - SLOTS, 3 * D), BF16)
    flat = jnp.concatenate([r.small[REL_AT : REL_AT + 1, :], r.small[REL_AT + 1 : REL_AT + 2, :]], axis=1)
    r.bias[...] = dot(low(own_entries(jnp.broadcast_to(flat, (H, 2 * ROW)))), low(bucket_map()))

    def project(j):
        at = part(j, 256)
        r.qkv[0:SLOTS, at] = low(dot(r.nrm_t[...], r.w_qkv[:, at]))

    each(3 * D // 256, project)
    valid = lax.broadcasted_iota(jnp.int32, (1, KEYS), 1) < length
    first_half = lax.broadcasted_iota(jnp.int32, (1, 128), 1) < HS

    def heads(pair):
        queries = r.qkv[0:SLOTS, part(pair, 128)]
        keys = r.qkv[:, part(pair + 4, 128)]
        values = r.qkv[:, part(pair + 8, 128)]
        outs = []
        for odd in range(2):
            head = 2 * pair + odd
            half = first_half if odd == 0 else jnp.logical_not(first_half)
            mine = jnp.where(half, queries, jnp.zeros_like(queries))
            spread = jnp.broadcast_to(r.bias[pl.ds(head, 1), :], (SLOTS, ROW))
            spread = pltpu.roll(spread, 0, 1, stride=1, stride_axis=0)[:, 0:KEYS]
            scores = jnp.where(valid, dot_t(mine, keys) * HS ** (-0.5) + spread, MASK_FILL)
            shifted = jnp.exp(scores - jnp.max(scores, axis=-1, keepdims=True))
            chances = low(shifted / jnp.sum(shifted, axis=-1, keepdims=True))
            r.probs[head] = chances
            outs.append(dot(chances, values))
        r.ctx[:, part(pair, 128)] = low(jnp.where(first_half, outs[0], outs[1]))

    each(H // 2, heads)

    def project_out(j):
        at = part(j, 256)
        r.cat[:, at] = dot(r.ctx[...], r.w[rows_of("att_out"), at])

    each(2, project_out)


def gating_forward(r, length):
    norm_rows(r.x1, r.small[2:3, :], r.nrm_c)

    def up(j):
        at = part(j, 256)
        r.hid[...] = dot(r.nrm_c[...], r.w_cg[:, at])
        for k in range(5):
            rows = part(k, 32)
            active, slope = gelu_parts(r.hid[rows, :])
            r.ug[rows, at] = active
            r.slope_c[rows, at] = low(slope)

    each(CG // 256, up)
    tiles = [slice(GATE + 128 * j, GATE + 128 * j + 128) for j in range(GATE // 128)]
    total = jnp.zeros((SLOTS, 128), F32)
    for at in tiles:
        total = total + r.ug[:, at]
    mean = lane_mean(total, GATE)
    total = jnp.zeros((SLOTS, 128), F32)
    for at in tiles:
        centered = r.ug[:, at] - mean
        total = total + centered * centered
    scale = lax.rsqrt(lane_mean(total, GATE) + NORM_EPS)
    r.gmean[...] = jnp.broadcast_to(mean, (SLOTS, 128))
    r.gscale[...] = jnp.broadcast_to(scale, (SLOTS, 128))
    scale = scale * valid_rows(length)
    for j, at in enumerate(tiles):
        gain = r.small[5 + j // 4 : 6 + j // 4, part(j % 4, 128)]
        r.gpad[PAD : PAD + SLOTS, part(j, 128)] = (r.ug[:, at] - mean) * scale * gain

    def finish(j, at, value):
        r.cv[:, at] = low(value)
        r.gated[:, at] = low(r.ug[:, at] * value)

    convolve(r.gpad, r.tiles, 0, GATE, finish)

    def down(j):
        r.cat[:, part(j + 2, 256)] = dot(r.gated[...], r.w[rows_of("cg_out"), part(j, 256)])

    each(2, down)


def merge_forward(r, length):
    valid = valid_rows(length)
    for j in range(8):
        at = part(j, 128)
        r.mpad[PAD : PAD + SLOTS, at] = r.cat[:, at] * valid

    def finish(j, at, value):
        r.mixed[:, at] = low(r.cat[:, at] + value)

    convolve(r.mpad, r.tiles, 3, 2 * D, finish)

    def merge(j):
        at = part(j, 256)
        r.x2[:, at] = r.x1[:, at] + dot(r.mixed[...], r.w[rows_of("merge"), at])

    each(2, merge)


def final_norm(r, length):
    gain = r.small[4:5, :]
    valid = valid_rows(length)
    total = jnp.zeros((1, D), F32)
    for k in range(2):
        rows = part(k, 80)
        hat, scale = normed(r.x3[rows, :])
        r.out[rows, :] = low(hat * gain * valid[80 * k : 80 * k + 80])
        mine = r.cot[rows, :].astype(F32) * valid[80 * k : 80 * k + 80]
        total = total + fold_rows(mine * hat)
        inner = mine * gain
        back = scale * (inner - (lane_mean(inner, D) + hat * lane_mean(inner * hat, D)))
        r.dx[rows, :] = back
        r.dout[rows, :] = low(0.5 * back)
    r.gains[4:5, :] = total


def merge_back(r, length, emits):
    for k in range(2):
        r.dout[part(k, 80), :] = low(r.dx[part(k, 80), :])
    w_merge = r.w.at[rows_of("merge")]

    def merge(j):
        at = part(j, 256)
        r.dpad[PAD : PAD + SLOTS, at] = dot_t(r.dout[...], w_merge[at, :])

    each(2 * D // 256, merge)
    weight_rows(r.mixed, r.dout, 2, r.left_t, w_merge)
    emits.put_tensor("merge", w_merge)

    def finish(j, at, value):
        r.djoin[:, at] = low(r.dpad[PAD : PAD + SLOTS, at] + value * valid_rows(length))

    convolve_back(r.dpad, r.mpad, r.tiles, 3, 2 * D, r.tgrad, finish)


def gating_back(r, length, emits):
    w_co = r.w.at[rows_of("cg_out")]

    def gate(j):
        at = part(j, 256)
        value = dot_t(r.djoin[:, D:], w_co[at, :])
        r.dhid[:, at] = low(value * r.cv[:, at].astype(F32) * r.slope_c[:, at].astype(F32))
        r.dpad[PAD : PAD + SLOTS, at] = value * r.ug[:, at]

    each(GATE // 256, gate)
    r.dout[...] = r.djoin[:, D:]
    weight_rows(r.gated, r.dout, 3, r.left_t, w_co)
    emits.put_tensor("cg_out", w_co)

    def finish(j, at, value):
        r.dgate[:, at] = value * valid_rows(length)

    convolve_back(r.dpad, r.gpad, r.tiles, 0, GATE, r.tgrad, finish)
    r.sum_inner[...] = jnp.zeros_like(r.sum_inner)
    r.sum_hat[...] = jnp.zeros_like(r.sum_hat)

    def gate_sums(j):
        row, lane = 5 + j // 4, j % 4
        hat = (r.ug[:, part(j + GATE // 128, 128)] - r.gmean[...]) * r.gscale[...]
        grad = r.dgate[:, part(j, 128)]
        r.tgrad[lane, pl.ds(row, 1), :] = fold_rows(grad * hat)
        inner = grad * r.tiles[lane, pl.ds(row, 1), :]
        r.sum_inner[...] += inner
        r.sum_hat[...] += inner * hat

    def gate_back(j):
        row, lane = 5 + j // 4, j % 4
        far = part(j + GATE // 128, 128)
        hat = (r.ug[:, far] - r.gmean[...]) * r.gscale[...]
        inner = r.dgate[:, part(j, 128)] * r.tiles[lane, pl.ds(row, 1), :]
        back = r.gscale[...] * (inner - r.sum_inner[...] - hat * r.sum_hat[...])
        r.dhid[:, far] = low(back * r.slope_c[:, far].astype(F32))

    each(GATE // 128, gate_sums)
    for sums in (r.sum_inner, r.sum_hat):
        sums[...] = jnp.broadcast_to(lane_mean(sums[...], GATE), (SLOTS, 128))
    each(GATE // 128, gate_back)

    def down(j):
        at = part(j, 256)
        r.dnrm[:, at] = dot_t(r.dhid[...], r.w_cg[at, :])

    each(2, down)
    g_cg = r.w.at[rows_of("cg_in")]
    weight_columns(r.nrm_c, r.dhid, 6, r.stage, r.left_t, g_cg)
    emits.put_tensor("cg_in", g_cg)

    def add(rows, back):
        r.dx[rows, :] += back

    r.gains[2:3, :] = norm_rows_back(r.x1, r.small[2:3, :], r.dnrm, add)


def forward_kernel(names, coords, length_ref, frames, cot, *refs):
    sources, refs = refs[: len(LAYOUT)], refs[len(LAYOUT) :]
    r = SimpleNamespace(**dict(zip(names, refs)))
    r.cot = cot
    length = length_ref[0]
    loads = Loads(coords, sources, r.w, r.seams, r.load_sems)
    kept = []

    def keep(source, target):
        copy = pltpu.make_async_copy(source, target, r.keep_sems.at[len(kept)])
        copy.start()
        kept.append(copy)

    for padded in (r.gpad, r.mpad, r.dpad):
        clear_margins(padded)
    r.tgrad[...] = jnp.zeros_like(r.tgrad)
    r.gains[...] = jnp.zeros_like(r.gains)
    loads.wait("small")
    r.small[...] = r.w[ROW * 31 : ROW * 31 + SMALL, :].astype(F32)
    for lane in range(4):
        r.tiles[lane] = r.small[:, part(lane, 128)]
    loads.wait("ffa_in")
    split_columns(r.w.at[rows_of("ffa_in")], r.w_ffa_in, 4, r.stage)
    keep(r.w_ffa_in, r.keep_ffa_in)
    loads.wait("ffa_out")
    keep(r.w.at[rows_of("ffa_out")], r.keep_ffa_out)
    feed_forward(frames, r.small[0:1, :], r.w_ffa_in, r.w.at[rows_of("ffa_out")], r.nrm, r.act, r.slope, r.x1)
    keep(r.nrm, r.keep_nrm)
    keep(r.act, r.keep_act)
    keep(r.slope, r.keep_slope)
    keep(r.x1, r.keep_x1)
    loads.wait("qkv")
    split_columns(r.w.at[rows_of("qkv")], r.w_qkv, 3, r.stage)
    keep(r.w_qkv, r.keep_qkv)
    loads.wait("att_out")
    keep(r.w.at[rows_of("att_out")], r.keep_att)
    attention_forward(r, length)
    keep(r.nrm_t, r.keep_nrm_t)
    keep(r.qkv, r.keep_heads)
    keep(r.probs, r.keep_probs)
    keep(r.ctx, r.keep_ctx)
    loads.wait("cg_in")
    split_columns(r.w.at[rows_of("cg_in")], r.w_cg, 6, r.stage)
    loads.wait("cg_out")
    gating_forward(r, length)
    loads.wait("merge")
    merge_forward(r, length)
    loads.wait("ffb_in")
    split_columns(r.w.at[rows_of("ffb_in")], r.w_ffb_in, 4, r.stage)
    loads.wait("ffb_out")
    w_out = r.w.at[rows_of("ffb_out")]
    feed_forward(r.x2, r.small[3:4, :], r.w_ffb_in, w_out, r.nrm_b, r.act_b, r.slope_b, r.x3)
    final_norm(r, length)
    emits = Emits(
        coords,
        ((r.low_kept, (r.low_near, r.low_far)), (r.high_kept, (r.high_near, r.high_far))),
        r.emit_sems,
    )
    feed_back(
        r.dout, r.w_ffb_in, w_out, r.nrm_b, r.act_b, r.slope_b, r.dhid, r.dnrm, r.stage, r.left_t,
        r.w.at[rows_of("ffb_in")], w_out, emits, "ffb",
    )

    def add(rows, back):
        r.dx[rows, :] += back

    r.gains[3:4, :] = norm_rows_back(r.x2, r.small[3:4, :], r.dnrm, add)
    merge_back(r, length, emits)
    keep(r.djoin, r.keep_djoin)
    gating_back(r, length, emits)
    keep(r.dx, r.keep_dx)
    for lane in range(4):
        at = part(lane, 128)
        r.gains[5:8, at] = r.tgrad[lane, 5:8, :]
        r.w[ROW * 31 : ROW * 31 + SMALL, at] = low(r.tgrad[lane])
    r.w[ROW * 31 : ROW * 31 + 16, :] = low(
        jnp.concatenate(
            [
                jnp.zeros((8, ROW), F32),
                jnp.concatenate([r.tgrad[lane, 8:16, :] for lane in range(4)], axis=1),
            ],
            axis=0,
        )
    )
    r.w[ROW * 31 + SMALL : ROW * 32, :] = jnp.zeros((ROW - SMALL, ROW), BF16)
    emits.put_tensor("small", r.w.at[rows_of("small")])
    for copy in kept:
        copy.wait()
    emits.wait()


def attention_back(r, emits):
    def project(j):
        at = part(j, 256)
        r.dctx[:, at] = low(dot_t(r.datt[...], r.w_att[at, :]))

    each(2, project)
    weight_rows(r.ctx, r.datt, 1, r.left_t, r.w_att)
    emits.put_tensor("att_out", r.w_att)
    first_half = lax.broadcasted_iota(jnp.int32, (1, 128), 1) < HS
    at_row = lax.broadcasted_iota(jnp.int32, (SLOTS, SLOTS), 0)
    at_column = lax.broadcasted_iota(jnp.int32, (SLOTS, SLOTS), 1)
    flip = low((at_row + at_column == SLOTS - 1).astype(F32))

    def heads(pair):
        queries = r.qkv[0:SLOTS, part(pair, 128)]
        keys = r.qkv[:, part(pair + 4, 128)]
        values = r.qkv[:, part(pair + 8, 128)]
        context = r.dctx[:, part(pair, 128)]
        q_parts, k_parts, v_parts = [], [], []
        for odd in range(2):
            head = 2 * pair + odd
            half = first_half if odd == 0 else jnp.logical_not(first_half)
            chances = r.probs[head]
            v_parts.append(t_dot(chances, context)[0:SLOTS])
            wide_chances = chances.astype(F32)
            chance_grad = dot_t(jnp.where(half, context, jnp.zeros_like(context)), values)
            inner = jnp.sum(wide_chances * chance_grad, axis=-1, keepdims=True)
            score_grad = low(wide_chances * (chance_grad - inner))
            q_parts.append(dot(score_grad, keys))
            k_parts.append(t_dot(score_grad, queries)[0:SLOTS])
            wide = jnp.concatenate([dot(flip, score_grad), jnp.zeros((SLOTS, ROW - KEYS), F32)], axis=1)
            wide = pltpu.roll(wide, ROW - SLOTS + 1, 1, stride=1, stride_axis=0)
            r.sums[pl.ds(head, 1), :] = fold_rows(wide)
        scale = HS ** (-0.5)
        r.dhid[:, part(pair, 128)] = low(jnp.where(first_half, q_parts[0], q_parts[1]) * scale)
        r.dhid[:, part(pair + 4, 128)] = low(jnp.where(first_half, k_parts[0], k_parts[1]) * scale)
        r.dhid[:, part(pair + 8, 128)] = low(jnp.where(first_half, v_parts[0], v_parts[1]))

    each(H // 2, heads)

    def down(j):
        at = part(j, 256)
        r.dnrm[:, at] = dot_t(r.dhid[:, 0 : 3 * D], r.w_qkv[at, :])

    each(2, down)

    def add(rows, back):
        r.dx[rows, :] += back
        r.dout[rows, :] = low(0.5 * r.dx[rows, :])

    r.late[1:2, :] = norm_rows_back(r.x1, r.gain_rows[1:2, :], r.dnrm, add)


def attention_weights_back(r, emits):
    weight_columns(r.nrm_t, r.dhid, 3, r.stage, r.left_t, r.g_qkv)
    emits.put_tensor("qkv", r.g_qkv)
    by_entry = lax.dot_general(
        r.sums[...],
        bucket_map(),
        (((1,), (1,)), ((), ())),
        precision=lax.Precision.HIGHEST,
        preferred_element_type=F32,
    )
    flat = fold_rows(own_entries(by_entry))
    r.late[8:9, :] = flat[:, 0:ROW]
    r.late[9:10, :] = flat[:, ROW:]


def backward_kernel(names, coords, frames, gains, gain_rows, *refs):
    r = SimpleNamespace(**dict(zip(names, refs)))
    r.gain_rows = gain_rows
    waits = {}
    for at, (name, source, target) in enumerate(
        (
            ("att", r.in_att, r.w_att),
            ("djoin", r.in_djoin.at[:, 0:D], r.datt),
            ("ctx", r.in_ctx, r.ctx),
            ("heads", r.in_heads, r.qkv),
            ("probs", r.in_probs, r.probs),
            ("qkv", r.in_qkv, r.w_qkv),
            ("x1", r.in_x1, r.x1),
            ("dx", r.in_dx, r.dx),
            ("nrm_t", r.in_nrm_t, r.nrm_t),
            ("ffa_out", r.in_ffa_out, r.w_ffa_out),
            ("slope", r.in_slope, r.slope),
            ("act", r.in_act, r.act),
            ("ffa_in", r.in_ffa_in, r.w_ffa_in),
            ("nrm", r.in_nrm, r.nrm),
        )
    ):
        waits[name] = pltpu.make_async_copy(source, target, r.load_sems.at[at])
        waits[name].start()
    r.late[...] = jnp.zeros_like(r.late)
    emits = Emits(coords, ((r.low_kept, (r.low_near, r.low_far)),), r.emit_sems)
    for name in ("att", "djoin", "ctx", "heads", "probs", "qkv", "x1", "dx"):
        waits[name].wait()
    attention_back(r, emits)
    waits["nrm_t"].wait()
    attention_weights_back(r, emits)
    for name in ("ffa_out", "slope", "act", "ffa_in", "nrm"):
        waits[name].wait()
    feed_back(
        r.dout, r.w_ffa_in, r.w_ffa_out, r.nrm, r.act, r.slope, r.dhid, r.dnrm, r.stage, r.left_t, r.g_ffa_in,
        r.w_ffa_out, emits, "ffa",
    )

    def add(rows, back):
        r.fgrad[rows, :] = low(r.dx[rows, :] + back)

    r.late[0:1, :] = norm_rows_back(frames, gain_rows[0:1, :], r.dnrm, add)
    r.late[2:8, :] = gains[2:8, :]
    emits.wait()


VM = pl.BlockSpec(memory_space=pltpu.VMEM)
SM = pl.BlockSpec(memory_space=pltpu.SMEM)
ANY = pl.BlockSpec(memory_space=pl.ANY)
WIDE, THIN = ((SLOTS, D), F32), ((SLOTS, D), BF16)
FULL = ((SLOTS, FF), BF16)
KEPT, SENT = ((8, SPAN, ROW), BF16), ((4, SPAN, ROW), BF16)

FORWARD_OUT = {
    "out": (VM, THIN),
    "gains": (VM, ((8, ROW), F32)),
    "small": (VM, ((SMALL, ROW), F32)),
    "high_kept": (ANY, KEPT),
    "high_near": (ANY, SENT),
    "high_far": (ANY, SENT),
    "low_kept": (ANY, KEPT),
    "low_near": (ANY, SENT),
    "low_far": (ANY, SENT),
    "keep_ffa_in": (ANY, ((D, FF), BF16)),
    "keep_ffa_out": (ANY, ((FF, D), BF16)),
    "keep_qkv": (ANY, ((D, 3 * D), BF16)),
    "keep_att": (ANY, ((D, D), BF16)),
    "keep_nrm": (ANY, THIN),
    "keep_act": (ANY, FULL),
    "keep_slope": (ANY, FULL),
    "keep_x1": (ANY, WIDE),
    "keep_nrm_t": (ANY, THIN),
    "keep_heads": (ANY, ((KEYS, 3 * D), BF16)),
    "keep_probs": (ANY, ((H, SLOTS, KEYS), BF16)),
    "keep_ctx": (ANY, THIN),
    "keep_djoin": (ANY, ((SLOTS, 2 * D), BF16)),
    "keep_dx": (ANY, WIDE),
}
FORWARD_SCRATCH = {
    "w": ((32 * ROW, ROW), BF16),
    "w_ffa_in": ((D, FF), BF16),
    "w_qkv": ((D, 3 * D), BF16),
    "w_cg": ((D, CG), BF16),
    "w_ffb_in": ((D, FF), BF16),
    "stage": ((4, 6 * ROW, 128), F32),
    "left_t": ((ROW, SLOTS), BF16),
    "tiles": ((4, SMALL, 128), F32),
    "tgrad": ((4, SMALL, 128), F32),
    "bias": ((H, ROW), F32),
    "nrm": THIN,
    "act": FULL,
    "slope": FULL,
    "nrm_t": THIN,
    "qkv": ((KEYS, 3 * D), BF16),
    "probs": ((H, SLOTS, KEYS), BF16),
    "ctx": THIN,
    "nrm_c": THIN,
    "hid": ((SLOTS, 256), F32),
    "ug": ((SLOTS, CG), F32),
    "slope_c": ((SLOTS, CG), BF16),
    "gmean": ((SLOTS, 128), F32),
    "gscale": ((SLOTS, 128), F32),
    "sum_inner": ((SLOTS, 128), F32),
    "sum_hat": ((SLOTS, 128), F32),
    "gpad": ((PADDED, GATE), F32),
    "cv": ((SLOTS, GATE), BF16),
    "gated": ((SLOTS, GATE), BF16),
    "cat": ((SLOTS, 2 * D), F32),
    "mpad": ((PADDED, 2 * D), F32),
    "mixed": ((SLOTS, 2 * D), BF16),
    "nrm_b": THIN,
    "act_b": FULL,
    "slope_b": FULL,
    "dpad": ((PADDED, GATE), F32),
    "djoin": ((SLOTS, 2 * D), BF16),
    "dgate": ((SLOTS, GATE), F32),
    "dhid": ((SLOTS, CG), BF16),
    "dnrm": WIDE,
    "dout": THIN,
    "dx": WIDE,
    "x1": WIDE,
    "x2": WIDE,
    "x3": WIDE,
    "seams": ((PARTS + 1, 2, TILE, ROW), BF16),
    "load_sems": PARTS,
    "keep_sems": 16,
    "emit_sems": 40,
}
BACKWARD_IN = (
    "ffa_in", "ffa_out", "qkv", "att", "nrm", "act", "slope", "x1", "nrm_t", "heads", "probs", "ctx", "djoin", "dx",
)
PASSED = ("low_kept", "low_near", "low_far")
BACKWARD_OUT = {
    "fgrad": (VM, THIN),
    "late": (VM, ((16, ROW), F32)),
    "low_kept": (ANY, KEPT),
    "low_near": (ANY, SENT),
    "low_far": (ANY, SENT),
}
BACKWARD_SCRATCH = {
    "w_ffa_in": ((D, FF), BF16),
    "w_ffa_out": ((FF, D), BF16),
    "w_qkv": ((D, 3 * D), BF16),
    "w_att": ((D, D), BF16),
    "g_ffa_in": ((FF, D), BF16),
    "g_qkv": ((3 * D, D), BF16),
    "stage": ((4, 4 * ROW, 128), F32),
    "left_t": ((ROW, SLOTS), BF16),
    "sums": ((H, ROW), F32),
    "nrm": THIN,
    "act": FULL,
    "slope": FULL,
    "nrm_t": THIN,
    "qkv": ((KEYS, 3 * D), BF16),
    "probs": ((H, SLOTS, KEYS), BF16),
    "ctx": THIN,
    "datt": THIN,
    "dctx": THIN,
    "dhid": FULL,
    "dnrm": WIDE,
    "dout": THIN,
    "dx": WIDE,
    "x1": WIDE,
    "load_sems": 14,
    "emit_sems": 24,
}


def call(kernel, name, ins, outs, scratch, limit, aliases=None):
    return pl.pallas_call(
        kernel,
        name=name,
        in_specs=[space for space, _ in ins],
        out_specs=[space for space, _ in outs],
        out_shape=[jax.ShapeDtypeStruct(*kind) for _, kind in outs],
        scratch_shapes=[
            pltpu.SemaphoreType.DMA((each_one,)) if isinstance(each_one, int) else pltpu.VMEM(*each_one)
            for each_one in scratch
        ],
        input_output_aliases=aliases or {},
        compiler_params=pltpu.CompilerParams(vmem_limit_bytes=limit * 2**20),
    )(*[array for _, array in ins])


def forward(coords, length, frames, cot, blocks):
    def kernel(*refs):
        forward_kernel([*FORWARD_OUT, *FORWARD_SCRATCH], *refs)

    outs = call(
        kernel,
        "forward",
        [(SM, coords), (SM, length), (VM, frames), (VM, cot)] + [(ANY, block) for block in blocks],
        list(FORWARD_OUT.values()),
        list(FORWARD_SCRATCH.values()),
        58,
    )
    return dict(zip(FORWARD_OUT, outs))


def backward(coords, frames, state):
    def kernel(*refs):
        names = ["in_" + name for name in BACKWARD_IN + PASSED]
        backward_kernel([*names, *BACKWARD_OUT, *BACKWARD_SCRATCH], *refs)

    ins = [(SM, coords), (VM, frames), (VM, state["gains"]), (VM, state["small"])]
    ins += [(ANY, state["keep_" + name]) for name in BACKWARD_IN]
    ins += [(ANY, state[name]) for name in PASSED]
    outs = call(
        kernel,
        "backward",
        ins,
        list(BACKWARD_OUT.values()),
        list(BACKWARD_SCRATCH.values()),
        58,
        {len(ins) - 3 + at: 2 + at for at in range(3)},
    )
    return dict(zip(BACKWARD_OUT, outs))


def segment_bounds():
    bounds = [0]
    for extent in segment_shapes():
        bounds.append(bounds[-1] + math.prod(extent))
    return bounds


def fast_mesh():
    return lax.axis_size("dp") == 4 and lax.axis_size("fsdp") == 8


def over_x(value):
    return lax.ppermute(value, "fsdp", [(i, i ^ 1) for i in range(8)])


def over_y(value):
    return lax.ppermute(value, "dp", [(i, i ^ 2) for i in range(4)])


def over_core(value):
    return lax.ppermute(value, "dp", [(i, i ^ 1) for i in range(4)])


def round_z(value):
    return lax.ppermute(value, "fsdp", [(i, (i + 2) % 8) for i in range(8)])


def over_z(value, step):
    return lax.ppermute(value, "fsdp", [(i, i ^ (2 * step)) for i in range(8)])


def after(value, *others):
    return lax.optimization_barrier((value, *others))[0]


def shard_offset(me, shard_size):
    return me * shard_size - start_of(me) * ROW


def gather_shards(shard, me):
    shard_size = shard.shape[0]
    if not fast_mesh():
        whole = lax.all_gather(shard, AXES, axis=0, tiled=True)
        whole = jnp.pad(whole, (0, (STARTS[-1] + SPAN) * ROW - whole.shape[0])).reshape(-1, ROW)
        spans = [whole[start : start + SPAN] for start in STARTS[:-1]]
        spans = spans[:1] + [jnp.concatenate([jnp.zeros((TILE, ROW), BF16), span[TILE:]]) for span in spans[1:]]
        return [
            jnp.concatenate([spans[source_part((0, 0, 0, 0), piece)][piece[4] : piece[5]] for piece in pieces])
            for pieces in LAYOUT
        ]
    most = TILE * ROW
    padded = jnp.pad(shard, (most, SPAN * ROW - shard_size))
    span = lax.dynamic_slice(padded, (most - shard_offset(me, shard_size),), (SPAN * ROW,)).reshape(SPAN, ROW)
    own, by_x, by_y = [span], [], []
    for back in range(4):
        if back < 3:
            own.append(round_z(own[back]))
        if back < 2:
            by_x.append(over_x(own[back]))
            by_y.append(over_y(own[back]))
        else:
            by_x.append(over_x(jnp.concatenate([own[back], by_y[back - 2][:HALF]])))
            by_y.append(over_y(jnp.concatenate([own[back], by_x[back - 2][HALF:SPAN]])))
    for back in (2, 3):
        by_x.append(over_x(by_y[back][:HALF]))
        by_y.append(over_y(by_x[back][HALF:SPAN]))
    far_own = [over_core(after(own[0], own[1])), over_core(after(own[1], own[2])), over_core(after(own[2], own[3]))]
    far_own.append(over_core(after(own[3], by_x[1])))
    until = [own[3], by_x[2], by_x[3], by_x[4], by_x[5]]
    far_x = [over_core(after(each_one, until[at])) for at, each_one in enumerate(by_x[:5])] + [over_core(by_x[5])]
    far_y = [over_core(after(each_one, until[at])) for at, each_one in enumerate(by_y[:5])] + [over_core(by_y[5])]
    return own + by_x + by_y + far_own + far_x + far_y


def added(*parts):
    total = parts[0].astype(F32)
    for each_one in parts[1:]:
        total = total + each_one.astype(F32)
    return total


def late_rows(late, above, below):
    gains = jnp.pad(late[0:8], ((above, below - 8), (0, 0)))
    return gains + jnp.pad(late[8:10], ((above + REL_AT, below - REL_AT - 2), (0, 0)))


def scatter_slow(state, back, shard_size, padded):
    late = back["late"]
    pieces = []
    for source, half in ((back, "low"), (state, "high")):
        for core in range(2):
            for at in range(8):
                z, x = at // 2, at % 2
                if core == 0:
                    span = source[half + "_kept"][4 * x + 3 - z]
                else:
                    span = source[half + ("_near", "_far")[x]][3 - z]
                d = len(pieces)
                pieces.append(span[: STARTS[d + 1] - STARTS[d] if d < PARTS - 1 else SPAN])
    rows = jnp.concatenate(pieces)
    first = ROW * BLOCK["small"][0]
    rows = low(rows.astype(F32) + late_rows(late, first, rows.shape[0] - first))
    flat = rows.reshape(-1)[: segment_bounds()[-1]]
    shard = lax.psum_scatter(flat, AXES, scatter_dimension=0, tiled=True)
    return jnp.pad(shard, (0, padded - shard_size)).astype(F32), lax.psum(late[0:8], AXES)


def scatter_grads(state, back, coords, me, shard_size, padded):
    if not fast_mesh():
        return scatter_slow(state, back, shard_size, padded)
    high = coords[0] == 1
    high_kept, low_kept = state["high_kept"], back["low_kept"]
    high_got = [over_core(state["high_near"]), over_core(state["high_far"])]
    low_far = over_core(back["low_far"])
    low_got = [over_core(after(back["low_near"], low_far)), low_far]

    def chip_sum(own_half, x, first, last):
        here = slice(4 * x + first, 4 * x + last)
        of_high = added(high_kept[here], high_got[x][first:last])
        of_low = added(low_kept[here], low_got[x][first:last])
        return low(jnp.where(high == own_half, of_high, of_low))

    from_y = over_y(chip_sum(False, 1, 0, 2))
    from_x = over_x(chip_sum(False, 1, 2, 4))
    to_y = chip_sum(False, 0, 0, 2)
    sent_y = [over_y(to_y[0]), over_y(to_y[1])]
    to_x_late = chip_sum(True, 1, 2, 4)
    to_x = low(added(chip_sum(True, 1, 0, 2), from_y))
    sent_x = [over_x(to_x[0]), over_x(to_x[1])]
    to_y_late = low(added(chip_sum(False, 0, 2, 4), from_x))
    sent_x += [over_x(to_x_late[0]), over_x(to_x_late[1])]
    sent_y += [over_y(to_y_late[0]), over_y(to_y_late[1])]
    mine = chip_sum(True, 0, 0, 4)
    late = back["late"]
    late = late + over_core(late)
    late = late + over_x(after(late, from_x))
    late = late + over_y(after(late, sent_x[0]))
    running = low(added(mine[0], sent_x[0], sent_y[0]))
    running = low(added(mine[1], sent_x[1], sent_y[1], round_z(running)))
    late = late + over_z(after(late, sent_x[1]), 1)
    running = low(added(mine[2], sent_x[2], sent_y[2], round_z(running)))
    late = late + over_z(after(late, sent_x[2]), 2)
    total = added(mine[3], sent_x[3], sent_y[3], round_z(running))
    first = ROW * BLOCK["small"][0] - STARTS[PARTS - 1]
    total = total + jnp.where(me == PARTS - 1, 1.0, 0.0) * late_rows(late, first, SPAN - first)
    flat = jnp.pad(total.reshape(-1), (0, max(0, TILE * ROW + padded - SPAN * ROW)))
    return lax.dynamic_slice(flat, (shard_offset(me, shard_size),), (padded,)), late[0:8]


def sum_everywhere(vector):
    if not fast_mesh():
        return lax.psum(vector, AXES)
    vector = vector + over_core(vector)
    vector = vector + over_x(vector)
    vector = vector + over_y(vector)
    vector = vector + over_z(vector, 1)
    return vector + over_z(vector, 2)


def most_segments(shard_size, devices):
    bounds = segment_bounds()
    most = 1
    for at in range(devices):
        low_end, high_end = at * shard_size, (at + 1) * shard_size
        most = max(most, sum(1 for b in bounds[1:-1] if low_end < b < high_end) + 1)
    return most


LANES = 128
CHUNK = 512


def chunk_spans(segments, step):
    first, last = step * (CHUNK * LANES), (step + 1) * (CHUNK * LANES)
    for at in range(segments.shape[0] - 2):
        start, end = segments[1 + at], segments[2 + at]
        whole = (start <= first) & (last <= end)
        some = (start < last) & (end > first) & jnp.logical_not(whole)

        def inside(first=first, start=start, end=end):
            row = lax.broadcasted_iota(jnp.int32, (CHUNK, LANES), 0)
            place = first + row * LANES + lax.broadcasted_iota(jnp.int32, (CHUNK, LANES), 1)
            return (place >= start) & (place < end)

        yield at, whole, some, inside


def update_kernel(segments, params, first, second, grad, new_first, new_second, update, sums):
    step = pl.program_id(0)

    @pl.when(step == 0)
    def _():
        sums[...] = jnp.zeros_like(sums)

    grads = grad[...]
    firsts = BETA_FIRST * first[...] + (1.0 - BETA_FIRST) * grads
    seconds = BETA_SECOND * second[...] + (1.0 - BETA_SECOND) * grads * grads
    new_first[...] = firsts
    new_second[...] = seconds
    first_hat = firsts * (1.0 / (1.0 - BETA_FIRST**STEP))
    second_hat = seconds * (1.0 / (1.0 - BETA_SECOND**STEP))
    update[...] = first_hat / (jnp.sqrt(second_hat) + ADAM_EPS) + WEIGHT_DECAY * params[...]
    lane = lax.broadcasted_iota(jnp.int32, (1, LANES), 1)

    def add_squares(at, pick):
        for row, entries in enumerate((params, update)):
            values = entries[...]
            total = jnp.sum(pick(values * values), axis=0, keepdims=True)
            total = jnp.sum(total, axis=1, keepdims=True)
            sums[row : row + 1, :] += jnp.where(lane == segments[0] + at, total, 0.0)

    for at, whole, some, inside in chunk_spans(segments, step):

        @pl.when(whole)
        def _(at=at):
            add_squares(at, lambda squares: squares)

        @pl.when(some)
        def _(at=at, inside=inside):
            add_squares(at, lambda squares: jnp.where(inside(), squares, 0.0))


def apply_kernel(segments, sums, params, update, new_params, norms):
    step = pl.program_id(0)
    roots = jnp.sqrt(sums[0:2, :])
    trust = roots[0:1, :] / (roots[1:2, :] + ADAM_EPS)
    norms[0:2, :] = roots
    norms[2:3, :] = trust
    norms[3:8, :] = jnp.zeros((5, LANES), F32)
    lane = lax.broadcasted_iota(jnp.int32, (1, LANES), 1)
    for at, whole, some, inside in chunk_spans(segments, step):

        def moved(at=at):
            scale = LEARN_RATE * jnp.sum(jnp.where(lane == segments[0] + at, trust, 0.0), axis=1, keepdims=True)
            return params[...] - scale * update[...]

        @pl.when(whole)
        def _(moved=moved):
            new_params[...] = moved()

        @pl.when(some)
        def _(moved=moved, inside=inside):
            new_params[...] = jnp.where(inside(), moved(), new_params[...])


def shards(frames, lengths, cotangent, params, first_moment, second_moment):
    shard_size = params.shape[0]
    devices = lax.axis_size("dp") * lax.axis_size("fsdp")
    me = lax.axis_index(AXES)
    if fast_mesh():
        dp, fsdp = lax.axis_index("dp"), lax.axis_index("fsdp")
        coords = jnp.stack([dp // 2, dp % 2, fsdp // 2, fsdp % 2]).astype(jnp.int32)
    else:
        coords = jnp.zeros((4,), jnp.int32)
    state = forward(coords, lengths, frames[0], cotangent[0], gather_shards(low(params), me))
    back = backward(coords, frames[0], state)
    steps = -(-shard_size // (LANES * CHUNK))
    padded = steps * LANES * CHUNK
    grad_shard, gain_grads = scatter_grads(state, back, coords, me, shard_size, padded)

    def square(flat):
        return jnp.pad(flat, (0, padded - flat.shape[0])).reshape(-1, LANES)

    bounds = segment_bounds()
    spans = most_segments(shard_size, devices)
    shard_low = me * shard_size
    first_segment = sum((shard_low >= b).astype(jnp.int32) for b in bounds[1:-1])
    table = jnp.asarray(bounds[1:] + [bounds[-1]] * spans, jnp.int32)
    ends = jnp.clip(lax.dynamic_slice(table, (first_segment,), (spans,)) - shard_low, 0, shard_size)
    segments = jnp.concatenate([first_segment[None], jnp.zeros((1,), jnp.int32), ends]).astype(jnp.int32)
    grid = pl.BlockSpec((CHUNK, LANES), lambda step: (step, 0))
    whole = pl.BlockSpec((8, LANES), lambda step: (0, 0))
    flat_kind = jax.ShapeDtypeStruct((padded // LANES, LANES), F32)
    tile_kind = jax.ShapeDtypeStruct((8, LANES), F32)
    params_square = square(params)
    new_first, new_second, update, sums = pl.pallas_call(
        update_kernel,
        name="update",
        grid=(steps,),
        in_specs=[SM] + [grid] * 4,
        out_specs=[grid] * 3 + [whole],
        out_shape=[flat_kind] * 3 + [tile_kind],
    )(segments, params_square, square(first_moment), square(second_moment), grad_shard.reshape(-1, LANES))
    sums = sum_everywhere(sums)
    new_params, norms = pl.pallas_call(
        apply_kernel,
        name="apply",
        grid=(steps,),
        in_specs=[SM, whole, grid, grid],
        out_specs=[grid, whole],
        out_shape=[flat_kind, tile_kind],
    )(segments, sums, params_square, update)
    count = len(segment_shapes())
    return (
        state["out"].reshape(frames.shape),
        back["fgrad"].reshape(frames.shape),
        new_params.reshape(-1)[:shard_size],
        new_first.reshape(-1)[:shard_size],
        new_second.reshape(-1)[:shard_size],
        norms[0, :count],
        norms[1, :count],
        norms[2, :count],
        gain_grads.reshape(-1),
    )


def solution(mesh):
    placed = (
        P(("dp", "fsdp"), None, None),
        P(("dp", "fsdp")),
        P(("dp", "fsdp"), None, None),
        P(("dp", "fsdp")),
        P(("dp", "fsdp")),
        P(("dp", "fsdp")),
    )
    return jax.shard_map(
        shards,
        mesh=mesh,
        in_specs=placed,
        out_specs=(
            P(("dp", "fsdp"), None, None),
            P(("dp", "fsdp"), None, None),
            P(("dp", "fsdp")),
            P(("dp", "fsdp")),
            P(("dp", "fsdp")),
            P(),
            P(),
            P(),
            P(),
        ),
        check_vma=False,
    )
```

```python
import math
from types import SimpleNamespace

import jax
import jax.numpy as jnp
from jax import lax
from jax.experimental import pallas as pl
from jax.experimental.pallas import tpu as pltpu
from jax.sharding import PartitionSpec as P

STEP = 8
BETA_FIRST = 0.5
BETA_SECOND = 0.5
LEARN_RATE = 0.5
WEIGHT_DECAY = 0.01
ADAM_EPS = 1e-06
AXES = ("dp", "fsdp")


def segment_shapes():
    gate_width = CG // 2
    return [
        (D, FF),
        (FF, D),
        (D, 3 * D),
        (D, D),
        (D, CG),
        (gate_width, D),
        (2 * D, D),
        (D, FF),
        (FF, D),
        (5 * D + gate_width,),
        (KER, gate_width + 2 * D),
        (RELW, H),
    ]


D = 512
H = 8
HS = 64
FF = 2048
CG = 3072
KER = 31
RELW = 128
NORM_EPS = 1e-05
MASK_FILL = -1000000000.0
ROW = 512
HALF = ROW // 2
SLOTS = 160
KEYS = 256
PAD = 16
PADDED = SLOTS + 2 * PAD
GATE = CG // 2
BLOCK = {
    "ffa_in": (0, 4),
    "ffa_out": (4, 4),
    "qkv": (8, 3),
    "att_out": (11, 1),
    "cg_in": (12, 6),
    "cg_out": (18, 3),
    "merge": (21, 2),
    "ffb_in": (23, 4),
    "ffb_out": (27, 4),
    "small": (31, 1),
}
TAPS_AT = 8
REL_AT = 8 + 5 * KER
SMALL = 176
F32, BF16 = jnp.float32, jnp.bfloat16


def dot(left, right):
    return lax.dot_general(left, right, (((1,), (0,)), ((), ())), preferred_element_type=F32)


def dot_t(left, right):
    return lax.dot_general(left, right, (((1,), (1,)), ((), ())), preferred_element_type=F32)


def t_dot(left, right):
    return lax.dot_general(left, right, (((0,), (0,)), ((), ())), preferred_element_type=F32)


def low(values):
    return values.astype(BF16)


def each(count, body):
    for at in range(count):
        body(at)


def each_loop(count, body):
    def step(at, carry):
        body(at)
        return carry

    lax.fori_loop(0, count, step, 0)


def part(at, size):
    if isinstance(at, int):
        return slice(at * size, at * size + size)
    return pl.ds(pl.multiple_of(at * size, size), size)


def rows_of(name):
    first, count = BLOCK[name]
    return slice(ROW * first, ROW * (first + count))


def lane_mean(values, width):
    return jnp.sum(values, axis=-1, keepdims=True) * (1.0 / width)


def normed(values):
    centered = values - lane_mean(values, values.shape[-1])
    scale = lax.rsqrt(lane_mean(centered * centered, values.shape[-1]) + NORM_EPS)
    return centered * scale, scale


def valid_rows(length):
    return (lax.broadcasted_iota(jnp.int32, (SLOTS, 1), 0) < length).astype(F32)


def fold_rows(values):
    return jnp.sum(values, axis=0, keepdims=True)


def norm_rows(source, gain, target):
    for k in range(2):
        hat, _ = normed(source[part(k, 80), :].astype(F32))
        target[part(k, 80), :] = low(hat * gain)


def norm_rows_back(values, gain, grad, add):
    total = jnp.zeros((1, values.shape[1]), F32)
    for k in range(2):
        rows = part(k, 80)
        hat, scale = normed(values[rows, :].astype(F32))
        mine = grad[rows, :]
        total = total + fold_rows(mine * hat)
        inner = mine * gain
        width = values.shape[1]
        moved = lane_mean(inner, width) + hat * lane_mean(inner * hat, width)
        add(rows, scale * (inner - moved))
    return total


TOTAL_ROWS = 16037
PARTS = 32
TILE = 16
SPAN = 528
STARTS = [TILE * (TOTAL_ROWS * d // (PARTS * TILE)) for d in range(PARTS + 1)]
FIRST_PARTS = max(d for d in range(PARTS) if STARTS[d] < ROW * sum(BLOCK["ffa_out"]))
SHORTEST = min(high - first for first, high in zip(STARTS, STARTS[1:]))


def start_of(d):
    return ((TOTAL_ROWS * d) >> 9) * TILE


def gathered_layout():
    layout = []
    for core in range(2):
        layout += [[(core, 0, 0, back, 0, SPAN, 0)] for back in range(4)]
        for y, x, first, last in ((0, 1, 0, HALF), (1, 0, HALF, SPAN)):
            whole = [(core, y, x, back, 0, SPAN, 0) for back in range(4)]
            diagonal = [(core, 1, 1, back, first, last) for back in range(4)]
            layout += [[whole[0]], [whole[1]]]
            layout += [[whole[2], (*diagonal[0], SPAN)], [whole[3], (*diagonal[1], SPAN)]]
            layout += [[(*diagonal[2], 0)], [(*diagonal[3], 0)]]
    return layout


LAYOUT = gathered_layout()


def source_part(coords, piece):
    y, c, z, x = coords[0], coords[1], coords[2], coords[3]
    yy, cc, xx, zz = y ^ piece[1], c ^ piece[0], x ^ piece[2], (z + 4 - piece[3]) & 3
    return ((yy * 2 + cc) * 4 + zz) * 2 + xx


class Loads:
    def __init__(self, coords, sources, target, seams, sems):
        self.target, self.seams, self.sems = target, seams, sems
        self.here, self.joined = set(), set()
        seams[0, 0] = jnp.zeros((TILE, ROW), BF16)
        seams[PARTS, 1] = jnp.zeros((TILE, ROW), BF16)

        for soon in (True, False):
            for pieces, source in zip(LAYOUT, sources):
                for piece in pieces:
                    d = source_part(coords, piece)
                    first_ones = (d <= FIRST_PARTS) | (d == PARTS - 1)

                    @pl.when(first_ones if soon else jnp.logical_not(first_ones))
                    def _(piece=piece, source=source, d=d):
                        self.start(piece, source, d)

    def start(self, piece, source, d):
        def rows(at, size):
            return pl.ds(pl.multiple_of(at, TILE), size)

        first, last, offset = piece[4:]
        offset = offset - first
        start = start_of(d)
        length = start_of(d + 1) - start
        inner, outer = max(first, TILE), min(last, SHORTEST)
        sem = self.sems.at[d]
        pltpu.make_async_copy(
            source.at[offset + inner : offset + outer], self.target.at[rows(start + inner, outer - inner)], sem
        ).start()
        if first == 0:
            pltpu.make_async_copy(source.at[offset : offset + TILE], self.seams.at[d, 1], sem).start()
        if last == SPAN:

            @pl.when(length > SHORTEST)
            def _():
                pltpu.make_async_copy(
                    source.at[offset + SHORTEST : offset + SHORTEST + TILE],
                    self.target.at[rows(start + SHORTEST, TILE)],
                    sem,
                ).start()

            pltpu.make_async_copy(source.at[rows(offset + length, TILE)], self.seams.at[d + 1, 0], sem).start()

    def wait_part(self, d):
        if d in self.here or not 0 <= d < PARTS:
            return
        self.here.add(d)
        size = STARTS[d + 1] - STARTS[d] + TILE
        pltpu.make_async_copy(self.target.at[0:size], self.target.at[0:size], self.sems.at[d]).wait()

    def wait(self, name):
        rows = rows_of(name)
        last = min(rows.stop, STARTS[-1] + TILE)
        for d in range(PARTS + 1):
            if STARTS[d] < last and STARTS[d] + TILE > rows.start and d not in self.joined:
                self.wait_part(d - 1)
                self.wait_part(d)
                self.joined.add(d)
                self.target[STARTS[d] : STARTS[d] + TILE, :] = self.seams[d, 0] + self.seams[d, 1]
            if d < PARTS and STARTS[d] + TILE < last and STARTS[d + 1] > rows.start:
                self.wait_part(d)


class Emits:
    def __init__(self, coords, halves, sems):
        self.coords, self.halves, self.sems = coords, halves, sems
        self.pending = []

    def put(self, d, values, rows):
        core, z, x = (d // 8) % 2, (d // 2) % 4, d % 2
        kept, sent = self.halves[d // 16]
        far_x = self.coords[3] ^ x
        place = (self.coords[2] + 3 - z) & 3
        sem = self.sems.at[len(self.pending)]

        @pl.when(self.coords[1] == core)
        def _():
            pltpu.make_async_copy(values, kept.at[4 * far_x + place, rows], sem).start()

        @pl.when((self.coords[1] != core) & (far_x == 0))
        def _():
            pltpu.make_async_copy(values, sent[0].at[place, rows], sem).start()

        @pl.when((self.coords[1] != core) & (far_x == 1))
        def _():
            pltpu.make_async_copy(values, sent[1].at[place, rows], sem).start()

        self.pending.append(pltpu.make_async_copy(values, kept.at[0, rows], sem))

    def put_tensor(self, name, values):
        rows = rows_of(name)
        for d in range(PARTS):
            first, last = max(rows.start, STARTS[d]), min(rows.stop, STARTS[d] + SPAN)
            if first < last:
                self.put(d, values.at[first - rows.start : last - rows.start], slice(first - STARTS[d], last - STARTS[d]))

    def wait(self):
        for copy in self.pending:
            copy.wait()


def split_columns(raw, target, wide, stage):
    def chunk(k):
        rows = part(k, 128 * wide)
        for lane in range(4):
            stage[lane, 0 : 128 * wide, :] = raw[rows, lane * 128 : lane * 128 + 128].astype(F32)
        for c in range(wide):
            for lane in range(4):
                place = ROW * c + lane * 128
                target[part(k, 128), place : place + 128] = low(stage[lane, pl.ds(c, 128, stride=wide), :])

    each(4, chunk)


def weight_columns(left, grads, wide, stage, left_t, target):
    left_t[...] = left[...].T

    def chunk(j):
        value = dot(left_t[...], grads[:, part(j, 256)])
        c, pair = j // 2, (j % 2) * 2
        for half in range(2):
            stage[pair + half, pl.ds(c, ROW, stride=wide), :] = value[:, 128 * half : 128 * half + 128]

    each(2 * wide, chunk)

    def lower(k):
        rows = part(k, ROW)
        for lane in range(4):
            target[rows, lane * 128 : lane * 128 + 128] = low(stage[lane, rows, :])

    each(wide, lower)


def weight_rows(left, grads, count, left_t, target):
    def chunk(k):
        left_t[...] = left[:, part(k, ROW)].T
        for at in range(2):
            target[part(k, ROW), 256 * at : 256 * at + 256] = low(dot(left_t[...], grads[:, 256 * at : 256 * at + 256]))

    each(count, chunk)


def feed_forward(inputs, gain, w_in, w_out, nrm, act, slope, result):
    norm_rows(inputs, gain, nrm)

    def up(j):
        at = part(j, 256)
        hidden = dot(nrm[...], w_in[:, at])
        sig = jax.nn.sigmoid(hidden)
        active = hidden * sig
        act[:, at] = low(active)
        slope[:, at] = low(sig + active * (1.0 - sig))

    each(FF // 256, up)

    def down(j):
        at = part(j, 256)
        result[:, at] = inputs[:, at].astype(F32) + 0.5 * dot(act[...], w_out[:, at])

    each(2, down)


def feed_back(dout, w_in, w_out, nrm, act, slope, dhid, dnrm, stage, left_t, g_in, g_out, emits, name):
    def up(j):
        at = part(j, 256)
        grad = dot_t(dout[...], w_out[at, :])
        dhid[:, at] = low(grad * slope[:, at].astype(F32))

    each(FF // 256, up)
    weight_rows(act, dout, 4, left_t, g_out)
    emits.put_tensor(name + "_out", g_out)

    def down(j):
        at = part(j, 256)
        dnrm[:, at] = dot_t(dhid[:, 0:FF], w_in[at, :])

    each(2, down)
    weight_columns(nrm, dhid, 4, stage, left_t, g_in)
    emits.put_tensor(name + "_in", g_in)


def bucket_map():
    entry = lax.broadcasted_iota(jnp.int32, (2 * ROW, ROW), 0) // H
    far = lax.broadcasted_iota(jnp.int32, (2 * ROW, ROW), 1)
    far = jnp.where(far >= ROW // 2, far - ROW, far)
    bucket = jnp.clip(far, -(RELW // 2), RELW // 2 - 1) + RELW // 2
    return (entry == bucket).astype(F32)


def own_entries(flat):
    entry = lax.broadcasted_iota(jnp.int32, (H, 2 * ROW), 1)
    head = lax.broadcasted_iota(jnp.int32, (H, 2 * ROW), 0)
    return jnp.where(lax.rem(entry, H) == head, flat, 0.0)


def tap_row(small, tap, row, lane):
    return small[lane, pl.ds(TAPS_AT + 5 * tap + row, 1), :]


def shifted_sum(padded, at, factor):
    total = None
    for low_part in range(8):
        slab = padded[low_part : low_part + SLOTS + 24, at]
        inner = None
        for high_part in range(4):
            offset = 8 * high_part + low_part
            if offset:
                term = factor(offset) * slab[8 * high_part : 8 * high_part + SLOTS]
                inner = term if inner is None else inner + term
        total = inner if total is None else total + inner
    return total


def convolve(padded, small, first_row, width, finish):

    def chunk(j):
        at = part(j, 128)
        row, lane = first_row + j // 4, j % 4
        finish(j, at, shifted_sum(padded, at, lambda offset: tap_row(small, offset - 1, row, lane)))

    each_loop(width // 128, chunk)


def convolve_back(grads, padded, small, first_row, width, sgrad, finish):

    def chunk(j):
        at = part(j, 128)
        row, lane = first_row + j // 4, j % 4
        finish(j, at, shifted_sum(grads, at, lambda offset: tap_row(small, KER - offset, row, lane)))
        own = grads[PAD : PAD + SLOTS, at]
        for low_part in range(8):
            slab = padded[low_part : low_part + SLOTS + 24, at]
            for high_part in range(4):
                offset = 8 * high_part + low_part
                if offset:
                    tile = slab[8 * high_part : 8 * high_part + SLOTS]
                    sgrad[lane, pl.ds(TAPS_AT + 5 * (offset - 1) + row, 1), :] = fold_rows(own * tile)

    each_loop(width // 128, chunk)


def clear_margins(padded):
    padded[0:PAD, :] = jnp.zeros((PAD, padded.shape[1]), F32)
    padded[PAD + SLOTS : PADDED, :] = jnp.zeros((PAD, padded.shape[1]), F32)


def gelu_parts(hidden):
    bell = jnp.exp(-0.5 * hidden * hidden)
    spread = 1.0 + (0.3275911 * 2.0**-0.5) * jnp.abs(hidden)
    near = pl.reciprocal(spread, approx=True)
    near = near * (2.0 - spread * near)
    tail = jnp.full_like(near, 0.5 * 1.061405429)
    for factor in (-1.453152027, 1.421413741, -0.284496736, 0.254829592):
        tail = tail * near + 0.5 * factor
    tail = tail * near * bell
    below = jnp.where(hidden >= 0.0, 1.0 - tail, tail)
    return hidden * below, below + hidden * bell * ((2.0 * math.pi) ** -0.5)


def attention_forward(r, length):
    norm_rows(r.x1, r.small[1:2, :], r.nrm_t)
    r.qkv[SLOTS:KEYS, :] = jnp.zeros((KEYS - SLOTS, 3 * D), BF16)
    flat = jnp.concatenate([r.small[REL_AT : REL_AT + 1, :], r.small[REL_AT + 1 : REL_AT + 2, :]], axis=1)
    r.bias[...] = dot(low(own_entries(jnp.broadcast_to(flat, (H, 2 * ROW)))), low(bucket_map()))

    def project(j):
        at = part(j, 256)
        r.qkv[0:SLOTS, at] = low(dot(r.nrm_t[...], r.w_qkv[:, at]))

    each(3 * D // 256, project)
    valid = lax.broadcasted_iota(jnp.int32, (1, KEYS), 1) < length
    first_half = lax.broadcasted_iota(jnp.int32, (1, 128), 1) < HS

    def heads(pair):
        queries = r.qkv[0:SLOTS, part(pair, 128)]
        keys = r.qkv[:, part(pair + 4, 128)]
        values = r.qkv[:, part(pair + 8, 128)]
        outs = []
        for odd in range(2):
            head = 2 * pair + odd
            half = first_half if odd == 0 else jnp.logical_not(first_half)
            mine = jnp.where(half, queries, jnp.zeros_like(queries))
            spread = jnp.broadcast_to(r.bias[pl.ds(head, 1), :], (SLOTS, ROW))
            spread = pltpu.roll(spread, 0, 1, stride=1, stride_axis=0)[:, 0:KEYS]
            scores = jnp.where(valid, dot_t(mine, keys) * HS ** (-0.5) + spread, MASK_FILL)
            shifted = jnp.exp(scores - jnp.max(scores, axis=-1, keepdims=True))
            chances = low(shifted / jnp.sum(shifted, axis=-1, keepdims=True))
            r.probs[head] = chances
            outs.append(dot(chances, values))
        r.ctx[:, part(pair, 128)] = low(jnp.where(first_half, outs[0], outs[1]))

    each(H // 2, heads)

    def project_out(j):
        at = part(j, 256)
        r.cat[:, at] = dot(r.ctx[...], r.w[rows_of("att_out"), at])

    each(2, project_out)


def gating_forward(r, length):
    norm_rows(r.x1, r.small[2:3, :], r.nrm_c)

    def up(j):
        at = part(j, 256)
        r.hid[...] = dot(r.nrm_c[...], r.w_cg[:, at])
        for k in range(5):
            rows = part(k, 32)
            active, slope = gelu_parts(r.hid[rows, :])
            r.ug[rows, at] = active
            r.slope_c[rows, at] = low(slope)

    each(CG // 256, up)
    tiles = [slice(GATE + 128 * j, GATE + 128 * j + 128) for j in range(GATE // 128)]
    total = jnp.zeros((SLOTS, 128), F32)
    for at in tiles:
        total = total + r.ug[:, at]
    mean = lane_mean(total, GATE)
    total = jnp.zeros((SLOTS, 128), F32)
    for at in tiles:
        centered = r.ug[:, at] - mean
        total = total + centered * centered
    scale = lax.rsqrt(lane_mean(total, GATE) + NORM_EPS)
    r.gmean[...] = jnp.broadcast_to(mean, (SLOTS, 128))
    r.gscale[...] = jnp.broadcast_to(scale, (SLOTS, 128))
    scale = scale * valid_rows(length)
    for j, at in enumerate(tiles):
        gain = r.small[5 + j // 4 : 6 + j // 4, part(j % 4, 128)]
        r.gpad[PAD : PAD + SLOTS, part(j, 128)] = (r.ug[:, at] - mean) * scale * gain

    def finish(j, at, value):
        r.cv[:, at] = low(value)
        r.gated[:, at] = low(r.ug[:, at] * value)

    convolve(r.gpad, r.tiles, 0, GATE, finish)

    def down(j):
        r.cat[:, part(j + 2, 256)] = dot(r.gated[...], r.w[rows_of("cg_out"), part(j, 256)])

    each(2, down)


def merge_forward(r, length):
    valid = valid_rows(length)
    for j in range(8):
        at = part(j, 128)
        r.mpad[PAD : PAD + SLOTS, at] = r.cat[:, at] * valid

    def finish(j, at, value):
        r.mixed[:, at] = low(r.cat[:, at] + value)

    convolve(r.mpad, r.tiles, 3, 2 * D, finish)

    def merge(j):
        at = part(j, 256)
        r.x2[:, at] = r.x1[:, at] + dot(r.mixed[...], r.w[rows_of("merge"), at])

    each(2, merge)


def final_norm(r, length):
    gain = r.small[4:5, :]
    valid = valid_rows(length)
    total = jnp.zeros((1, D), F32)
    for k in range(2):
        rows = part(k, 80)
        hat, scale = normed(r.x3[rows, :])
        r.out[rows, :] = low(hat * gain * valid[80 * k : 80 * k + 80])
        mine = r.cot[rows, :].astype(F32) * valid[80 * k : 80 * k + 80]
        total = total + fold_rows(mine * hat)
        inner = mine * gain
        back = scale * (inner - (lane_mean(inner, D) + hat * lane_mean(inner * hat, D)))
        r.dx[rows, :] = back
        r.dout[rows, :] = low(0.5 * back)
    r.gains[4:5, :] = total


def merge_back(r, length, emits):
    for k in range(2):
        r.dout[part(k, 80), :] = low(r.dx[part(k, 80), :])
    w_merge = r.w.at[rows_of("merge")]

    def merge(j):
        at = part(j, 256)
        r.dpad[PAD : PAD + SLOTS, at] = dot_t(r.dout[...], w_merge[at, :])

    each(2 * D // 256, merge)
    weight_rows(r.mixed, r.dout, 2, r.left_t, w_merge)
    emits.put_tensor("merge", w_merge)

    def finish(j, at, value):
        r.djoin[:, at] = low(r.dpad[PAD : PAD + SLOTS, at] + value * valid_rows(length))

    convolve_back(r.dpad, r.mpad, r.tiles, 3, 2 * D, r.tgrad, finish)


def gating_back(r, length, emits):
    w_co = r.w.at[rows_of("cg_out")]

    def gate(j):
        at = part(j, 256)
        value = dot_t(r.djoin[:, D:], w_co[at, :])
        r.dhid[:, at] = low(value * r.cv[:, at].astype(F32) * r.slope_c[:, at].astype(F32))
        r.dpad[PAD : PAD + SLOTS, at] = value * r.ug[:, at]

    each(GATE // 256, gate)
    r.dout[...] = r.djoin[:, D:]
    weight_rows(r.gated, r.dout, 3, r.left_t, w_co)
    emits.put_tensor("cg_out", w_co)

    def finish(j, at, value):
        r.dgate[:, at] = value * valid_rows(length)

    convolve_back(r.dpad, r.gpad, r.tiles, 0, GATE, r.tgrad, finish)
    tiles = GATE // 128
    for quarter in range(4):
        rows = part(quarter, SLOTS // 4)
        mean, scale = r.gmean[rows, :], r.gscale[rows, :]
        total, total_hat = jnp.zeros_like(mean), jnp.zeros_like(mean)

        def parts(j, rows=rows, mean=mean, scale=scale):
            row, lane = 5 + j // 4, part(j % 4, 128)
            hat = (r.ug[rows, part(j + tiles, 128)] - mean) * scale
            grad = r.dgate[rows, part(j, 128)]
            return hat, grad, grad * r.small[row : row + 1, lane]

        for j in range(tiles):
            hat, grad, inner = parts(j)
            products = jnp.sum((grad * hat).reshape(-1, 8, 128), axis=0)
            r.gate_sums[part(j, 8), :] = products if quarter == 0 else r.gate_sums[part(j, 8), :] + products
            total = total + inner
            total_hat = total_hat + inner * hat
        total = jnp.broadcast_to(lane_mean(total, GATE), total.shape)
        total_hat = jnp.broadcast_to(lane_mean(total_hat, GATE), total.shape)
        for j in range(tiles):
            hat, _, inner = parts(j)
            far = part(j + tiles, 128)
            r.dgate[rows, part(j, 128)] = scale * (inner - total - hat * total_hat)
    for j in range(tiles):
        far = part(j + tiles, 128)
        r.dhid[:, far] = low(r.dgate[:, part(j, 128)] * r.slope_c[:, far].astype(F32))
        r.tgrad[j % 4, 5 + j // 4 : 6 + j // 4, :] = fold_rows(r.gate_sums[part(j, 8), :])

    def down(j):
        at = part(j, 256)
        r.dnrm[:, at] = dot_t(r.dhid[...], r.w_cg[at, :])

    each(2, down)
    g_cg = r.w.at[rows_of("cg_in")]
    weight_columns(r.nrm_c, r.dhid, 6, r.stage, r.left_t, g_cg)
    emits.put_tensor("cg_in", g_cg)

    def add(rows, back):
        r.dx[rows, :] += back

    r.gains[2:3, :] = norm_rows_back(r.x1, r.small[2:3, :], r.dnrm, add)


def forward_kernel(names, coords, length_ref, frames, cot, *refs):
    sources, refs = refs[: len(LAYOUT)], refs[len(LAYOUT) :]
    r = SimpleNamespace(**dict(zip(names, refs)))
    r.cot = cot
    length = length_ref[0]
    loads = Loads(coords, sources, r.w, r.seams, r.load_sems)
    kept = []

    def keep(source, target):
        copy = pltpu.make_async_copy(source, target, r.keep_sems.at[len(kept)])
        copy.start()
        kept.append(copy)

    for padded in (r.gpad, r.mpad, r.dpad):
        clear_margins(padded)
    r.tgrad[...] = jnp.zeros_like(r.tgrad)
    r.gains[...] = jnp.zeros_like(r.gains)
    loads.wait("small")
    r.small[...] = r.w[ROW * 31 : ROW * 31 + SMALL, :].astype(F32)
    for lane in range(4):
        r.tiles[lane] = r.small[:, part(lane, 128)]
    loads.wait("ffa_in")
    split_columns(r.w.at[rows_of("ffa_in")], r.w_ffa_in, 4, r.stage)
    keep(r.w_ffa_in, r.keep_ffa_in)
    loads.wait("ffa_out")
    keep(r.w.at[rows_of("ffa_out")], r.keep_ffa_out)
    feed_forward(frames, r.small[0:1, :], r.w_ffa_in, r.w.at[rows_of("ffa_out")], r.nrm, r.act, r.slope, r.x1)
    keep(r.nrm, r.keep_nrm)
    keep(r.act, r.keep_act)
    keep(r.slope, r.keep_slope)
    keep(r.x1, r.keep_x1)
    loads.wait("qkv")
    split_columns(r.w.at[rows_of("qkv")], r.w_qkv, 3, r.stage)
    keep(r.w_qkv, r.keep_qkv)
    loads.wait("att_out")
    keep(r.w.at[rows_of("att_out")], r.keep_att)
    attention_forward(r, length)
    keep(r.nrm_t, r.keep_nrm_t)
    keep(r.qkv, r.keep_heads)
    keep(r.probs, r.keep_probs)
    keep(r.ctx, r.keep_ctx)
    loads.wait("cg_in")
    split_columns(r.w.at[rows_of("cg_in")], r.w_cg, 6, r.stage)
    loads.wait("cg_out")
    gating_forward(r, length)
    loads.wait("merge")
    merge_forward(r, length)
    loads.wait("ffb_in")
    split_columns(r.w.at[rows_of("ffb_in")], r.w_ffb_in, 4, r.stage)
    loads.wait("ffb_out")
    w_out = r.w.at[rows_of("ffb_out")]
    feed_forward(r.x2, r.small[3:4, :], r.w_ffb_in, w_out, r.nrm_b, r.act_b, r.slope_b, r.x3)
    final_norm(r, length)
    emits = Emits(
        coords,
        ((r.low_kept, (r.low_near, r.low_far)), (r.high_kept, (r.high_near, r.high_far))),
        r.emit_sems,
    )
    feed_back(
        r.dout, r.w_ffb_in, w_out, r.nrm_b, r.act_b, r.slope_b, r.dhid, r.dnrm, r.stage, r.left_t,
        r.w.at[rows_of("ffb_in")], w_out, emits, "ffb",
    )

    def add(rows, back):
        r.dx[rows, :] += back

    r.gains[3:4, :] = norm_rows_back(r.x2, r.small[3:4, :], r.dnrm, add)
    merge_back(r, length, emits)
    keep(r.djoin, r.keep_djoin)
    gating_back(r, length, emits)
    keep(r.dx, r.keep_dx)
    for lane in range(4):
        at = part(lane, 128)
        r.gains[5:8, at] = r.tgrad[lane, 5:8, :]
        r.w[ROW * 31 : ROW * 31 + SMALL, at] = low(r.tgrad[lane])
    r.w[ROW * 31 : ROW * 31 + 16, :] = low(
        jnp.concatenate(
            [
                jnp.zeros((8, ROW), F32),
                jnp.concatenate([r.tgrad[lane, 8:16, :] for lane in range(4)], axis=1),
            ],
            axis=0,
        )
    )
    r.w[ROW * 31 + SMALL : ROW * 32, :] = jnp.zeros((ROW - SMALL, ROW), BF16)
    emits.put_tensor("small", r.w.at[rows_of("small")])
    for copy in kept:
        copy.wait()
    emits.wait()


def attention_back(r, emits):
    def project(j):
        at = part(j, 256)
        r.dctx[:, at] = low(dot_t(r.datt[...], r.w_att[at, :]))

    each(2, project)
    weight_rows(r.ctx, r.datt, 1, r.left_t, r.w_att)
    emits.put_tensor("att_out", r.w_att)
    first_half = lax.broadcasted_iota(jnp.int32, (1, 128), 1) < HS
    at_row = lax.broadcasted_iota(jnp.int32, (SLOTS, SLOTS), 0)
    at_column = lax.broadcasted_iota(jnp.int32, (SLOTS, SLOTS), 1)
    flip = low((at_row + at_column == SLOTS - 1).astype(F32))

    def heads(pair):
        queries = r.qkv[0:SLOTS, part(pair, 128)]
        keys = r.qkv[:, part(pair + 4, 128)]
        values = r.qkv[:, part(pair + 8, 128)]
        context = r.dctx[:, part(pair, 128)]
        q_parts, k_parts, v_parts = [], [], []
        for odd in range(2):
            head = 2 * pair + odd
            half = first_half if odd == 0 else jnp.logical_not(first_half)
            chances = r.probs[head]
            v_parts.append(t_dot(chances, context)[0:SLOTS])
            wide_chances = chances.astype(F32)
            chance_grad = dot_t(jnp.where(half, context, jnp.zeros_like(context)), values)
            inner = jnp.sum(wide_chances * chance_grad, axis=-1, keepdims=True)
            score_grad = low(wide_chances * (chance_grad - inner))
            q_parts.append(dot(score_grad, keys))
            k_parts.append(t_dot(score_grad, queries)[0:SLOTS])
            wide = jnp.concatenate([dot(flip, score_grad), jnp.zeros((SLOTS, ROW - KEYS), F32)], axis=1)
            wide = pltpu.roll(wide, ROW - SLOTS + 1, 1, stride=1, stride_axis=0)
            r.sums[pl.ds(head, 1), :] = fold_rows(wide)
        scale = HS ** (-0.5)
        r.dhid[:, part(pair, 128)] = low(jnp.where(first_half, q_parts[0], q_parts[1]) * scale)
        r.dhid[:, part(pair + 4, 128)] = low(jnp.where(first_half, k_parts[0], k_parts[1]) * scale)
        r.dhid[:, part(pair + 8, 128)] = low(jnp.where(first_half, v_parts[0], v_parts[1]))

    each(H // 2, heads)

    def down(j):
        at = part(j, 256)
        r.dnrm[:, at] = dot_t(r.dhid[:, 0 : 3 * D], r.w_qkv[at, :])

    each(2, down)

    def add(rows, back):
        r.dx[rows, :] += back
        r.dout[rows, :] = low(0.5 * r.dx[rows, :])

    r.late[1:2, :] = norm_rows_back(r.x1, r.gain_rows[1:2, :], r.dnrm, add)


def attention_weights_back(r, emits):
    weight_columns(r.nrm_t, r.dhid, 3, r.stage, r.left_t, r.g_qkv)
    emits.put_tensor("qkv", r.g_qkv)
    by_entry = lax.dot_general(
        r.sums[...],
        bucket_map(),
        (((1,), (1,)), ((), ())),
        precision=lax.Precision.HIGHEST,
        preferred_element_type=F32,
    )
    flat = fold_rows(own_entries(by_entry))
    r.late[8:9, :] = flat[:, 0:ROW]
    r.late[9:10, :] = flat[:, ROW:]


def backward_kernel(names, coords, frames, gains, gain_rows, *refs):
    r = SimpleNamespace(**dict(zip(names, refs)))
    r.gain_rows = gain_rows
    waits = {}
    for at, (name, source, target) in enumerate(
        (
            ("att", r.in_att, r.w_att),
            ("djoin", r.in_djoin.at[:, 0:D], r.datt),
            ("ctx", r.in_ctx, r.ctx),
            ("heads", r.in_heads, r.qkv),
            ("probs", r.in_probs, r.probs),
            ("qkv", r.in_qkv, r.w_qkv),
            ("x1", r.in_x1, r.x1),
            ("dx", r.in_dx, r.dx),
            ("nrm_t", r.in_nrm_t, r.nrm_t),
            ("ffa_out", r.in_ffa_out, r.w_ffa_out),
            ("slope", r.in_slope, r.slope),
            ("act", r.in_act, r.act),
            ("ffa_in", r.in_ffa_in, r.w_ffa_in),
            ("nrm", r.in_nrm, r.nrm),
        )
    ):
        waits[name] = pltpu.make_async_copy(source, target, r.load_sems.at[at])
        waits[name].start()
    r.late[...] = jnp.zeros_like(r.late)
    emits = Emits(coords, ((r.low_kept, (r.low_near, r.low_far)),), r.emit_sems)
    for name in ("att", "djoin", "ctx", "heads", "probs", "qkv", "x1", "dx"):
        waits[name].wait()
    attention_back(r, emits)
    waits["nrm_t"].wait()
    attention_weights_back(r, emits)
    for name in ("ffa_out", "slope", "act", "ffa_in", "nrm"):
        waits[name].wait()
    feed_back(
        r.dout, r.w_ffa_in, r.w_ffa_out, r.nrm, r.act, r.slope, r.dhid, r.dnrm, r.stage, r.left_t, r.g_ffa_in,
        r.w_ffa_out, emits, "ffa",
    )

    def add(rows, back):
        r.fgrad[rows, :] = low(r.dx[rows, :] + back)

    r.late[0:1, :] = norm_rows_back(frames, gain_rows[0:1, :], r.dnrm, add)
    r.late[2:8, :] = gains[2:8, :]
    emits.wait()


VM = pl.BlockSpec(memory_space=pltpu.VMEM)
SM = pl.BlockSpec(memory_space=pltpu.SMEM)
ANY = pl.BlockSpec(memory_space=pl.ANY)
WIDE, THIN = ((SLOTS, D), F32), ((SLOTS, D), BF16)
FULL = ((SLOTS, FF), BF16)
KEPT, SENT = ((8, SPAN, ROW), BF16), ((4, SPAN, ROW), BF16)

FORWARD_OUT = {
    "out": (VM, THIN),
    "gains": (VM, ((8, ROW), F32)),
    "small": (VM, ((SMALL, ROW), F32)),
    "high_kept": (ANY, KEPT),
    "high_near": (ANY, SENT),
    "high_far": (ANY, SENT),
    "low_kept": (ANY, KEPT),
    "low_near": (ANY, SENT),
    "low_far": (ANY, SENT),
    "keep_ffa_in": (ANY, ((D, FF), BF16)),
    "keep_ffa_out": (ANY, ((FF, D), BF16)),
    "keep_qkv": (ANY, ((D, 3 * D), BF16)),
    "keep_att": (ANY, ((D, D), BF16)),
    "keep_nrm": (ANY, THIN),
    "keep_act": (ANY, FULL),
    "keep_slope": (ANY, FULL),
    "keep_x1": (ANY, WIDE),
    "keep_nrm_t": (ANY, THIN),
    "keep_heads": (ANY, ((KEYS, 3 * D), BF16)),
    "keep_probs": (ANY, ((H, SLOTS, KEYS), BF16)),
    "keep_ctx": (ANY, THIN),
    "keep_djoin": (ANY, ((SLOTS, 2 * D), BF16)),
    "keep_dx": (ANY, WIDE),
}
FORWARD_SCRATCH = {
    "w": ((32 * ROW, ROW), BF16),
    "w_ffa_in": ((D, FF), BF16),
    "w_qkv": ((D, 3 * D), BF16),
    "w_cg": ((D, CG), BF16),
    "w_ffb_in": ((D, FF), BF16),
    "stage": ((4, 6 * ROW, 128), F32),
    "left_t": ((ROW, SLOTS), BF16),
    "tiles": ((4, SMALL, 128), F32),
    "tgrad": ((4, SMALL, 128), F32),
    "bias": ((H, ROW), F32),
    "nrm": THIN,
    "act": FULL,
    "slope": FULL,
    "nrm_t": THIN,
    "qkv": ((KEYS, 3 * D), BF16),
    "probs": ((H, SLOTS, KEYS), BF16),
    "ctx": THIN,
    "nrm_c": THIN,
    "hid": ((SLOTS, 256), F32),
    "ug": ((SLOTS, CG), F32),
    "slope_c": ((SLOTS, CG), BF16),
    "gmean": ((SLOTS, 128), F32),
    "gscale": ((SLOTS, 128), F32),
    "gate_sums": ((8 * GATE // 128, 128), F32),
    "gpad": ((PADDED, GATE), F32),
    "cv": ((SLOTS, GATE), BF16),
    "gated": ((SLOTS, GATE), BF16),
    "cat": ((SLOTS, 2 * D), F32),
    "mpad": ((PADDED, 2 * D), F32),
    "mixed": ((SLOTS, 2 * D), BF16),
    "nrm_b": THIN,
    "act_b": FULL,
    "slope_b": FULL,
    "dpad": ((PADDED, GATE), F32),
    "djoin": ((SLOTS, 2 * D), BF16),
    "dgate": ((SLOTS, GATE), F32),
    "dhid": ((SLOTS, CG), BF16),
    "dnrm": WIDE,
    "dout": THIN,
    "dx": WIDE,
    "x1": WIDE,
    "x2": WIDE,
    "x3": WIDE,
    "seams": ((PARTS + 1, 2, TILE, ROW), BF16),
    "load_sems": PARTS,
    "keep_sems": 16,
    "emit_sems": 40,
}
BACKWARD_IN = (
    "ffa_in", "ffa_out", "qkv", "att", "nrm", "act", "slope", "x1", "nrm_t", "heads", "probs", "ctx", "djoin", "dx",
)
PASSED = ("low_kept", "low_near", "low_far")
BACKWARD_OUT = {
    "fgrad": (VM, THIN),
    "late": (VM, ((16, ROW), F32)),
    "low_kept": (ANY, KEPT),
    "low_near": (ANY, SENT),
    "low_far": (ANY, SENT),
}
BACKWARD_SCRATCH = {
    "w_ffa_in": ((D, FF), BF16),
    "w_ffa_out": ((FF, D), BF16),
    "w_qkv": ((D, 3 * D), BF16),
    "w_att": ((D, D), BF16),
    "g_ffa_in": ((FF, D), BF16),
    "g_qkv": ((3 * D, D), BF16),
    "stage": ((4, 4 * ROW, 128), F32),
    "left_t": ((ROW, SLOTS), BF16),
    "sums": ((H, ROW), F32),
    "nrm": THIN,
    "act": FULL,
    "slope": FULL,
    "nrm_t": THIN,
    "qkv": ((KEYS, 3 * D), BF16),
    "probs": ((H, SLOTS, KEYS), BF16),
    "ctx": THIN,
    "datt": THIN,
    "dctx": THIN,
    "dhid": FULL,
    "dnrm": WIDE,
    "dout": THIN,
    "dx": WIDE,
    "x1": WIDE,
    "load_sems": 14,
    "emit_sems": 24,
}


def call(kernel, name, ins, outs, scratch, limit, aliases=None):
    return pl.pallas_call(
        kernel,
        name=name,
        in_specs=[space for space, _ in ins],
        out_specs=[space for space, _ in outs],
        out_shape=[jax.ShapeDtypeStruct(*kind) for _, kind in outs],
        scratch_shapes=[
            pltpu.SemaphoreType.DMA((each_one,)) if isinstance(each_one, int) else pltpu.VMEM(*each_one)
            for each_one in scratch
        ],
        input_output_aliases=aliases or {},
        compiler_params=pltpu.CompilerParams(vmem_limit_bytes=limit * 2**20),
    )(*[array for _, array in ins])


def forward(coords, length, frames, cot, blocks):
    def kernel(*refs):
        forward_kernel([*FORWARD_OUT, *FORWARD_SCRATCH], *refs)

    outs = call(
        kernel,
        "forward",
        [(SM, coords), (SM, length), (VM, frames), (VM, cot)] + [(ANY, block) for block in blocks],
        list(FORWARD_OUT.values()),
        list(FORWARD_SCRATCH.values()),
        58,
    )
    return dict(zip(FORWARD_OUT, outs))


def backward(coords, frames, state):
    def kernel(*refs):
        names = ["in_" + name for name in BACKWARD_IN + PASSED]
        backward_kernel([*names, *BACKWARD_OUT, *BACKWARD_SCRATCH], *refs)

    ins = [(SM, coords), (VM, frames), (VM, state["gains"]), (VM, state["small"])]
    ins += [(ANY, state["keep_" + name]) for name in BACKWARD_IN]
    ins += [(ANY, state[name]) for name in PASSED]
    outs = call(
        kernel,
        "backward",
        ins,
        list(BACKWARD_OUT.values()),
        list(BACKWARD_SCRATCH.values()),
        58,
        {len(ins) - 3 + at: 2 + at for at in range(3)},
    )
    return dict(zip(BACKWARD_OUT, outs))


def segment_bounds():
    bounds = [0]
    for extent in segment_shapes():
        bounds.append(bounds[-1] + math.prod(extent))
    return bounds


def fast_mesh():
    return lax.axis_size("dp") == 4 and lax.axis_size("fsdp") == 8


def over_x(value):
    return lax.ppermute(value, "fsdp", [(i, i ^ 1) for i in range(8)])


def over_y(value):
    return lax.ppermute(value, "dp", [(i, i ^ 2) for i in range(4)])


def over_core(value):
    return lax.ppermute(value, "dp", [(i, i ^ 1) for i in range(4)])


def round_z(value):
    return lax.ppermute(value, "fsdp", [(i, (i + 2) % 8) for i in range(8)])


def over_z(value, step):
    return lax.ppermute(value, "fsdp", [(i, i ^ (2 * step)) for i in range(8)])


def after(value, *others):
    return lax.optimization_barrier((value, *others))[0]


def shard_offset(me, shard_size):
    return me * shard_size - start_of(me) * ROW


def gather_shards(shard, me):
    shard_size = shard.shape[0]
    if not fast_mesh():
        whole = lax.all_gather(shard, AXES, axis=0, tiled=True)
        whole = jnp.pad(whole, (0, (STARTS[-1] + SPAN) * ROW - whole.shape[0])).reshape(-1, ROW)
        spans = [whole[start : start + SPAN] for start in STARTS[:-1]]
        spans = spans[:1] + [jnp.concatenate([jnp.zeros((TILE, ROW), BF16), span[TILE:]]) for span in spans[1:]]
        return [
            jnp.concatenate([spans[source_part((0, 0, 0, 0), piece)][piece[4] : piece[5]] for piece in pieces])
            for pieces in LAYOUT
        ]
    most = TILE * ROW
    padded = jnp.pad(shard, (most, SPAN * ROW - shard_size))
    span = lax.dynamic_slice(padded, (most - shard_offset(me, shard_size),), (SPAN * ROW,)).reshape(SPAN, ROW)
    own, by_x, by_y = [span], [], []
    for back in range(4):
        if back < 3:
            own.append(round_z(own[back]))
        if back < 2:
            by_x.append(over_x(own[back]))
            by_y.append(over_y(own[back]))
            own[back + 1], by_x[back], by_y[back] = lax.optimization_barrier((own[back + 1], by_x[back], by_y[back]))
        else:
            by_x.append(over_x(jnp.concatenate([own[back], by_y[back - 2][:HALF]])))
            by_y.append(over_y(jnp.concatenate([own[back], by_x[back - 2][HALF:SPAN]])))
    by_x.append(over_x(by_y[2][:HALF]))
    by_y.append(over_y(by_x[2][HALF:SPAN]))
    last_x, last_y = by_y[3][:HALF], by_x[3][HALF:SPAN]
    by_x.append(over_x(after(last_x, by_x[4])))
    by_y.append(over_y(after(last_y, by_y[4])))
    late_ones = (by_x[3], by_y[3])
    far_own = [over_core(each_one) for each_one in own[:2]] + [over_core(after(each_one, *late_ones)) for each_one in own[2:]]
    far = [far_own]
    for way in (by_x, by_y):
        far.append([over_core(way[0])] + [over_core(after(way[at], *late_ones)) for at in (1, 2)])
        far[-1] += [over_core(way[at]) for at in (3, 4, 5)]
    return own + by_x + by_y + far[0] + far[1] + far[2]


def added(*parts):
    total = parts[0].astype(F32)
    for each_one in parts[1:]:
        total = total + each_one.astype(F32)
    return total


def late_rows(late, above, below):
    gains = jnp.pad(late[0:8], ((above, below - 8), (0, 0)))
    return gains + jnp.pad(late[8:10], ((above + REL_AT, below - REL_AT - 2), (0, 0)))


def scatter_slow(state, back, shard_size, padded):
    late = back["late"]
    pieces = []
    for source, half in ((back, "low"), (state, "high")):
        for core in range(2):
            for at in range(8):
                z, x = at // 2, at % 2
                if core == 0:
                    span = source[half + "_kept"][4 * x + 3 - z]
                else:
                    span = source[half + ("_near", "_far")[x]][3 - z]
                d = len(pieces)
                pieces.append(span[: STARTS[d + 1] - STARTS[d] if d < PARTS - 1 else SPAN])
    rows = jnp.concatenate(pieces)
    first = ROW * BLOCK["small"][0]
    rows = low(rows.astype(F32) + late_rows(late, first, rows.shape[0] - first))
    flat = rows.reshape(-1)[: segment_bounds()[-1]]
    shard = lax.psum_scatter(flat, AXES, scatter_dimension=0, tiled=True)
    return jnp.pad(shard, (0, padded - shard_size)).astype(F32), lax.psum(late[0:8], AXES)


def scatter_grads(state, back, coords, me, shard_size, padded):
    if not fast_mesh():
        return scatter_slow(state, back, shard_size, padded)
    high = coords[0] == 1
    high_kept, low_kept = state["high_kept"], back["low_kept"]
    high_got = [over_core(state["high_near"]), over_core(state["high_far"])]
    low_far = over_core(back["low_far"])

    def chip_sum(own_half, x, first, last):
        here = slice(4 * x + first, 4 * x + last)
        of_high = added(high_kept[here], high_got[x][first:last])
        of_low = added(low_kept[here], (low_far if x else low_near)[first:last])
        return low(jnp.where(high == own_half, of_high, of_low))

    late = back["late"]
    late = late + over_core(late)
    late = late + over_x(late)
    late = late + over_y(late)
    late = late + over_z(late, 1)
    late = late + over_z(late, 2)
    for_y, for_x = chip_sum(False, 1, 0, 2), chip_sum(False, 1, 2, 4)
    for_y, for_x, late = lax.optimization_barrier((for_y, for_x, late))
    from_y, from_x = over_y(for_y), over_x(for_x)
    low_near = over_core(after(back["low_near"], for_y, for_x))
    to_y = chip_sum(False, 0, 0, 2)
    sent_y = [over_y(to_y[0]), over_y(to_y[1])]
    to_x_late = chip_sum(True, 1, 2, 4)
    to_x = low(added(chip_sum(True, 1, 0, 2), from_y))
    sent_x = [over_x(to_x[0]), over_x(to_x[1])]
    to_y_late = low(added(chip_sum(False, 0, 2, 4), from_x))
    sent_x += [over_x(to_x_late[0]), over_x(to_x_late[1])]
    sent_y += [over_y(to_y_late[0]), over_y(to_y_late[1])]
    mine = chip_sum(True, 0, 0, 4)
    halves = []
    for rows in (slice(0, HALF), slice(HALF, SPAN)):
        running = None
        for at in range(4):
            parts = [mine[at][rows], sent_x[at][rows], sent_y[at][rows]]
            if at:
                parts.append(round_z(running))
            running = added(*parts)
            running = low(running) if at < 3 else running
        halves.append(running)
    total = jnp.concatenate(halves)
    first = ROW * BLOCK["small"][0] - STARTS[PARTS - 1]
    total = total + jnp.where(me == PARTS - 1, 1.0, 0.0) * late_rows(late, first, SPAN - first)
    flat = jnp.pad(total.reshape(-1), (0, max(0, TILE * ROW + padded - SPAN * ROW)))
    return lax.dynamic_slice(flat, (shard_offset(me, shard_size),), (padded,)), late[0:8]


def sum_everywhere(vector):
    if not fast_mesh():
        return lax.psum(vector, AXES)
    vector = vector + over_core(vector)
    vector = vector + over_x(vector)
    vector = vector + over_y(vector)
    vector = vector + over_z(vector, 1)
    return vector + over_z(vector, 2)


def most_segments(shard_size, devices):
    bounds = segment_bounds()
    most = 1
    for at in range(devices):
        low_end, high_end = at * shard_size, (at + 1) * shard_size
        most = max(most, sum(1 for b in bounds[1:-1] if low_end < b < high_end) + 1)
    return most


LANES = 128
CHUNK = 512


def chunk_spans(segments, step):
    first, last = step * (CHUNK * LANES), (step + 1) * (CHUNK * LANES)
    for at in range(segments.shape[0] - 2):
        start, end = segments[1 + at], segments[2 + at]
        whole = (start <= first) & (last <= end)
        some = (start < last) & (end > first) & jnp.logical_not(whole)

        def inside(first=first, start=start, end=end):
            row = lax.broadcasted_iota(jnp.int32, (CHUNK, LANES), 0)
            place = first + row * LANES + lax.broadcasted_iota(jnp.int32, (CHUNK, LANES), 1)
            return (place >= start) & (place < end)

        yield at, whole, some, inside


def update_kernel(segments, params, first, second, grad, new_first, new_second, update, sums):
    step = pl.program_id(0)

    @pl.when(step == 0)
    def _():
        sums[...] = jnp.zeros_like(sums)

    grads = grad[...]
    firsts = BETA_FIRST * first[...] + (1.0 - BETA_FIRST) * grads
    seconds = BETA_SECOND * second[...] + (1.0 - BETA_SECOND) * grads * grads
    new_first[...] = firsts
    new_second[...] = seconds
    first_hat = firsts * (1.0 / (1.0 - BETA_FIRST**STEP))
    second_hat = seconds * (1.0 / (1.0 - BETA_SECOND**STEP))
    update[...] = first_hat / (jnp.sqrt(second_hat) + ADAM_EPS) + WEIGHT_DECAY * params[...]
    lane = lax.broadcasted_iota(jnp.int32, (1, LANES), 1)

    def add_squares(at, pick):
        for row, entries in enumerate((params, update)):
            values = entries[...]
            total = jnp.sum(pick(values * values), axis=0, keepdims=True)
            total = jnp.sum(total, axis=1, keepdims=True)
            sums[row : row + 1, :] += jnp.where(lane == segments[0] + at, total, 0.0)

    for at, whole, some, inside in chunk_spans(segments, step):

        @pl.when(whole)
        def _(at=at):
            add_squares(at, lambda squares: squares)

        @pl.when(some)
        def _(at=at, inside=inside):
            add_squares(at, lambda squares: jnp.where(inside(), squares, 0.0))


def apply_kernel(segments, sums, params, update, new_params, norms):
    step = pl.program_id(0)
    roots = jnp.sqrt(sums[0:2, :])
    trust = roots[0:1, :] / (roots[1:2, :] + ADAM_EPS)
    norms[0:2, :] = roots
    norms[2:3, :] = trust
    norms[3:8, :] = jnp.zeros((5, LANES), F32)
    lane = lax.broadcasted_iota(jnp.int32, (1, LANES), 1)
    for at, whole, some, inside in chunk_spans(segments, step):

        def moved(at=at):
            scale = LEARN_RATE * jnp.sum(jnp.where(lane == segments[0] + at, trust, 0.0), axis=1, keepdims=True)
            return params[...] - scale * update[...]

        @pl.when(whole)
        def _(moved=moved):
            new_params[...] = moved()

        @pl.when(some)
        def _(moved=moved, inside=inside):
            new_params[...] = jnp.where(inside(), moved(), new_params[...])


def shards(frames, lengths, cotangent, params, first_moment, second_moment):
    shard_size = params.shape[0]
    devices = lax.axis_size("dp") * lax.axis_size("fsdp")
    me = lax.axis_index(AXES)
    if fast_mesh():
        dp, fsdp = lax.axis_index("dp"), lax.axis_index("fsdp")
        coords = jnp.stack([dp // 2, dp % 2, fsdp // 2, fsdp % 2]).astype(jnp.int32)
    else:
        coords = jnp.zeros((4,), jnp.int32)
    state = forward(coords, lengths, frames[0], cotangent[0], gather_shards(low(params), me))
    back = backward(coords, frames[0], state)
    steps = -(-shard_size // (LANES * CHUNK))
    padded = steps * LANES * CHUNK
    grad_shard, gain_grads = scatter_grads(state, back, coords, me, shard_size, padded)

    def square(flat):
        return jnp.pad(flat, (0, padded - flat.shape[0])).reshape(-1, LANES)

    bounds = segment_bounds()
    spans = most_segments(shard_size, devices)
    shard_low = me * shard_size
    first_segment = sum((shard_low >= b).astype(jnp.int32) for b in bounds[1:-1])
    table = jnp.asarray(bounds[1:] + [bounds[-1]] * spans, jnp.int32)
    ends = jnp.clip(lax.dynamic_slice(table, (first_segment,), (spans,)) - shard_low, 0, shard_size)
    segments = jnp.concatenate([first_segment[None], jnp.zeros((1,), jnp.int32), ends]).astype(jnp.int32)
    grid = pl.BlockSpec((CHUNK, LANES), lambda step: (step, 0))
    whole = pl.BlockSpec((8, LANES), lambda step: (0, 0))
    flat_kind = jax.ShapeDtypeStruct((padded // LANES, LANES), F32)
    tile_kind = jax.ShapeDtypeStruct((8, LANES), F32)
    params_square = square(params)
    new_first, new_second, update, sums = pl.pallas_call(
        update_kernel,
        name="update",
        grid=(steps,),
        in_specs=[SM] + [grid] * 4,
        out_specs=[grid] * 3 + [whole],
        out_shape=[flat_kind] * 3 + [tile_kind],
    )(segments, params_square, square(first_moment), square(second_moment), grad_shard.reshape(-1, LANES))
    sums = sum_everywhere(sums)
    new_params, norms = pl.pallas_call(
        apply_kernel,
        name="apply",
        grid=(steps,),
        in_specs=[SM, whole, grid, grid],
        out_specs=[grid, whole],
        out_shape=[flat_kind, tile_kind],
    )(segments, sums, params_square, update)
    count = len(segment_shapes())
    return (
        state["out"].reshape(frames.shape),
        back["fgrad"].reshape(frames.shape),
        new_params.reshape(-1)[:shard_size],
        new_first.reshape(-1)[:shard_size],
        new_second.reshape(-1)[:shard_size],
        norms[0, :count],
        norms[1, :count],
        norms[2, :count],
        gain_grads.reshape(-1),
    )


def solution(mesh):
    placed = (
        P(("dp", "fsdp"), None, None),
        P(("dp", "fsdp")),
        P(("dp", "fsdp"), None, None),
        P(("dp", "fsdp")),
        P(("dp", "fsdp")),
        P(("dp", "fsdp")),
    )
    return jax.shard_map(
        shards,
        mesh=mesh,
        in_specs=placed,
        out_specs=(
            P(("dp", "fsdp"), None, None),
            P(("dp", "fsdp"), None, None),
            P(("dp", "fsdp")),
            P(("dp", "fsdp")),
            P(("dp", "fsdp")),
            P(),
            P(),
            P(),
            P(),
        ),
        check_vma=False,
    )
```

```python
import math
from types import SimpleNamespace

import jax
import jax.numpy as jnp
from jax import lax
from jax.experimental import pallas as pl
from jax.experimental.pallas import tpu as pltpu
from jax.sharding import PartitionSpec as P

STEP = 8
BETA_FIRST = 0.5
BETA_SECOND = 0.5
LEARN_RATE = 0.5
WEIGHT_DECAY = 0.01
ADAM_EPS = 1e-06
AXES = ("dp", "fsdp")


def segment_shapes():
    gate_width = CG // 2
    return [
        (D, FF),
        (FF, D),
        (D, 3 * D),
        (D, D),
        (D, CG),
        (gate_width, D),
        (2 * D, D),
        (D, FF),
        (FF, D),
        (5 * D + gate_width,),
        (KER, gate_width + 2 * D),
        (RELW, H),
    ]


D = 512
H = 8
HS = 64
FF = 2048
CG = 3072
KER = 31
RELW = 128
NORM_EPS = 1e-05
MASK_FILL = -1000000000.0
ROW = 512
HALF = ROW // 2
SLOTS = 160
KEYS = 256
PAD = 16
PADDED = SLOTS + 2 * PAD
GATE = CG // 2
BLOCK = {
    "ffa_in": (0, 4),
    "ffa_out": (4, 4),
    "qkv": (8, 3),
    "att_out": (11, 1),
    "cg_in": (12, 6),
    "cg_out": (18, 3),
    "merge": (21, 2),
    "ffb_in": (23, 4),
    "ffb_out": (27, 4),
    "small": (31, 1),
}
TAPS_AT = 8
REL_AT = 8 + 5 * KER
SMALL = 176
F32, BF16 = jnp.float32, jnp.bfloat16


def dot(left, right):
    return lax.dot_general(left, right, (((1,), (0,)), ((), ())), preferred_element_type=F32)


def dot_t(left, right):
    return lax.dot_general(left, right, (((1,), (1,)), ((), ())), preferred_element_type=F32)


def t_dot(left, right):
    return lax.dot_general(left, right, (((0,), (0,)), ((), ())), preferred_element_type=F32)


def low(values):
    return values.astype(BF16)


def each(count, body):
    for at in range(count):
        body(at)


def each_loop(count, body):
    def step(at, carry):
        body(at)
        return carry

    lax.fori_loop(0, count, step, 0)


def part(at, size):
    if isinstance(at, int):
        return slice(at * size, at * size + size)
    return pl.ds(pl.multiple_of(at * size, size), size)


def rows_of(name):
    first, count = BLOCK[name]
    return slice(ROW * first, ROW * (first + count))


def lane_mean(values, width):
    return jnp.sum(values, axis=-1, keepdims=True) * (1.0 / width)


def normed(values):
    centered = values - lane_mean(values, values.shape[-1])
    scale = lax.rsqrt(lane_mean(centered * centered, values.shape[-1]) + NORM_EPS)
    return centered * scale, scale


def valid_rows(length):
    return (lax.broadcasted_iota(jnp.int32, (SLOTS, 1), 0) < length).astype(F32)


def fold_rows(values):
    return jnp.sum(values, axis=0, keepdims=True)


def norm_rows(source, gain, target):
    for k in range(2):
        hat, _ = normed(source[part(k, 80), :].astype(F32))
        target[part(k, 80), :] = low(hat * gain)


def norm_rows_back(values, gain, grad, add):
    total = jnp.zeros((1, values.shape[1]), F32)
    for k in range(2):
        rows = part(k, 80)
        hat, scale = normed(values[rows, :].astype(F32))
        mine = grad[rows, :]
        total = total + fold_rows(mine * hat)
        inner = mine * gain
        width = values.shape[1]
        moved = lane_mean(inner, width) + hat * lane_mean(inner * hat, width)
        add(rows, scale * (inner - moved))
    return total


TOTAL_ROWS = 16037
PARTS = 32
TILE = 16
SPAN = 528
STARTS = [TILE * (TOTAL_ROWS * d // (PARTS * TILE)) for d in range(PARTS + 1)]
FIRST_PARTS = max(d for d in range(PARTS) if STARTS[d] < ROW * sum(BLOCK["ffa_out"]))
SHORTEST = min(high - first for first, high in zip(STARTS, STARTS[1:]))


def start_of(d):
    return ((TOTAL_ROWS * d) >> 9) * TILE


def gathered_layout():
    layout = []
    for core in range(2):
        layout += [[(core, 0, 0, back, 0, SPAN, 0)] for back in range(4)]
        for y, x, first, last in ((0, 1, 0, HALF), (1, 0, HALF, SPAN)):
            whole = [(core, y, x, back, 0, SPAN, 0) for back in range(4)]
            diagonal = [(core, 1, 1, back, first, last) for back in range(4)]
            layout += [[whole[0]], [whole[1]]]
            layout += [[whole[2], (*diagonal[0], SPAN)], [whole[3], (*diagonal[1], SPAN)]]
            layout += [[(*diagonal[2], 0)], [(*diagonal[3], 0)]]
    return layout


LAYOUT = gathered_layout()


def source_part(coords, piece):
    y, c, z, x = coords[0], coords[1], coords[2], coords[3]
    yy, cc, xx, zz = y ^ piece[1], c ^ piece[0], x ^ piece[2], (z + 4 - piece[3]) & 3
    return ((yy * 2 + cc) * 4 + zz) * 2 + xx


class Loads:
    def __init__(self, coords, sources, target, seams, sems):
        self.target, self.seams, self.sems = target, seams, sems
        self.here, self.joined = set(), set()
        seams[0, 0] = jnp.zeros((TILE, ROW), BF16)
        seams[PARTS, 1] = jnp.zeros((TILE, ROW), BF16)

        for soon in (True, False):
            for pieces, source in zip(LAYOUT, sources):
                for piece in pieces:
                    d = source_part(coords, piece)
                    first_ones = (d <= FIRST_PARTS) | (d == PARTS - 1)

                    @pl.when(first_ones if soon else jnp.logical_not(first_ones))
                    def _(piece=piece, source=source, d=d):
                        self.start(piece, source, d)

    def start(self, piece, source, d):
        def rows(at, size):
            return pl.ds(pl.multiple_of(at, TILE), size)

        first, last, offset = piece[4:]
        offset = offset - first
        start = start_of(d)
        length = start_of(d + 1) - start
        inner, outer = max(first, TILE), min(last, SHORTEST)
        sem = self.sems.at[d]
        pltpu.make_async_copy(
            source.at[offset + inner : offset + outer], self.target.at[rows(start + inner, outer - inner)], sem
        ).start()
        if first == 0:
            pltpu.make_async_copy(source.at[offset : offset + TILE], self.seams.at[d, 1], sem).start()
        if last == SPAN:

            @pl.when(length > SHORTEST)
            def _():
                pltpu.make_async_copy(
                    source.at[offset + SHORTEST : offset + SHORTEST + TILE],
                    self.target.at[rows(start + SHORTEST, TILE)],
                    sem,
                ).start()

            pltpu.make_async_copy(source.at[rows(offset + length, TILE)], self.seams.at[d + 1, 0], sem).start()

    def wait_part(self, d):
        if d in self.here or not 0 <= d < PARTS:
            return
        self.here.add(d)
        size = STARTS[d + 1] - STARTS[d] + TILE
        pltpu.make_async_copy(self.target.at[0:size], self.target.at[0:size], self.sems.at[d]).wait()

    def wait(self, name):
        rows = rows_of(name)
        last = min(rows.stop, STARTS[-1] + TILE)
        for d in range(PARTS + 1):
            if STARTS[d] < last and STARTS[d] + TILE > rows.start and d not in self.joined:
                self.wait_part(d - 1)
                self.wait_part(d)
                self.joined.add(d)
                self.target[STARTS[d] : STARTS[d] + TILE, :] = self.seams[d, 0] + self.seams[d, 1]
            if d < PARTS and STARTS[d] + TILE < last and STARTS[d + 1] > rows.start:
                self.wait_part(d)


class Emits:
    def __init__(self, coords, halves, sems):
        self.coords, self.halves, self.sems = coords, halves, sems
        self.pending = []

    def put(self, d, values, rows):
        core, z, x = (d // 8) % 2, (d // 2) % 4, d % 2
        kept, sent = self.halves[d // 16]
        far_x = self.coords[3] ^ x
        place = (self.coords[2] + 3 - z) & 3
        sem = self.sems.at[len(self.pending)]

        @pl.when(self.coords[1] == core)
        def _():
            pltpu.make_async_copy(values, kept.at[4 * far_x + place, rows], sem).start()

        @pl.when((self.coords[1] != core) & (far_x == 0))
        def _():
            pltpu.make_async_copy(values, sent[0].at[place, rows], sem).start()

        @pl.when((self.coords[1] != core) & (far_x == 1))
        def _():
            pltpu.make_async_copy(values, sent[1].at[place, rows], sem).start()

        self.pending.append(pltpu.make_async_copy(values, kept.at[0, rows], sem))

    def put_tensor(self, name, values):
        rows = rows_of(name)
        for d in range(PARTS):
            first, last = max(rows.start, STARTS[d]), min(rows.stop, STARTS[d] + SPAN)
            if first < last:
                self.put(d, values.at[first - rows.start : last - rows.start], slice(first - STARTS[d], last - STARTS[d]))

    def wait(self):
        for copy in self.pending:
            copy.wait()


def split_columns(raw, target, wide, stage):
    def chunk(k):
        rows = part(k, 128 * wide)
        for lane in range(4):
            stage[lane, 0 : 128 * wide, :] = raw[rows, lane * 128 : lane * 128 + 128].astype(F32)
        for c in range(wide):
            for lane in range(4):
                place = ROW * c + lane * 128
                target[part(k, 128), place : place + 128] = low(stage[lane, pl.ds(c, 128, stride=wide), :])

    each(4, chunk)


def weight_columns(left, grads, wide, stage, left_t, target):
    left_t[...] = left[...].T

    def chunk(j):
        value = dot(left_t[...], grads[:, part(j, 256)])
        c, pair = j // 2, (j % 2) * 2
        for half in range(2):
            stage[pair + half, pl.ds(c, ROW, stride=wide), :] = value[:, 128 * half : 128 * half + 128]

    each(2 * wide, chunk)

    def lower(k):
        rows = part(k, ROW)
        for lane in range(4):
            target[rows, lane * 128 : lane * 128 + 128] = low(stage[lane, rows, :])

    each(wide, lower)


def weight_rows(left, grads, count, left_t, target):
    def chunk(k):
        left_t[...] = left[:, part(k, ROW)].T
        for at in range(2):
            target[part(k, ROW), 256 * at : 256 * at + 256] = low(dot(left_t[...], grads[:, 256 * at : 256 * at + 256]))

    each(count, chunk)


def feed_forward(inputs, gain, w_in, w_out, nrm, act, slope, result):
    norm_rows(inputs, gain, nrm)

    def up(j):
        at = part(j, 256)
        hidden = dot(nrm[...], w_in[:, at])
        sig = jax.nn.sigmoid(hidden)
        active = hidden * sig
        act[:, at] = low(active)
        slope[:, at] = low(sig + active * (1.0 - sig))

    each(FF // 256, up)

    def down(j):
        at = part(j, 256)
        result[:, at] = inputs[:, at].astype(F32) + 0.5 * dot(act[...], w_out[:, at])

    each(2, down)


def feed_back(dout, w_in, w_out, nrm, act, slope, dhid, dnrm, stage, left_t, g_in, g_out, emits, name):
    def up(j):
        at = part(j, 256)
        grad = dot_t(dout[...], w_out[at, :])
        dhid[:, at] = low(grad * slope[:, at].astype(F32))

    each(FF // 256, up)
    weight_rows(act, dout, 4, left_t, g_out)
    emits.put_tensor(name + "_out", g_out)

    def down(j):
        at = part(j, 256)
        dnrm[:, at] = dot_t(dhid[:, 0:FF], w_in[at, :])

    each(2, down)
    weight_columns(nrm, dhid, 4, stage, left_t, g_in)
    emits.put_tensor(name + "_in", g_in)


def bucket_map():
    entry = lax.broadcasted_iota(jnp.int32, (2 * ROW, ROW), 0) // H
    far = lax.broadcasted_iota(jnp.int32, (2 * ROW, ROW), 1)
    far = jnp.where(far >= ROW // 2, far - ROW, far)
    bucket = jnp.clip(far, -(RELW // 2), RELW // 2 - 1) + RELW // 2
    return (entry == bucket).astype(F32)


def own_entries(flat):
    entry = lax.broadcasted_iota(jnp.int32, (H, 2 * ROW), 1)
    head = lax.broadcasted_iota(jnp.int32, (H, 2 * ROW), 0)
    return jnp.where(lax.rem(entry, H) == head, flat, 0.0)


def tap_row(small, tap, row, lane):
    return small[lane, pl.ds(TAPS_AT + 5 * tap + row, 1), :]


def shifted_sum(padded, at, factor):
    total = None
    for low_part in range(8):
        slab = padded[low_part : low_part + SLOTS + 24, at]
        inner = None
        for high_part in range(4):
            offset = 8 * high_part + low_part
            if offset:
                term = factor(offset) * slab[8 * high_part : 8 * high_part + SLOTS]
                inner = term if inner is None else inner + term
        total = inner if total is None else total + inner
    return total


def convolve(padded, small, first_row, width, finish):

    def chunk(j):
        at = part(j, 128)
        row, lane = first_row + j // 4, j % 4
        finish(j, at, shifted_sum(padded, at, lambda offset: tap_row(small, offset - 1, row, lane)))

    each_loop(width // 128, chunk)


def convolve_back(grads, padded, small, first_row, width, sgrad, finish):

    def chunk(j):
        at = part(j, 128)
        row, lane = first_row + j // 4, j % 4
        finish(j, at, shifted_sum(grads, at, lambda offset: tap_row(small, KER - offset, row, lane)))
        own = grads[PAD : PAD + SLOTS, at]
        for low_part in range(8):
            slab = padded[low_part : low_part + SLOTS + 24, at]
            for high_part in range(4):
                offset = 8 * high_part + low_part
                if offset:
                    tile = slab[8 * high_part : 8 * high_part + SLOTS]
                    sgrad[lane, pl.ds(TAPS_AT + 5 * (offset - 1) + row, 1), :] = fold_rows(own * tile)

    each_loop(width // 128, chunk)


def clear_margins(padded):
    padded[0:PAD, :] = jnp.zeros((PAD, padded.shape[1]), F32)
    padded[PAD + SLOTS : PADDED, :] = jnp.zeros((PAD, padded.shape[1]), F32)


def gelu_parts(hidden):
    bell = jnp.exp(-0.5 * hidden * hidden)
    spread = 1.0 + (0.3275911 * 2.0**-0.5) * jnp.abs(hidden)
    near = pl.reciprocal(spread, approx=True)
    near = near * (2.0 - spread * near)
    tail = jnp.full_like(near, 0.5 * 1.061405429)
    for factor in (-1.453152027, 1.421413741, -0.284496736, 0.254829592):
        tail = tail * near + 0.5 * factor
    tail = tail * near * bell
    below = jnp.where(hidden >= 0.0, 1.0 - tail, tail)
    return hidden * below, below + hidden * bell * ((2.0 * math.pi) ** -0.5)


def attention_forward(r, length):
    norm_rows(r.x1, r.small[1:2, :], r.nrm_t)
    r.qkv[SLOTS:KEYS, :] = jnp.zeros((KEYS - SLOTS, 3 * D), BF16)
    flat = jnp.concatenate([r.small[REL_AT : REL_AT + 1, :], r.small[REL_AT + 1 : REL_AT + 2, :]], axis=1)
    r.bias[...] = dot(low(own_entries(jnp.broadcast_to(flat, (H, 2 * ROW)))), low(bucket_map()))

    def project(j):
        at = part(j, 256)
        r.qkv[0:SLOTS, at] = low(dot(r.nrm_t[...], r.w_qkv[:, at]))

    each(3 * D // 256, project)
    valid = lax.broadcasted_iota(jnp.int32, (1, KEYS), 1) < length
    first_half = lax.broadcasted_iota(jnp.int32, (1, 128), 1) < HS

    def heads(pair):
        queries = r.qkv[0:SLOTS, part(pair, 128)]
        keys = r.qkv[:, part(pair + 4, 128)]
        values = r.qkv[:, part(pair + 8, 128)]
        outs = []
        for odd in range(2):
            head = 2 * pair + odd
            half = first_half if odd == 0 else jnp.logical_not(first_half)
            mine = jnp.where(half, queries, jnp.zeros_like(queries))
            spread = jnp.broadcast_to(r.bias[pl.ds(head, 1), :], (SLOTS, ROW))
            spread = pltpu.roll(spread, 0, 1, stride=1, stride_axis=0)[:, 0:KEYS]
            scores = jnp.where(valid, dot_t(mine, keys) * HS ** (-0.5) + spread, MASK_FILL)
            shifted = jnp.exp(scores - jnp.max(scores, axis=-1, keepdims=True))
            chances = low(shifted / jnp.sum(shifted, axis=-1, keepdims=True))
            r.probs[head] = chances
            outs.append(dot(chances, values))
        r.ctx[:, part(pair, 128)] = low(jnp.where(first_half, outs[0], outs[1]))

    each(H // 2, heads)

    def project_out(j):
        at = part(j, 256)
        r.cat[:, at] = dot(r.ctx[...], r.w[rows_of("att_out"), at])

    each(2, project_out)


def gating_forward(r, length):
    norm_rows(r.x1, r.small[2:3, :], r.nrm_c)

    def up(j):
        at = part(j, 256)
        r.hid[...] = dot(r.nrm_c[...], r.w_cg[:, at])
        for k in range(5):
            rows = part(k, 32)
            active, slope = gelu_parts(r.hid[rows, :])
            r.ug[rows, at] = active
            r.slope_c[rows, at] = low(slope)

    each(CG // 256, up)
    tiles = [slice(GATE + 128 * j, GATE + 128 * j + 128) for j in range(GATE // 128)]
    total = jnp.zeros((SLOTS, 128), F32)
    for at in tiles:
        total = total + r.ug[:, at]
    mean = lane_mean(total, GATE)
    total = jnp.zeros((SLOTS, 128), F32)
    for at in tiles:
        centered = r.ug[:, at] - mean
        total = total + centered * centered
    scale = lax.rsqrt(lane_mean(total, GATE) + NORM_EPS)
    r.gmean[...] = jnp.broadcast_to(mean, (SLOTS, 128))
    r.gscale[...] = jnp.broadcast_to(scale, (SLOTS, 128))
    scale = scale * valid_rows(length)
    for j, at in enumerate(tiles):
        gain = r.small[5 + j // 4 : 6 + j // 4, part(j % 4, 128)]
        r.gpad[PAD : PAD + SLOTS, part(j, 128)] = (r.ug[:, at] - mean) * scale * gain

    def finish(j, at, value):
        r.cv[:, at] = low(value)
        r.gated[:, at] = low(r.ug[:, at] * value)

    convolve(r.gpad, r.tiles, 0, GATE, finish)

    def down(j):
        r.cat[:, part(j + 2, 256)] = dot(r.gated[...], r.w[rows_of("cg_out"), part(j, 256)])

    each(2, down)


def merge_forward(r, length):
    valid = valid_rows(length)
    for j in range(8):
        at = part(j, 128)
        r.mpad[PAD : PAD + SLOTS, at] = r.cat[:, at] * valid

    def finish(j, at, value):
        r.mixed[:, at] = low(r.cat[:, at] + value)

    convolve(r.mpad, r.tiles, 3, 2 * D, finish)

    def merge(j):
        at = part(j, 256)
        r.x2[:, at] = r.x1[:, at] + dot(r.mixed[...], r.w[rows_of("merge"), at])

    each(2, merge)


def final_norm(r, length):
    gain = r.small[4:5, :]
    valid = valid_rows(length)
    total = jnp.zeros((1, D), F32)
    for k in range(2):
        rows = part(k, 80)
        hat, scale = normed(r.x3[rows, :])
        r.out[rows, :] = low(hat * gain * valid[80 * k : 80 * k + 80])
        mine = r.cot[rows, :].astype(F32) * valid[80 * k : 80 * k + 80]
        total = total + fold_rows(mine * hat)
        inner = mine * gain
        back = scale * (inner - (lane_mean(inner, D) + hat * lane_mean(inner * hat, D)))
        r.dx[rows, :] = back
        r.dout[rows, :] = low(0.5 * back)
    r.gains[4:5, :] = total


def merge_back(r, length, emits):
    for k in range(2):
        r.dout[part(k, 80), :] = low(r.dx[part(k, 80), :])
    w_merge = r.w.at[rows_of("merge")]

    def merge(j):
        at = part(j, 256)
        r.dpad[PAD : PAD + SLOTS, at] = dot_t(r.dout[...], w_merge[at, :])

    each(2 * D // 256, merge)
    weight_rows(r.mixed, r.dout, 2, r.left_t, w_merge)
    emits.put_tensor("merge", w_merge)

    def finish(j, at, value):
        r.djoin[:, at] = low(r.dpad[PAD : PAD + SLOTS, at] + value * valid_rows(length))

    convolve_back(r.dpad, r.mpad, r.tiles, 3, 2 * D, r.tgrad, finish)


def gating_back(r, length, emits):
    w_co = r.w.at[rows_of("cg_out")]

    def gate(j):
        at = part(j, 256)
        value = dot_t(r.djoin[:, D:], w_co[at, :])
        r.dhid[:, at] = low(value * r.cv[:, at].astype(F32) * r.slope_c[:, at].astype(F32))
        r.dpad[PAD : PAD + SLOTS, at] = value * r.ug[:, at]

    each(GATE // 256, gate)
    r.dout[...] = r.djoin[:, D:]
    weight_rows(r.gated, r.dout, 3, r.left_t, w_co)
    emits.put_tensor("cg_out", w_co)

    def finish(j, at, value):
        r.dgate[:, at] = value * valid_rows(length)

    convolve_back(r.dpad, r.gpad, r.tiles, 0, GATE, r.tgrad, finish)
    tiles = GATE // 128
    for quarter in range(4):
        rows = part(quarter, SLOTS // 4)
        mean, scale = r.gmean[rows, :], r.gscale[rows, :]
        total, total_hat = jnp.zeros_like(mean), jnp.zeros_like(mean)

        def parts(j, rows=rows, mean=mean, scale=scale):
            row, lane = 5 + j // 4, part(j % 4, 128)
            hat = (r.ug[rows, part(j + tiles, 128)] - mean) * scale
            grad = r.dgate[rows, part(j, 128)]
            return hat, grad, grad * r.small[row : row + 1, lane]

        for j in range(tiles):
            hat, grad, inner = parts(j)
            products = jnp.sum((grad * hat).reshape(-1, 8, 128), axis=0)
            r.gate_sums[part(j, 8), :] = products if quarter == 0 else r.gate_sums[part(j, 8), :] + products
            total = total + inner
            total_hat = total_hat + inner * hat
        total = jnp.broadcast_to(lane_mean(total, GATE), total.shape)
        total_hat = jnp.broadcast_to(lane_mean(total_hat, GATE), total.shape)
        for j in range(tiles):
            hat, _, inner = parts(j)
            far = part(j + tiles, 128)
            r.dgate[rows, part(j, 128)] = scale * (inner - total - hat * total_hat)
    for j in range(tiles):
        far = part(j + tiles, 128)
        r.dhid[:, far] = low(r.dgate[:, part(j, 128)] * r.slope_c[:, far].astype(F32))
        r.tgrad[j % 4, 5 + j // 4 : 6 + j // 4, :] = fold_rows(r.gate_sums[part(j, 8), :])

    def down(j):
        at = part(j, 256)
        r.dnrm[:, at] = dot_t(r.dhid[...], r.w_cg[at, :])

    each(2, down)
    g_cg = r.w.at[rows_of("cg_in")]
    weight_columns(r.nrm_c, r.dhid, 6, r.stage, r.left_t, g_cg)
    emits.put_tensor("cg_in", g_cg)

    def add(rows, back):
        r.dx[rows, :] += back

    r.gains[2:3, :] = norm_rows_back(r.x1, r.small[2:3, :], r.dnrm, add)


def forward_kernel(names, coords, length_ref, frames, cot, *refs):
    sources, refs = refs[: len(LAYOUT)], refs[len(LAYOUT) :]
    r = SimpleNamespace(**dict(zip(names, refs)))
    r.cot = cot
    length = length_ref[0]
    loads = Loads(coords, sources, r.w, r.seams, r.load_sems)
    kept = []

    def keep(source, target):
        copy = pltpu.make_async_copy(source, target, r.keep_sems.at[len(kept)])
        copy.start()
        kept.append(copy)

    for padded in (r.gpad, r.mpad, r.dpad):
        clear_margins(padded)
    r.tgrad[...] = jnp.zeros_like(r.tgrad)
    r.gains[...] = jnp.zeros_like(r.gains)
    loads.wait("small")
    r.small[...] = r.w[ROW * 31 : ROW * 31 + SMALL, :].astype(F32)
    for lane in range(4):
        r.tiles[lane] = r.small[:, part(lane, 128)]
    loads.wait("ffa_in")
    split_columns(r.w.at[rows_of("ffa_in")], r.w_ffa_in, 4, r.stage)
    keep(r.w_ffa_in, r.keep_ffa_in)
    loads.wait("ffa_out")
    keep(r.w.at[rows_of("ffa_out")], r.keep_ffa_out)
    feed_forward(frames, r.small[0:1, :], r.w_ffa_in, r.w.at[rows_of("ffa_out")], r.nrm, r.act, r.slope, r.x1)
    keep(r.nrm, r.keep_nrm)
    keep(r.act, r.keep_act)
    keep(r.slope, r.keep_slope)
    keep(r.x1, r.keep_x1)
    loads.wait("qkv")
    split_columns(r.w.at[rows_of("qkv")], r.w_qkv, 3, r.stage)
    keep(r.w_qkv, r.keep_qkv)
    loads.wait("att_out")
    keep(r.w.at[rows_of("att_out")], r.keep_att)
    attention_forward(r, length)
    keep(r.nrm_t, r.keep_nrm_t)
    keep(r.qkv, r.keep_heads)
    keep(r.probs, r.keep_probs)
    keep(r.ctx, r.keep_ctx)
    loads.wait("cg_in")
    split_columns(r.w.at[rows_of("cg_in")], r.w_cg, 6, r.stage)
    loads.wait("cg_out")
    gating_forward(r, length)
    loads.wait("merge")
    merge_forward(r, length)
    loads.wait("ffb_in")
    split_columns(r.w.at[rows_of("ffb_in")], r.w_ffb_in, 4, r.stage)
    loads.wait("ffb_out")
    w_out = r.w.at[rows_of("ffb_out")]
    feed_forward(r.x2, r.small[3:4, :], r.w_ffb_in, w_out, r.nrm_b, r.act_b, r.slope_b, r.x3)
    final_norm(r, length)
    emits = Emits(
        coords,
        ((r.low_kept, (r.low_near, r.low_far)), (r.high_kept, (r.high_near, r.high_far))),
        r.emit_sems,
    )
    feed_back(
        r.dout, r.w_ffb_in, w_out, r.nrm_b, r.act_b, r.slope_b, r.dhid, r.dnrm, r.stage, r.left_t,
        r.w.at[rows_of("ffb_in")], w_out, emits, "ffb",
    )

    def add(rows, back):
        r.dx[rows, :] += back

    r.gains[3:4, :] = norm_rows_back(r.x2, r.small[3:4, :], r.dnrm, add)
    merge_back(r, length, emits)
    keep(r.djoin, r.keep_djoin)
    gating_back(r, length, emits)
    keep(r.dx, r.keep_dx)
    for lane in range(4):
        at = part(lane, 128)
        r.gains[5:8, at] = r.tgrad[lane, 5:8, :]
        r.w[ROW * 31 : ROW * 31 + SMALL, at] = low(r.tgrad[lane])
    r.w[ROW * 31 : ROW * 31 + 16, :] = low(
        jnp.concatenate(
            [
                jnp.zeros((8, ROW), F32),
                jnp.concatenate([r.tgrad[lane, 8:16, :] for lane in range(4)], axis=1),
            ],
            axis=0,
        )
    )
    r.w[ROW * 31 + SMALL : ROW * 32, :] = jnp.zeros((ROW - SMALL, ROW), BF16)
    emits.put_tensor("small", r.w.at[rows_of("small")])
    for copy in kept:
        copy.wait()
    emits.wait()


def attention_back(r, emits):
    def project(j):
        at = part(j, 256)
        r.dctx[:, at] = low(dot_t(r.datt[...], r.w_att[at, :]))

    each(2, project)
    weight_rows(r.ctx, r.datt, 1, r.left_t, r.w_att)
    emits.put_tensor("att_out", r.w_att)
    first_half = lax.broadcasted_iota(jnp.int32, (1, 128), 1) < HS
    at_row = lax.broadcasted_iota(jnp.int32, (SLOTS, SLOTS), 0)
    at_column = lax.broadcasted_iota(jnp.int32, (SLOTS, SLOTS), 1)
    flip = low((at_row + at_column == SLOTS - 1).astype(F32))

    def heads(pair):
        queries = r.qkv[0:SLOTS, part(pair, 128)]
        keys = r.qkv[:, part(pair + 4, 128)]
        values = r.qkv[:, part(pair + 8, 128)]
        context = r.dctx[:, part(pair, 128)]
        q_parts, k_parts, v_parts = [], [], []
        for odd in range(2):
            head = 2 * pair + odd
            half = first_half if odd == 0 else jnp.logical_not(first_half)
            chances = r.probs[head]
            v_parts.append(t_dot(chances, context)[0:SLOTS])
            wide_chances = chances.astype(F32)
            chance_grad = dot_t(jnp.where(half, context, jnp.zeros_like(context)), values)
            inner = jnp.sum(wide_chances * chance_grad, axis=-1, keepdims=True)
            score_grad = low(wide_chances * (chance_grad - inner))
            q_parts.append(dot(score_grad, keys))
            k_parts.append(t_dot(score_grad, queries)[0:SLOTS])
            wide = jnp.concatenate([dot(flip, score_grad), jnp.zeros((SLOTS, ROW - KEYS), F32)], axis=1)
            wide = pltpu.roll(wide, ROW - SLOTS + 1, 1, stride=1, stride_axis=0)
            r.sums[pl.ds(head, 1), :] = fold_rows(wide)
        scale = HS ** (-0.5)
        r.dhid[:, part(pair, 128)] = low(jnp.where(first_half, q_parts[0], q_parts[1]) * scale)
        r.dhid[:, part(pair + 4, 128)] = low(jnp.where(first_half, k_parts[0], k_parts[1]) * scale)
        r.dhid[:, part(pair + 8, 128)] = low(jnp.where(first_half, v_parts[0], v_parts[1]))

    each(H // 2, heads)

    def down(j):
        at = part(j, 256)
        r.dnrm[:, at] = dot_t(r.dhid[:, 0 : 3 * D], r.w_qkv[at, :])

    each(2, down)

    def add(rows, back):
        r.dx[rows, :] += back
        r.dout[rows, :] = low(0.5 * r.dx[rows, :])

    r.late[1:2, :] = norm_rows_back(r.x1, r.gain_rows[1:2, :], r.dnrm, add)


def attention_weights_back(r, emits):
    weight_columns(r.nrm_t, r.dhid, 3, r.stage, r.left_t, r.g_qkv)
    emits.put_tensor("qkv", r.g_qkv)
    by_entry = lax.dot_general(
        r.sums[...],
        bucket_map(),
        (((1,), (1,)), ((), ())),
        precision=lax.Precision.HIGHEST,
        preferred_element_type=F32,
    )
    flat = fold_rows(own_entries(by_entry))
    r.late[8:9, :] = flat[:, 0:ROW]
    r.late[9:10, :] = flat[:, ROW:]


def backward_kernel(names, coords, frames, gains, gain_rows, *refs):
    r = SimpleNamespace(**dict(zip(names, refs)))
    r.gain_rows = gain_rows
    waits = {}
    for at, (name, source, target) in enumerate(
        (
            ("att", r.in_att, r.w_att),
            ("djoin", r.in_djoin.at[:, 0:D], r.datt),
            ("ctx", r.in_ctx, r.ctx),
            ("heads", r.in_heads, r.qkv),
            ("probs", r.in_probs, r.probs),
            ("qkv", r.in_qkv, r.w_qkv),
            ("x1", r.in_x1, r.x1),
            ("dx", r.in_dx, r.dx),
            ("nrm_t", r.in_nrm_t, r.nrm_t),
            ("ffa_out", r.in_ffa_out, r.w_ffa_out),
            ("slope", r.in_slope, r.slope),
            ("act", r.in_act, r.act),
            ("ffa_in", r.in_ffa_in, r.w_ffa_in),
            ("nrm", r.in_nrm, r.nrm),
        )
    ):
        waits[name] = pltpu.make_async_copy(source, target, r.load_sems.at[at])
        waits[name].start()
    r.late[...] = jnp.zeros_like(r.late)
    emits = Emits(coords, ((r.low_kept, (r.low_near, r.low_far)),), r.emit_sems)
    for name in ("att", "djoin", "ctx", "heads", "probs", "qkv", "x1", "dx"):
        waits[name].wait()
    attention_back(r, emits)
    waits["nrm_t"].wait()
    attention_weights_back(r, emits)
    for name in ("ffa_out", "slope", "act", "ffa_in", "nrm"):
        waits[name].wait()
    feed_back(
        r.dout, r.w_ffa_in, r.w_ffa_out, r.nrm, r.act, r.slope, r.dhid, r.dnrm, r.stage, r.left_t, r.g_ffa_in,
        r.w_ffa_out, emits, "ffa",
    )

    def add(rows, back):
        r.fgrad[rows, :] = low(r.dx[rows, :] + back)

    r.late[0:1, :] = norm_rows_back(frames, gain_rows[0:1, :], r.dnrm, add)
    r.late[2:8, :] = gains[2:8, :]
    emits.wait()


VM = pl.BlockSpec(memory_space=pltpu.VMEM)
SM = pl.BlockSpec(memory_space=pltpu.SMEM)
ANY = pl.BlockSpec(memory_space=pl.ANY)
WIDE, THIN = ((SLOTS, D), F32), ((SLOTS, D), BF16)
FULL = ((SLOTS, FF), BF16)
KEPT, SENT = ((8, SPAN, ROW), BF16), ((4, SPAN, ROW), BF16)

FORWARD_OUT = {
    "out": (VM, THIN),
    "gains": (VM, ((8, ROW), F32)),
    "small": (VM, ((SMALL, ROW), F32)),
    "high_kept": (ANY, KEPT),
    "high_near": (ANY, SENT),
    "high_far": (ANY, SENT),
    "low_kept": (ANY, KEPT),
    "low_near": (ANY, SENT),
    "low_far": (ANY, SENT),
    "keep_ffa_in": (ANY, ((D, FF), BF16)),
    "keep_ffa_out": (ANY, ((FF, D), BF16)),
    "keep_qkv": (ANY, ((D, 3 * D), BF16)),
    "keep_att": (ANY, ((D, D), BF16)),
    "keep_nrm": (ANY, THIN),
    "keep_act": (ANY, FULL),
    "keep_slope": (ANY, FULL),
    "keep_x1": (ANY, WIDE),
    "keep_nrm_t": (ANY, THIN),
    "keep_heads": (ANY, ((KEYS, 3 * D), BF16)),
    "keep_probs": (ANY, ((H, SLOTS, KEYS), BF16)),
    "keep_ctx": (ANY, THIN),
    "keep_djoin": (ANY, ((SLOTS, 2 * D), BF16)),
    "keep_dx": (ANY, WIDE),
}
FORWARD_SCRATCH = {
    "w": ((32 * ROW, ROW), BF16),
    "w_ffa_in": ((D, FF), BF16),
    "w_qkv": ((D, 3 * D), BF16),
    "w_cg": ((D, CG), BF16),
    "w_ffb_in": ((D, FF), BF16),
    "stage": ((4, 6 * ROW, 128), F32),
    "left_t": ((ROW, SLOTS), BF16),
    "tiles": ((4, SMALL, 128), F32),
    "tgrad": ((4, SMALL, 128), F32),
    "bias": ((H, ROW), F32),
    "nrm": THIN,
    "act": FULL,
    "slope": FULL,
    "nrm_t": THIN,
    "qkv": ((KEYS, 3 * D), BF16),
    "probs": ((H, SLOTS, KEYS), BF16),
    "ctx": THIN,
    "nrm_c": THIN,
    "hid": ((SLOTS, 256), F32),
    "ug": ((SLOTS, CG), F32),
    "slope_c": ((SLOTS, CG), BF16),
    "gmean": ((SLOTS, 128), F32),
    "gscale": ((SLOTS, 128), F32),
    "gate_sums": ((8 * GATE // 128, 128), F32),
    "gpad": ((PADDED, GATE), F32),
    "cv": ((SLOTS, GATE), BF16),
    "gated": ((SLOTS, GATE), BF16),
    "cat": ((SLOTS, 2 * D), F32),
    "mpad": ((PADDED, 2 * D), F32),
    "mixed": ((SLOTS, 2 * D), BF16),
    "nrm_b": THIN,
    "act_b": FULL,
    "slope_b": FULL,
    "dpad": ((PADDED, GATE), F32),
    "djoin": ((SLOTS, 2 * D), BF16),
    "dgate": ((SLOTS, GATE), F32),
    "dhid": ((SLOTS, CG), BF16),
    "dnrm": WIDE,
    "dout": THIN,
    "dx": WIDE,
    "x1": WIDE,
    "x2": WIDE,
    "x3": WIDE,
    "seams": ((PARTS + 1, 2, TILE, ROW), BF16),
    "load_sems": PARTS,
    "keep_sems": 16,
    "emit_sems": 40,
}
BACKWARD_IN = (
    "ffa_in", "ffa_out", "qkv", "att", "nrm", "act", "slope", "x1", "nrm_t", "heads", "probs", "ctx", "djoin", "dx",
)
PASSED = ("low_kept", "low_near", "low_far")
BACKWARD_OUT = {
    "fgrad": (VM, THIN),
    "late": (VM, ((16, ROW), F32)),
    "low_kept": (ANY, KEPT),
    "low_near": (ANY, SENT),
    "low_far": (ANY, SENT),
}
BACKWARD_SCRATCH = {
    "w_ffa_in": ((D, FF), BF16),
    "w_ffa_out": ((FF, D), BF16),
    "w_qkv": ((D, 3 * D), BF16),
    "w_att": ((D, D), BF16),
    "g_ffa_in": ((FF, D), BF16),
    "g_qkv": ((3 * D, D), BF16),
    "stage": ((4, 4 * ROW, 128), F32),
    "left_t": ((ROW, SLOTS), BF16),
    "sums": ((H, ROW), F32),
    "nrm": THIN,
    "act": FULL,
    "slope": FULL,
    "nrm_t": THIN,
    "qkv": ((KEYS, 3 * D), BF16),
    "probs": ((H, SLOTS, KEYS), BF16),
    "ctx": THIN,
    "datt": THIN,
    "dctx": THIN,
    "dhid": FULL,
    "dnrm": WIDE,
    "dout": THIN,
    "dx": WIDE,
    "x1": WIDE,
    "load_sems": 14,
    "emit_sems": 24,
}


def call(kernel, name, ins, outs, scratch, limit, aliases=None):
    return pl.pallas_call(
        kernel,
        name=name,
        in_specs=[space for space, _ in ins],
        out_specs=[space for space, _ in outs],
        out_shape=[jax.ShapeDtypeStruct(*kind) for _, kind in outs],
        scratch_shapes=[
            pltpu.SemaphoreType.DMA((each_one,)) if isinstance(each_one, int) else pltpu.VMEM(*each_one)
            for each_one in scratch
        ],
        input_output_aliases=aliases or {},
        compiler_params=pltpu.CompilerParams(vmem_limit_bytes=limit * 2**20),
    )(*[array for _, array in ins])


def forward(coords, length, frames, cot, blocks):
    def kernel(*refs):
        forward_kernel([*FORWARD_OUT, *FORWARD_SCRATCH], *refs)

    outs = call(
        kernel,
        "forward",
        [(SM, coords), (SM, length), (VM, frames), (VM, cot)] + [(ANY, block) for block in blocks],
        list(FORWARD_OUT.values()),
        list(FORWARD_SCRATCH.values()),
        58,
    )
    return dict(zip(FORWARD_OUT, outs))


def backward(coords, frames, state):
    def kernel(*refs):
        names = ["in_" + name for name in BACKWARD_IN + PASSED]
        backward_kernel([*names, *BACKWARD_OUT, *BACKWARD_SCRATCH], *refs)

    ins = [(SM, coords), (VM, frames), (VM, state["gains"]), (VM, state["small"])]
    ins += [(ANY, state["keep_" + name]) for name in BACKWARD_IN]
    ins += [(ANY, state[name]) for name in PASSED]
    outs = call(
        kernel,
        "backward",
        ins,
        list(BACKWARD_OUT.values()),
        list(BACKWARD_SCRATCH.values()),
        58,
        {len(ins) - 3 + at: 2 + at for at in range(3)},
    )
    return dict(zip(BACKWARD_OUT, outs))


def segment_bounds():
    bounds = [0]
    for extent in segment_shapes():
        bounds.append(bounds[-1] + math.prod(extent))
    return bounds


def fast_mesh():
    return lax.axis_size("dp") == 4 and lax.axis_size("fsdp") == 8


def over_x(value):
    return lax.ppermute(value, "fsdp", [(i, i ^ 1) for i in range(8)])


def over_y(value):
    return lax.ppermute(value, "dp", [(i, i ^ 2) for i in range(4)])


def over_core(value):
    return lax.ppermute(value, "dp", [(i, i ^ 1) for i in range(4)])


def round_z(value):
    return lax.ppermute(value, "fsdp", [(i, (i + 2) % 8) for i in range(8)])


def over_z(value, step):
    return lax.ppermute(value, "fsdp", [(i, i ^ (2 * step)) for i in range(8)])


def after(value, *others):
    return lax.optimization_barrier((value, *others))[0]


def shard_offset(me, shard_size):
    return me * shard_size - start_of(me) * ROW


def gather_shards(shard, me):
    shard_size = shard.shape[0]
    if not fast_mesh():
        whole = lax.all_gather(shard, AXES, axis=0, tiled=True)
        whole = jnp.pad(whole, (0, (STARTS[-1] + SPAN) * ROW - whole.shape[0])).reshape(-1, ROW)
        spans = [whole[start : start + SPAN] for start in STARTS[:-1]]
        spans = spans[:1] + [jnp.concatenate([jnp.zeros((TILE, ROW), BF16), span[TILE:]]) for span in spans[1:]]
        return [
            jnp.concatenate([spans[source_part((0, 0, 0, 0), piece)][piece[4] : piece[5]] for piece in pieces])
            for pieces in LAYOUT
        ]
    most = TILE * ROW
    padded = jnp.pad(shard, (most, SPAN * ROW - shard_size))
    span = lax.dynamic_slice(padded, (most - shard_offset(me, shard_size),), (SPAN * ROW,)).reshape(SPAN, ROW)
    own, by_x, by_y = [span], [], []
    for back in range(4):
        if back < 3:
            own.append(round_z(own[back]))
        if back < 2:
            by_x.append(over_x(own[back]))
            by_y.append(over_y(own[back]))
            own[back + 1], by_x[back], by_y[back] = lax.optimization_barrier((own[back + 1], by_x[back], by_y[back]))
        else:
            by_x.append(over_x(jnp.concatenate([own[back], by_y[back - 2][:HALF]])))
            by_y.append(over_y(jnp.concatenate([own[back], by_x[back - 2][HALF:SPAN]])))
    by_x.append(over_x(by_y[2][:HALF]))
    by_y.append(over_y(by_x[2][HALF:SPAN]))
    last_x, last_y = by_y[3][:HALF], by_x[3][HALF:SPAN]
    by_x.append(over_x(after(last_x, by_x[4])))
    by_y.append(over_y(after(last_y, by_y[4])))
    late_ones = (by_x[3], by_y[3])
    far_own = [over_core(each_one) for each_one in own[:2]] + [over_core(after(each_one, *late_ones)) for each_one in own[2:]]
    far = [far_own]
    for way in (by_x, by_y):
        far.append([over_core(way[0])] + [over_core(after(way[at], *late_ones)) for at in (1, 2)])
        far[-1] += [over_core(way[at]) for at in (3, 4, 5)]
    return own + by_x + by_y + far[0] + far[1] + far[2]


def added(*parts):
    total = parts[0].astype(F32)
    for each_one in parts[1:]:
        total = total + each_one.astype(F32)
    return total


SIDES = (slice(0, HALF), slice(HALF, SPAN))


def span_sums(coords, own_half, x, places, low_kept, low_got, high_kept, high_got, sides=None):
    count = len(places)
    pieces = [(at, rows) for at in range(count) for rows in sides or ()]

    def kernel(coords, low_kept, low_got, high_kept, high_got, *refs):
        outs, (kept, got, total, sems, out_sems) = refs[:-5], refs[-5:]
        high = coords[0] == int(own_half)
        for source, other, wanted in ((low_kept, low_got, jnp.logical_not(high)), (high_kept, high_got, high)):

            @pl.when(wanted)
            def _(source=source, other=other):
                for at, place in enumerate(places):
                    pltpu.make_async_copy(source.at[4 * x + place], kept.at[at], sems.at[2 * at]).start()
                    pltpu.make_async_copy(other.at[place], got.at[at], sems.at[2 * at + 1]).start()

        copies = []
        for at in range(count):
            pltpu.make_async_copy(low_kept.at[at], kept.at[at], sems.at[2 * at]).wait()
            pltpu.make_async_copy(low_got.at[at], got.at[at], sems.at[2 * at + 1]).wait()
            total[at] = low(kept[at].astype(F32) + got[at].astype(F32))
            if sides is None:
                copies.append(pltpu.make_async_copy(total.at[at], outs[0].at[at], out_sems.at[at]))
                copies[-1].start()
            for which, (mine, rows) in enumerate(pieces):
                if mine == at:
                    copies.append(pltpu.make_async_copy(total.at[at, rows], outs[which], out_sems.at[which]))
                    copies[-1].start()
        for copy in copies:
            copy.wait()

    spans = ((count, SPAN, ROW), BF16)
    arrays = [(ANY, each_one) for each_one in (low_kept, low_got, high_kept, high_got)]
    outs = [(ANY, ((rows.stop - rows.start, ROW), BF16)) for _, rows in pieces] or [(ANY, spans)]
    sums = call(
        kernel, "span_sums", [(SM, coords)] + arrays, outs, [spans] * 3 + [2 * count, max(count, len(pieces))], 40
    )
    return sums[0] if sides is None else [sums[len(sides) * at : len(sides) * (at + 1)] for at in range(count)]


def late_rows(late, above, below):
    gains = jnp.pad(late[0:8], ((above, below - 8), (0, 0)))
    return gains + jnp.pad(late[8:10], ((above + REL_AT, below - REL_AT - 2), (0, 0)))


def scatter_slow(state, back, shard_size, padded):
    late = back["late"]
    pieces = []
    for source, half in ((back, "low"), (state, "high")):
        for core in range(2):
            for at in range(8):
                z, x = at // 2, at % 2
                if core == 0:
                    span = source[half + "_kept"][4 * x + 3 - z]
                else:
                    span = source[half + ("_near", "_far")[x]][3 - z]
                d = len(pieces)
                pieces.append(span[: STARTS[d + 1] - STARTS[d] if d < PARTS - 1 else SPAN])
    rows = jnp.concatenate(pieces)
    first = ROW * BLOCK["small"][0]
    rows = low(rows.astype(F32) + late_rows(late, first, rows.shape[0] - first))
    flat = rows.reshape(-1)[: segment_bounds()[-1]]
    shard = lax.psum_scatter(flat, AXES, scatter_dimension=0, tiled=True)
    return jnp.pad(shard, (0, padded - shard_size)).astype(F32), lax.psum(late[0:8], AXES)


def scatter_grads(state, back, coords, me, shard_size, padded):
    if not fast_mesh():
        return scatter_slow(state, back, shard_size, padded)
    high = coords[0] == 1
    high_kept, low_kept = state["high_kept"], back["low_kept"]
    high_got = [over_core(state["high_near"]), over_core(state["high_far"])]
    low_far = over_core(back["low_far"])

    def chip_sum(own_half, x, places, sides=None):
        got = (low_far if x else low_near, high_got[x])
        return span_sums(coords, own_half, x, places, low_kept, got[0], high_kept, got[1], sides)

    late = back["late"]
    late = late + over_x(late)
    late = late + over_y(late)
    for_x, for_y = chip_sum(False, 1, (2, 3)), chip_sum(False, 1, (0, 1))
    for_x, for_y, late = lax.optimization_barrier((for_x, for_y, late))
    from_x, from_y = over_x(for_x), over_y(for_y)
    low_near = over_core(after(back["low_near"], for_x, for_y))
    late = late + over_core(late)
    late = late + over_z(late, 1)
    late = late + over_z(late, 2)
    to_x, to_y, mine = [
        chip_sum(own_half, x, range(4), SIDES) for own_half, x in ((True, 1), (False, 0), (True, 0))
    ]
    from_x, from_y, to_x, to_y, mine, late = lax.optimization_barrier((from_x, from_y, to_x, to_y, mine, late))
    running = [None, None]
    before = [(), ()]
    for at in range(4):
        for side, rows in enumerate(SIDES):
            send_x, send_y = to_x[at][side], to_y[at][side]
            if at < 2:
                send_x = low(added(send_x, from_y[at, rows]))
            else:
                send_y = low(added(send_y, from_x[at - 2, rows]))
            got_x, got_y = over_x(after(send_x, *before[side])), over_y(after(send_y, *before[side]))
            before[side] = (got_x, got_y)
            parts = [mine[at][side], got_x, got_y]
            if at:
                parts.append(round_z(running[side]))
            running[side] = added(*parts)
            if at < 3:
                running[side] = low(running[side])
    total = jnp.concatenate(running)
    first = ROW * BLOCK["small"][0] - STARTS[PARTS - 1]
    total = total + jnp.where(me == PARTS - 1, 1.0, 0.0) * late_rows(late, first, SPAN - first)
    flat = jnp.pad(total.reshape(-1), (0, max(0, TILE * ROW + padded - SPAN * ROW)))
    return lax.dynamic_slice(flat, (shard_offset(me, shard_size),), (padded,)), late[0:8]


def sum_everywhere(vector):
    if not fast_mesh():
        return lax.psum(vector, AXES)
    vector = vector + over_core(vector)
    vector = vector + over_x(vector)
    vector = vector + over_y(vector)
    vector = vector + over_z(vector, 1)
    return vector + over_z(vector, 2)


def most_segments(shard_size, devices):
    bounds = segment_bounds()
    most = 1
    for at in range(devices):
        low_end, high_end = at * shard_size, (at + 1) * shard_size
        most = max(most, sum(1 for b in bounds[1:-1] if low_end < b < high_end) + 1)
    return most


LANES = 128
CHUNK = 1024 * LANES


def chunk_spans(segments, step):
    first, last = step * CHUNK, (step + 1) * CHUNK
    for at in range(segments.shape[0] - 2):
        start, end = segments[1 + at], segments[2 + at]
        whole = (start <= first) & (last <= end)
        some = (start < last) & (end > first) & jnp.logical_not(whole)

        def inside(first=first, start=start, end=end):
            row = lax.broadcasted_iota(jnp.int32, (CHUNK // LANES, LANES), 0)
            place = first + row * LANES + lax.broadcasted_iota(jnp.int32, (CHUNK // LANES, LANES), 1)
            return (place >= start) & (place < end)

        yield at, whole, some, inside


def square(entries):
    return entries[...].reshape(CHUNK // LANES, LANES)


def update_kernel(segments, params, first, second, grad, new_first, new_second, update, sums):
    step = pl.program_id(0)

    @pl.when(step == 0)
    def _():
        sums[...] = jnp.zeros_like(sums)

    grads = grad[...]
    firsts = BETA_FIRST * first[...] + (1.0 - BETA_FIRST) * grads
    seconds = BETA_SECOND * second[...] + (1.0 - BETA_SECOND) * grads * grads
    new_first[...] = firsts
    new_second[...] = seconds
    first_hat = firsts * (1.0 / (1.0 - BETA_FIRST**STEP))
    second_hat = seconds * (1.0 / (1.0 - BETA_SECOND**STEP))
    update[...] = first_hat / (jnp.sqrt(second_hat) + ADAM_EPS) + WEIGHT_DECAY * params[...]
    lane = lax.broadcasted_iota(jnp.int32, (1, LANES), 1)

    def add_squares(at, pick):
        for row, entries in enumerate((params, update)):
            values = square(entries)
            total = jnp.sum(pick(values * values), axis=0, keepdims=True)
            total = jnp.sum(total, axis=1, keepdims=True)
            sums[row : row + 1, :] += jnp.where(lane == segments[0] + at, total, 0.0)

    for at, whole, some, inside in chunk_spans(segments, step):

        @pl.when(whole)
        def _(at=at):
            add_squares(at, lambda squares: squares)

        @pl.when(some)
        def _(at=at, inside=inside):
            add_squares(at, lambda squares: jnp.where(inside(), squares, 0.0))


def apply_kernel(segments, sums, params, update, new_params, norms):
    step = pl.program_id(0)
    roots = jnp.sqrt(sums[0:2, :])
    trust = roots[0:1, :] / (roots[1:2, :] + ADAM_EPS)
    norms[0:2, :] = roots
    norms[2:3, :] = trust
    norms[3:8, :] = jnp.zeros((5, LANES), F32)
    lane = lax.broadcasted_iota(jnp.int32, (1, LANES), 1)
    for at, whole, some, inside in chunk_spans(segments, step):

        def moved(at=at):
            scale = LEARN_RATE * jnp.sum(jnp.where(lane == segments[0] + at, trust, 0.0), axis=1, keepdims=True)
            return (square(params) - scale * square(update)).reshape(CHUNK)

        @pl.when(whole)
        def _(moved=moved):
            new_params[...] = moved()

        @pl.when(some)
        def _(moved=moved, inside=inside):
            chosen = jnp.where(inside(), moved().reshape(CHUNK // LANES, LANES), square(new_params))
            new_params[...] = chosen.reshape(CHUNK)


def shards(frames, lengths, cotangent, params, first_moment, second_moment):
    shard_size = params.shape[0]
    devices = lax.axis_size("dp") * lax.axis_size("fsdp")
    me = lax.axis_index(AXES)
    if fast_mesh():
        dp, fsdp = lax.axis_index("dp"), lax.axis_index("fsdp")
        coords = jnp.stack([dp // 2, dp % 2, fsdp // 2, fsdp % 2]).astype(jnp.int32)
    else:
        coords = jnp.zeros((4,), jnp.int32)
    state = forward(coords, lengths, frames[0], cotangent[0], gather_shards(low(params), me))
    back = backward(coords, frames[0], state)
    steps = -(-shard_size // CHUNK)
    size = max(shard_size, CHUNK)
    grad_shard, gain_grads = scatter_grads(state, back, coords, me, shard_size, size)

    def filled(flat):
        return jnp.pad(flat, (0, size - shard_size)) if size > shard_size else flat

    bounds = segment_bounds()
    spans = most_segments(shard_size, devices)
    shard_low = me * shard_size
    first_segment = sum((shard_low >= b).astype(jnp.int32) for b in bounds[1:-1])
    table = jnp.asarray(bounds[1:] + [bounds[-1]] * spans, jnp.int32)
    ends = jnp.clip(lax.dynamic_slice(table, (first_segment,), (spans,)) - shard_low, 0, shard_size)
    segments = jnp.concatenate([first_segment[None], jnp.zeros((1,), jnp.int32), ends]).astype(jnp.int32)
    grid = pl.BlockSpec((CHUNK,), lambda step: (step,))
    whole = pl.BlockSpec((8, LANES), lambda step: (0, 0))
    flat_kind = jax.ShapeDtypeStruct((size,), F32)
    tile_kind = jax.ShapeDtypeStruct((8, LANES), F32)
    weights = filled(params)
    new_first, new_second, update, sums = pl.pallas_call(
        update_kernel,
        name="update",
        grid=(steps,),
        in_specs=[SM] + [grid] * 4,
        out_specs=[grid] * 3 + [whole],
        out_shape=[flat_kind] * 3 + [tile_kind],
    )(segments, weights, filled(first_moment), filled(second_moment), grad_shard)
    sums = sum_everywhere(sums)
    new_params, norms = pl.pallas_call(
        apply_kernel,
        name="apply",
        grid=(steps,),
        in_specs=[SM, whole, grid, grid],
        out_specs=[grid, whole],
        out_shape=[flat_kind, tile_kind],
    )(segments, sums, weights, update)
    count = len(segment_shapes())
    return (
        state["out"].reshape(frames.shape),
        back["fgrad"].reshape(frames.shape),
        new_params[:shard_size],
        new_first[:shard_size],
        new_second[:shard_size],
        norms[0, :count],
        norms[1, :count],
        norms[2, :count],
        gain_grads.reshape(-1),
    )


def solution(mesh):
    placed = (
        P(("dp", "fsdp"), None, None),
        P(("dp", "fsdp")),
        P(("dp", "fsdp"), None, None),
        P(("dp", "fsdp")),
        P(("dp", "fsdp")),
        P(("dp", "fsdp")),
    )
    return jax.shard_map(
        shards,
        mesh=mesh,
        in_specs=placed,
        out_specs=(
            P(("dp", "fsdp"), None, None),
            P(("dp", "fsdp"), None, None),
            P(("dp", "fsdp")),
            P(("dp", "fsdp")),
            P(("dp", "fsdp")),
            P(),
            P(),
            P(),
            P(),
        ),
        check_vma=False,
    )
```

```python
import math
from types import SimpleNamespace

import jax
import jax.numpy as jnp
from jax import lax
from jax.experimental import pallas as pl
from jax.experimental.pallas import tpu as pltpu
from jax.sharding import PartitionSpec as P

STEP = 8
BETA_FIRST = 0.5
BETA_SECOND = 0.5
LEARN_RATE = 0.5
WEIGHT_DECAY = 0.01
ADAM_EPS = 1e-06
AXES = ("dp", "fsdp")


def segment_shapes():
    gate_width = CG // 2
    return [
        (D, FF),
        (FF, D),
        (D, 3 * D),
        (D, D),
        (D, CG),
        (gate_width, D),
        (2 * D, D),
        (D, FF),
        (FF, D),
        (5 * D + gate_width,),
        (KER, gate_width + 2 * D),
        (RELW, H),
    ]


D = 512
H = 8
HS = 64
FF = 2048
CG = 3072
KER = 31
RELW = 128
NORM_EPS = 1e-05
MASK_FILL = -1000000000.0
ROW = 512
HALF = ROW // 2
SLOTS = 160
KEYS = 256
PAD = 16
PADDED = SLOTS + 2 * PAD
GATE = CG // 2
BLOCK = {
    "ffa_in": (0, 4),
    "ffa_out": (4, 4),
    "qkv": (8, 3),
    "att_out": (11, 1),
    "cg_in": (12, 6),
    "cg_out": (18, 3),
    "merge": (21, 2),
    "ffb_in": (23, 4),
    "ffb_out": (27, 4),
    "small": (31, 1),
}
TAPS_AT = 8
REL_AT = 8 + 5 * KER
SMALL = 176
F32, BF16 = jnp.float32, jnp.bfloat16


def dot(left, right):
    return lax.dot_general(left, right, (((1,), (0,)), ((), ())), preferred_element_type=F32)


def dot_t(left, right):
    return lax.dot_general(left, right, (((1,), (1,)), ((), ())), preferred_element_type=F32)


def t_dot(left, right):
    return lax.dot_general(left, right, (((0,), (0,)), ((), ())), preferred_element_type=F32)


def low(values):
    return values.astype(BF16)


def each(count, body):
    for at in range(count):
        body(at)


def each_loop(count, body, together=1):
    def step(at, carry):
        for inner in range(together):
            body(at * together + inner)
        return carry

    lax.fori_loop(0, count // together, step, 0)


def part(at, size):
    if isinstance(at, int):
        return slice(at * size, at * size + size)
    return pl.ds(pl.multiple_of(at * size, size), size)


def rows_of(name):
    first, count = BLOCK[name]
    return slice(ROW * first, ROW * (first + count))


def lane_mean(values, width):
    return jnp.sum(values, axis=-1, keepdims=True) * (1.0 / width)


def normed(values):
    centered = values - lane_mean(values, values.shape[-1])
    scale = lax.rsqrt(lane_mean(centered * centered, values.shape[-1]) + NORM_EPS)
    return centered * scale, scale


def valid_rows(length):
    return (lax.broadcasted_iota(jnp.int32, (SLOTS, 1), 0) < length).astype(F32)


def fold_rows(values):
    return jnp.sum(values, axis=0, keepdims=True)


def norm_rows(source, gain, target):
    for k in range(2):
        hat, _ = normed(source[part(k, 80), :].astype(F32))
        target[part(k, 80), :] = low(hat * gain)


def norm_rows_back(values, gain, grad, add):
    total = jnp.zeros((1, values.shape[1]), F32)
    for k in range(2):
        rows = part(k, 80)
        hat, scale = normed(values[rows, :].astype(F32))
        mine = grad[rows, :]
        total = total + fold_rows(mine * hat)
        inner = mine * gain
        width = values.shape[1]
        moved = lane_mean(inner, width) + hat * lane_mean(inner * hat, width)
        add(rows, scale * (inner - moved))
    return total


TOTAL_ROWS = 16037
PARTS = 32
TILE = 16
SPAN = 528
STARTS = [TILE * (TOTAL_ROWS * d // (PARTS * TILE)) for d in range(PARTS + 1)]
FIRST_PARTS = max(d for d in range(PARTS) if STARTS[d] < ROW * sum(BLOCK["ffa_out"]))
SHORTEST = min(high - first for first, high in zip(STARTS, STARTS[1:]))


def start_of(d):
    return ((TOTAL_ROWS * d) >> 9) * TILE


def gathered_layout():
    layout = []
    for core in range(2):
        layout += [[(core, 0, 0, back, 0, SPAN, 0)] for back in range(4)]
        for y, x, first, last in ((0, 1, 0, HALF), (1, 0, HALF, SPAN)):
            whole = [(core, y, x, back, 0, SPAN, 0) for back in range(4)]
            diagonal = [(core, 1, 1, back, first, last) for back in range(4)]
            layout += [[whole[0]], [whole[1]]]
            layout += [[whole[2], (*diagonal[0], SPAN)], [whole[3], (*diagonal[1], SPAN)]]
            layout += [[(*diagonal[2], 0)], [(*diagonal[3], 0)]]
    return layout


LAYOUT = gathered_layout()


def source_part(coords, piece):
    y, c, z, x = coords[0], coords[1], coords[2], coords[3]
    yy, cc, xx, zz = y ^ piece[1], c ^ piece[0], x ^ piece[2], (z + 4 - piece[3]) & 3
    return ((yy * 2 + cc) * 4 + zz) * 2 + xx


class Loads:
    def __init__(self, coords, sources, target, seams, sems):
        self.target, self.seams, self.sems = target, seams, sems
        self.here, self.joined = set(), set()
        seams[0, 0] = jnp.zeros((TILE, ROW), BF16)
        seams[PARTS, 1] = jnp.zeros((TILE, ROW), BF16)

        for soon in (True, False):
            for pieces, source in zip(LAYOUT, sources):
                for piece in pieces:
                    d = source_part(coords, piece)
                    first_ones = (d <= FIRST_PARTS) | (d == PARTS - 1)

                    @pl.when(first_ones if soon else jnp.logical_not(first_ones))
                    def _(piece=piece, source=source, d=d):
                        self.start(piece, source, d)

    def start(self, piece, source, d):
        def rows(at, size):
            return pl.ds(pl.multiple_of(at, TILE), size)

        first, last, offset = piece[4:]
        offset = offset - first
        start = start_of(d)
        length = start_of(d + 1) - start
        inner, outer = max(first, TILE), min(last, SHORTEST)
        sem = self.sems.at[d]
        pltpu.make_async_copy(
            source.at[offset + inner : offset + outer], self.target.at[rows(start + inner, outer - inner)], sem
        ).start()
        if first == 0:
            pltpu.make_async_copy(source.at[offset : offset + TILE], self.seams.at[d, 1], sem).start()
        if last == SPAN:

            @pl.when(length > SHORTEST)
            def _():
                pltpu.make_async_copy(
                    source.at[offset + SHORTEST : offset + SHORTEST + TILE],
                    self.target.at[rows(start + SHORTEST, TILE)],
                    sem,
                ).start()

            pltpu.make_async_copy(source.at[rows(offset + length, TILE)], self.seams.at[d + 1, 0], sem).start()

    def wait_part(self, d):
        if d in self.here or not 0 <= d < PARTS:
            return
        self.here.add(d)
        size = STARTS[d + 1] - STARTS[d] + TILE
        pltpu.make_async_copy(self.target.at[0:size], self.target.at[0:size], self.sems.at[d]).wait()

    def wait(self, name):
        rows = rows_of(name)
        last = min(rows.stop, STARTS[-1] + TILE)
        for d in range(PARTS + 1):
            if STARTS[d] < last and STARTS[d] + TILE > rows.start and d not in self.joined:
                self.wait_part(d - 1)
                self.wait_part(d)
                self.joined.add(d)
                self.target[STARTS[d] : STARTS[d] + TILE, :] = self.seams[d, 0] + self.seams[d, 1]
            if d < PARTS and STARTS[d] + TILE < last and STARTS[d + 1] > rows.start:
                self.wait_part(d)


class Emits:
    def __init__(self, coords, halves, sems):
        self.coords, self.halves, self.sems = coords, halves, sems
        self.pending = []

    def put(self, d, values, rows):
        core, z, x = (d // 8) % 2, (d // 2) % 4, d % 2
        kept, sent = self.halves[d // 16]
        far_x = self.coords[3] ^ x
        place = (self.coords[2] + 3 - z) & 3
        sem = self.sems.at[len(self.pending)]

        @pl.when(self.coords[1] == core)
        def _():
            pltpu.make_async_copy(values, kept.at[4 * far_x + place, rows], sem).start()

        @pl.when((self.coords[1] != core) & (far_x == 0))
        def _():
            pltpu.make_async_copy(values, sent[0].at[place, rows], sem).start()

        @pl.when((self.coords[1] != core) & (far_x == 1))
        def _():
            pltpu.make_async_copy(values, sent[1].at[place, rows], sem).start()

        self.pending.append(pltpu.make_async_copy(values, kept.at[0, rows], sem))

    def put_tensor(self, name, values):
        rows = rows_of(name)
        for d in range(PARTS):
            first, last = max(rows.start, STARTS[d]), min(rows.stop, STARTS[d] + SPAN)
            if first < last:
                self.put(d, values.at[first - rows.start : last - rows.start], slice(first - STARTS[d], last - STARTS[d]))

    def wait(self):
        for copy in self.pending:
            copy.wait()


def split_columns(raw, target, wide, stage):
    def chunk(k):
        rows = part(k, 128 * wide)
        for lane in range(4):
            stage[lane, 0 : 128 * wide, :] = raw[rows, lane * 128 : lane * 128 + 128].astype(F32)
        for c in range(wide):
            for lane in range(4):
                place = ROW * c + lane * 128
                target[part(k, 128), place : place + 128] = low(stage[lane, pl.ds(c, 128, stride=wide), :])

    each_loop(4, chunk)


def weight_columns(left, grads, wide, stage, left_t, target):
    left_t[...] = left[...].T

    def chunk(j):
        value = dot(left_t[...], grads[:, part(j, 256)])
        c, pair = j // 2, (j % 2) * 2
        for half in range(2):
            stage[pair + half, pl.ds(c, ROW, stride=wide), :] = value[:, 128 * half : 128 * half + 128]

    each(2 * wide, chunk)

    def lower(k):
        rows = part(k, ROW)
        for lane in range(4):
            target[rows, lane * 128 : lane * 128 + 128] = low(stage[lane, rows, :])

    each_loop(wide, lower)


def weight_rows(left, grads, count, left_t, target):
    def chunk(k):
        left_t[...] = left[:, part(k, ROW)].T
        for at in range(2):
            target[part(k, ROW), 256 * at : 256 * at + 256] = low(dot(left_t[...], grads[:, 256 * at : 256 * at + 256]))

    each(count, chunk)


def feed_forward(inputs, gain, w_in, w_out, nrm, act, slope, result):
    norm_rows(inputs, gain, nrm)

    def up(j):
        at = part(j, 256)
        hidden = dot(nrm[...], w_in[:, at])
        sig = jax.nn.sigmoid(hidden)
        active = hidden * sig
        act[:, at] = low(active)
        slope[:, at] = low(sig + active * (1.0 - sig))

    each(FF // 256, up)

    def down(j):
        at = part(j, 256)
        result[:, at] = inputs[:, at].astype(F32) + 0.5 * dot(act[...], w_out[:, at])

    each(2, down)


def feed_back(dout, w_in, w_out, nrm, act, slope, dhid, dnrm, stage, left_t, g_in, g_out, emits, name):
    def up(j):
        at = part(j, 256)
        grad = dot_t(dout[...], w_out[at, :])
        dhid[:, at] = low(grad * slope[:, at].astype(F32))

    each(FF // 256, up)
    weight_rows(act, dout, 4, left_t, g_out)
    emits.put_tensor(name + "_out", g_out)

    def down(j):
        at = part(j, 256)
        dnrm[:, at] = dot_t(dhid[:, 0:FF], w_in[at, :])

    each(2, down)
    weight_columns(nrm, dhid, 4, stage, left_t, g_in)
    emits.put_tensor(name + "_in", g_in)


def bucket_map():
    entry = lax.broadcasted_iota(jnp.int32, (2 * ROW, ROW), 0) // H
    far = lax.broadcasted_iota(jnp.int32, (2 * ROW, ROW), 1)
    far = jnp.where(far >= ROW // 2, far - ROW, far)
    bucket = jnp.clip(far, -(RELW // 2), RELW // 2 - 1) + RELW // 2
    return (entry == bucket).astype(F32)


def own_entries(flat):
    entry = lax.broadcasted_iota(jnp.int32, (H, 2 * ROW), 1)
    head = lax.broadcasted_iota(jnp.int32, (H, 2 * ROW), 0)
    return jnp.where(lax.rem(entry, H) == head, flat, 0.0)


def tap_row(small, tap, row, lane):
    return small[lane, pl.ds(TAPS_AT + 5 * tap + row, 1), :]


def shifted_sum(padded, at, factor):
    total = None
    for low_part in range(8):
        slab = padded[low_part : low_part + SLOTS + 24, at]
        inner = None
        for high_part in range(4):
            offset = 8 * high_part + low_part
            if offset:
                term = factor(offset) * slab[8 * high_part : 8 * high_part + SLOTS]
                inner = term if inner is None else inner + term
        total = inner if total is None else total + inner
    return total


def convolve(padded, small, first_row, width, finish):

    def chunk(j):
        at = part(j, 128)
        row, lane = first_row + j // 4, j % 4
        finish(j, at, shifted_sum(padded, at, lambda offset: tap_row(small, offset - 1, row, lane)))

    each_loop(width // 128, chunk)


def convolve_back(grads, padded, small, first_row, width, sgrad, finish):

    def chunk(j):
        at = part(j, 128)
        row, lane = first_row + j // 4, j % 4
        finish(j, at, shifted_sum(grads, at, lambda offset: tap_row(small, KER - offset, row, lane)))
        own = grads[PAD : PAD + SLOTS, at]
        for low_part in range(8):
            slab = padded[low_part : low_part + SLOTS + 24, at]
            for high_part in range(4):
                offset = 8 * high_part + low_part
                if offset:
                    tile = slab[8 * high_part : 8 * high_part + SLOTS]
                    sgrad[lane, pl.ds(TAPS_AT + 5 * (offset - 1) + row, 1), :] = fold_rows(own * tile)

    each_loop(width // 128, chunk)


def clear_margins(padded):
    padded[0:PAD, :] = jnp.zeros((PAD, padded.shape[1]), F32)
    padded[PAD + SLOTS : PADDED, :] = jnp.zeros((PAD, padded.shape[1]), F32)


def gelu_parts(hidden):
    bell = jnp.exp(-0.5 * hidden * hidden)
    spread = 1.0 + (0.3275911 * 2.0**-0.5) * jnp.abs(hidden)
    near = pl.reciprocal(spread, approx=True)
    near = near * (2.0 - spread * near)
    tail = jnp.full_like(near, 0.5 * 1.061405429)
    for factor in (-1.453152027, 1.421413741, -0.284496736, 0.254829592):
        tail = tail * near + 0.5 * factor
    tail = tail * near * bell
    below = jnp.where(hidden >= 0.0, 1.0 - tail, tail)
    return hidden * below, below + hidden * bell * ((2.0 * math.pi) ** -0.5)


def attention_forward(r, length):
    norm_rows(r.x1, r.small[1:2, :], r.nrm_t)
    r.qkv[SLOTS:KEYS, :] = jnp.zeros((KEYS - SLOTS, 3 * D), BF16)
    flat = jnp.concatenate([r.small[REL_AT : REL_AT + 1, :], r.small[REL_AT + 1 : REL_AT + 2, :]], axis=1)
    r.bias[...] = dot(low(own_entries(jnp.broadcast_to(flat, (H, 2 * ROW)))), low(bucket_map()))

    def project(j):
        at = part(j, 256)
        r.qkv[0:SLOTS, at] = low(dot(r.nrm_t[...], r.w_qkv[:, at]))

    each(3 * D // 256, project)
    valid = lax.broadcasted_iota(jnp.int32, (1, KEYS), 1) < length
    first_half = lax.broadcasted_iota(jnp.int32, (1, 128), 1) < HS

    def heads(pair):
        queries = r.qkv[0:SLOTS, part(pair, 128)]
        keys = r.qkv[:, part(pair + 4, 128)]
        values = r.qkv[:, part(pair + 8, 128)]
        outs = []
        for odd in range(2):
            head = 2 * pair + odd
            half = first_half if odd == 0 else jnp.logical_not(first_half)
            mine = jnp.where(half, queries, jnp.zeros_like(queries))
            spread = jnp.broadcast_to(r.bias[pl.ds(head, 1), :], (SLOTS, ROW))
            spread = pltpu.roll(spread, 0, 1, stride=1, stride_axis=0)[:, 0:KEYS]
            scores = jnp.where(valid, dot_t(mine, keys) * HS ** (-0.5) + spread, MASK_FILL)
            shifted = jnp.exp(scores - jnp.max(scores, axis=-1, keepdims=True))
            chances = low(shifted / jnp.sum(shifted, axis=-1, keepdims=True))
            r.probs[head] = chances
            outs.append(dot(chances, values))
        r.ctx[:, part(pair, 128)] = low(jnp.where(first_half, outs[0], outs[1]))

    each(H // 2, heads)

    def project_out(j):
        at = part(j, 256)
        r.cat[:, at] = dot(r.ctx[...], r.w[rows_of("att_out"), at])

    each(2, project_out)


def gating_forward(r, length):
    norm_rows(r.x1, r.small[2:3, :], r.nrm_c)

    def up(j):
        at = part(j, 256)
        r.hid[...] = dot(r.nrm_c[...], r.w_cg[:, at])
        for k in range(5):
            rows = part(k, 32)
            active, slope = gelu_parts(r.hid[rows, :])
            r.ug[rows, at] = active
            r.slope_c[rows, at] = low(slope)

    each_loop(CG // 256, up, 2)
    tiles = [slice(GATE + 128 * j, GATE + 128 * j + 128) for j in range(GATE // 128)]
    total = jnp.zeros((SLOTS, 128), F32)
    for at in tiles:
        total = total + r.ug[:, at]
    mean = lane_mean(total, GATE)
    total = jnp.zeros((SLOTS, 128), F32)
    for at in tiles:
        centered = r.ug[:, at] - mean
        total = total + centered * centered
    scale = lax.rsqrt(lane_mean(total, GATE) + NORM_EPS)
    r.gmean[...] = jnp.broadcast_to(mean, (SLOTS, 128))
    r.gscale[...] = jnp.broadcast_to(scale, (SLOTS, 128))
    scale = scale * valid_rows(length)
    for j, at in enumerate(tiles):
        gain = r.small[5 + j // 4 : 6 + j // 4, part(j % 4, 128)]
        r.gpad[PAD : PAD + SLOTS, part(j, 128)] = (r.ug[:, at] - mean) * scale * gain

    def finish(j, at, value):
        r.cv[:, at] = low(value)
        r.gated[:, at] = low(r.ug[:, at] * value)

    convolve(r.gpad, r.tiles, 0, GATE, finish)

    def down(j):
        r.cat[:, part(j + 2, 256)] = dot(r.gated[...], r.w[rows_of("cg_out"), part(j, 256)])

    each(2, down)


def merge_forward(r, length):
    valid = valid_rows(length)
    for j in range(8):
        at = part(j, 128)
        r.mpad[PAD : PAD + SLOTS, at] = r.cat[:, at] * valid

    def finish(j, at, value):
        r.mixed[:, at] = low(r.cat[:, at] + value)

    convolve(r.mpad, r.tiles, 3, 2 * D, finish)

    def merge(j):
        at = part(j, 256)
        r.x2[:, at] = r.x1[:, at] + dot(r.mixed[...], r.w[rows_of("merge"), at])

    each(2, merge)


def final_norm(r, length):
    gain = r.small[4:5, :]
    valid = valid_rows(length)
    total = jnp.zeros((1, D), F32)
    for k in range(2):
        rows = part(k, 80)
        hat, scale = normed(r.x3[rows, :])
        r.out[rows, :] = low(hat * gain * valid[80 * k : 80 * k + 80])
        mine = r.cot[rows, :].astype(F32) * valid[80 * k : 80 * k + 80]
        total = total + fold_rows(mine * hat)
        inner = mine * gain
        back = scale * (inner - (lane_mean(inner, D) + hat * lane_mean(inner * hat, D)))
        r.dx[rows, :] = back
        r.dout[rows, :] = low(0.5 * back)
    r.gains[4:5, :] = total


def merge_back(r, length, emits):
    for k in range(2):
        r.dout[part(k, 80), :] = low(r.dx[part(k, 80), :])
    w_merge = r.w.at[rows_of("merge")]

    def merge(j):
        at = part(j, 256)
        r.dpad[PAD : PAD + SLOTS, at] = dot_t(r.dout[...], w_merge[at, :])

    each(2 * D // 256, merge)
    weight_rows(r.mixed, r.dout, 2, r.left_t, w_merge)
    emits.put_tensor("merge", w_merge)

    def finish(j, at, value):
        r.djoin[:, at] = low(r.dpad[PAD : PAD + SLOTS, at] + value * valid_rows(length))

    convolve_back(r.dpad, r.mpad, r.tiles, 3, 2 * D, r.tgrad, finish)


def gating_back(r, length, emits):
    w_co = r.w.at[rows_of("cg_out")]

    def gate(j):
        at = part(j, 256)
        value = dot_t(r.djoin[:, D:], w_co[at, :])
        r.dhid[:, at] = low(value * r.cv[:, at].astype(F32) * r.slope_c[:, at].astype(F32))
        r.dpad[PAD : PAD + SLOTS, at] = value * r.ug[:, at]

    each(GATE // 256, gate)
    r.dout[...] = r.djoin[:, D:]
    weight_rows(r.gated, r.dout, 3, r.left_t, w_co)
    emits.put_tensor("cg_out", w_co)

    def finish(j, at, value):
        r.dgate[:, at] = value * valid_rows(length)

    convolve_back(r.dpad, r.gpad, r.tiles, 0, GATE, r.tgrad, finish)
    tiles = GATE // 128
    for quarter in range(4):
        rows = part(quarter, SLOTS // 4)
        mean, scale = r.gmean[rows, :], r.gscale[rows, :]
        total, total_hat = jnp.zeros_like(mean), jnp.zeros_like(mean)

        def parts(j, rows=rows, mean=mean, scale=scale):
            row, lane = 5 + j // 4, part(j % 4, 128)
            hat = (r.ug[rows, part(j + tiles, 128)] - mean) * scale
            grad = r.dgate[rows, part(j, 128)]
            return hat, grad, grad * r.small[row : row + 1, lane]

        for j in range(tiles):
            hat, grad, inner = parts(j)
            products = jnp.sum((grad * hat).reshape(-1, 8, 128), axis=0)
            r.gate_sums[part(j, 8), :] = products if quarter == 0 else r.gate_sums[part(j, 8), :] + products
            total = total + inner
            total_hat = total_hat + inner * hat
        total = jnp.broadcast_to(lane_mean(total, GATE), total.shape)
        total_hat = jnp.broadcast_to(lane_mean(total_hat, GATE), total.shape)
        for j in range(tiles):
            hat, _, inner = parts(j)
            far = part(j + tiles, 128)
            r.dgate[rows, part(j, 128)] = scale * (inner - total - hat * total_hat)
    for j in range(tiles):
        far = part(j + tiles, 128)
        r.dhid[:, far] = low(r.dgate[:, part(j, 128)] * r.slope_c[:, far].astype(F32))
        r.tgrad[j % 4, 5 + j // 4 : 6 + j // 4, :] = fold_rows(r.gate_sums[part(j, 8), :])

    def down(j):
        at = part(j, 256)
        r.dnrm[:, at] = dot_t(r.dhid[...], r.w_cg[at, :])

    each(2, down)
    g_cg = r.w.at[rows_of("cg_in")]
    weight_columns(r.nrm_c, r.dhid, 6, r.stage, r.left_t, g_cg)
    emits.put_tensor("cg_in", g_cg)

    def add(rows, back):
        r.dx[rows, :] += back

    r.gains[2:3, :] = norm_rows_back(r.x1, r.small[2:3, :], r.dnrm, add)


def forward_kernel(names, coords, length_ref, frames, cot, *refs):
    sources, refs = refs[: len(LAYOUT)], refs[len(LAYOUT) :]
    r = SimpleNamespace(**dict(zip(names, refs)))
    r.cot = cot
    length = length_ref[0]
    loads = Loads(coords, sources, r.w, r.seams, r.load_sems)
    kept = []

    def keep(source, target):
        copy = pltpu.make_async_copy(source, target, r.keep_sems.at[len(kept)])
        copy.start()
        kept.append(copy)

    for padded in (r.gpad, r.mpad, r.dpad):
        clear_margins(padded)
    r.tgrad[...] = jnp.zeros_like(r.tgrad)
    r.gains[...] = jnp.zeros_like(r.gains)
    loads.wait("small")
    r.small[...] = r.w[ROW * 31 : ROW * 31 + SMALL, :].astype(F32)
    for lane in range(4):
        r.tiles[lane] = r.small[:, part(lane, 128)]
    loads.wait("ffa_in")
    split_columns(r.w.at[rows_of("ffa_in")], r.w_ffa_in, 4, r.stage)
    keep(r.w_ffa_in, r.keep_ffa_in)
    loads.wait("ffa_out")
    keep(r.w.at[rows_of("ffa_out")], r.keep_ffa_out)
    feed_forward(frames, r.small[0:1, :], r.w_ffa_in, r.w.at[rows_of("ffa_out")], r.nrm, r.act, r.slope, r.x1)
    keep(r.nrm, r.keep_nrm)
    keep(r.act, r.keep_act)
    keep(r.slope, r.keep_slope)
    keep(r.x1, r.keep_x1)
    loads.wait("qkv")
    split_columns(r.w.at[rows_of("qkv")], r.w_qkv, 3, r.stage)
    keep(r.w_qkv, r.keep_qkv)
    loads.wait("att_out")
    keep(r.w.at[rows_of("att_out")], r.keep_att)
    attention_forward(r, length)
    keep(r.nrm_t, r.keep_nrm_t)
    keep(r.qkv, r.keep_heads)
    keep(r.probs, r.keep_probs)
    keep(r.ctx, r.keep_ctx)
    loads.wait("cg_in")
    split_columns(r.w.at[rows_of("cg_in")], r.w_cg, 6, r.stage)
    loads.wait("cg_out")
    gating_forward(r, length)
    loads.wait("merge")
    merge_forward(r, length)
    loads.wait("ffb_in")
    split_columns(r.w.at[rows_of("ffb_in")], r.w_ffb_in, 4, r.stage)
    loads.wait("ffb_out")
    w_out = r.w.at[rows_of("ffb_out")]
    feed_forward(r.x2, r.small[3:4, :], r.w_ffb_in, w_out, r.nrm_b, r.act_b, r.slope_b, r.x3)
    final_norm(r, length)
    emits = Emits(
        coords,
        ((r.low_kept, (r.low_near, r.low_far)), (r.high_kept, (r.high_near, r.high_far))),
        r.emit_sems,
    )
    feed_back(
        r.dout, r.w_ffb_in, w_out, r.nrm_b, r.act_b, r.slope_b, r.dhid, r.dnrm, r.stage, r.left_t,
        r.w.at[rows_of("ffb_in")], w_out, emits, "ffb",
    )

    def add(rows, back):
        r.dx[rows, :] += back

    r.gains[3:4, :] = norm_rows_back(r.x2, r.small[3:4, :], r.dnrm, add)
    merge_back(r, length, emits)
    keep(r.djoin, r.keep_djoin)
    gating_back(r, length, emits)
    keep(r.dx, r.keep_dx)
    for lane in range(4):
        at = part(lane, 128)
        r.gains[5:8, at] = r.tgrad[lane, 5:8, :]
        r.w[ROW * 31 : ROW * 31 + SMALL, at] = low(r.tgrad[lane])
    r.w[ROW * 31 : ROW * 31 + 16, :] = low(
        jnp.concatenate(
            [
                jnp.zeros((8, ROW), F32),
                jnp.concatenate([r.tgrad[lane, 8:16, :] for lane in range(4)], axis=1),
            ],
            axis=0,
        )
    )
    r.w[ROW * 31 + SMALL : ROW * 32, :] = jnp.zeros((ROW - SMALL, ROW), BF16)
    emits.put_tensor("small", r.w.at[rows_of("small")])
    for copy in kept:
        copy.wait()
    emits.wait()


def attention_back(r, emits):
    def project(j):
        at = part(j, 256)
        r.dctx[:, at] = low(dot_t(r.datt[...], r.w_att[at, :]))

    each(2, project)
    weight_rows(r.ctx, r.datt, 1, r.left_t, r.w_att)
    emits.put_tensor("att_out", r.w_att)
    first_half = lax.broadcasted_iota(jnp.int32, (1, 128), 1) < HS
    at_row = lax.broadcasted_iota(jnp.int32, (SLOTS, SLOTS), 0)
    at_column = lax.broadcasted_iota(jnp.int32, (SLOTS, SLOTS), 1)
    flip = low((at_row + at_column == SLOTS - 1).astype(F32))

    def heads(pair):
        queries = r.qkv[0:SLOTS, part(pair, 128)]
        keys = r.qkv[:, part(pair + 4, 128)]
        values = r.qkv[:, part(pair + 8, 128)]
        context = r.dctx[:, part(pair, 128)]
        q_parts, k_parts, v_parts = [], [], []
        for odd in range(2):
            head = 2 * pair + odd
            half = first_half if odd == 0 else jnp.logical_not(first_half)
            chances = r.probs[head]
            v_parts.append(t_dot(chances, context)[0:SLOTS])
            wide_chances = chances.astype(F32)
            chance_grad = dot_t(jnp.where(half, context, jnp.zeros_like(context)), values)
            inner = jnp.sum(wide_chances * chance_grad, axis=-1, keepdims=True)
            score_grad = low(wide_chances * (chance_grad - inner))
            q_parts.append(dot(score_grad, keys))
            k_parts.append(t_dot(score_grad, queries)[0:SLOTS])
            wide = jnp.concatenate([dot(flip, score_grad), jnp.zeros((SLOTS, ROW - KEYS), F32)], axis=1)
            wide = pltpu.roll(wide, ROW - SLOTS + 1, 1, stride=1, stride_axis=0)
            r.sums[pl.ds(head, 1), :] = fold_rows(wide)
        scale = HS ** (-0.5)
        r.dhid[:, part(pair, 128)] = low(jnp.where(first_half, q_parts[0], q_parts[1]) * scale)
        r.dhid[:, part(pair + 4, 128)] = low(jnp.where(first_half, k_parts[0], k_parts[1]) * scale)
        r.dhid[:, part(pair + 8, 128)] = low(jnp.where(first_half, v_parts[0], v_parts[1]))

    each(H // 2, heads)

    def down(j):
        at = part(j, 256)
        r.dnrm[:, at] = dot_t(r.dhid[:, 0 : 3 * D], r.w_qkv[at, :])

    each(2, down)

    def add(rows, back):
        r.dx[rows, :] += back
        r.dout[rows, :] = low(0.5 * r.dx[rows, :])

    r.late[1:2, :] = norm_rows_back(r.x1, r.gain_rows[1:2, :], r.dnrm, add)


def attention_weights_back(r, emits):
    weight_columns(r.nrm_t, r.dhid, 3, r.stage, r.left_t, r.g_qkv)
    emits.put_tensor("qkv", r.g_qkv)
    by_entry = lax.dot_general(
        r.sums[...],
        bucket_map(),
        (((1,), (1,)), ((), ())),
        precision=lax.Precision.HIGHEST,
        preferred_element_type=F32,
    )
    flat = fold_rows(own_entries(by_entry))
    r.late[8:9, :] = flat[:, 0:ROW]
    r.late[9:10, :] = flat[:, ROW:]


def backward_kernel(names, coords, frames, gains, gain_rows, *refs):
    r = SimpleNamespace(**dict(zip(names, refs)))
    r.gain_rows = gain_rows
    waits = {}
    for at, (name, source, target) in enumerate(
        (
            ("att", r.in_att, r.w_att),
            ("djoin", r.in_djoin.at[:, 0:D], r.datt),
            ("ctx", r.in_ctx, r.ctx),
            ("heads", r.in_heads, r.qkv),
            ("probs", r.in_probs, r.probs),
            ("qkv", r.in_qkv, r.w_qkv),
            ("x1", r.in_x1, r.x1),
            ("dx", r.in_dx, r.dx),
            ("nrm_t", r.in_nrm_t, r.nrm_t),
            ("ffa_out", r.in_ffa_out, r.w_ffa_out),
            ("slope", r.in_slope, r.slope),
            ("act", r.in_act, r.act),
            ("ffa_in", r.in_ffa_in, r.w_ffa_in),
            ("nrm", r.in_nrm, r.nrm),
        )
    ):
        waits[name] = pltpu.make_async_copy(source, target, r.load_sems.at[at])
        waits[name].start()
    r.late[...] = jnp.zeros_like(r.late)
    emits = Emits(coords, ((r.low_kept, (r.low_near, r.low_far)),), r.emit_sems)
    for name in ("att", "djoin", "ctx", "heads", "probs", "qkv", "x1", "dx"):
        waits[name].wait()
    attention_back(r, emits)
    waits["nrm_t"].wait()
    attention_weights_back(r, emits)
    for name in ("ffa_out", "slope", "act", "ffa_in", "nrm"):
        waits[name].wait()
    feed_back(
        r.dout, r.w_ffa_in, r.w_ffa_out, r.nrm, r.act, r.slope, r.dhid, r.dnrm, r.stage, r.left_t, r.g_ffa_in,
        r.w_ffa_out, emits, "ffa",
    )

    def add(rows, back):
        r.fgrad[rows, :] = low(r.dx[rows, :] + back)

    r.late[0:1, :] = norm_rows_back(frames, gain_rows[0:1, :], r.dnrm, add)
    r.late[2:8, :] = gains[2:8, :]
    emits.wait()


VM = pl.BlockSpec(memory_space=pltpu.VMEM)
SM = pl.BlockSpec(memory_space=pltpu.SMEM)
ANY = pl.BlockSpec(memory_space=pl.ANY)
WIDE, THIN = ((SLOTS, D), F32), ((SLOTS, D), BF16)
FULL = ((SLOTS, FF), BF16)
KEPT, SENT = ((8, SPAN, ROW), BF16), ((4, SPAN, ROW), BF16)

FORWARD_OUT = {
    "out": (VM, THIN),
    "gains": (VM, ((8, ROW), F32)),
    "small": (VM, ((SMALL, ROW), F32)),
    "high_kept": (ANY, KEPT),
    "high_near": (ANY, SENT),
    "high_far": (ANY, SENT),
    "low_kept": (ANY, KEPT),
    "low_near": (ANY, SENT),
    "low_far": (ANY, SENT),
    "keep_ffa_in": (ANY, ((D, FF), BF16)),
    "keep_ffa_out": (ANY, ((FF, D), BF16)),
    "keep_qkv": (ANY, ((D, 3 * D), BF16)),
    "keep_att": (ANY, ((D, D), BF16)),
    "keep_nrm": (ANY, THIN),
    "keep_act": (ANY, FULL),
    "keep_slope": (ANY, FULL),
    "keep_x1": (ANY, WIDE),
    "keep_nrm_t": (ANY, THIN),
    "keep_heads": (ANY, ((KEYS, 3 * D), BF16)),
    "keep_probs": (ANY, ((H, SLOTS, KEYS), BF16)),
    "keep_ctx": (ANY, THIN),
    "keep_djoin": (ANY, ((SLOTS, 2 * D), BF16)),
    "keep_dx": (ANY, WIDE),
}
FORWARD_SCRATCH = {
    "w": ((32 * ROW, ROW), BF16),
    "w_ffa_in": ((D, FF), BF16),
    "w_qkv": ((D, 3 * D), BF16),
    "w_cg": ((D, CG), BF16),
    "w_ffb_in": ((D, FF), BF16),
    "stage": ((4, 6 * ROW, 128), F32),
    "left_t": ((ROW, SLOTS), BF16),
    "tiles": ((4, SMALL, 128), F32),
    "tgrad": ((4, SMALL, 128), F32),
    "bias": ((H, ROW), F32),
    "nrm": THIN,
    "act": FULL,
    "slope": FULL,
    "nrm_t": THIN,
    "qkv": ((KEYS, 3 * D), BF16),
    "probs": ((H, SLOTS, KEYS), BF16),
    "ctx": THIN,
    "nrm_c": THIN,
    "hid": ((SLOTS, 256), F32),
    "ug": ((SLOTS, CG), F32),
    "slope_c": ((SLOTS, CG), BF16),
    "gmean": ((SLOTS, 128), F32),
    "gscale": ((SLOTS, 128), F32),
    "gate_sums": ((8 * GATE // 128, 128), F32),
    "gpad": ((PADDED, GATE), F32),
    "cv": ((SLOTS, GATE), BF16),
    "gated": ((SLOTS, GATE), BF16),
    "cat": ((SLOTS, 2 * D), F32),
    "mpad": ((PADDED, 2 * D), F32),
    "mixed": ((SLOTS, 2 * D), BF16),
    "nrm_b": THIN,
    "act_b": FULL,
    "slope_b": FULL,
    "dpad": ((PADDED, GATE), F32),
    "djoin": ((SLOTS, 2 * D), BF16),
    "dgate": ((SLOTS, GATE), F32),
    "dhid": ((SLOTS, CG), BF16),
    "dnrm": WIDE,
    "dout": THIN,
    "dx": WIDE,
    "x1": WIDE,
    "x2": WIDE,
    "x3": WIDE,
    "seams": ((PARTS + 1, 2, TILE, ROW), BF16),
    "load_sems": PARTS,
    "keep_sems": 16,
    "emit_sems": 40,
}
BACKWARD_IN = (
    "ffa_in", "ffa_out", "qkv", "att", "nrm", "act", "slope", "x1", "nrm_t", "heads", "probs", "ctx", "djoin", "dx",
)
PASSED = ("low_kept", "low_near", "low_far")
BACKWARD_OUT = {
    "fgrad": (VM, THIN),
    "late": (VM, ((16, ROW), F32)),
    "low_kept": (ANY, KEPT),
    "low_near": (ANY, SENT),
    "low_far": (ANY, SENT),
}
BACKWARD_SCRATCH = {
    "w_ffa_in": ((D, FF), BF16),
    "w_ffa_out": ((FF, D), BF16),
    "w_qkv": ((D, 3 * D), BF16),
    "w_att": ((D, D), BF16),
    "g_ffa_in": ((FF, D), BF16),
    "g_qkv": ((3 * D, D), BF16),
    "stage": ((4, 4 * ROW, 128), F32),
    "left_t": ((ROW, SLOTS), BF16),
    "sums": ((H, ROW), F32),
    "nrm": THIN,
    "act": FULL,
    "slope": FULL,
    "nrm_t": THIN,
    "qkv": ((KEYS, 3 * D), BF16),
    "probs": ((H, SLOTS, KEYS), BF16),
    "ctx": THIN,
    "datt": THIN,
    "dctx": THIN,
    "dhid": FULL,
    "dnrm": WIDE,
    "dout": THIN,
    "dx": WIDE,
    "x1": WIDE,
    "load_sems": 14,
    "emit_sems": 24,
}


def call(kernel, name, ins, outs, scratch, limit, aliases=None):
    return pl.pallas_call(
        kernel,
        name=name,
        in_specs=[space for space, _ in ins],
        out_specs=[space for space, _ in outs],
        out_shape=[jax.ShapeDtypeStruct(*kind) for _, kind in outs],
        scratch_shapes=[
            pltpu.SemaphoreType.DMA((each_one,)) if isinstance(each_one, int) else pltpu.VMEM(*each_one)
            for each_one in scratch
        ],
        input_output_aliases=aliases or {},
        compiler_params=pltpu.CompilerParams(vmem_limit_bytes=limit * 2**20),
    )(*[array for _, array in ins])


def forward(coords, length, frames, cot, blocks):
    def kernel(*refs):
        forward_kernel([*FORWARD_OUT, *FORWARD_SCRATCH], *refs)

    outs = call(
        kernel,
        "forward",
        [(SM, coords), (SM, length), (VM, frames), (VM, cot)] + [(ANY, block) for block in blocks],
        list(FORWARD_OUT.values()),
        list(FORWARD_SCRATCH.values()),
        58,
    )
    return dict(zip(FORWARD_OUT, outs))


def backward(coords, frames, state):
    def kernel(*refs):
        names = ["in_" + name for name in BACKWARD_IN + PASSED]
        backward_kernel([*names, *BACKWARD_OUT, *BACKWARD_SCRATCH], *refs)

    ins = [(SM, coords), (VM, frames), (VM, state["gains"]), (VM, state["small"])]
    ins += [(ANY, state["keep_" + name]) for name in BACKWARD_IN]
    ins += [(ANY, state[name]) for name in PASSED]
    outs = call(
        kernel,
        "backward",
        ins,
        list(BACKWARD_OUT.values()),
        list(BACKWARD_SCRATCH.values()),
        58,
        {len(ins) - 3 + at: 2 + at for at in range(3)},
    )
    return dict(zip(BACKWARD_OUT, outs))


def segment_bounds():
    bounds = [0]
    for extent in segment_shapes():
        bounds.append(bounds[-1] + math.prod(extent))
    return bounds


def fast_mesh():
    return lax.axis_size("dp") == 4 and lax.axis_size("fsdp") == 8


def over_x(value):
    return lax.ppermute(value, "fsdp", [(i, i ^ 1) for i in range(8)])


def over_y(value):
    return lax.ppermute(value, "dp", [(i, i ^ 2) for i in range(4)])


def over_core(value):
    return lax.ppermute(value, "dp", [(i, i ^ 1) for i in range(4)])


def round_z(value):
    return lax.ppermute(value, "fsdp", [(i, (i + 2) % 8) for i in range(8)])


def over_z(value, step):
    return lax.ppermute(value, "fsdp", [(i, i ^ (2 * step)) for i in range(8)])


def after(value, *others):
    return lax.optimization_barrier((value, *others))[0]


def shard_offset(me, shard_size):
    return me * shard_size - start_of(me) * ROW


def gather_shards(shard, me):
    shard_size = shard.shape[0]
    if not fast_mesh():
        whole = lax.all_gather(shard, AXES, axis=0, tiled=True)
        whole = jnp.pad(whole, (0, (STARTS[-1] + SPAN) * ROW - whole.shape[0])).reshape(-1, ROW)
        spans = [whole[start : start + SPAN] for start in STARTS[:-1]]
        spans = spans[:1] + [jnp.concatenate([jnp.zeros((TILE, ROW), BF16), span[TILE:]]) for span in spans[1:]]
        return [
            jnp.concatenate([spans[source_part((0, 0, 0, 0), piece)][piece[4] : piece[5]] for piece in pieces])
            for pieces in LAYOUT
        ]
    most = TILE * ROW
    padded = jnp.pad(shard, (most, SPAN * ROW - shard_size))
    span = lax.dynamic_slice(padded, (most - shard_offset(me, shard_size),), (SPAN * ROW,)).reshape(SPAN, ROW)
    own, by_x, by_y = [span], [], []
    for back in range(4):
        if back < 3:
            own.append(round_z(own[back]))
        if back < 2:
            by_x.append(over_x(own[back]))
            by_y.append(over_y(own[back]))
            own[back + 1], by_x[back], by_y[back] = lax.optimization_barrier((own[back + 1], by_x[back], by_y[back]))
        else:
            by_x.append(over_x(jnp.concatenate([own[back], by_y[back - 2][:HALF]])))
            by_y.append(over_y(jnp.concatenate([own[back], by_x[back - 2][HALF:SPAN]])))
    by_x.append(over_x(by_y[2][:HALF]))
    by_y.append(over_y(by_x[2][HALF:SPAN]))
    last_x, last_y = by_y[3][:HALF], by_x[3][HALF:SPAN]
    by_x.append(over_x(after(last_x, by_x[4])))
    by_y.append(over_y(after(last_y, by_y[4])))
    late_ones = (by_x[3], by_y[3])
    far_own = [over_core(each_one) for each_one in own[:2]] + [over_core(after(each_one, *late_ones)) for each_one in own[2:]]
    far = [far_own]
    for way in (by_x, by_y):
        far.append([over_core(way[0])] + [over_core(after(way[at], *late_ones)) for at in (1, 2)])
        far[-1] += [over_core(way[at]) for at in (3, 4, 5)]
    return own + by_x + by_y + far[0] + far[1] + far[2]


def added(*parts):
    total = parts[0].astype(F32)
    for each_one in parts[1:]:
        total = total + each_one.astype(F32)
    return total


SIDES = (slice(0, HALF), slice(HALF, SPAN))


def span_sums(coords, own_half, x, places, low_kept, low_got, high_kept, high_got, sides=None):
    count = len(places)
    pieces = [(at, rows) for at in range(count) for rows in sides or ()]

    def kernel(coords, low_kept, low_got, high_kept, high_got, *refs):
        outs, (kept, got, total, sems, out_sems) = refs[:-5], refs[-5:]
        high = coords[0] == int(own_half)
        for source, other, wanted in ((low_kept, low_got, jnp.logical_not(high)), (high_kept, high_got, high)):

            @pl.when(wanted)
            def _(source=source, other=other):
                for at, place in enumerate(places):
                    pltpu.make_async_copy(source.at[4 * x + place], kept.at[at], sems.at[2 * at]).start()
                    pltpu.make_async_copy(other.at[place], got.at[at], sems.at[2 * at + 1]).start()

        copies = []
        for at in range(count):
            pltpu.make_async_copy(low_kept.at[at], kept.at[at], sems.at[2 * at]).wait()
            pltpu.make_async_copy(low_got.at[at], got.at[at], sems.at[2 * at + 1]).wait()

            def add(k, at=at):
                rows = part(k, SPAN // 11)
                total[at, rows] = low(kept[at, rows].astype(F32) + got[at, rows].astype(F32))

            each_loop(11, add)
            if sides is None:
                copies.append(pltpu.make_async_copy(total.at[at], outs[0].at[at], out_sems.at[at]))
                copies[-1].start()
            for which, (mine, rows) in enumerate(pieces):
                if mine == at:
                    copies.append(pltpu.make_async_copy(total.at[at, rows], outs[which], out_sems.at[which]))
                    copies[-1].start()
        for copy in copies:
            copy.wait()

    spans = ((count, SPAN, ROW), BF16)
    arrays = [(ANY, each_one) for each_one in (low_kept, low_got, high_kept, high_got)]
    outs = [(ANY, ((rows.stop - rows.start, ROW), BF16)) for _, rows in pieces] or [(ANY, spans)]
    sums = call(
        kernel, "span_sums", [(SM, coords)] + arrays, outs, [spans] * 3 + [2 * count, max(count, len(pieces))], 40
    )
    return sums[0] if sides is None else [sums[len(sides) * at : len(sides) * (at + 1)] for at in range(count)]


def late_rows(late, above, below):
    gains = jnp.pad(late[0:8], ((above, below - 8), (0, 0)))
    return gains + jnp.pad(late[8:10], ((above + REL_AT, below - REL_AT - 2), (0, 0)))


def scatter_slow(state, back, shard_size, padded):
    late = back["late"]
    pieces = []
    for source, half in ((back, "low"), (state, "high")):
        for core in range(2):
            for at in range(8):
                z, x = at // 2, at % 2
                if core == 0:
                    span = source[half + "_kept"][4 * x + 3 - z]
                else:
                    span = source[half + ("_near", "_far")[x]][3 - z]
                d = len(pieces)
                pieces.append(span[: STARTS[d + 1] - STARTS[d] if d < PARTS - 1 else SPAN])
    rows = jnp.concatenate(pieces)
    first = ROW * BLOCK["small"][0]
    rows = low(rows.astype(F32) + late_rows(late, first, rows.shape[0] - first))
    flat = rows.reshape(-1)[: segment_bounds()[-1]]
    shard = lax.psum_scatter(flat, AXES, scatter_dimension=0, tiled=True)
    return jnp.pad(shard, (0, padded - shard_size)).astype(F32), lax.psum(late[0:8], AXES)


def scatter_grads(state, back, coords, me, shard_size, padded):
    if not fast_mesh():
        return scatter_slow(state, back, shard_size, padded)
    high = coords[0] == 1
    high_kept, low_kept = state["high_kept"], back["low_kept"]
    high_got = [over_core(state["high_near"]), over_core(state["high_far"])]
    low_far = over_core(back["low_far"])

    def chip_sum(own_half, x, places, sides=None):
        got = (low_far if x else low_near, high_got[x])
        return span_sums(coords, own_half, x, places, low_kept, got[0], high_kept, got[1], sides)

    late = back["late"]
    late = late + over_x(late)
    late = late + over_y(late)
    for_x, for_y = chip_sum(False, 1, (2, 3)), chip_sum(False, 1, (0, 1))
    for_x, for_y, late = lax.optimization_barrier((for_x, for_y, late))
    from_x, from_y = over_x(for_x), over_y(for_y)
    low_near = over_core(after(back["low_near"], for_x, for_y))
    late = late + over_core(late)
    late = late + over_z(late, 1)
    late = late + over_z(late, 2)
    to_x, to_y, mine = [
        chip_sum(own_half, x, range(4), SIDES) for own_half, x in ((True, 1), (False, 0), (True, 0))
    ]
    from_x, from_y, to_x, to_y, mine, late = lax.optimization_barrier((from_x, from_y, to_x, to_y, mine, late))
    running = [None, None]
    before = [(), ()]
    for at in range(4):
        for side, rows in enumerate(SIDES):
            send_x, send_y = to_x[at][side], to_y[at][side]
            if at < 2:
                send_x = low(added(send_x, from_y[at, rows]))
            else:
                send_y = low(added(send_y, from_x[at - 2, rows]))
            got_x, got_y = over_x(after(send_x, *before[side])), over_y(after(send_y, *before[side]))
            before[side] = (got_x, got_y)
            parts = [mine[at][side], got_x, got_y]
            if at:
                parts.append(round_z(running[side]))
            running[side] = added(*parts)
            if at < 3:
                running[side] = low(running[side])
    total = jnp.concatenate(running)
    first = ROW * BLOCK["small"][0] - STARTS[PARTS - 1]
    total = total + jnp.where(me == PARTS - 1, 1.0, 0.0) * late_rows(late, first, SPAN - first)
    flat = jnp.pad(total.reshape(-1), (0, max(0, TILE * ROW + padded - SPAN * ROW)))
    return lax.dynamic_slice(flat, (shard_offset(me, shard_size),), (padded,)), late[0:8]


def sum_everywhere(vector):
    if not fast_mesh():
        return lax.psum(vector, AXES)
    vector = vector + over_core(vector)
    vector = vector + over_x(vector)
    vector = vector + over_y(vector)
    vector = vector + over_z(vector, 1)
    return vector + over_z(vector, 2)


def most_segments(shard_size, devices):
    bounds = segment_bounds()
    most = 1
    for at in range(devices):
        low_end, high_end = at * shard_size, (at + 1) * shard_size
        most = max(most, sum(1 for b in bounds[1:-1] if low_end < b < high_end) + 1)
    return most


LANES = 128
CHUNK = 1024 * LANES
STRIP = 128 * LANES


def chunk_spans(segments, step):
    first, last = step * CHUNK, (step + 1) * CHUNK
    for at in range(segments.shape[0] - 2):
        start, end = segments[1 + at], segments[2 + at]
        whole = (start <= first) & (last <= end)
        some = (start < last) & (end > first) & jnp.logical_not(whole)
        yield at, whole, some, start - first, end - first


def strips(body, start=None):
    return lax.fori_loop(0, CHUNK // STRIP, lambda at, carry: body(part(at, STRIP), at * STRIP, carry), start)


def square(entries, strip):
    return entries[strip].reshape(STRIP // LANES, LANES)


def inside(place, start, end):
    row = lax.broadcasted_iota(jnp.int32, (STRIP // LANES, LANES), 0)
    place = place + row * LANES + lax.broadcasted_iota(jnp.int32, (STRIP // LANES, LANES), 1)
    return (place >= start) & (place < end)


def fold(values):
    return jnp.sum(values.reshape(-1, 8, LANES), axis=0)


def update_kernel(segments, params, first, second, grad, new_first, new_second, update, sums):
    step = pl.program_id(0)
    nothing = jnp.zeros((8, LANES), F32)

    @pl.when(step == 0)
    def _():
        sums[...] = nothing

    def move(strip, place, totals):
        grads = grad[strip]
        firsts = BETA_FIRST * first[strip] + (1.0 - BETA_FIRST) * grads
        seconds = BETA_SECOND * second[strip] + (1.0 - BETA_SECOND) * grads * grads
        new_first[strip] = firsts
        new_second[strip] = seconds
        first_hat = firsts * (1.0 / (1.0 - BETA_FIRST**STEP))
        second_hat = seconds * (1.0 / (1.0 - BETA_SECOND**STEP))
        weights = params[strip]
        change = first_hat / (jnp.sqrt(second_hat) + ADAM_EPS) + WEIGHT_DECAY * weights
        update[strip] = change
        squares = [(each_one * each_one).reshape(STRIP // LANES, LANES) for each_one in (weights, change)]
        return totals[0] + fold(squares[0]), totals[1] + fold(squares[1])

    totals = strips(move, (nothing, nothing))
    lane = lax.broadcasted_iota(jnp.int32, (1, LANES), 1)

    def add(at, totals):
        for row, total in enumerate(totals):
            total = jnp.sum(jnp.sum(total, axis=0, keepdims=True), axis=1, keepdims=True)
            sums[row : row + 1, :] += jnp.where(lane == segments[0] + at, total, 0.0)

    for at, whole, some, start, end in chunk_spans(segments, step):

        @pl.when(whole)
        def _(at=at):
            add(at, totals)

        @pl.when(some)
        def _(at=at, start=start, end=end):
            def squares(strip, place, totals):
                here = inside(place, start, end)
                own = [square(entries, strip) for entries in (params, update)]
                own = [fold(jnp.where(here, each_one * each_one, 0.0)) for each_one in own]
                return totals[0] + own[0], totals[1] + own[1]

            add(at, strips(squares, (nothing, nothing)))


def apply_kernel(segments, sums, params, update, new_params, norms):
    step = pl.program_id(0)
    roots = jnp.sqrt(sums[0:2, :])
    trust = roots[0:1, :] / (roots[1:2, :] + ADAM_EPS)
    norms[0:2, :] = roots
    norms[2:3, :] = trust
    norms[3:8, :] = jnp.zeros((5, LANES), F32)
    lane = lax.broadcasted_iota(jnp.int32, (1, LANES), 1)
    for at, whole, some, start, end in chunk_spans(segments, step):

        scale = LEARN_RATE * jnp.sum(jnp.where(lane == segments[0] + at, trust, 0.0), axis=1, keepdims=True)
        scale = jnp.broadcast_to(scale, (1, LANES))

        def moved(strip, scale=scale):
            return square(params, strip) - scale * square(update, strip)

        @pl.when(whole)
        def _(moved=moved):
            def all_of(strip, place, carry):
                new_params[strip] = moved(strip).reshape(STRIP)
                return carry

            strips(all_of, 0)

        @pl.when(some)
        def _(moved=moved, start=start, end=end):
            def part_of(strip, place, carry):
                chosen = jnp.where(inside(place, start, end), moved(strip), square(new_params, strip))
                new_params[strip] = chosen.reshape(STRIP)
                return carry

            strips(part_of, 0)


def shards(frames, lengths, cotangent, params, first_moment, second_moment):
    shard_size = params.shape[0]
    devices = lax.axis_size("dp") * lax.axis_size("fsdp")
    me = lax.axis_index(AXES)
    if fast_mesh():
        dp, fsdp = lax.axis_index("dp"), lax.axis_index("fsdp")
        coords = jnp.stack([dp // 2, dp % 2, fsdp // 2, fsdp % 2]).astype(jnp.int32)
    else:
        coords = jnp.zeros((4,), jnp.int32)
    state = forward(coords, lengths, frames[0], cotangent[0], gather_shards(low(params), me))
    back = backward(coords, frames[0], state)
    steps = -(-shard_size // CHUNK)
    size = max(shard_size, CHUNK)
    grad_shard, gain_grads = scatter_grads(state, back, coords, me, shard_size, size)

    def filled(flat):
        return jnp.pad(flat, (0, size - shard_size)) if size > shard_size else flat

    bounds = segment_bounds()
    spans = most_segments(shard_size, devices)
    shard_low = me * shard_size
    first_segment = sum((shard_low >= b).astype(jnp.int32) for b in bounds[1:-1])
    table = jnp.asarray(bounds[1:] + [bounds[-1]] * spans, jnp.int32)
    ends = jnp.clip(lax.dynamic_slice(table, (first_segment,), (spans,)) - shard_low, 0, shard_size)
    segments = jnp.concatenate([first_segment[None], jnp.zeros((1,), jnp.int32), ends]).astype(jnp.int32)
    grid = pl.BlockSpec((CHUNK,), lambda step: (step,))
    whole = pl.BlockSpec((8, LANES), lambda step: (0, 0))
    flat_kind = jax.ShapeDtypeStruct((size,), F32)
    tile_kind = jax.ShapeDtypeStruct((8, LANES), F32)
    weights = filled(params)
    new_first, new_second, update, sums = pl.pallas_call(
        update_kernel,
        name="update",
        grid=(steps,),
        in_specs=[SM] + [grid] * 4,
        out_specs=[grid] * 3 + [whole],
        out_shape=[flat_kind] * 3 + [tile_kind],
    )(segments, weights, filled(first_moment), filled(second_moment), grad_shard)
    sums = sum_everywhere(sums)
    new_params, norms = pl.pallas_call(
        apply_kernel,
        name="apply",
        grid=(steps,),
        in_specs=[SM, whole, grid, grid],
        out_specs=[grid, whole],
        out_shape=[flat_kind, tile_kind],
    )(segments, sums, weights, update)
    count = len(segment_shapes())
    return (
        state["out"].reshape(frames.shape),
        back["fgrad"].reshape(frames.shape),
        new_params[:shard_size],
        new_first[:shard_size],
        new_second[:shard_size],
        norms[0, :count],
        norms[1, :count],
        norms[2, :count],
        gain_grads.reshape(-1),
    )


def solution(mesh):
    placed = (
        P(("dp", "fsdp"), None, None),
        P(("dp", "fsdp")),
        P(("dp", "fsdp"), None, None),
        P(("dp", "fsdp")),
        P(("dp", "fsdp")),
        P(("dp", "fsdp")),
    )
    return jax.shard_map(
        shards,
        mesh=mesh,
        in_specs=placed,
        out_specs=(
            P(("dp", "fsdp"), None, None),
            P(("dp", "fsdp"), None, None),
            P(("dp", "fsdp")),
            P(("dp", "fsdp")),
            P(("dp", "fsdp")),
            P(),
            P(),
            P(),
            P(),
        ),
        check_vma=False,
    )
```

```python
import math
from types import SimpleNamespace

import jax
import jax.numpy as jnp
from jax import lax
from jax.experimental import pallas as pl
from jax.experimental.pallas import tpu as pltpu
from jax.sharding import PartitionSpec as P

STEP = 8
BETA_FIRST = 0.5
BETA_SECOND = 0.5
LEARN_RATE = 0.5
WEIGHT_DECAY = 0.01
ADAM_EPS = 1e-06
AXES = ("dp", "fsdp")


def segment_shapes():
    gate_width = CG // 2
    return [
        (D, FF),
        (FF, D),
        (D, 3 * D),
        (D, D),
        (D, CG),
        (gate_width, D),
        (2 * D, D),
        (D, FF),
        (FF, D),
        (5 * D + gate_width,),
        (KER, gate_width + 2 * D),
        (RELW, H),
    ]


D = 512
H = 8
HS = 64
FF = 2048
CG = 3072
KER = 31
RELW = 128
NORM_EPS = 1e-05
MASK_FILL = -1000000000.0
ROW = 512
HALF = ROW // 2
SLOTS = 160
KEYS = 256
PAD = 16
PADDED = SLOTS + 2 * PAD
GATE = CG // 2
BLOCK = {
    "ffa_in": (0, 4),
    "ffa_out": (4, 4),
    "qkv": (8, 3),
    "att_out": (11, 1),
    "cg_in": (12, 6),
    "cg_out": (18, 3),
    "merge": (21, 2),
    "ffb_in": (23, 4),
    "ffb_out": (27, 4),
    "small": (31, 1),
}
TAPS_AT = 8
REL_AT = 8 + 5 * KER
SMALL = 176
F32, BF16 = jnp.float32, jnp.bfloat16


def dot(left, right):
    return lax.dot_general(left, right, (((1,), (0,)), ((), ())), preferred_element_type=F32)


def dot_t(left, right):
    return lax.dot_general(left, right, (((1,), (1,)), ((), ())), preferred_element_type=F32)


def t_dot(left, right):
    return lax.dot_general(left, right, (((0,), (0,)), ((), ())), preferred_element_type=F32)


def low(values):
    return values.astype(BF16)


def each(count, body):
    for at in range(count):
        body(at)


def each_loop(count, body, together=1):
    def step(at, carry):
        for inner in range(together):
            body(at * together + inner)
        return carry

    lax.fori_loop(0, count // together, step, 0)


def part(at, size):
    if isinstance(at, int):
        return slice(at * size, at * size + size)
    return pl.ds(pl.multiple_of(at * size, size), size)


def rows_of(name):
    first, count = BLOCK[name]
    return slice(ROW * first, ROW * (first + count))


def lane_mean(values, width):
    return jnp.sum(values, axis=-1, keepdims=True) * (1.0 / width)


def normed(values):
    centered = values - lane_mean(values, values.shape[-1])
    scale = lax.rsqrt(lane_mean(centered * centered, values.shape[-1]) + NORM_EPS)
    return centered * scale, scale


def valid_rows(length):
    return (lax.broadcasted_iota(jnp.int32, (SLOTS, 1), 0) < length).astype(F32)


def fold_rows(values):
    return jnp.sum(values, axis=0, keepdims=True)


def norm_rows(source, gain, target):
    for k in range(2):
        hat, _ = normed(source[part(k, 80), :].astype(F32))
        target[part(k, 80), :] = low(hat * gain)


def norm_rows_back(values, gain, grad, add):
    total = jnp.zeros((1, values.shape[1]), F32)
    for k in range(2):
        rows = part(k, 80)
        hat, scale = normed(values[rows, :].astype(F32))
        mine = grad[rows, :]
        total = total + fold_rows(mine * hat)
        inner = mine * gain
        width = values.shape[1]
        moved = lane_mean(inner, width) + hat * lane_mean(inner * hat, width)
        add(rows, scale * (inner - moved))
    return total


TOTAL_ROWS = 16037
PARTS = 32
TILE = 16
SPAN = 528
STARTS = [TILE * (TOTAL_ROWS * d // (PARTS * TILE)) for d in range(PARTS + 1)]
FIRST_PARTS = max(d for d in range(PARTS) if STARTS[d] < ROW * sum(BLOCK["ffa_out"]))
SHORTEST = min(high - first for first, high in zip(STARTS, STARTS[1:]))


def start_of(d):
    return ((TOTAL_ROWS * d) >> 9) * TILE


def gathered_layout():
    layout = []
    for core in range(2):
        layout += [[(core, 0, 0, back, 0, SPAN, 0)] for back in range(4)]
        for y, x, first, last in ((0, 1, 0, HALF), (1, 0, HALF, SPAN)):
            whole = [(core, y, x, back, 0, SPAN, 0) for back in range(4)]
            diagonal = [(core, 1, 1, back, first, last) for back in range(4)]
            layout += [[whole[0]], [whole[1]]]
            layout += [[whole[2], (*diagonal[0], SPAN)], [whole[3], (*diagonal[1], SPAN)]]
            layout += [[(*diagonal[2], 0)], [(*diagonal[3], 0)]]
    return layout


LAYOUT = gathered_layout()


def source_part(coords, piece):
    y, c, z, x = coords[0], coords[1], coords[2], coords[3]
    yy, cc, xx, zz = y ^ piece[1], c ^ piece[0], x ^ piece[2], (z + 4 - piece[3]) & 3
    return ((yy * 2 + cc) * 4 + zz) * 2 + xx


class Loads:
    def __init__(self, coords, sources, target, seams, sems):
        self.target, self.seams, self.sems = target, seams, sems
        self.here, self.joined = set(), set()
        seams[0, 0] = jnp.zeros((TILE, ROW), BF16)
        seams[PARTS, 1] = jnp.zeros((TILE, ROW), BF16)

        for soon in (True, False):
            for pieces, source in zip(LAYOUT, sources):
                for piece in pieces:
                    d = source_part(coords, piece)
                    first_ones = (d <= FIRST_PARTS) | (d == PARTS - 1)

                    @pl.when(first_ones if soon else jnp.logical_not(first_ones))
                    def _(piece=piece, source=source, d=d):
                        self.start(piece, source, d)

    def start(self, piece, source, d):
        def rows(at, size):
            return pl.ds(pl.multiple_of(at, TILE), size)

        first, last, offset = piece[4:]
        offset = offset - first
        start = start_of(d)
        length = start_of(d + 1) - start
        inner, outer = max(first, TILE), min(last, SHORTEST)
        sem = self.sems.at[d]
        pltpu.make_async_copy(
            source.at[offset + inner : offset + outer], self.target.at[rows(start + inner, outer - inner)], sem
        ).start()
        if first == 0:
            pltpu.make_async_copy(source.at[offset : offset + TILE], self.seams.at[d, 1], sem).start()
        if last == SPAN:

            @pl.when(length > SHORTEST)
            def _():
                pltpu.make_async_copy(
                    source.at[offset + SHORTEST : offset + SHORTEST + TILE],
                    self.target.at[rows(start + SHORTEST, TILE)],
                    sem,
                ).start()

            pltpu.make_async_copy(source.at[rows(offset + length, TILE)], self.seams.at[d + 1, 0], sem).start()

    def wait_part(self, d):
        if d in self.here or not 0 <= d < PARTS:
            return
        self.here.add(d)
        size = STARTS[d + 1] - STARTS[d] + TILE
        pltpu.make_async_copy(self.target.at[0:size], self.target.at[0:size], self.sems.at[d]).wait()

    def wait(self, name):
        rows = rows_of(name)
        last = min(rows.stop, STARTS[-1] + TILE)
        for d in range(PARTS + 1):
            if STARTS[d] < last and STARTS[d] + TILE > rows.start and d not in self.joined:
                self.wait_part(d - 1)
                self.wait_part(d)
                self.joined.add(d)
                self.target[STARTS[d] : STARTS[d] + TILE, :] = self.seams[d, 0] + self.seams[d, 1]
            if d < PARTS and STARTS[d] + TILE < last and STARTS[d + 1] > rows.start:
                self.wait_part(d)


class Emits:
    def __init__(self, coords, halves, sems):
        self.coords, self.halves, self.sems = coords, halves, sems
        self.pending = []

    def put(self, d, values, rows):
        core, z, x = (d // 8) % 2, (d // 2) % 4, d % 2
        kept, sent = self.halves[d // 16]
        far_x = self.coords[3] ^ x
        place = (self.coords[2] + 3 - z) & 3
        sem = self.sems.at[len(self.pending)]

        @pl.when(self.coords[1] == core)
        def _():
            pltpu.make_async_copy(values, kept.at[4 * far_x + place, rows], sem).start()

        @pl.when((self.coords[1] != core) & (far_x == 0))
        def _():
            pltpu.make_async_copy(values, sent[0].at[place, rows], sem).start()

        @pl.when((self.coords[1] != core) & (far_x == 1))
        def _():
            pltpu.make_async_copy(values, sent[1].at[place, rows], sem).start()

        self.pending.append(pltpu.make_async_copy(values, kept.at[0, rows], sem))

    def put_tensor(self, name, values):
        rows = rows_of(name)
        for d in range(PARTS):
            first, last = max(rows.start, STARTS[d]), min(rows.stop, STARTS[d] + SPAN)
            if first < last:
                self.put(d, values.at[first - rows.start : last - rows.start], slice(first - STARTS[d], last - STARTS[d]))

    def wait(self):
        for copy in self.pending:
            copy.wait()


def split_columns(raw, target, wide, stage):
    def chunk(k):
        rows = part(k, 128 * wide)
        for lane in range(4):
            stage[lane, 0 : 128 * wide, :] = raw[rows, lane * 128 : lane * 128 + 128].astype(F32)
        for c in range(wide):
            for lane in range(4):
                place = ROW * c + lane * 128
                target[part(k, 128), place : place + 128] = low(stage[lane, pl.ds(c, 128, stride=wide), :])

    each_loop(4, chunk)


def weight_columns(left, grads, wide, stage, left_t, target):
    left_t[...] = left[...].T

    def chunk(j):
        value = dot(left_t[...], grads[:, part(j, 256)])
        c, pair = j // 2, (j % 2) * 2
        for half in range(2):
            stage[pair + half, pl.ds(c, ROW, stride=wide), :] = value[:, 128 * half : 128 * half + 128]

    each(2 * wide, chunk)

    def lower(k):
        rows = part(k, ROW)
        for lane in range(4):
            target[rows, lane * 128 : lane * 128 + 128] = low(stage[lane, rows, :])

    each(wide, lower)


def weight_rows(left, grads, count, left_t, target):
    def chunk(k):
        left_t[...] = left[:, part(k, ROW)].T
        for at in range(2):
            target[part(k, ROW), 256 * at : 256 * at + 256] = low(dot(left_t[...], grads[:, 256 * at : 256 * at + 256]))

    each(count, chunk)


def feed_forward(inputs, gain, w_in, w_out, nrm, act, slope, result):
    norm_rows(inputs, gain, nrm)

    def up(j):
        at = part(j, 256)
        hidden = dot(nrm[...], w_in[:, at])
        sig = jax.nn.sigmoid(hidden)
        active = hidden * sig
        act[:, at] = low(active)
        slope[:, at] = low(sig + active * (1.0 - sig))

    each(FF // 256, up)

    def down(j):
        at = part(j, 256)
        result[:, at] = inputs[:, at].astype(F32) + 0.5 * dot(act[...], w_out[:, at])

    each(2, down)


def feed_back(dout, w_in, w_out, nrm, act, slope, dhid, dnrm, stage, left_t, g_in, g_out, emits, name):
    def up(j):
        at = part(j, 256)
        grad = dot_t(dout[...], w_out[at, :])
        dhid[:, at] = low(grad * slope[:, at].astype(F32))

    each(FF // 256, up)
    weight_rows(act, dout, 4, left_t, g_out)
    emits.put_tensor(name + "_out", g_out)

    def down(j):
        at = part(j, 256)
        dnrm[:, at] = dot_t(dhid[:, 0:FF], w_in[at, :])

    each(2, down)
    weight_columns(nrm, dhid, 4, stage, left_t, g_in)
    emits.put_tensor(name + "_in", g_in)


def bucket_map():
    entry = lax.broadcasted_iota(jnp.int32, (2 * ROW, ROW), 0) // H
    far = lax.broadcasted_iota(jnp.int32, (2 * ROW, ROW), 1)
    far = jnp.where(far >= ROW // 2, far - ROW, far)
    bucket = jnp.clip(far, -(RELW // 2), RELW // 2 - 1) + RELW // 2
    return (entry == bucket).astype(F32)


def own_entries(flat):
    entry = lax.broadcasted_iota(jnp.int32, (H, 2 * ROW), 1)
    head = lax.broadcasted_iota(jnp.int32, (H, 2 * ROW), 0)
    return jnp.where(lax.rem(entry, H) == head, flat, 0.0)


def tap_row(small, tap, row, lane):
    return small[lane, pl.ds(TAPS_AT + 5 * tap + row, 1), :]


def shifted_sum(padded, at, factor):
    total = None
    for low_part in range(8):
        slab = padded[low_part : low_part + SLOTS + 24, at]
        inner = None
        for high_part in range(4):
            offset = 8 * high_part + low_part
            if offset:
                term = factor(offset) * slab[8 * high_part : 8 * high_part + SLOTS]
                inner = term if inner is None else inner + term
        total = inner if total is None else total + inner
    return total


def convolve(padded, small, first_row, width, finish):

    def chunk(j):
        at = part(j, 128)
        row, lane = first_row + j // 4, j % 4
        finish(j, at, shifted_sum(padded, at, lambda offset: tap_row(small, offset - 1, row, lane)))

    each_loop(width // 128, chunk)


def convolve_back(grads, padded, small, first_row, width, sgrad, finish):

    def chunk(j):
        at = part(j, 128)
        row, lane = first_row + j // 4, j % 4
        finish(j, at, shifted_sum(grads, at, lambda offset: tap_row(small, KER - offset, row, lane)))
        own = grads[PAD : PAD + SLOTS, at]
        for low_part in range(8):
            slab = padded[low_part : low_part + SLOTS + 24, at]
            for high_part in range(4):
                offset = 8 * high_part + low_part
                if offset:
                    tile = slab[8 * high_part : 8 * high_part + SLOTS]
                    sgrad[lane, pl.ds(TAPS_AT + 5 * (offset - 1) + row, 1), :] = fold_rows(own * tile)

    each_loop(width // 128, chunk)


def clear_margins(padded):
    padded[0:PAD, :] = jnp.zeros((PAD, padded.shape[1]), F32)
    padded[PAD + SLOTS : PADDED, :] = jnp.zeros((PAD, padded.shape[1]), F32)


def gelu_parts(hidden):
    bell = jnp.exp(-0.5 * hidden * hidden)
    spread = 1.0 + (0.3275911 * 2.0**-0.5) * jnp.abs(hidden)
    near = pl.reciprocal(spread, approx=True)
    near = near * (2.0 - spread * near)
    tail = jnp.full_like(near, 0.5 * 1.061405429)
    for factor in (-1.453152027, 1.421413741, -0.284496736, 0.254829592):
        tail = tail * near + 0.5 * factor
    tail = tail * near * bell
    below = jnp.where(hidden >= 0.0, 1.0 - tail, tail)
    return hidden * below, below + hidden * bell * ((2.0 * math.pi) ** -0.5)


def attention_forward(r, length):
    norm_rows(r.x1, r.small[1:2, :], r.nrm_t)
    r.qkv[SLOTS:KEYS, :] = jnp.zeros((KEYS - SLOTS, 3 * D), BF16)
    flat = jnp.concatenate([r.small[REL_AT : REL_AT + 1, :], r.small[REL_AT + 1 : REL_AT + 2, :]], axis=1)
    r.bias[...] = dot(low(own_entries(jnp.broadcast_to(flat, (H, 2 * ROW)))), low(bucket_map()))

    def project(j):
        at = part(j, 256)
        r.qkv[0:SLOTS, at] = low(dot(r.nrm_t[...], r.w_qkv[:, at]))

    each(3 * D // 256, project)
    valid = lax.broadcasted_iota(jnp.int32, (1, KEYS), 1) < length
    first_half = lax.broadcasted_iota(jnp.int32, (1, 128), 1) < HS

    def heads(pair):
        queries = r.qkv[0:SLOTS, part(pair, 128)]
        keys = r.qkv[:, part(pair + 4, 128)]
        values = r.qkv[:, part(pair + 8, 128)]
        outs = []
        for odd in range(2):
            head = 2 * pair + odd
            half = first_half if odd == 0 else jnp.logical_not(first_half)
            mine = jnp.where(half, queries, jnp.zeros_like(queries))
            spread = jnp.broadcast_to(r.bias[pl.ds(head, 1), :], (SLOTS, ROW))
            spread = pltpu.roll(spread, 0, 1, stride=1, stride_axis=0)[:, 0:KEYS]
            scores = jnp.where(valid, dot_t(mine, keys) * HS ** (-0.5) + spread, MASK_FILL)
            shifted = jnp.exp(scores - jnp.max(scores, axis=-1, keepdims=True))
            chances = low(shifted / jnp.sum(shifted, axis=-1, keepdims=True))
            r.probs[head] = chances
            outs.append(dot(chances, values))
        r.ctx[:, part(pair, 128)] = low(jnp.where(first_half, outs[0], outs[1]))

    each(H // 2, heads)

    def project_out(j):
        at = part(j, 256)
        r.cat[:, at] = dot(r.ctx[...], r.w[rows_of("att_out"), at])

    each(2, project_out)


def gating_forward(r, length):
    norm_rows(r.x1, r.small[2:3, :], r.nrm_c)

    def up(j):
        at = part(j, 256)
        r.hid[...] = dot(r.nrm_c[...], r.w_cg[:, at])
        for k in range(5):
            rows = part(k, 32)
            active, slope = gelu_parts(r.hid[rows, :])
            r.ug[rows, at] = active
            r.slope_c[rows, at] = low(slope)

    each_loop(CG // 256, up, 2)
    tiles = [slice(GATE + 128 * j, GATE + 128 * j + 128) for j in range(GATE // 128)]
    total = jnp.zeros((SLOTS, 128), F32)
    for at in tiles:
        total = total + r.ug[:, at]
    mean = lane_mean(total, GATE)
    total = jnp.zeros((SLOTS, 128), F32)
    for at in tiles:
        centered = r.ug[:, at] - mean
        total = total + centered * centered
    scale = lax.rsqrt(lane_mean(total, GATE) + NORM_EPS)
    r.gmean[...] = jnp.broadcast_to(mean, (SLOTS, 128))
    r.gscale[...] = jnp.broadcast_to(scale, (SLOTS, 128))
    scale = scale * valid_rows(length)
    for j, at in enumerate(tiles):
        gain = r.small[5 + j // 4 : 6 + j // 4, part(j % 4, 128)]
        r.gpad[PAD : PAD + SLOTS, part(j, 128)] = (r.ug[:, at] - mean) * scale * gain

    def finish(j, at, value):
        r.cv[:, at] = low(value)
        r.gated[:, at] = low(r.ug[:, at] * value)

    convolve(r.gpad, r.tiles, 0, GATE, finish)

    def down(j):
        r.cat[:, part(j + 2, 256)] = dot(r.gated[...], r.w[rows_of("cg_out"), part(j, 256)])

    each(2, down)


def merge_forward(r, length):
    valid = valid_rows(length)
    for j in range(8):
        at = part(j, 128)
        r.mpad[PAD : PAD + SLOTS, at] = r.cat[:, at] * valid

    def finish(j, at, value):
        r.mixed[:, at] = low(r.cat[:, at] + value)

    convolve(r.mpad, r.tiles, 3, 2 * D, finish)

    def merge(j):
        at = part(j, 256)
        r.x2[:, at] = r.x1[:, at] + dot(r.mixed[...], r.w[rows_of("merge"), at])

    each(2, merge)


def final_norm(r, length):
    gain = r.small[4:5, :]
    valid = valid_rows(length)
    total = jnp.zeros((1, D), F32)
    for k in range(2):
        rows = part(k, 80)
        hat, scale = normed(r.x3[rows, :])
        r.out[rows, :] = low(hat * gain * valid[80 * k : 80 * k + 80])
        mine = r.cot[rows, :].astype(F32) * valid[80 * k : 80 * k + 80]
        total = total + fold_rows(mine * hat)
        inner = mine * gain
        back = scale * (inner - (lane_mean(inner, D) + hat * lane_mean(inner * hat, D)))
        r.dx[rows, :] = back
        r.dout[rows, :] = low(0.5 * back)
    r.gains[4:5, :] = total


def merge_back(r, length, emits):
    for k in range(2):
        r.dout[part(k, 80), :] = low(r.dx[part(k, 80), :])
    w_merge = r.w.at[rows_of("merge")]

    def merge(j):
        at = part(j, 256)
        r.dpad[PAD : PAD + SLOTS, at] = dot_t(r.dout[...], w_merge[at, :])

    each(2 * D // 256, merge)
    weight_rows(r.mixed, r.dout, 2, r.left_t, w_merge)
    emits.put_tensor("merge", w_merge)

    def finish(j, at, value):
        r.djoin[:, at] = low(r.dpad[PAD : PAD + SLOTS, at] + value * valid_rows(length))

    convolve_back(r.dpad, r.mpad, r.tiles, 3, 2 * D, r.tgrad, finish)


def gating_back(r, length, emits):
    w_co = r.w.at[rows_of("cg_out")]

    def gate(j):
        at = part(j, 256)
        value = dot_t(r.djoin[:, D:], w_co[at, :])
        r.dhid[:, at] = low(value * r.cv[:, at].astype(F32) * r.slope_c[:, at].astype(F32))
        r.dpad[PAD : PAD + SLOTS, at] = value * r.ug[:, at]

    each(GATE // 256, gate)
    r.dout[...] = r.djoin[:, D:]
    weight_rows(r.gated, r.dout, 3, r.left_t, w_co)
    emits.put_tensor("cg_out", w_co)

    def finish(j, at, value):
        r.dgate[:, at] = value * valid_rows(length)

    convolve_back(r.dpad, r.gpad, r.tiles, 0, GATE, r.tgrad, finish)
    tiles = GATE // 128
    for quarter in range(4):
        rows = part(quarter, SLOTS // 4)
        mean, scale = r.gmean[rows, :], r.gscale[rows, :]
        total, total_hat = jnp.zeros_like(mean), jnp.zeros_like(mean)

        def parts(j, rows=rows, mean=mean, scale=scale):
            row, lane = 5 + j // 4, part(j % 4, 128)
            hat = (r.ug[rows, part(j + tiles, 128)] - mean) * scale
            grad = r.dgate[rows, part(j, 128)]
            return hat, grad, grad * r.small[row : row + 1, lane]

        for j in range(tiles):
            hat, grad, inner = parts(j)
            products = jnp.sum((grad * hat).reshape(-1, 8, 128), axis=0)
            r.gate_sums[part(j, 8), :] = products if quarter == 0 else r.gate_sums[part(j, 8), :] + products
            total = total + inner
            total_hat = total_hat + inner * hat
        total = jnp.broadcast_to(lane_mean(total, GATE), total.shape)
        total_hat = jnp.broadcast_to(lane_mean(total_hat, GATE), total.shape)
        for j in range(tiles):
            hat, _, inner = parts(j)
            far = part(j + tiles, 128)
            r.dgate[rows, part(j, 128)] = scale * (inner - total - hat * total_hat)
    for j in range(tiles):
        far = part(j + tiles, 128)
        r.dhid[:, far] = low(r.dgate[:, part(j, 128)] * r.slope_c[:, far].astype(F32))
        r.tgrad[j % 4, 5 + j // 4 : 6 + j // 4, :] = fold_rows(r.gate_sums[part(j, 8), :])

    def down(j):
        at = part(j, 256)
        r.dnrm[:, at] = dot_t(r.dhid[...], r.w_cg[at, :])

    each(2, down)
    g_cg = r.w.at[rows_of("cg_in")]
    weight_columns(r.nrm_c, r.dhid, 6, r.stage, r.left_t, g_cg)
    emits.put_tensor("cg_in", g_cg)

    def add(rows, back):
        r.dx[rows, :] += back

    r.gains[2:3, :] = norm_rows_back(r.x1, r.small[2:3, :], r.dnrm, add)


def forward_kernel(names, coords, length_ref, frames, cot, *refs):
    sources, refs = refs[: len(LAYOUT)], refs[len(LAYOUT) :]
    r = SimpleNamespace(**dict(zip(names, refs)))
    r.cot = cot
    length = length_ref[0]
    loads = Loads(coords, sources, r.w, r.seams, r.load_sems)
    kept = []

    def keep(source, target):
        copy = pltpu.make_async_copy(source, target, r.keep_sems.at[len(kept)])
        copy.start()
        kept.append(copy)

    for padded in (r.gpad, r.mpad, r.dpad):
        clear_margins(padded)
    r.tgrad[...] = jnp.zeros_like(r.tgrad)
    r.gains[...] = jnp.zeros_like(r.gains)
    loads.wait("small")
    r.small[...] = r.w[ROW * 31 : ROW * 31 + SMALL, :].astype(F32)
    for lane in range(4):
        r.tiles[lane] = r.small[:, part(lane, 128)]
    loads.wait("ffa_in")
    split_columns(r.w.at[rows_of("ffa_in")], r.w_ffa_in, 4, r.stage)
    keep(r.w_ffa_in, r.keep_ffa_in)
    loads.wait("ffa_out")
    keep(r.w.at[rows_of("ffa_out")], r.keep_ffa_out)
    feed_forward(frames, r.small[0:1, :], r.w_ffa_in, r.w.at[rows_of("ffa_out")], r.nrm, r.act, r.slope, r.x1)
    keep(r.nrm, r.keep_nrm)
    keep(r.act, r.keep_act)
    keep(r.slope, r.keep_slope)
    keep(r.x1, r.keep_x1)
    loads.wait("qkv")
    split_columns(r.w.at[rows_of("qkv")], r.w_qkv, 3, r.stage)
    keep(r.w_qkv, r.keep_qkv)
    loads.wait("att_out")
    keep(r.w.at[rows_of("att_out")], r.keep_att)
    attention_forward(r, length)
    keep(r.nrm_t, r.keep_nrm_t)
    keep(r.qkv, r.keep_heads)
    keep(r.probs, r.keep_probs)
    keep(r.ctx, r.keep_ctx)
    loads.wait("cg_in")
    split_columns(r.w.at[rows_of("cg_in")], r.w_cg, 6, r.stage)
    loads.wait("cg_out")
    gating_forward(r, length)
    loads.wait("merge")
    merge_forward(r, length)
    loads.wait("ffb_in")
    split_columns(r.w.at[rows_of("ffb_in")], r.w_ffb_in, 4, r.stage)
    loads.wait("ffb_out")
    w_out = r.w.at[rows_of("ffb_out")]
    feed_forward(r.x2, r.small[3:4, :], r.w_ffb_in, w_out, r.nrm_b, r.act_b, r.slope_b, r.x3)
    final_norm(r, length)
    emits = Emits(
        coords,
        ((r.low_kept, (r.low_near, r.low_far)), (r.high_kept, (r.high_near, r.high_far))),
        r.emit_sems,
    )
    feed_back(
        r.dout, r.w_ffb_in, w_out, r.nrm_b, r.act_b, r.slope_b, r.dhid, r.dnrm, r.stage, r.left_t,
        r.w.at[rows_of("ffb_in")], w_out, emits, "ffb",
    )

    def add(rows, back):
        r.dx[rows, :] += back

    r.gains[3:4, :] = norm_rows_back(r.x2, r.small[3:4, :], r.dnrm, add)
    merge_back(r, length, emits)
    keep(r.djoin, r.keep_djoin)
    gating_back(r, length, emits)
    keep(r.dx, r.keep_dx)
    for lane in range(4):
        at = part(lane, 128)
        r.gains[5:8, at] = r.tgrad[lane, 5:8, :]
        r.w[ROW * 31 : ROW * 31 + SMALL, at] = low(r.tgrad[lane])
    r.w[ROW * 31 : ROW * 31 + 16, :] = low(
        jnp.concatenate(
            [
                jnp.zeros((8, ROW), F32),
                jnp.concatenate([r.tgrad[lane, 8:16, :] for lane in range(4)], axis=1),
            ],
            axis=0,
        )
    )
    r.w[ROW * 31 + SMALL : ROW * 32, :] = jnp.zeros((ROW - SMALL, ROW), BF16)
    emits.put_tensor("small", r.w.at[rows_of("small")])
    for copy in kept:
        copy.wait()
    emits.wait()


def attention_back(r, emits):
    def project(j):
        at = part(j, 256)
        r.dctx[:, at] = low(dot_t(r.datt[...], r.w_att[at, :]))

    each(2, project)
    weight_rows(r.ctx, r.datt, 1, r.left_t, r.w_att)
    emits.put_tensor("att_out", r.w_att)
    first_half = lax.broadcasted_iota(jnp.int32, (1, 128), 1) < HS
    at_row = lax.broadcasted_iota(jnp.int32, (SLOTS, SLOTS), 0)
    at_column = lax.broadcasted_iota(jnp.int32, (SLOTS, SLOTS), 1)
    flip = low((at_row + at_column == SLOTS - 1).astype(F32))

    def heads(pair):
        queries = r.qkv[0:SLOTS, part(pair, 128)]
        keys = r.qkv[:, part(pair + 4, 128)]
        values = r.qkv[:, part(pair + 8, 128)]
        context = r.dctx[:, part(pair, 128)]
        q_parts, k_parts, v_parts = [], [], []
        for odd in range(2):
            head = 2 * pair + odd
            half = first_half if odd == 0 else jnp.logical_not(first_half)
            chances = r.probs[head]
            v_parts.append(t_dot(chances, context)[0:SLOTS])
            wide_chances = chances.astype(F32)
            chance_grad = dot_t(jnp.where(half, context, jnp.zeros_like(context)), values)
            inner = jnp.sum(wide_chances * chance_grad, axis=-1, keepdims=True)
            score_grad = low(wide_chances * (chance_grad - inner))
            q_parts.append(dot(score_grad, keys))
            k_parts.append(t_dot(score_grad, queries)[0:SLOTS])
            wide = jnp.concatenate([dot(flip, score_grad), jnp.zeros((SLOTS, ROW - KEYS), F32)], axis=1)
            wide = pltpu.roll(wide, ROW - SLOTS + 1, 1, stride=1, stride_axis=0)
            r.sums[pl.ds(head, 1), :] = fold_rows(wide)
        scale = HS ** (-0.5)
        r.dhid[:, part(pair, 128)] = low(jnp.where(first_half, q_parts[0], q_parts[1]) * scale)
        r.dhid[:, part(pair + 4, 128)] = low(jnp.where(first_half, k_parts[0], k_parts[1]) * scale)
        r.dhid[:, part(pair + 8, 128)] = low(jnp.where(first_half, v_parts[0], v_parts[1]))

    each(H // 2, heads)

    def down(j):
        at = part(j, 256)
        r.dnrm[:, at] = dot_t(r.dhid[:, 0 : 3 * D], r.w_qkv[at, :])

    each(2, down)

    def add(rows, back):
        r.dx[rows, :] += back
        r.dout[rows, :] = low(0.5 * r.dx[rows, :])

    r.late[1:2, :] = norm_rows_back(r.x1, r.gain_rows[1:2, :], r.dnrm, add)


def attention_weights_back(r, emits):
    weight_columns(r.nrm_t, r.dhid, 3, r.stage, r.left_t, r.g_qkv)
    emits.put_tensor("qkv", r.g_qkv)
    by_entry = lax.dot_general(
        r.sums[...],
        bucket_map(),
        (((1,), (1,)), ((), ())),
        precision=lax.Precision.HIGHEST,
        preferred_element_type=F32,
    )
    flat = fold_rows(own_entries(by_entry))
    r.late[8:9, :] = flat[:, 0:ROW]
    r.late[9:10, :] = flat[:, ROW:]


def backward_kernel(names, coords, frames, gains, gain_rows, *refs):
    r = SimpleNamespace(**dict(zip(names, refs)))
    r.gain_rows = gain_rows
    waits = {}
    for at, (name, source, target) in enumerate(
        (
            ("att", r.in_att, r.w_att),
            ("djoin", r.in_djoin.at[:, 0:D], r.datt),
            ("ctx", r.in_ctx, r.ctx),
            ("heads", r.in_heads, r.qkv),
            ("probs", r.in_probs, r.probs),
            ("qkv", r.in_qkv, r.w_qkv),
            ("x1", r.in_x1, r.x1),
            ("dx", r.in_dx, r.dx),
            ("nrm_t", r.in_nrm_t, r.nrm_t),
            ("ffa_out", r.in_ffa_out, r.w_ffa_out),
            ("slope", r.in_slope, r.slope),
            ("act", r.in_act, r.act),
            ("ffa_in", r.in_ffa_in, r.w_ffa_in),
            ("nrm", r.in_nrm, r.nrm),
        )
    ):
        waits[name] = pltpu.make_async_copy(source, target, r.load_sems.at[at])
        waits[name].start()
    r.late[...] = jnp.zeros_like(r.late)
    emits = Emits(coords, ((r.low_kept, (r.low_near, r.low_far)),), r.emit_sems)
    for name in ("att", "djoin", "ctx", "heads", "probs", "qkv", "x1", "dx"):
        waits[name].wait()
    attention_back(r, emits)
    waits["nrm_t"].wait()
    attention_weights_back(r, emits)
    for name in ("ffa_out", "slope", "act", "ffa_in", "nrm"):
        waits[name].wait()
    feed_back(
        r.dout, r.w_ffa_in, r.w_ffa_out, r.nrm, r.act, r.slope, r.dhid, r.dnrm, r.stage, r.left_t, r.g_ffa_in,
        r.w_ffa_out, emits, "ffa",
    )

    def add(rows, back):
        r.fgrad[rows, :] = low(r.dx[rows, :] + back)

    r.late[0:1, :] = norm_rows_back(frames, gain_rows[0:1, :], r.dnrm, add)
    r.late[2:8, :] = gains[2:8, :]
    emits.wait()


VM = pl.BlockSpec(memory_space=pltpu.VMEM)
SM = pl.BlockSpec(memory_space=pltpu.SMEM)
ANY = pl.BlockSpec(memory_space=pl.ANY)
WIDE, THIN = ((SLOTS, D), F32), ((SLOTS, D), BF16)
FULL = ((SLOTS, FF), BF16)
KEPT, SENT = ((8, SPAN, ROW), BF16), ((4, SPAN, ROW), BF16)

FORWARD_OUT = {
    "out": (VM, THIN),
    "gains": (VM, ((8, ROW), F32)),
    "small": (VM, ((SMALL, ROW), F32)),
    "high_kept": (ANY, KEPT),
    "high_near": (ANY, SENT),
    "high_far": (ANY, SENT),
    "low_kept": (ANY, KEPT),
    "low_near": (ANY, SENT),
    "low_far": (ANY, SENT),
    "keep_ffa_in": (ANY, ((D, FF), BF16)),
    "keep_ffa_out": (ANY, ((FF, D), BF16)),
    "keep_qkv": (ANY, ((D, 3 * D), BF16)),
    "keep_att": (ANY, ((D, D), BF16)),
    "keep_nrm": (ANY, THIN),
    "keep_act": (ANY, FULL),
    "keep_slope": (ANY, FULL),
    "keep_x1": (ANY, WIDE),
    "keep_nrm_t": (ANY, THIN),
    "keep_heads": (ANY, ((KEYS, 3 * D), BF16)),
    "keep_probs": (ANY, ((H, SLOTS, KEYS), BF16)),
    "keep_ctx": (ANY, THIN),
    "keep_djoin": (ANY, ((SLOTS, 2 * D), BF16)),
    "keep_dx": (ANY, WIDE),
}
FORWARD_SCRATCH = {
    "w": ((32 * ROW, ROW), BF16),
    "w_ffa_in": ((D, FF), BF16),
    "w_qkv": ((D, 3 * D), BF16),
    "w_cg": ((D, CG), BF16),
    "w_ffb_in": ((D, FF), BF16),
    "stage": ((4, 6 * ROW, 128), F32),
    "left_t": ((ROW, SLOTS), BF16),
    "tiles": ((4, SMALL, 128), F32),
    "tgrad": ((4, SMALL, 128), F32),
    "bias": ((H, ROW), F32),
    "nrm": THIN,
    "act": FULL,
    "slope": FULL,
    "nrm_t": THIN,
    "qkv": ((KEYS, 3 * D), BF16),
    "probs": ((H, SLOTS, KEYS), BF16),
    "ctx": THIN,
    "nrm_c": THIN,
    "hid": ((SLOTS, 256), F32),
    "ug": ((SLOTS, CG), F32),
    "slope_c": ((SLOTS, CG), BF16),
    "gmean": ((SLOTS, 128), F32),
    "gscale": ((SLOTS, 128), F32),
    "gate_sums": ((8 * GATE // 128, 128), F32),
    "gpad": ((PADDED, GATE), F32),
    "cv": ((SLOTS, GATE), BF16),
    "gated": ((SLOTS, GATE), BF16),
    "cat": ((SLOTS, 2 * D), F32),
    "mpad": ((PADDED, 2 * D), F32),
    "mixed": ((SLOTS, 2 * D), BF16),
    "nrm_b": THIN,
    "act_b": FULL,
    "slope_b": FULL,
    "dpad": ((PADDED, GATE), F32),
    "djoin": ((SLOTS, 2 * D), BF16),
    "dgate": ((SLOTS, GATE), F32),
    "dhid": ((SLOTS, CG), BF16),
    "dnrm": WIDE,
    "dout": THIN,
    "dx": WIDE,
    "x1": WIDE,
    "x2": WIDE,
    "x3": WIDE,
    "seams": ((PARTS + 1, 2, TILE, ROW), BF16),
    "load_sems": PARTS,
    "keep_sems": 16,
    "emit_sems": 40,
}
BACKWARD_IN = (
    "ffa_in", "ffa_out", "qkv", "att", "nrm", "act", "slope", "x1", "nrm_t", "heads", "probs", "ctx", "djoin", "dx",
)
PASSED = ("low_kept", "low_near", "low_far")
BACKWARD_OUT = {
    "fgrad": (VM, THIN),
    "late": (VM, ((16, ROW), F32)),
    "low_kept": (ANY, KEPT),
    "low_near": (ANY, SENT),
    "low_far": (ANY, SENT),
}
BACKWARD_SCRATCH = {
    "w_ffa_in": ((D, FF), BF16),
    "w_ffa_out": ((FF, D), BF16),
    "w_qkv": ((D, 3 * D), BF16),
    "w_att": ((D, D), BF16),
    "g_ffa_in": ((FF, D), BF16),
    "g_qkv": ((3 * D, D), BF16),
    "stage": ((4, 4 * ROW, 128), F32),
    "left_t": ((ROW, SLOTS), BF16),
    "sums": ((H, ROW), F32),
    "nrm": THIN,
    "act": FULL,
    "slope": FULL,
    "nrm_t": THIN,
    "qkv": ((KEYS, 3 * D), BF16),
    "probs": ((H, SLOTS, KEYS), BF16),
    "ctx": THIN,
    "datt": THIN,
    "dctx": THIN,
    "dhid": FULL,
    "dnrm": WIDE,
    "dout": THIN,
    "dx": WIDE,
    "x1": WIDE,
    "load_sems": 14,
    "emit_sems": 24,
}


def call(kernel, name, ins, outs, scratch, limit, aliases=None):
    return pl.pallas_call(
        kernel,
        name=name,
        in_specs=[space for space, _ in ins],
        out_specs=[space for space, _ in outs],
        out_shape=[jax.ShapeDtypeStruct(*kind) for _, kind in outs],
        scratch_shapes=[
            pltpu.SemaphoreType.DMA((each_one,)) if isinstance(each_one, int) else pltpu.VMEM(*each_one)
            for each_one in scratch
        ],
        input_output_aliases=aliases or {},
        compiler_params=pltpu.CompilerParams(vmem_limit_bytes=limit * 2**20),
    )(*[array for _, array in ins])


def forward(coords, length, frames, cot, blocks):
    def kernel(*refs):
        forward_kernel([*FORWARD_OUT, *FORWARD_SCRATCH], *refs)

    outs = call(
        kernel,
        "forward",
        [(SM, coords), (SM, length), (VM, frames), (VM, cot)] + [(ANY, block) for block in blocks],
        list(FORWARD_OUT.values()),
        list(FORWARD_SCRATCH.values()),
        58,
    )
    return dict(zip(FORWARD_OUT, outs))


def backward(coords, frames, state):
    def kernel(*refs):
        names = ["in_" + name for name in BACKWARD_IN + PASSED]
        backward_kernel([*names, *BACKWARD_OUT, *BACKWARD_SCRATCH], *refs)

    ins = [(SM, coords), (VM, frames), (VM, state["gains"]), (VM, state["small"])]
    ins += [(ANY, state["keep_" + name]) for name in BACKWARD_IN]
    ins += [(ANY, state[name]) for name in PASSED]
    outs = call(
        kernel,
        "backward",
        ins,
        list(BACKWARD_OUT.values()),
        list(BACKWARD_SCRATCH.values()),
        58,
        {len(ins) - 3 + at: 2 + at for at in range(3)},
    )
    return dict(zip(BACKWARD_OUT, outs))


def segment_bounds():
    bounds = [0]
    for extent in segment_shapes():
        bounds.append(bounds[-1] + math.prod(extent))
    return bounds


def fast_mesh():
    return lax.axis_size("dp") == 4 and lax.axis_size("fsdp") == 8


def over_x(value):
    return lax.ppermute(value, "fsdp", [(i, i ^ 1) for i in range(8)])


def over_y(value):
    return lax.ppermute(value, "dp", [(i, i ^ 2) for i in range(4)])


def over_core(value):
    return lax.ppermute(value, "dp", [(i, i ^ 1) for i in range(4)])


def round_z(value):
    return lax.ppermute(value, "fsdp", [(i, (i + 2) % 8) for i in range(8)])


def over_z(value, step):
    return lax.ppermute(value, "fsdp", [(i, i ^ (2 * step)) for i in range(8)])


def after(value, *others):
    return lax.optimization_barrier((value, *others))[0]


def shard_offset(me, shard_size):
    return me * shard_size - start_of(me) * ROW


def gather_shards(shard, me):
    shard_size = shard.shape[0]
    if not fast_mesh():
        whole = lax.all_gather(shard, AXES, axis=0, tiled=True)
        whole = jnp.pad(whole, (0, (STARTS[-1] + SPAN) * ROW - whole.shape[0])).reshape(-1, ROW)
        spans = [whole[start : start + SPAN] for start in STARTS[:-1]]
        spans = spans[:1] + [jnp.concatenate([jnp.zeros((TILE, ROW), BF16), span[TILE:]]) for span in spans[1:]]
        return [
            jnp.concatenate([spans[source_part((0, 0, 0, 0), piece)][piece[4] : piece[5]] for piece in pieces])
            for pieces in LAYOUT
        ]
    most = TILE * ROW
    padded = jnp.pad(shard, (most, SPAN * ROW - shard_size))
    span = lax.dynamic_slice(padded, (most - shard_offset(me, shard_size),), (SPAN * ROW,)).reshape(SPAN, ROW)
    own, by_x, by_y = [span], [], []
    for back in range(4):
        if back < 3:
            own.append(round_z(own[back]))
        if back < 2:
            by_x.append(over_x(own[back]))
            by_y.append(over_y(own[back]))
            own[back + 1], by_x[back], by_y[back] = lax.optimization_barrier((own[back + 1], by_x[back], by_y[back]))
        else:
            by_x.append(over_x(jnp.concatenate([own[back], by_y[back - 2][:HALF]])))
            by_y.append(over_y(jnp.concatenate([own[back], by_x[back - 2][HALF:SPAN]])))
    by_x.append(over_x(by_y[2][:HALF]))
    by_y.append(over_y(by_x[2][HALF:SPAN]))
    last_x, last_y = by_y[3][:HALF], by_x[3][HALF:SPAN]
    by_x.append(over_x(after(last_x, by_x[4])))
    by_y.append(over_y(after(last_y, by_y[4])))
    late_ones = (by_x[3], by_y[3])
    far_own = [over_core(each_one) for each_one in own[:2]] + [over_core(after(each_one, *late_ones)) for each_one in own[2:]]
    far = [far_own]
    for way in (by_x, by_y):
        far.append([over_core(way[0]), over_core(way[1]), over_core(after(way[2], *late_ones))])
        far[-1] += [over_core(way[at]) for at in (3, 4, 5)]
    return own + by_x + by_y + far[0] + far[1] + far[2]


def added(*parts):
    total = parts[0].astype(F32)
    for each_one in parts[1:]:
        total = total + each_one.astype(F32)
    return total


SIDES = (slice(0, HALF), slice(HALF, SPAN))


HBM = pl.BlockSpec(memory_space=pltpu.HBM)


def span_sums(coords, own_half, x, places, low_kept, low_got, high_kept, high_got, sides):
    count = len(places)
    together = sides if isinstance(sides, int) else 0
    pieces = [(at, rows) for at in range(count) for rows in (() if together else sides)]

    def kernel(coords, low_kept, low_got, high_kept, high_got, *refs):
        outs, (kept, got, total, sems, out_sems) = refs[:-5], refs[-5:]
        high = coords[0] == int(own_half)
        for source, other, wanted in ((low_kept, low_got, jnp.logical_not(high)), (high_kept, high_got, high)):

            @pl.when(wanted)
            def _(source=source, other=other):
                for at, place in enumerate(places):
                    pltpu.make_async_copy(source.at[4 * x + place], kept.at[at], sems.at[2 * at]).start()
                    pltpu.make_async_copy(other.at[place], got.at[at], sems.at[2 * at + 1]).start()

        copies = []
        for at in range(count):
            pltpu.make_async_copy(low_kept.at[at], kept.at[at], sems.at[2 * at]).wait()
            pltpu.make_async_copy(low_got.at[at], got.at[at], sems.at[2 * at + 1]).wait()

            def add(k, at=at):
                rows = part(k, SPAN // 11)
                total[at, rows] = low(kept[at, rows].astype(F32) + got[at, rows].astype(F32))

            each_loop(11, add)
            if together:
                out = outs[at // together].at[at % together]
                copies.append(pltpu.make_async_copy(total.at[at], out, out_sems.at[at]))
                copies[-1].start()
            for which, (mine, rows) in enumerate(pieces):
                if mine == at:
                    copies.append(pltpu.make_async_copy(total.at[at, rows], outs[which], out_sems.at[which]))
                    copies[-1].start()
        for copy in copies:
            copy.wait()

    spans = ((count, SPAN, ROW), BF16)
    arrays = [(HBM, low_kept), (ANY, low_got), (HBM, high_kept), (ANY, high_got)]
    if together:
        outs = [(ANY, ((together, SPAN, ROW), BF16))] * (count // together)
    else:
        outs = [(ANY, ((rows.stop - rows.start, ROW), BF16)) for _, rows in pieces]
    sums = call(
        kernel, "span_sums", [(SM, coords)] + arrays, outs, [spans] * 3 + [2 * count, max(count, len(pieces))], 56
    )
    return sums if together else [sums[len(sides) * at : len(sides) * (at + 1)] for at in range(count)]


def late_rows(late, above, below):
    gains = jnp.pad(late[0:8], ((above, below - 8), (0, 0)))
    return gains + jnp.pad(late[8:10], ((above + REL_AT, below - REL_AT - 2), (0, 0)))


def scatter_slow(state, back, shard_size, padded):
    late = back["late"]
    pieces = []
    for source, half in ((back, "low"), (state, "high")):
        for core in range(2):
            for at in range(8):
                z, x = at // 2, at % 2
                if core == 0:
                    span = source[half + "_kept"][4 * x + 3 - z]
                else:
                    span = source[half + ("_near", "_far")[x]][3 - z]
                d = len(pieces)
                pieces.append(span[: STARTS[d + 1] - STARTS[d] if d < PARTS - 1 else SPAN])
    rows = jnp.concatenate(pieces)
    first = ROW * BLOCK["small"][0]
    rows = low(rows.astype(F32) + late_rows(late, first, rows.shape[0] - first))
    flat = rows.reshape(-1)[: segment_bounds()[-1]]
    shard = lax.psum_scatter(flat, AXES, scatter_dimension=0, tiled=True)
    return jnp.pad(shard, (0, padded - shard_size)).astype(F32), lax.psum(late[0:8], AXES)


def scatter_grads(state, back, coords, me, shard_size, padded):
    if not fast_mesh():
        return scatter_slow(state, back, shard_size, padded)
    high = coords[0] == 1
    high_kept, low_kept = state["high_kept"], back["low_kept"]
    high_got = [over_core(state["high_near"]), over_core(state["high_far"])]
    low_far = over_core(back["low_far"])

    def chip_sum(own_half, x, places, sides):
        got = (low_far if x else low_near, high_got[x])
        return span_sums(coords, own_half, x, places, low_kept, got[0], high_kept, got[1], sides)

    for_y, for_x = chip_sum(False, 1, range(4), 2)
    from_x, from_y = over_x(for_x), over_y(for_y)
    low_near = over_core(after(back["low_near"], for_x, for_y))
    to_x, to_y, mine = [
        chip_sum(own_half, x, range(4), SIDES) for own_half, x in ((True, 1), (False, 0), (True, 0))
    ]
    late = after(back["late"], mine[3][1], to_x[3][1], to_y[3][1])
    late = late + over_core(late)
    late = late + over_z(late, 1)
    late = late + over_z(late, 2)
    from_x, from_y, to_x, to_y, mine, late = lax.optimization_barrier((from_x, from_y, to_x, to_y, mine, late))
    late = late + over_x(late)
    late = late + over_y(late)
    running = [None, None]
    before = [(), ()]
    for at in range(4):
        for side, rows in enumerate(SIDES):
            send_x, send_y = to_x[at][side], to_y[at][side]
            if at < 2:
                send_x = low(added(send_x, from_y[at, rows]))
            else:
                send_y = low(added(send_y, from_x[at - 2, rows]))
            got_x, got_y = over_x(after(send_x, *before[side])), over_y(after(send_y, *before[side]))
            before[side] = (got_x, got_y)
            parts = [mine[at][side], got_x, got_y]
            if at:
                parts.append(round_z(running[side]))
            running[side] = added(*parts)
            if at < 3:
                running[side] = low(running[side])
    total = jnp.concatenate(running)
    first = ROW * BLOCK["small"][0] - STARTS[PARTS - 1]
    total = total + jnp.where(me == PARTS - 1, 1.0, 0.0) * late_rows(late, first, SPAN - first)
    flat = jnp.pad(total.reshape(-1), (0, max(0, TILE * ROW + padded - SPAN * ROW)))
    return lax.dynamic_slice(flat, (shard_offset(me, shard_size),), (padded,)), late[0:8]


def sum_everywhere(vector):
    if not fast_mesh():
        return lax.psum(vector, AXES)
    vector = vector + over_core(vector)
    vector = vector + over_x(vector)
    vector = vector + over_y(vector)
    vector = vector + over_z(vector, 1)
    return vector + over_z(vector, 2)


def most_segments(shard_size, devices):
    bounds = segment_bounds()
    most = 1
    for at in range(devices):
        low_end, high_end = at * shard_size, (at + 1) * shard_size
        most = max(most, sum(1 for b in bounds[1:-1] if low_end < b < high_end) + 1)
    return most


LANES = 128
CHUNK = 1024 * LANES
STRIP = 128 * LANES


def chunk_spans(segments, step):
    first, last = step * CHUNK, (step + 1) * CHUNK
    for at in range(segments.shape[0] - 2):
        start, end = segments[1 + at], segments[2 + at]
        whole = (start <= first) & (last <= end)
        some = (start < last) & (end > first) & jnp.logical_not(whole)
        yield at, whole, some, start - first, end - first


def strips(body, start=None):
    return lax.fori_loop(0, CHUNK // STRIP, lambda at, carry: body(part(at, STRIP), at * STRIP, carry), start)


def square(entries, strip):
    return entries[strip].reshape(STRIP // LANES, LANES)


def inside(place, start, end):
    row = lax.broadcasted_iota(jnp.int32, (STRIP // LANES, LANES), 0)
    place = place + row * LANES + lax.broadcasted_iota(jnp.int32, (STRIP // LANES, LANES), 1)
    return (place >= start) & (place < end)


def fold(values):
    return jnp.sum(values.reshape(-1, 8, LANES), axis=0)


def update_kernel(segments, params, first, second, grad, new_first, new_second, update, sums):
    step = pl.program_id(0)
    nothing = jnp.zeros((8, LANES), F32)

    @pl.when(step == 0)
    def _():
        sums[...] = nothing

    def move(strip, place, totals):
        grads = grad[strip]
        firsts = BETA_FIRST * first[strip] + (1.0 - BETA_FIRST) * grads
        seconds = BETA_SECOND * second[strip] + (1.0 - BETA_SECOND) * grads * grads
        new_first[strip] = firsts
        new_second[strip] = seconds
        first_hat = firsts * (1.0 / (1.0 - BETA_FIRST**STEP))
        second_hat = seconds * (1.0 / (1.0 - BETA_SECOND**STEP))
        weights = params[strip]
        change = first_hat / (jnp.sqrt(second_hat) + ADAM_EPS) + WEIGHT_DECAY * weights
        update[strip] = change
        squares = [(each_one * each_one).reshape(STRIP // LANES, LANES) for each_one in (weights, change)]
        return totals[0] + fold(squares[0]), totals[1] + fold(squares[1])

    totals = strips(move, (nothing, nothing))
    lane = lax.broadcasted_iota(jnp.int32, (1, LANES), 1)

    def add(at, totals):
        for row, total in enumerate(totals):
            total = jnp.sum(jnp.sum(total, axis=0, keepdims=True), axis=1, keepdims=True)
            sums[row : row + 1, :] += jnp.where(lane == segments[0] + at, total, 0.0)

    for at, whole, some, start, end in chunk_spans(segments, step):

        @pl.when(whole)
        def _(at=at):
            add(at, totals)

        @pl.when(some)
        def _(at=at, start=start, end=end):
            def squares(strip, place, totals):
                here = inside(place, start, end)
                own = [square(entries, strip) for entries in (params, update)]
                own = [fold(jnp.where(here, each_one * each_one, 0.0)) for each_one in own]
                return totals[0] + own[0], totals[1] + own[1]

            add(at, strips(squares, (nothing, nothing)))


def apply_kernel(segments, sums, params, update, new_params, norms):
    step = pl.program_id(0)
    roots = jnp.sqrt(sums[0:2, :])
    trust = roots[0:1, :] / (roots[1:2, :] + ADAM_EPS)
    norms[0:2, :] = roots
    norms[2:3, :] = trust
    norms[3:8, :] = jnp.zeros((5, LANES), F32)
    lane = lax.broadcasted_iota(jnp.int32, (1, LANES), 1)
    for at, whole, some, start, end in chunk_spans(segments, step):

        scale = LEARN_RATE * jnp.sum(jnp.where(lane == segments[0] + at, trust, 0.0), axis=1, keepdims=True)
        scale = jnp.broadcast_to(scale, (1, LANES))

        def moved(strip, scale=scale):
            return square(params, strip) - scale * square(update, strip)

        @pl.when(whole)
        def _(moved=moved):
            def all_of(strip, place, carry):
                new_params[strip] = moved(strip).reshape(STRIP)
                return carry

            strips(all_of, 0)

        @pl.when(some)
        def _(moved=moved, start=start, end=end):
            def part_of(strip, place, carry):
                chosen = jnp.where(inside(place, start, end), moved(strip), square(new_params, strip))
                new_params[strip] = chosen.reshape(STRIP)
                return carry

            strips(part_of, 0)


def shards(frames, lengths, cotangent, params, first_moment, second_moment):
    shard_size = params.shape[0]
    devices = lax.axis_size("dp") * lax.axis_size("fsdp")
    me = lax.axis_index(AXES)
    if fast_mesh():
        dp, fsdp = lax.axis_index("dp"), lax.axis_index("fsdp")
        coords = jnp.stack([dp // 2, dp % 2, fsdp // 2, fsdp % 2]).astype(jnp.int32)
    else:
        coords = jnp.zeros((4,), jnp.int32)
    state = forward(coords, lengths, frames[0], cotangent[0], gather_shards(low(params), me))
    back = backward(coords, frames[0], state)
    steps = -(-shard_size // CHUNK)
    size = max(shard_size, CHUNK)
    grad_shard, gain_grads = scatter_grads(state, back, coords, me, shard_size, size)

    def filled(flat):
        return jnp.pad(flat, (0, size - shard_size)) if size > shard_size else flat

    bounds = segment_bounds()
    spans = most_segments(shard_size, devices)
    shard_low = me * shard_size
    first_segment = sum((shard_low >= b).astype(jnp.int32) for b in bounds[1:-1])
    table = jnp.asarray(bounds[1:] + [bounds[-1]] * spans, jnp.int32)
    ends = jnp.clip(lax.dynamic_slice(table, (first_segment,), (spans,)) - shard_low, 0, shard_size)
    segments = jnp.concatenate([first_segment[None], jnp.zeros((1,), jnp.int32), ends]).astype(jnp.int32)
    grid = pl.BlockSpec((CHUNK,), lambda step: (step,))
    whole = pl.BlockSpec((8, LANES), lambda step: (0, 0))
    flat_kind = jax.ShapeDtypeStruct((size,), F32)
    tile_kind = jax.ShapeDtypeStruct((8, LANES), F32)
    weights = filled(params)
    new_first, new_second, update, sums = pl.pallas_call(
        update_kernel,
        name="update",
        grid=(steps,),
        in_specs=[SM] + [grid] * 4,
        out_specs=[grid] * 3 + [whole],
        out_shape=[flat_kind] * 3 + [tile_kind],
    )(segments, weights, filled(first_moment), filled(second_moment), grad_shard)
    sums = sum_everywhere(sums)
    new_params, norms = pl.pallas_call(
        apply_kernel,
        name="apply",
        grid=(steps,),
        in_specs=[SM, whole, grid, grid],
        out_specs=[grid, whole],
        out_shape=[flat_kind, tile_kind],
    )(segments, sums, weights, update)
    count = len(segment_shapes())
    return (
        state["out"].reshape(frames.shape),
        back["fgrad"].reshape(frames.shape),
        new_params[:shard_size],
        new_first[:shard_size],
        new_second[:shard_size],
        norms[0, :count],
        norms[1, :count],
        norms[2, :count],
        gain_grads.reshape(-1),
    )


def solution(mesh):
    placed = (
        P(("dp", "fsdp"), None, None),
        P(("dp", "fsdp")),
        P(("dp", "fsdp"), None, None),
        P(("dp", "fsdp")),
        P(("dp", "fsdp")),
        P(("dp", "fsdp")),
    )
    return jax.shard_map(
        shards,
        mesh=mesh,
        in_specs=placed,
        out_specs=(
            P(("dp", "fsdp"), None, None),
            P(("dp", "fsdp"), None, None),
            P(("dp", "fsdp")),
            P(("dp", "fsdp")),
            P(("dp", "fsdp")),
            P(),
            P(),
            P(),
            P(),
        ),
        check_vma=False,
    )
```

```python
import math
from types import SimpleNamespace

import jax
import jax.numpy as jnp
from jax import lax
from jax.experimental import pallas as pl
from jax.experimental.pallas import tpu as pltpu
from jax.sharding import PartitionSpec as P

STEP = 8
BETA_FIRST = 0.5
BETA_SECOND = 0.5
LEARN_RATE = 0.5
WEIGHT_DECAY = 0.01
ADAM_EPS = 1e-06
AXES = ("dp", "fsdp")


def segment_shapes():
    gate_width = CG // 2
    return [
        (D, FF),
        (FF, D),
        (D, 3 * D),
        (D, D),
        (D, CG),
        (gate_width, D),
        (2 * D, D),
        (D, FF),
        (FF, D),
        (5 * D + gate_width,),
        (KER, gate_width + 2 * D),
        (RELW, H),
    ]


D = 512
H = 8
HS = 64
FF = 2048
CG = 3072
KER = 31
RELW = 128
NORM_EPS = 1e-05
MASK_FILL = -1000000000.0
ROW = 512
HALF = ROW // 2
SLOTS = 160
KEYS = 256
PAD = 16
PADDED = SLOTS + 2 * PAD
GATE = CG // 2
BLOCK = {
    "ffa_in": (0, 4),
    "ffa_out": (4, 4),
    "qkv": (8, 3),
    "att_out": (11, 1),
    "cg_in": (12, 6),
    "cg_out": (18, 3),
    "merge": (21, 2),
    "ffb_in": (23, 4),
    "ffb_out": (27, 4),
    "small": (31, 1),
}
TAPS_AT = 8
REL_AT = 8 + 5 * KER
SMALL = 176
F32, BF16 = jnp.float32, jnp.bfloat16


def dot(left, right):
    return lax.dot_general(left, right, (((1,), (0,)), ((), ())), preferred_element_type=F32)


def dot_t(left, right):
    return lax.dot_general(left, right, (((1,), (1,)), ((), ())), preferred_element_type=F32)


def t_dot(left, right):
    return lax.dot_general(left, right, (((0,), (0,)), ((), ())), preferred_element_type=F32)


def low(values):
    return values.astype(BF16)


def each(count, body):
    for at in range(count):
        body(at)


def each_loop(count, body, together=1):
    def step(at, carry):
        for inner in range(together):
            body(at * together + inner)
        return carry

    lax.fori_loop(0, count // together, step, 0)


def part(at, size):
    if isinstance(at, int):
        return slice(at * size, at * size + size)
    return pl.ds(pl.multiple_of(at * size, size), size)


def rows_of(name):
    first, count = BLOCK[name]
    return slice(ROW * first, ROW * (first + count))


def lane_mean(values, width):
    return jnp.sum(values, axis=-1, keepdims=True) * (1.0 / width)


def normed(values):
    centered = values - lane_mean(values, values.shape[-1])
    scale = lax.rsqrt(lane_mean(centered * centered, values.shape[-1]) + NORM_EPS)
    return centered * scale, scale


def valid_rows(length):
    return (lax.broadcasted_iota(jnp.int32, (SLOTS, 1), 0) < length).astype(F32)


def fold_rows(values):
    return jnp.sum(values, axis=0, keepdims=True)


def norm_rows(source, gain, target):
    for k in range(2):
        hat, _ = normed(source[part(k, 80), :].astype(F32))
        target[part(k, 80), :] = low(hat * gain)


def norm_rows_back(values, gain, grad, add):
    total = jnp.zeros((1, values.shape[1]), F32)
    for k in range(2):
        rows = part(k, 80)
        hat, scale = normed(values[rows, :].astype(F32))
        mine = grad[rows, :]
        total = total + fold_rows(mine * hat)
        inner = mine * gain
        width = values.shape[1]
        moved = lane_mean(inner, width) + hat * lane_mean(inner * hat, width)
        add(rows, scale * (inner - moved))
    return total


TOTAL_ROWS = 16037
PARTS = 32
TILE = 16
SPAN = 528
STARTS = [TILE * (TOTAL_ROWS * d // (PARTS * TILE)) for d in range(PARTS + 1)]
FIRST_PARTS = max(d for d in range(PARTS) if STARTS[d] < ROW * sum(BLOCK["ffa_out"]))
SHORTEST = min(high - first for first, high in zip(STARTS, STARTS[1:]))


def start_of(d):
    return ((TOTAL_ROWS * d) >> 9) * TILE


def gathered_layout():
    layout = []
    for core in range(2):
        layout += [[(core, 0, 0, back, 0, SPAN, 0)] for back in range(4)]
        for y, x, first, last in ((0, 1, 0, HALF), (1, 0, HALF, SPAN)):
            whole = [(core, y, x, back, 0, SPAN, 0) for back in range(4)]
            diagonal = [(core, 1, 1, back, first, last) for back in range(4)]
            layout += [[whole[0]], [whole[1]]]
            layout += [[whole[2], (*diagonal[0], SPAN)], [whole[3], (*diagonal[1], SPAN)]]
            layout += [[(*diagonal[2], 0), (*diagonal[3], last - first)]]
    return layout


LAYOUT = gathered_layout()


def source_part(coords, piece):
    y, c, z, x = coords[0], coords[1], coords[2], coords[3]
    yy, cc, xx, zz = y ^ piece[1], c ^ piece[0], x ^ piece[2], (z + 4 - piece[3]) & 3
    return ((yy * 2 + cc) * 4 + zz) * 2 + xx


class Loads:
    def __init__(self, coords, sources, target, seams, sems):
        self.target, self.seams, self.sems = target, seams, sems
        self.here, self.joined = set(), set()
        seams[0, 0] = jnp.zeros((TILE, ROW), BF16)
        seams[PARTS, 1] = jnp.zeros((TILE, ROW), BF16)

        for soon in (True, False):
            for pieces, source in zip(LAYOUT, sources):
                for piece in pieces:
                    d = source_part(coords, piece)
                    first_ones = (d <= FIRST_PARTS) | (d == PARTS - 1)

                    @pl.when(first_ones if soon else jnp.logical_not(first_ones))
                    def _(piece=piece, source=source, d=d):
                        self.start(piece, source, d)

    def start(self, piece, source, d):
        def rows(at, size):
            return pl.ds(pl.multiple_of(at, TILE), size)

        first, last, offset = piece[4:]
        offset = offset - first
        start = start_of(d)
        length = start_of(d + 1) - start
        inner, outer = max(first, TILE), min(last, SHORTEST)
        sem = self.sems.at[d]
        pltpu.make_async_copy(
            source.at[offset + inner : offset + outer], self.target.at[rows(start + inner, outer - inner)], sem
        ).start()
        if first == 0:
            pltpu.make_async_copy(source.at[offset : offset + TILE], self.seams.at[d, 1], sem).start()
        if last == SPAN:

            @pl.when(length > SHORTEST)
            def _():
                pltpu.make_async_copy(
                    source.at[offset + SHORTEST : offset + SHORTEST + TILE],
                    self.target.at[rows(start + SHORTEST, TILE)],
                    sem,
                ).start()

            pltpu.make_async_copy(source.at[rows(offset + length, TILE)], self.seams.at[d + 1, 0], sem).start()

    def wait_part(self, d):
        if d in self.here or not 0 <= d < PARTS:
            return
        self.here.add(d)
        size = STARTS[d + 1] - STARTS[d] + TILE
        pltpu.make_async_copy(self.target.at[0:size], self.target.at[0:size], self.sems.at[d]).wait()

    def wait(self, name):
        rows = rows_of(name)
        last = min(rows.stop, STARTS[-1] + TILE)
        for d in range(PARTS + 1):
            if STARTS[d] < last and STARTS[d] + TILE > rows.start and d not in self.joined:
                self.wait_part(d - 1)
                self.wait_part(d)
                self.joined.add(d)
                self.target[STARTS[d] : STARTS[d] + TILE, :] = self.seams[d, 0] + self.seams[d, 1]
            if d < PARTS and STARTS[d] + TILE < last and STARTS[d + 1] > rows.start:
                self.wait_part(d)


class Emits:
    def __init__(self, coords, halves, sems):
        self.coords, self.halves, self.sems = coords, halves, sems
        self.pending = []

    def put(self, d, values, rows):
        core, z, x = (d // 8) % 2, (d // 2) % 4, d % 2
        kept, sent = self.halves[d // 16]
        far_x = self.coords[3] ^ x
        place = (self.coords[2] + 3 - z) & 3
        sem = self.sems.at[len(self.pending)]

        @pl.when(self.coords[1] == core)
        def _():
            pltpu.make_async_copy(values, kept.at[4 * far_x + place, rows], sem).start()

        @pl.when((self.coords[1] != core) & (far_x == 0))
        def _():
            pltpu.make_async_copy(values, sent[0].at[place, rows], sem).start()

        @pl.when((self.coords[1] != core) & (far_x == 1))
        def _():
            pltpu.make_async_copy(values, sent[1].at[place, rows], sem).start()

        self.pending.append(pltpu.make_async_copy(values, kept.at[0, rows], sem))

    def put_tensor(self, name, values):
        rows = rows_of(name)
        for d in range(PARTS):
            first, last = max(rows.start, STARTS[d]), min(rows.stop, STARTS[d] + SPAN)
            if first < last:
                self.put(d, values.at[first - rows.start : last - rows.start], slice(first - STARTS[d], last - STARTS[d]))

    def wait(self):
        for copy in self.pending:
            copy.wait()


def split_columns(raw, target, wide, stage):
    def chunk(k):
        rows = part(k, 128 * wide)
        for lane in range(4):
            stage[lane, 0 : 128 * wide, :] = raw[rows, lane * 128 : lane * 128 + 128].astype(F32)
        for c in range(wide):
            for lane in range(4):
                place = ROW * c + lane * 128
                target[part(k, 128), place : place + 128] = low(stage[lane, pl.ds(c, 128, stride=wide), :])

    each_loop(4, chunk)


def weight_columns(left, grads, wide, stage, left_t, target):
    left_t[...] = left[...].T

    def chunk(j):
        value = dot(left_t[...], grads[:, part(j, 256)])
        c, pair = j // 2, (j % 2) * 2
        for half in range(2):
            stage[pair + half, pl.ds(c, ROW, stride=wide), :] = value[:, 128 * half : 128 * half + 128]

    each(2 * wide, chunk)

    def lower(k):
        rows = part(k, ROW)
        for lane in range(4):
            target[rows, lane * 128 : lane * 128 + 128] = low(stage[lane, rows, :])

    each(wide, lower)


def weight_rows(left, grads, count, left_t, target):
    def chunk(k):
        left_t[...] = left[:, part(k, ROW)].T
        for at in range(2):
            target[part(k, ROW), 256 * at : 256 * at + 256] = low(dot(left_t[...], grads[:, 256 * at : 256 * at + 256]))

    each(count, chunk)


def feed_forward(inputs, gain, w_in, w_out, nrm, act, slope, result):
    norm_rows(inputs, gain, nrm)

    def up(j):
        at = part(j, 256)
        hidden = dot(nrm[...], w_in[:, at])
        sig = jax.nn.sigmoid(hidden)
        active = hidden * sig
        act[:, at] = low(active)
        slope[:, at] = low(sig + active * (1.0 - sig))

    each(FF // 256, up)

    def down(j):
        at = part(j, 256)
        result[:, at] = inputs[:, at].astype(F32) + 0.5 * dot(act[...], w_out[:, at])

    each(2, down)


def feed_back(dout, w_in, w_out, nrm, act, slope, dhid, dnrm, stage, left_t, g_in, g_out, emits, name):
    def up(j):
        at = part(j, 256)
        grad = dot_t(dout[...], w_out[at, :])
        dhid[:, at] = low(grad * slope[:, at].astype(F32))

    each(FF // 256, up)
    weight_rows(act, dout, 4, left_t, g_out)
    emits.put_tensor(name + "_out", g_out)

    def down(j):
        at = part(j, 256)
        dnrm[:, at] = dot_t(dhid[:, 0:FF], w_in[at, :])

    each(2, down)
    weight_columns(nrm, dhid, 4, stage, left_t, g_in)
    emits.put_tensor(name + "_in", g_in)


def bucket_map():
    entry = lax.broadcasted_iota(jnp.int32, (2 * ROW, ROW), 0) // H
    far = lax.broadcasted_iota(jnp.int32, (2 * ROW, ROW), 1)
    far = jnp.where(far >= ROW // 2, far - ROW, far)
    bucket = jnp.clip(far, -(RELW // 2), RELW // 2 - 1) + RELW // 2
    return (entry == bucket).astype(F32)


def own_entries(flat):
    entry = lax.broadcasted_iota(jnp.int32, (H, 2 * ROW), 1)
    head = lax.broadcasted_iota(jnp.int32, (H, 2 * ROW), 0)
    return jnp.where(lax.rem(entry, H) == head, flat, 0.0)


def tap_row(small, tap, row, lane):
    return small[lane, pl.ds(TAPS_AT + 5 * tap + row, 1), :]


def shifted_sum(padded, at, factor):
    total = None
    for low_part in range(8):
        slab = padded[low_part : low_part + SLOTS + 24, at]
        inner = None
        for high_part in range(4):
            offset = 8 * high_part + low_part
            if offset:
                term = factor(offset) * slab[8 * high_part : 8 * high_part + SLOTS]
                inner = term if inner is None else inner + term
        total = inner if total is None else total + inner
    return total


def convolve(padded, small, first_row, width, finish):

    def chunk(j):
        at = part(j, 128)
        row, lane = first_row + j // 4, j % 4
        finish(j, at, shifted_sum(padded, at, lambda offset: tap_row(small, offset - 1, row, lane)))

    each_loop(width // 128, chunk)


def convolve_back(grads, padded, small, first_row, width, sgrad, finish):

    def chunk(j):
        at = part(j, 128)
        row, lane = first_row + j // 4, j % 4
        finish(j, at, shifted_sum(grads, at, lambda offset: tap_row(small, KER - offset, row, lane)))
        own = grads[PAD : PAD + SLOTS, at]
        for low_part in range(8):
            slab = padded[low_part : low_part + SLOTS + 24, at]
            for high_part in range(4):
                offset = 8 * high_part + low_part
                if offset:
                    tile = slab[8 * high_part : 8 * high_part + SLOTS]
                    sgrad[lane, pl.ds(TAPS_AT + 5 * (offset - 1) + row, 1), :] = fold_rows(own * tile)

    each_loop(width // 128, chunk)


def clear_margins(padded):
    padded[0:PAD, :] = jnp.zeros((PAD, padded.shape[1]), F32)
    padded[PAD + SLOTS : PADDED, :] = jnp.zeros((PAD, padded.shape[1]), F32)


def gelu_parts(hidden):
    bell = jnp.exp(-0.5 * hidden * hidden)
    spread = 1.0 + (0.3275911 * 2.0**-0.5) * jnp.abs(hidden)
    near = pl.reciprocal(spread, approx=True)
    near = near * (2.0 - spread * near)
    tail = jnp.full_like(near, 0.5 * 1.061405429)
    for factor in (-1.453152027, 1.421413741, -0.284496736, 0.254829592):
        tail = tail * near + 0.5 * factor
    tail = tail * near * bell
    below = jnp.where(hidden >= 0.0, 1.0 - tail, tail)
    return hidden * below, below + hidden * bell * ((2.0 * math.pi) ** -0.5)


def attention_forward(r, length):
    norm_rows(r.x1, r.small[1:2, :], r.nrm_t)
    r.qkv[SLOTS:KEYS, :] = jnp.zeros((KEYS - SLOTS, 3 * D), BF16)
    flat = jnp.concatenate([r.small[REL_AT : REL_AT + 1, :], r.small[REL_AT + 1 : REL_AT + 2, :]], axis=1)
    r.bias[...] = dot(low(own_entries(jnp.broadcast_to(flat, (H, 2 * ROW)))), low(bucket_map()))

    def project(j):
        at = part(j, 256)
        r.qkv[0:SLOTS, at] = low(dot(r.nrm_t[...], r.w_qkv[:, at]))

    each(3 * D // 256, project)
    valid = lax.broadcasted_iota(jnp.int32, (1, KEYS), 1) < length
    first_half = lax.broadcasted_iota(jnp.int32, (1, 128), 1) < HS

    def heads(pair):
        queries = r.qkv[0:SLOTS, part(pair, 128)]
        keys = r.qkv[:, part(pair + 4, 128)]
        values = r.qkv[:, part(pair + 8, 128)]
        outs = []
        for odd in range(2):
            head = 2 * pair + odd
            half = first_half if odd == 0 else jnp.logical_not(first_half)
            mine = jnp.where(half, queries, jnp.zeros_like(queries))
            spread = jnp.broadcast_to(r.bias[pl.ds(head, 1), :], (SLOTS, ROW))
            spread = pltpu.roll(spread, 0, 1, stride=1, stride_axis=0)[:, 0:KEYS]
            scores = jnp.where(valid, dot_t(mine, keys) * HS ** (-0.5) + spread, MASK_FILL)
            shifted = jnp.exp(scores - jnp.max(scores, axis=-1, keepdims=True))
            chances = low(shifted / jnp.sum(shifted, axis=-1, keepdims=True))
            r.probs[head] = chances
            outs.append(dot(chances, values))
        r.ctx[:, part(pair, 128)] = low(jnp.where(first_half, outs[0], outs[1]))

    each(H // 2, heads)

    def project_out(j):
        at = part(j, 256)
        r.cat[:, at] = dot(r.ctx[...], r.w[rows_of("att_out"), at])

    each(2, project_out)


def gating_forward(r, length):
    norm_rows(r.x1, r.small[2:3, :], r.nrm_c)

    def up(j):
        at = part(j, 256)
        r.hid[...] = dot(r.nrm_c[...], r.w_cg[:, at])
        for k in range(5):
            rows = part(k, 32)
            active, slope = gelu_parts(r.hid[rows, :])
            r.ug[rows, at] = active
            r.slope_c[rows, at] = low(slope)

    each_loop(CG // 256, up, 4)
    tiles = [slice(GATE + 128 * j, GATE + 128 * j + 128) for j in range(GATE // 128)]
    total = jnp.zeros((SLOTS, 128), F32)
    for at in tiles:
        total = total + r.ug[:, at]
    mean = lane_mean(total, GATE)
    total = jnp.zeros((SLOTS, 128), F32)
    for at in tiles:
        centered = r.ug[:, at] - mean
        total = total + centered * centered
    scale = lax.rsqrt(lane_mean(total, GATE) + NORM_EPS)
    r.gmean[...] = jnp.broadcast_to(mean, (SLOTS, 128))
    r.gscale[...] = jnp.broadcast_to(scale, (SLOTS, 128))
    scale = scale * valid_rows(length)
    for j, at in enumerate(tiles):
        gain = r.small[5 + j // 4 : 6 + j // 4, part(j % 4, 128)]
        r.gpad[PAD : PAD + SLOTS, part(j, 128)] = (r.ug[:, at] - mean) * scale * gain

    def finish(j, at, value):
        r.cv[:, at] = low(value)
        r.gated[:, at] = low(r.ug[:, at] * value)

    convolve(r.gpad, r.tiles, 0, GATE, finish)

    def down(j):
        r.cat[:, part(j + 2, 256)] = dot(r.gated[...], r.w[rows_of("cg_out"), part(j, 256)])

    each(2, down)


def merge_forward(r, length):
    valid = valid_rows(length)
    for j in range(8):
        at = part(j, 128)
        r.mpad[PAD : PAD + SLOTS, at] = r.cat[:, at] * valid

    def finish(j, at, value):
        r.mixed[:, at] = low(r.cat[:, at] + value)

    convolve(r.mpad, r.tiles, 3, 2 * D, finish)

    def merge(j):
        at = part(j, 256)
        r.x2[:, at] = r.x1[:, at] + dot(r.mixed[...], r.w[rows_of("merge"), at])

    each(2, merge)


def final_norm(r, length):
    gain = r.small[4:5, :]
    valid = valid_rows(length)
    total = jnp.zeros((1, D), F32)
    for k in range(2):
        rows = part(k, 80)
        hat, scale = normed(r.x3[rows, :])
        r.out[rows, :] = low(hat * gain * valid[80 * k : 80 * k + 80])
        mine = r.cot[rows, :].astype(F32) * valid[80 * k : 80 * k + 80]
        total = total + fold_rows(mine * hat)
        inner = mine * gain
        back = scale * (inner - (lane_mean(inner, D) + hat * lane_mean(inner * hat, D)))
        r.dx[rows, :] = back
        r.dout[rows, :] = low(0.5 * back)
    r.gains[4:5, :] = total


def merge_back(r, length, emits):
    for k in range(2):
        r.dout[part(k, 80), :] = low(r.dx[part(k, 80), :])
    w_merge = r.w.at[rows_of("merge")]

    def merge(j):
        at = part(j, 256)
        r.dpad[PAD : PAD + SLOTS, at] = dot_t(r.dout[...], w_merge[at, :])

    each(2 * D // 256, merge)
    weight_rows(r.mixed, r.dout, 2, r.left_t, w_merge)
    emits.put_tensor("merge", w_merge)

    def finish(j, at, value):
        r.djoin[:, at] = low(r.dpad[PAD : PAD + SLOTS, at] + value * valid_rows(length))

    convolve_back(r.dpad, r.mpad, r.tiles, 3, 2 * D, r.tgrad, finish)


def gating_back(r, length, emits):
    w_co = r.w.at[rows_of("cg_out")]

    def gate(j):
        at = part(j, 256)
        value = dot_t(r.djoin[:, D:], w_co[at, :])
        r.dhid[:, at] = low(value * r.cv[:, at].astype(F32) * r.slope_c[:, at].astype(F32))
        r.dpad[PAD : PAD + SLOTS, at] = value * r.ug[:, at]

    each(GATE // 256, gate)
    r.dout[...] = r.djoin[:, D:]
    weight_rows(r.gated, r.dout, 3, r.left_t, w_co)
    emits.put_tensor("cg_out", w_co)

    def finish(j, at, value):
        r.dgate[:, at] = value * valid_rows(length)

    convolve_back(r.dpad, r.gpad, r.tiles, 0, GATE, r.tgrad, finish)
    tiles = GATE // 128
    for quarter in range(4):
        rows = part(quarter, SLOTS // 4)
        mean, scale = r.gmean[rows, :], r.gscale[rows, :]
        total, total_hat = jnp.zeros_like(mean), jnp.zeros_like(mean)

        def parts(j, rows=rows, mean=mean, scale=scale):
            row, lane = 5 + j // 4, part(j % 4, 128)
            hat = (r.ug[rows, part(j + tiles, 128)] - mean) * scale
            grad = r.dgate[rows, part(j, 128)]
            return hat, grad, grad * r.small[row : row + 1, lane]

        for j in range(tiles):
            hat, grad, inner = parts(j)
            products = jnp.sum((grad * hat).reshape(-1, 8, 128), axis=0)
            r.gate_sums[part(j, 8), :] = products if quarter == 0 else r.gate_sums[part(j, 8), :] + products
            total = total + inner
            total_hat = total_hat + inner * hat
        total = jnp.broadcast_to(lane_mean(total, GATE), total.shape)
        total_hat = jnp.broadcast_to(lane_mean(total_hat, GATE), total.shape)
        for j in range(tiles):
            hat, _, inner = parts(j)
            far = part(j + tiles, 128)
            r.dgate[rows, part(j, 128)] = scale * (inner - total - hat * total_hat)
    for j in range(tiles):
        far = part(j + tiles, 128)
        r.dhid[:, far] = low(r.dgate[:, part(j, 128)] * r.slope_c[:, far].astype(F32))
        r.tgrad[j % 4, 5 + j // 4 : 6 + j // 4, :] = fold_rows(r.gate_sums[part(j, 8), :])

    def down(j):
        at = part(j, 256)
        r.dnrm[:, at] = dot_t(r.dhid[...], r.w_cg[at, :])

    each(2, down)
    g_cg = r.w.at[rows_of("cg_in")]
    weight_columns(r.nrm_c, r.dhid, 6, r.stage, r.left_t, g_cg)
    emits.put_tensor("cg_in", g_cg)

    def add(rows, back):
        r.dx[rows, :] += back

    r.gains[2:3, :] = norm_rows_back(r.x1, r.small[2:3, :], r.dnrm, add)


def forward_kernel(names, coords, length_ref, frames, cot, *refs):
    sources, refs = refs[: len(LAYOUT)], refs[len(LAYOUT) :]
    r = SimpleNamespace(**dict(zip(names, refs)))
    r.cot = cot
    length = length_ref[0]
    loads = Loads(coords, sources, r.w, r.seams, r.load_sems)
    kept = []

    def keep(source, target):
        copy = pltpu.make_async_copy(source, target, r.keep_sems.at[len(kept)])
        copy.start()
        kept.append(copy)

    for padded in (r.gpad, r.mpad, r.dpad):
        clear_margins(padded)
    r.tgrad[...] = jnp.zeros_like(r.tgrad)
    r.gains[...] = jnp.zeros_like(r.gains)
    loads.wait("small")
    r.small[...] = r.w[ROW * 31 : ROW * 31 + SMALL, :].astype(F32)
    for lane in range(4):
        r.tiles[lane] = r.small[:, part(lane, 128)]
    loads.wait("ffa_in")
    split_columns(r.w.at[rows_of("ffa_in")], r.w_ffa_in, 4, r.stage)
    keep(r.w_ffa_in, r.keep_ffa_in)
    loads.wait("ffa_out")
    keep(r.w.at[rows_of("ffa_out")], r.keep_ffa_out)
    feed_forward(frames, r.small[0:1, :], r.w_ffa_in, r.w.at[rows_of("ffa_out")], r.nrm, r.act, r.slope, r.x1)
    keep(r.nrm, r.keep_nrm)
    keep(r.act, r.keep_act)
    keep(r.slope, r.keep_slope)
    keep(r.x1, r.keep_x1)
    loads.wait("qkv")
    split_columns(r.w.at[rows_of("qkv")], r.w_qkv, 3, r.stage)
    keep(r.w_qkv, r.keep_qkv)
    loads.wait("att_out")
    keep(r.w.at[rows_of("att_out")], r.keep_att)
    attention_forward(r, length)
    keep(r.nrm_t, r.keep_nrm_t)
    keep(r.qkv, r.keep_heads)
    keep(r.probs, r.keep_probs)
    keep(r.ctx, r.keep_ctx)
    loads.wait("cg_in")
    split_columns(r.w.at[rows_of("cg_in")], r.w_cg, 6, r.stage)
    loads.wait("cg_out")
    gating_forward(r, length)
    loads.wait("merge")
    merge_forward(r, length)
    loads.wait("ffb_in")
    split_columns(r.w.at[rows_of("ffb_in")], r.w_ffb_in, 4, r.stage)
    loads.wait("ffb_out")
    w_out = r.w.at[rows_of("ffb_out")]
    feed_forward(r.x2, r.small[3:4, :], r.w_ffb_in, w_out, r.nrm_b, r.act_b, r.slope_b, r.x3)
    final_norm(r, length)
    emits = Emits(
        coords,
        ((r.low_kept, (r.low_near, r.low_far)), (r.high_kept, (r.high_near, r.high_far))),
        r.emit_sems,
    )
    feed_back(
        r.dout, r.w_ffb_in, w_out, r.nrm_b, r.act_b, r.slope_b, r.dhid, r.dnrm, r.stage, r.left_t,
        r.w.at[rows_of("ffb_in")], w_out, emits, "ffb",
    )

    def add(rows, back):
        r.dx[rows, :] += back

    r.gains[3:4, :] = norm_rows_back(r.x2, r.small[3:4, :], r.dnrm, add)
    merge_back(r, length, emits)
    keep(r.djoin, r.keep_djoin)
    gating_back(r, length, emits)
    keep(r.dx, r.keep_dx)
    for lane in range(4):
        at = part(lane, 128)
        r.gains[5:8, at] = r.tgrad[lane, 5:8, :]
        r.w[ROW * 31 : ROW * 31 + SMALL, at] = low(r.tgrad[lane])
    r.w[ROW * 31 : ROW * 31 + 16, :] = low(
        jnp.concatenate(
            [
                jnp.zeros((8, ROW), F32),
                jnp.concatenate([r.tgrad[lane, 8:16, :] for lane in range(4)], axis=1),
            ],
            axis=0,
        )
    )
    r.w[ROW * 31 + SMALL : ROW * 32, :] = jnp.zeros((ROW - SMALL, ROW), BF16)
    emits.put_tensor("small", r.w.at[rows_of("small")])
    for copy in kept:
        copy.wait()
    emits.wait()


def attention_back(r, emits):
    def project(j):
        at = part(j, 256)
        r.dctx[:, at] = low(dot_t(r.datt[...], r.w_att[at, :]))

    each(2, project)
    weight_rows(r.ctx, r.datt, 1, r.left_t, r.w_att)
    emits.put_tensor("att_out", r.w_att)
    first_half = lax.broadcasted_iota(jnp.int32, (1, 128), 1) < HS
    at_row = lax.broadcasted_iota(jnp.int32, (SLOTS, SLOTS), 0)
    at_column = lax.broadcasted_iota(jnp.int32, (SLOTS, SLOTS), 1)
    flip = low((at_row + at_column == SLOTS - 1).astype(F32))

    def heads(pair):
        queries = r.qkv[0:SLOTS, part(pair, 128)]
        keys = r.qkv[:, part(pair + 4, 128)]
        values = r.qkv[:, part(pair + 8, 128)]
        context = r.dctx[:, part(pair, 128)]
        q_parts, k_parts, v_parts = [], [], []
        for odd in range(2):
            head = 2 * pair + odd
            half = first_half if odd == 0 else jnp.logical_not(first_half)
            chances = r.probs[head]
            v_parts.append(t_dot(chances, context)[0:SLOTS])
            wide_chances = chances.astype(F32)
            chance_grad = dot_t(jnp.where(half, context, jnp.zeros_like(context)), values)
            inner = jnp.sum(wide_chances * chance_grad, axis=-1, keepdims=True)
            score_grad = low(wide_chances * (chance_grad - inner))
            q_parts.append(dot(score_grad, keys))
            k_parts.append(t_dot(score_grad, queries)[0:SLOTS])
            wide = jnp.concatenate([dot(flip, score_grad), jnp.zeros((SLOTS, ROW - KEYS), F32)], axis=1)
            wide = pltpu.roll(wide, ROW - SLOTS + 1, 1, stride=1, stride_axis=0)
            r.sums[pl.ds(head, 1), :] = fold_rows(wide)
        scale = HS ** (-0.5)
        r.dhid[:, part(pair, 128)] = low(jnp.where(first_half, q_parts[0], q_parts[1]) * scale)
        r.dhid[:, part(pair + 4, 128)] = low(jnp.where(first_half, k_parts[0], k_parts[1]) * scale)
        r.dhid[:, part(pair + 8, 128)] = low(jnp.where(first_half, v_parts[0], v_parts[1]))

    each(H // 2, heads)

    def down(j):
        at = part(j, 256)
        r.dnrm[:, at] = dot_t(r.dhid[:, 0 : 3 * D], r.w_qkv[at, :])

    each(2, down)

    def add(rows, back):
        r.dx[rows, :] += back
        r.dout[rows, :] = low(0.5 * r.dx[rows, :])

    r.late[1:2, :] = norm_rows_back(r.x1, r.gain_rows[1:2, :], r.dnrm, add)


def attention_weights_back(r, emits):
    weight_columns(r.nrm_t, r.dhid, 3, r.stage, r.left_t, r.g_qkv)
    emits.put_tensor("qkv", r.g_qkv)
    by_entry = lax.dot_general(
        r.sums[...],
        bucket_map(),
        (((1,), (1,)), ((), ())),
        precision=lax.Precision.HIGHEST,
        preferred_element_type=F32,
    )
    flat = fold_rows(own_entries(by_entry))
    r.late[8:9, :] = flat[:, 0:ROW]
    r.late[9:10, :] = flat[:, ROW:]


def backward_kernel(names, coords, frames, gains, gain_rows, *refs):
    r = SimpleNamespace(**dict(zip(names, refs)))
    r.gain_rows = gain_rows
    waits = {}
    for at, (name, source, target) in enumerate(
        (
            ("att", r.in_att, r.w_att),
            ("djoin", r.in_djoin.at[:, 0:D], r.datt),
            ("ctx", r.in_ctx, r.ctx),
            ("heads", r.in_heads, r.qkv),
            ("probs", r.in_probs, r.probs),
            ("qkv", r.in_qkv, r.w_qkv),
            ("x1", r.in_x1, r.x1),
            ("dx", r.in_dx, r.dx),
            ("nrm_t", r.in_nrm_t, r.nrm_t),
            ("ffa_out", r.in_ffa_out, r.w_ffa_out),
            ("slope", r.in_slope, r.slope),
            ("act", r.in_act, r.act),
            ("ffa_in", r.in_ffa_in, r.w_ffa_in),
            ("nrm", r.in_nrm, r.nrm),
        )
    ):
        waits[name] = pltpu.make_async_copy(source, target, r.load_sems.at[at])
        waits[name].start()
    r.late[...] = jnp.zeros_like(r.late)
    emits = Emits(coords, ((r.low_kept, (r.low_near, r.low_far)),), r.emit_sems)
    for name in ("att", "djoin", "ctx", "heads", "probs", "qkv", "x1", "dx"):
        waits[name].wait()
    attention_back(r, emits)
    waits["nrm_t"].wait()
    attention_weights_back(r, emits)
    for name in ("ffa_out", "slope", "act", "ffa_in", "nrm"):
        waits[name].wait()
    feed_back(
        r.dout, r.w_ffa_in, r.w_ffa_out, r.nrm, r.act, r.slope, r.dhid, r.dnrm, r.stage, r.left_t, r.g_ffa_in,
        r.w_ffa_out, emits, "ffa",
    )

    def add(rows, back):
        r.fgrad[rows, :] = low(r.dx[rows, :] + back)

    r.late[0:1, :] = norm_rows_back(frames, gain_rows[0:1, :], r.dnrm, add)
    r.late[2:8, :] = gains[2:8, :]
    emits.wait()


VM = pl.BlockSpec(memory_space=pltpu.VMEM)
SM = pl.BlockSpec(memory_space=pltpu.SMEM)
ANY = pl.BlockSpec(memory_space=pl.ANY)
WIDE, THIN = ((SLOTS, D), F32), ((SLOTS, D), BF16)
FULL = ((SLOTS, FF), BF16)
KEPT, SENT = ((8, SPAN, ROW), BF16), ((4, SPAN, ROW), BF16)

FORWARD_OUT = {
    "out": (VM, THIN),
    "gains": (VM, ((8, ROW), F32)),
    "small": (VM, ((SMALL, ROW), F32)),
    "high_kept": (ANY, KEPT),
    "high_near": (ANY, SENT),
    "high_far": (ANY, SENT),
    "low_kept": (ANY, KEPT),
    "low_near": (ANY, SENT),
    "low_far": (ANY, SENT),
    "keep_ffa_in": (ANY, ((D, FF), BF16)),
    "keep_ffa_out": (ANY, ((FF, D), BF16)),
    "keep_qkv": (ANY, ((D, 3 * D), BF16)),
    "keep_att": (ANY, ((D, D), BF16)),
    "keep_nrm": (ANY, THIN),
    "keep_act": (ANY, FULL),
    "keep_slope": (ANY, FULL),
    "keep_x1": (ANY, WIDE),
    "keep_nrm_t": (ANY, THIN),
    "keep_heads": (ANY, ((KEYS, 3 * D), BF16)),
    "keep_probs": (ANY, ((H, SLOTS, KEYS), BF16)),
    "keep_ctx": (ANY, THIN),
    "keep_djoin": (ANY, ((SLOTS, 2 * D), BF16)),
    "keep_dx": (ANY, WIDE),
}
FORWARD_SCRATCH = {
    "w": ((32 * ROW, ROW), BF16),
    "w_ffa_in": ((D, FF), BF16),
    "w_qkv": ((D, 3 * D), BF16),
    "w_cg": ((D, CG), BF16),
    "w_ffb_in": ((D, FF), BF16),
    "stage": ((4, 6 * ROW, 128), F32),
    "left_t": ((ROW, SLOTS), BF16),
    "tiles": ((4, SMALL, 128), F32),
    "tgrad": ((4, SMALL, 128), F32),
    "bias": ((H, ROW), F32),
    "nrm": THIN,
    "act": FULL,
    "slope": FULL,
    "nrm_t": THIN,
    "qkv": ((KEYS, 3 * D), BF16),
    "probs": ((H, SLOTS, KEYS), BF16),
    "ctx": THIN,
    "nrm_c": THIN,
    "hid": ((SLOTS, 256), F32),
    "ug": ((SLOTS, CG), F32),
    "slope_c": ((SLOTS, CG), BF16),
    "gmean": ((SLOTS, 128), F32),
    "gscale": ((SLOTS, 128), F32),
    "gate_sums": ((8 * GATE // 128, 128), F32),
    "gpad": ((PADDED, GATE), F32),
    "cv": ((SLOTS, GATE), BF16),
    "gated": ((SLOTS, GATE), BF16),
    "cat": ((SLOTS, 2 * D), F32),
    "mpad": ((PADDED, 2 * D), F32),
    "mixed": ((SLOTS, 2 * D), BF16),
    "nrm_b": THIN,
    "act_b": FULL,
    "slope_b": FULL,
    "dpad": ((PADDED, GATE), F32),
    "djoin": ((SLOTS, 2 * D), BF16),
    "dgate": ((SLOTS, GATE), F32),
    "dhid": ((SLOTS, CG), BF16),
    "dnrm": WIDE,
    "dout": THIN,
    "dx": WIDE,
    "x1": WIDE,
    "x2": WIDE,
    "x3": WIDE,
    "seams": ((PARTS + 1, 2, TILE, ROW), BF16),
    "load_sems": PARTS,
    "keep_sems": 16,
    "emit_sems": 40,
}
BACKWARD_IN = (
    "ffa_in", "ffa_out", "qkv", "att", "nrm", "act", "slope", "x1", "nrm_t", "heads", "probs", "ctx", "djoin", "dx",
)
PASSED = ("low_kept", "low_near", "low_far")
BACKWARD_OUT = {
    "fgrad": (VM, THIN),
    "late": (VM, ((16, ROW), F32)),
    "low_kept": (ANY, KEPT),
    "low_near": (ANY, SENT),
    "low_far": (ANY, SENT),
}
BACKWARD_SCRATCH = {
    "w_ffa_in": ((D, FF), BF16),
    "w_ffa_out": ((FF, D), BF16),
    "w_qkv": ((D, 3 * D), BF16),
    "w_att": ((D, D), BF16),
    "g_ffa_in": ((FF, D), BF16),
    "g_qkv": ((3 * D, D), BF16),
    "stage": ((4, 4 * ROW, 128), F32),
    "left_t": ((ROW, SLOTS), BF16),
    "sums": ((H, ROW), F32),
    "nrm": THIN,
    "act": FULL,
    "slope": FULL,
    "nrm_t": THIN,
    "qkv": ((KEYS, 3 * D), BF16),
    "probs": ((H, SLOTS, KEYS), BF16),
    "ctx": THIN,
    "datt": THIN,
    "dctx": THIN,
    "dhid": FULL,
    "dnrm": WIDE,
    "dout": THIN,
    "dx": WIDE,
    "x1": WIDE,
    "load_sems": 14,
    "emit_sems": 24,
}


def call(kernel, name, ins, outs, scratch, limit, aliases=None):
    return pl.pallas_call(
        kernel,
        name=name,
        in_specs=[space for space, _ in ins],
        out_specs=[space for space, _ in outs],
        out_shape=[jax.ShapeDtypeStruct(*kind) for _, kind in outs],
        scratch_shapes=[
            pltpu.SemaphoreType.DMA((each_one,)) if isinstance(each_one, int) else pltpu.VMEM(*each_one)
            for each_one in scratch
        ],
        input_output_aliases=aliases or {},
        compiler_params=pltpu.CompilerParams(vmem_limit_bytes=limit * 2**20),
    )(*[array for _, array in ins])


def forward(coords, length, frames, cot, blocks):
    def kernel(*refs):
        forward_kernel([*FORWARD_OUT, *FORWARD_SCRATCH], *refs)

    outs = call(
        kernel,
        "forward",
        [(SM, coords), (SM, length), (VM, frames), (VM, cot)] + [(ANY, block) for block in blocks],
        list(FORWARD_OUT.values()),
        list(FORWARD_SCRATCH.values()),
        58,
    )
    return dict(zip(FORWARD_OUT, outs))


def backward(coords, frames, state):
    def kernel(*refs):
        names = ["in_" + name for name in BACKWARD_IN + PASSED]
        backward_kernel([*names, *BACKWARD_OUT, *BACKWARD_SCRATCH], *refs)

    ins = [(SM, coords), (VM, frames), (VM, state["gains"]), (VM, state["small"])]
    ins += [(ANY, state["keep_" + name]) for name in BACKWARD_IN]
    ins += [(ANY, state[name]) for name in PASSED]
    outs = call(
        kernel,
        "backward",
        ins,
        list(BACKWARD_OUT.values()),
        list(BACKWARD_SCRATCH.values()),
        58,
        {len(ins) - 3 + at: 2 + at for at in range(3)},
    )
    return dict(zip(BACKWARD_OUT, outs))


def segment_bounds():
    bounds = [0]
    for extent in segment_shapes():
        bounds.append(bounds[-1] + math.prod(extent))
    return bounds


def fast_mesh():
    return lax.axis_size("dp") == 4 and lax.axis_size("fsdp") == 8


def over_x(value):
    return lax.ppermute(value, "fsdp", [(i, i ^ 1) for i in range(8)])


def over_y(value):
    return lax.ppermute(value, "dp", [(i, i ^ 2) for i in range(4)])


def over_core(value):
    return lax.ppermute(value, "dp", [(i, i ^ 1) for i in range(4)])


def round_z(value):
    return lax.ppermute(value, "fsdp", [(i, (i + 2) % 8) for i in range(8)])


def over_z(value, step):
    return lax.ppermute(value, "fsdp", [(i, i ^ (2 * step)) for i in range(8)])


def after(value, *others):
    return lax.optimization_barrier((value, *others))[0]


def shard_offset(me, shard_size):
    return me * shard_size - start_of(me) * ROW


def gather_shards(shard, me):
    shard_size = shard.shape[0]
    if not fast_mesh():
        whole = lax.all_gather(shard, AXES, axis=0, tiled=True)
        whole = jnp.pad(whole, (0, (STARTS[-1] + SPAN) * ROW - whole.shape[0])).reshape(-1, ROW)
        spans = [whole[start : start + SPAN] for start in STARTS[:-1]]
        spans = spans[:1] + [jnp.concatenate([jnp.zeros((TILE, ROW), BF16), span[TILE:]]) for span in spans[1:]]
        return [
            jnp.concatenate([spans[source_part((0, 0, 0, 0), piece)][piece[4] : piece[5]] for piece in pieces])
            for pieces in LAYOUT
        ]
    most = TILE * ROW
    padded = jnp.pad(shard, (most, SPAN * ROW - shard_size))
    span = lax.dynamic_slice(padded, (most - shard_offset(me, shard_size),), (SPAN * ROW,)).reshape(SPAN, ROW)
    own, by_x, by_y = [span], [], []
    for back in range(4):
        if back < 3:
            own.append(round_z(own[back]))
        if back < 2:
            by_x.append(over_x(own[back]))
            by_y.append(over_y(own[back]))
            own[back + 1], by_x[back], by_y[back] = lax.optimization_barrier((own[back + 1], by_x[back], by_y[back]))
        else:
            by_x.append(over_x(jnp.concatenate([own[back], by_y[back - 2][:HALF]])))
            by_y.append(over_y(jnp.concatenate([own[back], by_x[back - 2][HALF:SPAN]])))
    by_x.append(over_x(jnp.concatenate([by_y[2][:HALF], by_y[3][:HALF]])))
    by_y.append(over_y(jnp.concatenate([by_x[2][HALF:SPAN], by_x[3][HALF:SPAN]])))
    late_ones = (by_x[3], by_y[3])
    far_own = [over_core(each_one) for each_one in own[:2]] + [over_core(after(each_one, *late_ones)) for each_one in own[2:]]
    far = [far_own]
    for way in (by_x, by_y):
        far.append([over_core(way[0]), over_core(way[1]), over_core(after(way[2], *late_ones))])
        far[-1] += [over_core(way[at]) for at in (3, 4)]
    return own + by_x + by_y + far[0] + far[1] + far[2]


def added(*parts):
    total = parts[0].astype(F32)
    for each_one in parts[1:]:
        total = total + each_one.astype(F32)
    return total


SIDES = (slice(0, HALF), slice(HALF, SPAN))


HBM = pl.BlockSpec(memory_space=pltpu.HBM)


def span_sums(coords, own_half, x, places, low_kept, low_got, high_kept, high_got, sides):
    count = len(places)
    together = sides if isinstance(sides, int) else 0
    pieces = [(at, rows) for at in range(count) for rows in (() if together else sides)]

    def kernel(coords, low_kept, low_got, high_kept, high_got, *refs):
        outs, (kept, got, total, sems, out_sems) = refs[:-5], refs[-5:]
        high = coords[0] == int(own_half)
        for source, other, wanted in ((low_kept, low_got, jnp.logical_not(high)), (high_kept, high_got, high)):

            @pl.when(wanted)
            def _(source=source, other=other):
                for at, place in enumerate(places):
                    pltpu.make_async_copy(source.at[4 * x + place], kept.at[at], sems.at[2 * at]).start()
                    pltpu.make_async_copy(other.at[place], got.at[at], sems.at[2 * at + 1]).start()

        copies = []
        for at in range(count):
            pltpu.make_async_copy(low_kept.at[at], kept.at[at], sems.at[2 * at]).wait()
            pltpu.make_async_copy(low_got.at[at], got.at[at], sems.at[2 * at + 1]).wait()

            def add(k, at=at):
                rows = part(k, SPAN // 11)
                total[at, rows] = low(kept[at, rows].astype(F32) + got[at, rows].astype(F32))

            each_loop(11, add)
            if together:
                out = outs[at // together].at[at % together]
                copies.append(pltpu.make_async_copy(total.at[at], out, out_sems.at[at]))
                copies[-1].start()
            for which, (mine, rows) in enumerate(pieces):
                if mine == at:
                    copies.append(pltpu.make_async_copy(total.at[at, rows], outs[which], out_sems.at[which]))
                    copies[-1].start()
        for copy in copies:
            copy.wait()

    spans = ((count, SPAN, ROW), BF16)
    arrays = [(HBM, low_kept), (ANY, low_got), (HBM, high_kept), (ANY, high_got)]
    if together:
        outs = [(ANY, ((together, SPAN, ROW), BF16))] * (count // together)
    else:
        outs = [(ANY, ((rows.stop - rows.start, ROW), BF16)) for _, rows in pieces]
    sums = call(
        kernel, "span_sums", [(SM, coords)] + arrays, outs, [spans] * 3 + [2 * count, max(count, len(pieces))], 56
    )
    return sums if together else [sums[len(sides) * at : len(sides) * (at + 1)] for at in range(count)]


def late_rows(late, above, below):
    gains = jnp.pad(late[0:8], ((above, below - 8), (0, 0)))
    return gains + jnp.pad(late[8:10], ((above + REL_AT, below - REL_AT - 2), (0, 0)))


def scatter_slow(state, back, shard_size, padded):
    late = back["late"]
    pieces = []
    for source, half in ((back, "low"), (state, "high")):
        for core in range(2):
            for at in range(8):
                z, x = at // 2, at % 2
                if core == 0:
                    span = source[half + "_kept"][4 * x + 3 - z]
                else:
                    span = source[half + ("_near", "_far")[x]][3 - z]
                d = len(pieces)
                pieces.append(span[: STARTS[d + 1] - STARTS[d] if d < PARTS - 1 else SPAN])
    rows = jnp.concatenate(pieces)
    first = ROW * BLOCK["small"][0]
    rows = low(rows.astype(F32) + late_rows(late, first, rows.shape[0] - first))
    flat = rows.reshape(-1)[: segment_bounds()[-1]]
    shard = lax.psum_scatter(flat, AXES, scatter_dimension=0, tiled=True)
    return jnp.pad(shard, (0, padded - shard_size)).astype(F32), lax.psum(late[0:8], AXES)


def scatter_grads(state, back, coords, me, shard_size, padded):
    if not fast_mesh():
        return scatter_slow(state, back, shard_size, padded)
    high = coords[0] == 1
    high_kept, low_kept = state["high_kept"], back["low_kept"]
    high_got = [over_core(state["high_near"]), over_core(state["high_far"])]
    low_far = over_core(back["low_far"])

    def chip_sum(own_half, x, places, sides):
        got = (low_far if x else low_near, high_got[x])
        return span_sums(coords, own_half, x, places, low_kept, got[0], high_kept, got[1], sides)

    for_y, for_x = chip_sum(False, 1, range(4), 2)
    from_x, from_y = over_x(for_x), over_y(for_y)
    low_near = over_core(after(back["low_near"], for_x, for_y))
    to_x, to_y, mine = [
        chip_sum(own_half, x, range(4), SIDES) for own_half, x in ((True, 1), (False, 0), (True, 0))
    ]
    late = after(back["late"], mine[3][1], to_x[3][1], to_y[3][1])
    late = late + over_core(late)
    late = late + over_z(late, 1)
    late = late + over_z(late, 2)
    from_x, from_y, to_x, to_y, mine, late = lax.optimization_barrier((from_x, from_y, to_x, to_y, mine, late))
    late = late + over_x(late)
    late = late + over_y(late)
    running = [None, None]
    before = [(), ()]
    for at in range(4):
        for side, rows in enumerate(SIDES):
            send_x, send_y = to_x[at][side], to_y[at][side]
            if at < 2:
                send_x = low(added(send_x, from_y[at, rows]))
            else:
                send_y = low(added(send_y, from_x[at - 2, rows]))
            got_x, got_y = over_x(after(send_x, *before[side])), over_y(after(send_y, *before[side]))
            before[side] = (got_x, got_y)
            parts = [mine[at][side], got_x, got_y]
            if at:
                parts.append(round_z(running[side]))
            running[side] = added(*parts)
            if at < 3:
                running[side] = low(running[side])
    total = jnp.concatenate(running)
    first = ROW * BLOCK["small"][0] - STARTS[PARTS - 1]
    total = total + jnp.where(me == PARTS - 1, 1.0, 0.0) * late_rows(late, first, SPAN - first)
    flat = jnp.pad(total.reshape(-1), (0, max(0, TILE * ROW + padded - SPAN * ROW)))
    return lax.dynamic_slice(flat, (shard_offset(me, shard_size),), (padded,)), late[0:8]


def sum_everywhere(vector):
    if not fast_mesh():
        return lax.psum(vector, AXES)
    vector = vector + over_core(vector)
    vector = vector + over_x(vector)
    vector = vector + over_y(vector)
    vector = vector + over_z(vector, 1)
    return vector + over_z(vector, 2)


def most_segments(shard_size, devices):
    bounds = segment_bounds()
    most = 1
    for at in range(devices):
        low_end, high_end = at * shard_size, (at + 1) * shard_size
        most = max(most, sum(1 for b in bounds[1:-1] if low_end < b < high_end) + 1)
    return most


LANES = 128
CHUNK = 1024 * LANES
STRIP = 128 * LANES


def chunk_spans(segments, step):
    first, last = step * CHUNK, (step + 1) * CHUNK
    for at in range(segments.shape[0] - 2):
        start, end = segments[1 + at], segments[2 + at]
        whole = (start <= first) & (last <= end)
        some = (start < last) & (end > first) & jnp.logical_not(whole)
        yield at, whole, some, start - first, end - first


def strips(body, start=None):
    return lax.fori_loop(0, CHUNK // STRIP, lambda at, carry: body(part(at, STRIP), at * STRIP, carry), start)


def square(entries, strip):
    return entries[strip].reshape(STRIP // LANES, LANES)


def inside(place, start, end):
    row = lax.broadcasted_iota(jnp.int32, (STRIP // LANES, LANES), 0)
    place = place + row * LANES + lax.broadcasted_iota(jnp.int32, (STRIP // LANES, LANES), 1)
    return (place >= start) & (place < end)


def fold(values):
    return jnp.sum(values.reshape(-1, 8, LANES), axis=0)


def update_kernel(segments, params, first, second, grad, new_first, new_second, update, sums):
    step = pl.program_id(0)
    nothing = jnp.zeros((8, LANES), F32)

    @pl.when(step == 0)
    def _():
        sums[...] = nothing

    def move(strip, place, totals):
        grads = grad[strip]
        firsts = BETA_FIRST * first[strip] + (1.0 - BETA_FIRST) * grads
        seconds = BETA_SECOND * second[strip] + (1.0 - BETA_SECOND) * grads * grads
        new_first[strip] = firsts
        new_second[strip] = seconds
        first_hat = firsts * (1.0 / (1.0 - BETA_FIRST**STEP))
        second_hat = seconds * (1.0 / (1.0 - BETA_SECOND**STEP))
        weights = params[strip]
        change = first_hat / (jnp.sqrt(second_hat) + ADAM_EPS) + WEIGHT_DECAY * weights
        update[strip] = change
        squares = [(each_one * each_one).reshape(STRIP // LANES, LANES) for each_one in (weights, change)]
        return totals[0] + fold(squares[0]), totals[1] + fold(squares[1])

    totals = strips(move, (nothing, nothing))
    lane = lax.broadcasted_iota(jnp.int32, (1, LANES), 1)

    def add(at, totals):
        for row, total in enumerate(totals):
            total = jnp.sum(jnp.sum(total, axis=0, keepdims=True), axis=1, keepdims=True)
            sums[row : row + 1, :] += jnp.where(lane == segments[0] + at, total, 0.0)

    for at, whole, some, start, end in chunk_spans(segments, step):

        @pl.when(whole)
        def _(at=at):
            add(at, totals)

        @pl.when(some)
        def _(at=at, start=start, end=end):
            def squares(strip, place, totals):
                here = inside(place, start, end)
                own = [square(entries, strip) for entries in (params, update)]
                own = [fold(jnp.where(here, each_one * each_one, 0.0)) for each_one in own]
                return totals[0] + own[0], totals[1] + own[1]

            add(at, strips(squares, (nothing, nothing)))


def apply_kernel(segments, sums, params, update, new_params, *norms):
    step = pl.program_id(0)
    roots = jnp.sqrt(sums[0:2, :])
    trust = roots[0:1, :] / (roots[1:2, :] + ADAM_EPS)
    for out, row in zip(norms, (roots[0:1, :], roots[1:2, :], trust)):
        out[...] = row.reshape(LANES)[: out.shape[0]]
    lane = lax.broadcasted_iota(jnp.int32, (1, LANES), 1)
    for at, whole, some, start, end in chunk_spans(segments, step):

        scale = LEARN_RATE * jnp.sum(jnp.where(lane == segments[0] + at, trust, 0.0), axis=1, keepdims=True)
        scale = jnp.broadcast_to(scale, (1, LANES))

        def moved(strip, scale=scale):
            return square(params, strip) - scale * square(update, strip)

        @pl.when(whole)
        def _(moved=moved):
            def all_of(strip, place, carry):
                new_params[strip] = moved(strip).reshape(STRIP)
                return carry

            strips(all_of, 0)

        @pl.when(some)
        def _(moved=moved, start=start, end=end):
            def part_of(strip, place, carry):
                chosen = jnp.where(inside(place, start, end), moved(strip), square(new_params, strip))
                new_params[strip] = chosen.reshape(STRIP)
                return carry

            strips(part_of, 0)


def shards(frames, lengths, cotangent, params, first_moment, second_moment):
    shard_size = params.shape[0]
    devices = lax.axis_size("dp") * lax.axis_size("fsdp")
    me = lax.axis_index(AXES)
    if fast_mesh():
        dp, fsdp = lax.axis_index("dp"), lax.axis_index("fsdp")
        coords = jnp.stack([dp // 2, dp % 2, fsdp // 2, fsdp % 2]).astype(jnp.int32)
    else:
        coords = jnp.zeros((4,), jnp.int32)
    state = forward(coords, lengths, frames[0], cotangent[0], gather_shards(low(params), me))
    back = backward(coords, frames[0], state)
    steps = -(-shard_size // CHUNK)
    size = max(shard_size, CHUNK)
    grad_shard, gain_grads = scatter_grads(state, back, coords, me, shard_size, size)

    def filled(flat):
        return jnp.pad(flat, (0, size - shard_size)) if size > shard_size else flat

    bounds = segment_bounds()
    spans = most_segments(shard_size, devices)
    shard_low = me * shard_size
    first_segment = sum((shard_low >= b).astype(jnp.int32) for b in bounds[1:-1])
    table = jnp.asarray(bounds[1:] + [bounds[-1]] * spans, jnp.int32)
    ends = jnp.clip(lax.dynamic_slice(table, (first_segment,), (spans,)) - shard_low, 0, shard_size)
    segments = jnp.concatenate([first_segment[None], jnp.zeros((1,), jnp.int32), ends]).astype(jnp.int32)
    grid = pl.BlockSpec((CHUNK,), lambda step: (step,))
    whole = pl.BlockSpec((8, LANES), lambda step: (0, 0))
    flat_kind = jax.ShapeDtypeStruct((size,), F32)
    tile_kind = jax.ShapeDtypeStruct((8, LANES), F32)
    weights = filled(params)
    new_first, new_second, update, sums = pl.pallas_call(
        update_kernel,
        name="update",
        grid=(steps,),
        in_specs=[SM] + [grid] * 4,
        out_specs=[grid] * 3 + [whole],
        out_shape=[flat_kind] * 3 + [tile_kind],
    )(segments, weights, filled(first_moment), filled(second_moment), grad_shard)
    sums = sum_everywhere(sums)
    count = len(segment_shapes())
    new_params, *norms = pl.pallas_call(
        apply_kernel,
        name="apply",
        grid=(steps,),
        in_specs=[SM, whole, grid, grid],
        out_specs=[grid] + [pl.BlockSpec((count,), lambda step: (0,))] * 3,
        out_shape=[flat_kind] + [jax.ShapeDtypeStruct((count,), F32)] * 3,
    )(segments, sums, weights, update)
    return (
        state["out"].reshape(frames.shape),
        back["fgrad"].reshape(frames.shape),
        new_params[:shard_size],
        new_first[:shard_size],
        new_second[:shard_size],
        *norms,
        gain_grads.reshape(-1),
    )


def solution(mesh):
    placed = (
        P(("dp", "fsdp"), None, None),
        P(("dp", "fsdp")),
        P(("dp", "fsdp"), None, None),
        P(("dp", "fsdp")),
        P(("dp", "fsdp")),
        P(("dp", "fsdp")),
    )
    return jax.shard_map(
        shards,
        mesh=mesh,
        in_specs=placed,
        out_specs=(
            P(("dp", "fsdp"), None, None),
            P(("dp", "fsdp"), None, None),
            P(("dp", "fsdp")),
            P(("dp", "fsdp")),
            P(("dp", "fsdp")),
            P(),
            P(),
            P(),
            P(),
        ),
        check_vma=False,
    )
```

```python
import math
from types import SimpleNamespace

import jax
import jax.numpy as jnp
from jax import lax
from jax.experimental import pallas as pl
from jax.experimental.pallas import tpu as pltpu
from jax.sharding import PartitionSpec as P

STEP = 8
BETA_FIRST = 0.5
BETA_SECOND = 0.5
LEARN_RATE = 0.5
WEIGHT_DECAY = 0.01
ADAM_EPS = 1e-06
AXES = ("dp", "fsdp")


def segment_shapes():
    gate_width = CG // 2
    return [
        (D, FF),
        (FF, D),
        (D, 3 * D),
        (D, D),
        (D, CG),
        (gate_width, D),
        (2 * D, D),
        (D, FF),
        (FF, D),
        (5 * D + gate_width,),
        (KER, gate_width + 2 * D),
        (RELW, H),
    ]


D = 512
H = 8
HS = 64
FF = 2048
CG = 3072
KER = 31
RELW = 128
NORM_EPS = 1e-05
MASK_FILL = -1000000000.0
ROW = 512
HALF = ROW // 2
SLOTS = 160
KEYS = 256
PAD = 16
PADDED = SLOTS + 2 * PAD
GATE = CG // 2
BLOCK = {
    "ffa_in": (0, 4),
    "ffa_out": (4, 4),
    "qkv": (8, 3),
    "att_out": (11, 1),
    "cg_in": (12, 6),
    "cg_out": (18, 3),
    "merge": (21, 2),
    "ffb_in": (23, 4),
    "ffb_out": (27, 4),
    "small": (31, 1),
}
TAPS_AT = 8
REL_AT = 8 + 5 * KER
SMALL = 176
F32, BF16 = jnp.float32, jnp.bfloat16


def dot(left, right):
    return lax.dot_general(left, right, (((1,), (0,)), ((), ())), preferred_element_type=F32)


def dot_t(left, right):
    return lax.dot_general(left, right, (((1,), (1,)), ((), ())), preferred_element_type=F32)


def t_dot(left, right):
    return lax.dot_general(left, right, (((0,), (0,)), ((), ())), preferred_element_type=F32)


def low(values):
    return values.astype(BF16)


def each(count, body):
    for at in range(count):
        body(at)


def each_loop(count, body, together=1):
    def step(at, carry):
        for inner in range(together):
            body(at * together + inner)
        return carry

    lax.fori_loop(0, count // together, step, 0)


def part(at, size):
    if isinstance(at, int):
        return slice(at * size, at * size + size)
    return pl.ds(pl.multiple_of(at * size, size), size)


def rows_of(name):
    first, count = BLOCK[name]
    return slice(ROW * first, ROW * (first + count))


def lane_mean(values, width):
    return jnp.sum(values, axis=-1, keepdims=True) * (1.0 / width)


def normed(values):
    centered = values - lane_mean(values, values.shape[-1])
    scale = lax.rsqrt(lane_mean(centered * centered, values.shape[-1]) + NORM_EPS)
    return centered * scale, scale


def valid_rows(length):
    return (lax.broadcasted_iota(jnp.int32, (SLOTS, 1), 0) < length).astype(F32)


def fold_rows(values):
    return jnp.sum(values, axis=0, keepdims=True)


def norm_rows(source, gain, target):
    for k in range(2):
        hat, _ = normed(source[part(k, 80), :].astype(F32))
        target[part(k, 80), :] = low(hat * gain)


def norm_rows_back(values, gain, grad, add):
    total = jnp.zeros((1, values.shape[1]), F32)
    for k in range(2):
        rows = part(k, 80)
        hat, scale = normed(values[rows, :].astype(F32))
        mine = grad[rows, :]
        total = total + fold_rows(mine * hat)
        inner = mine * gain
        width = values.shape[1]
        moved = lane_mean(inner, width) + hat * lane_mean(inner * hat, width)
        add(rows, scale * (inner - moved))
    return total


TOTAL_ROWS = 16037
PARTS = 32
TILE = 16
SPAN = 528
STARTS = [TILE * (TOTAL_ROWS * d // (PARTS * TILE)) for d in range(PARTS + 1)]
FIRST_PARTS = max(d for d in range(PARTS) if STARTS[d] < ROW * sum(BLOCK["ffa_out"]))
SHORTEST = min(high - first for first, high in zip(STARTS, STARTS[1:]))


def start_of(d):
    return ((TOTAL_ROWS * d) >> 9) * TILE


def gathered_layout():
    layout = []
    for core in range(2):
        layout += [[(core, 0, 0, back, 0, SPAN, 0)] for back in range(4)]
        for y, x, first, last in ((0, 1, 0, HALF), (1, 0, HALF, SPAN)):
            whole = [(core, y, x, back, 0, SPAN, 0) for back in range(4)]
            diagonal = [(core, 1, 1, back, first, last) for back in range(4)]
            layout += [[whole[0]], [whole[1]]]
            layout += [[whole[2], (*diagonal[0], SPAN)], [whole[3], (*diagonal[1], SPAN)]]
            layout += [[(*diagonal[2], 0), (*diagonal[3], last - first)]]
    return layout


LAYOUT = gathered_layout()


def source_part(coords, piece):
    y, c, z, x = coords[0], coords[1], coords[2], coords[3]
    yy, cc, xx, zz = y ^ piece[1], c ^ piece[0], x ^ piece[2], (z + 4 - piece[3]) & 3
    return ((yy * 2 + cc) * 4 + zz) * 2 + xx


class Loads:
    def __init__(self, coords, sources, target, seams, sems):
        self.target, self.seams, self.sems = target, seams, sems
        self.here, self.joined = set(), set()
        seams[0, 0] = jnp.zeros((TILE, ROW), BF16)
        seams[PARTS, 1] = jnp.zeros((TILE, ROW), BF16)

        for soon in (True, False):
            for pieces, source in zip(LAYOUT, sources):
                for piece in pieces:
                    d = source_part(coords, piece)
                    first_ones = (d <= FIRST_PARTS) | (d == PARTS - 1)

                    @pl.when(first_ones if soon else jnp.logical_not(first_ones))
                    def _(piece=piece, source=source, d=d):
                        self.start(piece, source, d)

    def start(self, piece, source, d):
        def rows(at, size):
            return pl.ds(pl.multiple_of(at, TILE), size)

        first, last, offset = piece[4:]
        offset = offset - first
        start = start_of(d)
        length = start_of(d + 1) - start
        inner, outer = max(first, TILE), min(last, SHORTEST)
        sem = self.sems.at[d]
        pltpu.make_async_copy(
            source.at[offset + inner : offset + outer], self.target.at[rows(start + inner, outer - inner)], sem
        ).start()
        if first == 0:
            pltpu.make_async_copy(source.at[offset : offset + TILE], self.seams.at[d, 1], sem).start()
        if last == SPAN:

            @pl.when(length > SHORTEST)
            def _():
                pltpu.make_async_copy(
                    source.at[offset + SHORTEST : offset + SHORTEST + TILE],
                    self.target.at[rows(start + SHORTEST, TILE)],
                    sem,
                ).start()

            pltpu.make_async_copy(source.at[rows(offset + length, TILE)], self.seams.at[d + 1, 0], sem).start()

    def wait_part(self, d):
        if d in self.here or not 0 <= d < PARTS:
            return
        self.here.add(d)
        size = STARTS[d + 1] - STARTS[d] + TILE
        pltpu.make_async_copy(self.target.at[0:size], self.target.at[0:size], self.sems.at[d]).wait()

    def wait(self, name):
        rows = rows_of(name)
        last = min(rows.stop, STARTS[-1] + TILE)
        for d in range(PARTS + 1):
            if STARTS[d] < last and STARTS[d] + TILE > rows.start and d not in self.joined:
                self.wait_part(d - 1)
                self.wait_part(d)
                self.joined.add(d)
                self.target[STARTS[d] : STARTS[d] + TILE, :] = self.seams[d, 0] + self.seams[d, 1]
            if d < PARTS and STARTS[d] + TILE < last and STARTS[d + 1] > rows.start:
                self.wait_part(d)


class Emits:
    def __init__(self, coords, halves, sems):
        self.coords, self.halves, self.sems = coords, halves, sems
        self.pending = []

    def put(self, d, values, rows):
        core, z, x = (d // 8) % 2, (d // 2) % 4, d % 2
        kept, sent = self.halves[d // 16]
        far_x = self.coords[3] ^ x
        place = (self.coords[2] + 3 - z) & 3
        sem = self.sems.at[len(self.pending)]

        @pl.when(self.coords[1] == core)
        def _():
            pltpu.make_async_copy(values, kept.at[4 * far_x + place, rows], sem).start()

        @pl.when((self.coords[1] != core) & (far_x == 0))
        def _():
            pltpu.make_async_copy(values, sent[0].at[place, rows], sem).start()

        @pl.when((self.coords[1] != core) & (far_x == 1))
        def _():
            pltpu.make_async_copy(values, sent[1].at[place, rows], sem).start()

        self.pending.append(pltpu.make_async_copy(values, kept.at[0, rows], sem))

    def put_tensor(self, name, values):
        rows = rows_of(name)
        for d in range(PARTS):
            first, last = max(rows.start, STARTS[d]), min(rows.stop, STARTS[d] + SPAN)
            if first < last:
                self.put(d, values.at[first - rows.start : last - rows.start], slice(first - STARTS[d], last - STARTS[d]))

    def wait(self):
        for copy in self.pending:
            copy.wait()


def split_columns(raw, target, wide, stage):
    def chunk(k):
        rows = part(k, 128 * wide)
        for lane in range(4):
            stage[lane, 0 : 128 * wide, :] = raw[rows, lane * 128 : lane * 128 + 128].astype(F32)
        for c in range(wide):
            for lane in range(4):
                place = ROW * c + lane * 128
                target[part(k, 128), place : place + 128] = low(stage[lane, pl.ds(c, 128, stride=wide), :])

    each_loop(4, chunk)


def weight_columns(left, grads, wide, stage, left_t, target):
    left_t[...] = left[...].T

    def chunk(j):
        value = dot(left_t[...], grads[:, part(j, 256)])
        c, pair = j // 2, (j % 2) * 2
        for half in range(2):
            stage[pair + half, pl.ds(c, ROW, stride=wide), :] = value[:, 128 * half : 128 * half + 128]

    each(2 * wide, chunk)

    def lower(k):
        rows = part(k, ROW)
        for lane in range(4):
            target[rows, lane * 128 : lane * 128 + 128] = low(stage[lane, rows, :])

    each(wide, lower)


def weight_rows(left, grads, count, left_t, target):
    def chunk(k):
        left_t[...] = left[:, part(k, ROW)].T
        for at in range(2):
            target[part(k, ROW), 256 * at : 256 * at + 256] = low(dot(left_t[...], grads[:, 256 * at : 256 * at + 256]))

    each(count, chunk)


def feed_forward(inputs, gain, w_in, w_out, nrm, act, slope, result):
    norm_rows(inputs, gain, nrm)

    def up(j):
        at = part(j, 256)
        hidden = dot(nrm[...], w_in[:, at])
        sig = jax.nn.sigmoid(hidden)
        active = hidden * sig
        act[:, at] = low(active)
        slope[:, at] = low(sig + active * (1.0 - sig))

    each(FF // 256, up)

    def down(j):
        at = part(j, 256)
        result[:, at] = inputs[:, at].astype(F32) + 0.5 * dot(act[...], w_out[:, at])

    each(2, down)


def feed_back(dout, w_in, w_out, nrm, act, slope, dhid, dnrm, stage, left_t, g_in, g_out, emits, name):
    def up(j):
        at = part(j, 256)
        grad = dot_t(dout[...], w_out[at, :])
        dhid[:, at] = low(grad * slope[:, at].astype(F32))

    each(FF // 256, up)
    weight_rows(act, dout, 4, left_t, g_out)
    emits.put_tensor(name + "_out", g_out)

    def down(j):
        at = part(j, 256)
        dnrm[:, at] = dot_t(dhid[:, 0:FF], w_in[at, :])

    each(2, down)
    weight_columns(nrm, dhid, 4, stage, left_t, g_in)
    emits.put_tensor(name + "_in", g_in)


def bucket_map():
    entry = lax.broadcasted_iota(jnp.int32, (2 * ROW, ROW), 0) // H
    far = lax.broadcasted_iota(jnp.int32, (2 * ROW, ROW), 1)
    far = jnp.where(far >= ROW // 2, far - ROW, far)
    bucket = jnp.clip(far, -(RELW // 2), RELW // 2 - 1) + RELW // 2
    return (entry == bucket).astype(F32)


def own_entries(flat):
    entry = lax.broadcasted_iota(jnp.int32, (H, 2 * ROW), 1)
    head = lax.broadcasted_iota(jnp.int32, (H, 2 * ROW), 0)
    return jnp.where(lax.rem(entry, H) == head, flat, 0.0)


def tap_row(small, tap, row, lane):
    return small[lane, pl.ds(TAPS_AT + 5 * tap + row, 1), :]


def shifted_sum(padded, at, factor):
    total = None
    for low_part in range(8):
        slab = padded[low_part : low_part + SLOTS + 24, at]
        inner = None
        for high_part in range(4):
            offset = 8 * high_part + low_part
            if offset:
                term = factor(offset) * slab[8 * high_part : 8 * high_part + SLOTS]
                inner = term if inner is None else inner + term
        total = inner if total is None else total + inner
    return total


def convolve(padded, small, first_row, width, finish):

    def chunk(j):
        at = part(j, 128)
        row, lane = first_row + j // 4, j % 4
        finish(j, at, shifted_sum(padded, at, lambda offset: tap_row(small, offset - 1, row, lane)))

    each_loop(width // 128, chunk)


def convolve_back(grads, padded, small, first_row, width, sgrad, finish):

    def chunk(j):
        at = part(j, 128)
        row, lane = first_row + j // 4, j % 4
        finish(j, at, shifted_sum(grads, at, lambda offset: tap_row(small, KER - offset, row, lane)))
        own = grads[PAD : PAD + SLOTS, at]
        for low_part in range(8):
            slab = padded[low_part : low_part + SLOTS + 24, at]
            for high_part in range(4):
                offset = 8 * high_part + low_part
                if offset:
                    tile = slab[8 * high_part : 8 * high_part + SLOTS]
                    sgrad[lane, pl.ds(TAPS_AT + 5 * (offset - 1) + row, 1), :] = fold_rows(own * tile)

    each_loop(width // 128, chunk)


def clear_margins(padded):
    padded[0:PAD, :] = jnp.zeros((PAD, padded.shape[1]), F32)
    padded[PAD + SLOTS : PADDED, :] = jnp.zeros((PAD, padded.shape[1]), F32)


def gelu_parts(hidden):
    bell = jnp.exp(-0.5 * hidden * hidden)
    spread = 1.0 + (0.3275911 * 2.0**-0.5) * jnp.abs(hidden)
    near = pl.reciprocal(spread, approx=True)
    near = near * (2.0 - spread * near)
    tail = jnp.full_like(near, 0.5 * 1.061405429)
    for factor in (-1.453152027, 1.421413741, -0.284496736, 0.254829592):
        tail = tail * near + 0.5 * factor
    tail = tail * near * bell
    below = jnp.where(hidden >= 0.0, 1.0 - tail, tail)
    return hidden * below, below + hidden * bell * ((2.0 * math.pi) ** -0.5)


def attention_forward(r, length):
    norm_rows(r.x1, r.small[1:2, :], r.nrm_t)
    r.qkv[SLOTS:KEYS, :] = jnp.zeros((KEYS - SLOTS, 3 * D), BF16)
    flat = jnp.concatenate([r.small[REL_AT : REL_AT + 1, :], r.small[REL_AT + 1 : REL_AT + 2, :]], axis=1)
    r.bias[...] = dot(low(own_entries(jnp.broadcast_to(flat, (H, 2 * ROW)))), low(bucket_map()))

    def project(j):
        at = part(j, 256)
        r.qkv[0:SLOTS, at] = low(dot(r.nrm_t[...], r.w_qkv[:, at]))

    each(3 * D // 256, project)
    valid = lax.broadcasted_iota(jnp.int32, (1, KEYS), 1) < length
    first_half = lax.broadcasted_iota(jnp.int32, (1, 128), 1) < HS

    def heads(pair):
        queries = r.qkv[0:SLOTS, part(pair, 128)]
        keys = r.qkv[:, part(pair + 4, 128)]
        values = r.qkv[:, part(pair + 8, 128)]
        outs = []
        for odd in range(2):
            head = 2 * pair + odd
            half = first_half if odd == 0 else jnp.logical_not(first_half)
            mine = jnp.where(half, queries, jnp.zeros_like(queries))
            spread = jnp.broadcast_to(r.bias[pl.ds(head, 1), :], (SLOTS, ROW))
            spread = pltpu.roll(spread, 0, 1, stride=1, stride_axis=0)[:, 0:KEYS]
            scores = jnp.where(valid, dot_t(mine, keys) * HS ** (-0.5) + spread, MASK_FILL)
            shifted = jnp.exp(scores - jnp.max(scores, axis=-1, keepdims=True))
            chances = low(shifted / jnp.sum(shifted, axis=-1, keepdims=True))
            r.probs[head] = chances
            outs.append(dot(chances, values))
        r.ctx[:, part(pair, 128)] = low(jnp.where(first_half, outs[0], outs[1]))

    each(H // 2, heads)

    def project_out(j):
        at = part(j, 256)
        r.cat[:, at] = dot(r.ctx[...], r.w[rows_of("att_out"), at])

    each(2, project_out)


def gating_forward(r, length):
    norm_rows(r.x1, r.small[2:3, :], r.nrm_c)

    def up(j):
        at = part(j, 256)
        r.hid[...] = dot(r.nrm_c[...], r.w_cg[:, at])
        for k in range(5):
            rows = part(k, 32)
            active, slope = gelu_parts(r.hid[rows, :])
            r.ug[rows, at] = active
            r.slope_c[rows, at] = low(slope)

    each_loop(CG // 256, up, 4)
    tiles = [slice(GATE + 128 * j, GATE + 128 * j + 128) for j in range(GATE // 128)]
    total = jnp.zeros((SLOTS, 128), F32)
    for at in tiles:
        total = total + r.ug[:, at]
    mean = lane_mean(total, GATE)
    total = jnp.zeros((SLOTS, 128), F32)
    for at in tiles:
        centered = r.ug[:, at] - mean
        total = total + centered * centered
    scale = lax.rsqrt(lane_mean(total, GATE) + NORM_EPS)
    r.gmean[...] = jnp.broadcast_to(mean, (SLOTS, 128))
    r.gscale[...] = jnp.broadcast_to(scale, (SLOTS, 128))
    scale = scale * valid_rows(length)
    for j, at in enumerate(tiles):
        gain = r.small[5 + j // 4 : 6 + j // 4, part(j % 4, 128)]
        r.gpad[PAD : PAD + SLOTS, part(j, 128)] = (r.ug[:, at] - mean) * scale * gain

    def finish(j, at, value):
        r.cv[:, at] = low(value)
        r.gated[:, at] = low(r.ug[:, at] * value)

    convolve(r.gpad, r.tiles, 0, GATE, finish)

    def down(j):
        r.cat[:, part(j + 2, 256)] = dot(r.gated[...], r.w[rows_of("cg_out"), part(j, 256)])

    each(2, down)


def merge_forward(r, length):
    valid = valid_rows(length)
    for j in range(8):
        at = part(j, 128)
        r.mpad[PAD : PAD + SLOTS, at] = r.cat[:, at] * valid

    def finish(j, at, value):
        r.mixed[:, at] = low(r.cat[:, at] + value)

    convolve(r.mpad, r.tiles, 3, 2 * D, finish)

    def merge(j):
        at = part(j, 256)
        r.x2[:, at] = r.x1[:, at] + dot(r.mixed[...], r.w[rows_of("merge"), at])

    each(2, merge)


def final_norm(r, length):
    gain = r.small[4:5, :]
    valid = valid_rows(length)
    total = jnp.zeros((1, D), F32)
    for k in range(2):
        rows = part(k, 80)
        hat, scale = normed(r.x3[rows, :])
        r.out[rows, :] = low(hat * gain * valid[80 * k : 80 * k + 80])
        mine = r.cot[rows, :].astype(F32) * valid[80 * k : 80 * k + 80]
        total = total + fold_rows(mine * hat)
        inner = mine * gain
        back = scale * (inner - (lane_mean(inner, D) + hat * lane_mean(inner * hat, D)))
        r.dx[rows, :] = back
        r.dout[rows, :] = low(0.5 * back)
    r.gains[4:5, :] = total


def merge_back(r, length, emits):
    for k in range(2):
        r.dout[part(k, 80), :] = low(r.dx[part(k, 80), :])
    w_merge = r.w.at[rows_of("merge")]

    def merge(j):
        at = part(j, 256)
        r.dpad[PAD : PAD + SLOTS, at] = dot_t(r.dout[...], w_merge[at, :])

    each(2 * D // 256, merge)
    weight_rows(r.mixed, r.dout, 2, r.left_t, w_merge)
    emits.put_tensor("merge", w_merge)

    def finish(j, at, value):
        r.djoin[:, at] = low(r.dpad[PAD : PAD + SLOTS, at] + value * valid_rows(length))

    convolve_back(r.dpad, r.mpad, r.tiles, 3, 2 * D, r.tgrad, finish)


def gating_back(r, length, emits):
    w_co = r.w.at[rows_of("cg_out")]

    def gate(j):
        at = part(j, 256)
        value = dot_t(r.djoin[:, D:], w_co[at, :])
        r.dhid[:, at] = low(value * r.cv[:, at].astype(F32) * r.slope_c[:, at].astype(F32))
        r.dpad[PAD : PAD + SLOTS, at] = value * r.ug[:, at]

    each(GATE // 256, gate)
    r.dout[...] = r.djoin[:, D:]
    weight_rows(r.gated, r.dout, 3, r.left_t, w_co)
    emits.put_tensor("cg_out", w_co)

    def finish(j, at, value):
        r.dgate[:, at] = value * valid_rows(length)

    convolve_back(r.dpad, r.gpad, r.tiles, 0, GATE, r.tgrad, finish)
    tiles = GATE // 128
    for quarter in range(4):
        rows = part(quarter, SLOTS // 4)
        mean, scale = r.gmean[rows, :], r.gscale[rows, :]
        total, total_hat = jnp.zeros_like(mean), jnp.zeros_like(mean)

        def parts(j, rows=rows, mean=mean, scale=scale):
            row, lane = 5 + j // 4, part(j % 4, 128)
            hat = (r.ug[rows, part(j + tiles, 128)] - mean) * scale
            grad = r.dgate[rows, part(j, 128)]
            return hat, grad, grad * r.small[row : row + 1, lane]

        for j in range(tiles):
            hat, grad, inner = parts(j)
            products = jnp.sum((grad * hat).reshape(-1, 8, 128), axis=0)
            r.gate_sums[part(j, 8), :] = products if quarter == 0 else r.gate_sums[part(j, 8), :] + products
            total = total + inner
            total_hat = total_hat + inner * hat
        total = jnp.broadcast_to(lane_mean(total, GATE), total.shape)
        total_hat = jnp.broadcast_to(lane_mean(total_hat, GATE), total.shape)
        for j in range(tiles):
            hat, _, inner = parts(j)
            far = part(j + tiles, 128)
            r.dgate[rows, part(j, 128)] = scale * (inner - total - hat * total_hat)
    for j in range(tiles):
        far = part(j + tiles, 128)
        r.dhid[:, far] = low(r.dgate[:, part(j, 128)] * r.slope_c[:, far].astype(F32))
        r.tgrad[j % 4, 5 + j // 4 : 6 + j // 4, :] = fold_rows(r.gate_sums[part(j, 8), :])

    def down(j):
        at = part(j, 256)
        r.dnrm[:, at] = dot_t(r.dhid[...], r.w_cg[at, :])

    each(2, down)
    g_cg = r.w.at[rows_of("cg_in")]
    weight_columns(r.nrm_c, r.dhid, 6, r.stage, r.left_t, g_cg)
    emits.put_tensor("cg_in", g_cg)

    def add(rows, back):
        r.dx[rows, :] += back

    r.gains[2:3, :] = norm_rows_back(r.x1, r.small[2:3, :], r.dnrm, add)


def forward_kernel(names, coords, length_ref, frames, cot, *refs):
    sources, refs = refs[: len(LAYOUT)], refs[len(LAYOUT) :]
    r = SimpleNamespace(**dict(zip(names, refs)))
    r.cot = cot
    length = length_ref[0]
    loads = Loads(coords, sources, r.w, r.seams, r.load_sems)
    kept = []

    def keep(source, target):
        copy = pltpu.make_async_copy(source, target, r.keep_sems.at[len(kept)])
        copy.start()
        kept.append(copy)

    for padded in (r.gpad, r.mpad, r.dpad):
        clear_margins(padded)
    r.tgrad[...] = jnp.zeros_like(r.tgrad)
    r.gains[...] = jnp.zeros_like(r.gains)
    loads.wait("small")
    r.small[...] = r.w[ROW * 31 : ROW * 31 + SMALL, :].astype(F32)
    for lane in range(4):
        r.tiles[lane] = r.small[:, part(lane, 128)]
    loads.wait("ffa_in")
    split_columns(r.w.at[rows_of("ffa_in")], r.w_ffa_in, 4, r.stage)
    keep(r.w_ffa_in, r.keep_ffa_in)
    loads.wait("ffa_out")
    keep(r.w.at[rows_of("ffa_out")], r.keep_ffa_out)
    feed_forward(frames, r.small[0:1, :], r.w_ffa_in, r.w.at[rows_of("ffa_out")], r.nrm, r.act, r.slope, r.x1)
    keep(r.nrm, r.keep_nrm)
    keep(r.act, r.keep_act)
    keep(r.slope, r.keep_slope)
    keep(r.x1, r.keep_x1)
    loads.wait("qkv")
    split_columns(r.w.at[rows_of("qkv")], r.w_qkv, 3, r.stage)
    keep(r.w_qkv, r.keep_qkv)
    loads.wait("att_out")
    keep(r.w.at[rows_of("att_out")], r.keep_att)
    attention_forward(r, length)
    keep(r.nrm_t, r.keep_nrm_t)
    keep(r.qkv, r.keep_heads)
    keep(r.probs, r.keep_probs)
    keep(r.ctx, r.keep_ctx)
    loads.wait("cg_in")
    split_columns(r.w.at[rows_of("cg_in")], r.w_cg, 6, r.stage)
    loads.wait("cg_out")
    gating_forward(r, length)
    loads.wait("merge")
    merge_forward(r, length)
    loads.wait("ffb_in")
    split_columns(r.w.at[rows_of("ffb_in")], r.w_ffb_in, 4, r.stage)
    loads.wait("ffb_out")
    w_out = r.w.at[rows_of("ffb_out")]
    feed_forward(r.x2, r.small[3:4, :], r.w_ffb_in, w_out, r.nrm_b, r.act_b, r.slope_b, r.x3)
    final_norm(r, length)
    emits = Emits(
        coords,
        ((r.low_kept, (r.low_near, r.low_far)), (r.high_kept, (r.high_near, r.high_far))),
        r.emit_sems,
    )
    feed_back(
        r.dout, r.w_ffb_in, w_out, r.nrm_b, r.act_b, r.slope_b, r.dhid, r.dnrm, r.stage, r.left_t,
        r.w.at[rows_of("ffb_in")], w_out, emits, "ffb",
    )

    def add(rows, back):
        r.dx[rows, :] += back

    r.gains[3:4, :] = norm_rows_back(r.x2, r.small[3:4, :], r.dnrm, add)
    merge_back(r, length, emits)
    keep(r.djoin, r.keep_djoin)
    gating_back(r, length, emits)
    keep(r.dx, r.keep_dx)
    for lane in range(4):
        at = part(lane, 128)
        r.gains[5:8, at] = r.tgrad[lane, 5:8, :]
        r.w[ROW * 31 : ROW * 31 + SMALL, at] = low(r.tgrad[lane])
    r.w[ROW * 31 : ROW * 31 + 16, :] = low(
        jnp.concatenate(
            [
                jnp.zeros((8, ROW), F32),
                jnp.concatenate([r.tgrad[lane, 8:16, :] for lane in range(4)], axis=1),
            ],
            axis=0,
        )
    )
    r.w[ROW * 31 + SMALL : ROW * 32, :] = jnp.zeros((ROW - SMALL, ROW), BF16)
    emits.put_tensor("small", r.w.at[rows_of("small")])
    for copy in kept:
        copy.wait()
    emits.wait()


def attention_back(r, emits):
    def project(j):
        at = part(j, 256)
        r.dctx[:, at] = low(dot_t(r.datt[...], r.w_att[at, :]))

    each(2, project)
    weight_rows(r.ctx, r.datt, 1, r.left_t, r.w_att)
    emits.put_tensor("att_out", r.w_att)
    first_half = lax.broadcasted_iota(jnp.int32, (1, 128), 1) < HS
    at_row = lax.broadcasted_iota(jnp.int32, (SLOTS, SLOTS), 0)
    at_column = lax.broadcasted_iota(jnp.int32, (SLOTS, SLOTS), 1)
    flip = low((at_row + at_column == SLOTS - 1).astype(F32))

    def heads(pair):
        queries = r.qkv[0:SLOTS, part(pair, 128)]
        keys = r.qkv[:, part(pair + 4, 128)]
        values = r.qkv[:, part(pair + 8, 128)]
        context = r.dctx[:, part(pair, 128)]
        q_parts, k_parts, v_parts = [], [], []
        for odd in range(2):
            head = 2 * pair + odd
            half = first_half if odd == 0 else jnp.logical_not(first_half)
            chances = r.probs[head]
            v_parts.append(t_dot(chances, context)[0:SLOTS])
            wide_chances = chances.astype(F32)
            chance_grad = dot_t(jnp.where(half, context, jnp.zeros_like(context)), values)
            inner = jnp.sum(wide_chances * chance_grad, axis=-1, keepdims=True)
            score_grad = low(wide_chances * (chance_grad - inner))
            q_parts.append(dot(score_grad, keys))
            k_parts.append(t_dot(score_grad, queries)[0:SLOTS])
            wide = jnp.concatenate([dot(flip, score_grad), jnp.zeros((SLOTS, ROW - KEYS), F32)], axis=1)
            wide = pltpu.roll(wide, ROW - SLOTS + 1, 1, stride=1, stride_axis=0)
            r.sums[pl.ds(head, 1), :] = fold_rows(wide)
        scale = HS ** (-0.5)
        r.dhid[:, part(pair, 128)] = low(jnp.where(first_half, q_parts[0], q_parts[1]) * scale)
        r.dhid[:, part(pair + 4, 128)] = low(jnp.where(first_half, k_parts[0], k_parts[1]) * scale)
        r.dhid[:, part(pair + 8, 128)] = low(jnp.where(first_half, v_parts[0], v_parts[1]))

    each(H // 2, heads)

    def down(j):
        at = part(j, 256)
        r.dnrm[:, at] = dot_t(r.dhid[:, 0 : 3 * D], r.w_qkv[at, :])

    each(2, down)

    def add(rows, back):
        r.dx[rows, :] += back
        r.dout[rows, :] = low(0.5 * r.dx[rows, :])

    r.late[1:2, :] = norm_rows_back(r.x1, r.gain_rows[1:2, :], r.dnrm, add)


def attention_weights_back(r, emits):
    weight_columns(r.nrm_t, r.dhid, 3, r.stage, r.left_t, r.g_qkv)
    emits.put_tensor("qkv", r.g_qkv)
    by_entry = lax.dot_general(
        r.sums[...],
        bucket_map(),
        (((1,), (1,)), ((), ())),
        precision=lax.Precision.HIGHEST,
        preferred_element_type=F32,
    )
    flat = fold_rows(own_entries(by_entry))
    r.late[8:9, :] = flat[:, 0:ROW]
    r.late[9:10, :] = flat[:, ROW:]


def backward_kernel(names, coords, frames, gains, gain_rows, *refs):
    r = SimpleNamespace(**dict(zip(names, refs)))
    r.gain_rows = gain_rows
    waits = {}
    for at, (name, source, target) in enumerate(
        (
            ("att", r.in_att, r.w_att),
            ("djoin", r.in_djoin.at[:, 0:D], r.datt),
            ("ctx", r.in_ctx, r.ctx),
            ("heads", r.in_heads, r.qkv),
            ("probs", r.in_probs, r.probs),
            ("qkv", r.in_qkv, r.w_qkv),
            ("x1", r.in_x1, r.x1),
            ("dx", r.in_dx, r.dx),
            ("nrm_t", r.in_nrm_t, r.nrm_t),
            ("ffa_out", r.in_ffa_out, r.w_ffa_out),
            ("slope", r.in_slope, r.slope),
            ("act", r.in_act, r.act),
            ("ffa_in", r.in_ffa_in, r.w_ffa_in),
            ("nrm", r.in_nrm, r.nrm),
        )
    ):
        waits[name] = pltpu.make_async_copy(source, target, r.load_sems.at[at])
        waits[name].start()
    r.late[...] = jnp.zeros_like(r.late)
    emits = Emits(coords, ((r.low_kept, (r.low_near, r.low_far)),), r.emit_sems)
    for name in ("att", "djoin", "ctx", "heads", "probs", "qkv", "x1", "dx"):
        waits[name].wait()
    attention_back(r, emits)
    waits["nrm_t"].wait()
    attention_weights_back(r, emits)
    for name in ("ffa_out", "slope", "act", "ffa_in", "nrm"):
        waits[name].wait()
    feed_back(
        r.dout, r.w_ffa_in, r.w_ffa_out, r.nrm, r.act, r.slope, r.dhid, r.dnrm, r.stage, r.left_t, r.g_ffa_in,
        r.w_ffa_out, emits, "ffa",
    )

    def add(rows, back):
        r.fgrad[rows, :] = low(r.dx[rows, :] + back)

    r.late[0:1, :] = norm_rows_back(frames, gain_rows[0:1, :], r.dnrm, add)
    r.late[2:8, :] = gains[2:8, :]
    emits.wait()


VM = pl.BlockSpec(memory_space=pltpu.VMEM)
SM = pl.BlockSpec(memory_space=pltpu.SMEM)
ANY = pl.BlockSpec(memory_space=pl.ANY)
WIDE, THIN = ((SLOTS, D), F32), ((SLOTS, D), BF16)
FULL = ((SLOTS, FF), BF16)
KEPT, SENT = ((8, SPAN, ROW), BF16), ((4, SPAN, ROW), BF16)

FORWARD_OUT = {
    "out": (VM, THIN),
    "gains": (VM, ((8, ROW), F32)),
    "small": (VM, ((SMALL, ROW), F32)),
    "high_kept": (ANY, KEPT),
    "high_near": (ANY, SENT),
    "high_far": (ANY, SENT),
    "low_kept": (ANY, KEPT),
    "low_near": (ANY, SENT),
    "low_far": (ANY, SENT),
    "keep_ffa_in": (ANY, ((D, FF), BF16)),
    "keep_ffa_out": (ANY, ((FF, D), BF16)),
    "keep_qkv": (ANY, ((D, 3 * D), BF16)),
    "keep_att": (ANY, ((D, D), BF16)),
    "keep_nrm": (ANY, THIN),
    "keep_act": (ANY, FULL),
    "keep_slope": (ANY, FULL),
    "keep_x1": (ANY, WIDE),
    "keep_nrm_t": (ANY, THIN),
    "keep_heads": (ANY, ((KEYS, 3 * D), BF16)),
    "keep_probs": (ANY, ((H, SLOTS, KEYS), BF16)),
    "keep_ctx": (ANY, THIN),
    "keep_djoin": (ANY, ((SLOTS, 2 * D), BF16)),
    "keep_dx": (ANY, WIDE),
}
FORWARD_SCRATCH = {
    "w": ((32 * ROW, ROW), BF16),
    "w_ffa_in": ((D, FF), BF16),
    "w_qkv": ((D, 3 * D), BF16),
    "w_cg": ((D, CG), BF16),
    "w_ffb_in": ((D, FF), BF16),
    "stage": ((4, 6 * ROW, 128), F32),
    "left_t": ((ROW, SLOTS), BF16),
    "tiles": ((4, SMALL, 128), F32),
    "tgrad": ((4, SMALL, 128), F32),
    "bias": ((H, ROW), F32),
    "nrm": THIN,
    "act": FULL,
    "slope": FULL,
    "nrm_t": THIN,
    "qkv": ((KEYS, 3 * D), BF16),
    "probs": ((H, SLOTS, KEYS), BF16),
    "ctx": THIN,
    "nrm_c": THIN,
    "hid": ((SLOTS, 256), F32),
    "ug": ((SLOTS, CG), F32),
    "slope_c": ((SLOTS, CG), BF16),
    "gmean": ((SLOTS, 128), F32),
    "gscale": ((SLOTS, 128), F32),
    "gate_sums": ((8 * GATE // 128, 128), F32),
    "gpad": ((PADDED, GATE), F32),
    "cv": ((SLOTS, GATE), BF16),
    "gated": ((SLOTS, GATE), BF16),
    "cat": ((SLOTS, 2 * D), F32),
    "mpad": ((PADDED, 2 * D), F32),
    "mixed": ((SLOTS, 2 * D), BF16),
    "nrm_b": THIN,
    "act_b": FULL,
    "slope_b": FULL,
    "dpad": ((PADDED, GATE), F32),
    "djoin": ((SLOTS, 2 * D), BF16),
    "dgate": ((SLOTS, GATE), F32),
    "dhid": ((SLOTS, CG), BF16),
    "dnrm": WIDE,
    "dout": THIN,
    "dx": WIDE,
    "x1": WIDE,
    "x2": WIDE,
    "x3": WIDE,
    "seams": ((PARTS + 1, 2, TILE, ROW), BF16),
    "load_sems": PARTS,
    "keep_sems": 16,
    "emit_sems": 40,
}
BACKWARD_IN = (
    "ffa_in", "ffa_out", "qkv", "att", "nrm", "act", "slope", "x1", "nrm_t", "heads", "probs", "ctx", "djoin", "dx",
)
PASSED = ("low_kept", "low_near", "low_far")
BACKWARD_OUT = {
    "fgrad": (VM, THIN),
    "late": (VM, ((16, ROW), F32)),
    "low_kept": (ANY, KEPT),
    "low_near": (ANY, SENT),
    "low_far": (ANY, SENT),
}
BACKWARD_SCRATCH = {
    "w_ffa_in": ((D, FF), BF16),
    "w_ffa_out": ((FF, D), BF16),
    "w_qkv": ((D, 3 * D), BF16),
    "w_att": ((D, D), BF16),
    "g_ffa_in": ((FF, D), BF16),
    "g_qkv": ((3 * D, D), BF16),
    "stage": ((4, 4 * ROW, 128), F32),
    "left_t": ((ROW, SLOTS), BF16),
    "sums": ((H, ROW), F32),
    "nrm": THIN,
    "act": FULL,
    "slope": FULL,
    "nrm_t": THIN,
    "qkv": ((KEYS, 3 * D), BF16),
    "probs": ((H, SLOTS, KEYS), BF16),
    "ctx": THIN,
    "datt": THIN,
    "dctx": THIN,
    "dhid": FULL,
    "dnrm": WIDE,
    "dout": THIN,
    "dx": WIDE,
    "x1": WIDE,
    "load_sems": 14,
    "emit_sems": 24,
}


def call(kernel, name, ins, outs, scratch, limit, aliases=None):
    return pl.pallas_call(
        kernel,
        name=name,
        in_specs=[space for space, _ in ins],
        out_specs=[space for space, _ in outs],
        out_shape=[jax.ShapeDtypeStruct(*kind) for _, kind in outs],
        scratch_shapes=[
            pltpu.SemaphoreType.DMA((each_one,)) if isinstance(each_one, int) else pltpu.VMEM(*each_one)
            for each_one in scratch
        ],
        input_output_aliases=aliases or {},
        compiler_params=pltpu.CompilerParams(vmem_limit_bytes=limit * 2**20),
    )(*[array for _, array in ins])


def forward(coords, length, frames, cot, blocks):
    def kernel(*refs):
        forward_kernel([*FORWARD_OUT, *FORWARD_SCRATCH], *refs)

    outs = call(
        kernel,
        "forward",
        [(SM, coords), (SM, length), (VM, frames), (VM, cot)] + [(ANY, block) for block in blocks],
        list(FORWARD_OUT.values()),
        list(FORWARD_SCRATCH.values()),
        58,
    )
    return dict(zip(FORWARD_OUT, outs))


def backward(coords, frames, state):
    def kernel(*refs):
        names = ["in_" + name for name in BACKWARD_IN + PASSED]
        backward_kernel([*names, *BACKWARD_OUT, *BACKWARD_SCRATCH], *refs)

    ins = [(SM, coords), (VM, frames), (VM, state["gains"]), (VM, state["small"])]
    ins += [(ANY, state["keep_" + name]) for name in BACKWARD_IN]
    ins += [(ANY, state[name]) for name in PASSED]
    outs = call(
        kernel,
        "backward",
        ins,
        list(BACKWARD_OUT.values()),
        list(BACKWARD_SCRATCH.values()),
        58,
        {len(ins) - 3 + at: 2 + at for at in range(3)},
    )
    return dict(zip(BACKWARD_OUT, outs))


def segment_bounds():
    bounds = [0]
    for extent in segment_shapes():
        bounds.append(bounds[-1] + math.prod(extent))
    return bounds


def fast_mesh():
    return lax.axis_size("dp") == 4 and lax.axis_size("fsdp") == 8


def over_x(value):
    return lax.ppermute(value, "fsdp", [(i, i ^ 1) for i in range(8)])


def over_y(value):
    return lax.ppermute(value, "dp", [(i, i ^ 2) for i in range(4)])


def over_core(value):
    return lax.ppermute(value, "dp", [(i, i ^ 1) for i in range(4)])


def round_z(value):
    return lax.ppermute(value, "fsdp", [(i, (i + 2) % 8) for i in range(8)])


def over_z(value, step):
    return lax.ppermute(value, "fsdp", [(i, i ^ (2 * step)) for i in range(8)])


def after(value, *others):
    return lax.optimization_barrier((value, *others))[0]


def shard_offset(me, shard_size):
    return me * shard_size - start_of(me) * ROW


def gather_shards(shard, me):
    shard_size = shard.shape[0]
    if not fast_mesh():
        whole = lax.all_gather(shard, AXES, axis=0, tiled=True)
        whole = jnp.pad(whole, (0, (STARTS[-1] + SPAN) * ROW - whole.shape[0])).reshape(-1, ROW)
        spans = [whole[start : start + SPAN] for start in STARTS[:-1]]
        spans = spans[:1] + [jnp.concatenate([jnp.zeros((TILE, ROW), BF16), span[TILE:]]) for span in spans[1:]]
        return [
            jnp.concatenate([spans[source_part((0, 0, 0, 0), piece)][piece[4] : piece[5]] for piece in pieces])
            for pieces in LAYOUT
        ]
    most = TILE * ROW
    padded = jnp.pad(shard, (most, SPAN * ROW - shard_size))
    span = lax.dynamic_slice(padded, (most - shard_offset(me, shard_size),), (SPAN * ROW,)).reshape(SPAN, ROW)
    own, by_x, by_y = [span], [], []
    for back in range(4):
        if back < 3:
            own.append(round_z(own[back]))
        if back < 2:
            by_x.append(over_x(own[back]))
            by_y.append(over_y(own[back]))
            own[back + 1], by_x[back], by_y[back] = lax.optimization_barrier((own[back + 1], by_x[back], by_y[back]))
        else:
            by_x.append(over_x(jnp.concatenate([own[back], by_y[back - 2][:HALF]])))
            by_y.append(over_y(jnp.concatenate([own[back], by_x[back - 2][HALF:SPAN]])))
    by_x.append(over_x(jnp.concatenate([by_y[2][:HALF], by_y[3][:HALF]])))
    by_y.append(over_y(jnp.concatenate([by_x[2][HALF:SPAN], by_x[3][HALF:SPAN]])))
    late_ones = (by_x[3], by_y[3])
    far_own = [over_core(each_one) for each_one in own[:2]] + [over_core(after(each_one, *late_ones)) for each_one in own[2:]]
    far = [far_own]
    for way in (by_x, by_y):
        far.append([over_core(way[0]), over_core(way[1]), over_core(after(way[2], *late_ones))])
        far[-1] += [over_core(way[at]) for at in (3, 4)]
    return own + by_x + by_y + far[0] + far[1] + far[2]


def added(*parts):
    total = parts[0].astype(F32)
    for each_one in parts[1:]:
        total = total + each_one.astype(F32)
    return total


SIDES = (slice(0, HALF), slice(HALF, SPAN))


HBM = pl.BlockSpec(memory_space=pltpu.HBM)


def span_sums(coords, own_half, x, places, low_kept, low_got, high_kept, high_got, sides):
    count = len(places)
    together = sides if isinstance(sides, int) else 0
    pieces = [(at, rows) for at in range(count) for rows in (() if together else sides)]

    def kernel(coords, low_kept, low_got, high_kept, high_got, *refs):
        outs, (kept, got, total, sems, out_sems) = refs[:-5], refs[-5:]
        high = coords[0] == int(own_half)
        for source, other, wanted in ((low_kept, low_got, jnp.logical_not(high)), (high_kept, high_got, high)):

            @pl.when(wanted)
            def _(source=source, other=other):
                for at, place in enumerate(places):
                    pltpu.make_async_copy(source.at[4 * x + place], kept.at[at], sems.at[2 * at]).start()
                    pltpu.make_async_copy(other.at[place], got.at[at], sems.at[2 * at + 1]).start()

        copies = []
        for at in range(count):
            pltpu.make_async_copy(low_kept.at[at], kept.at[at], sems.at[2 * at]).wait()
            pltpu.make_async_copy(low_got.at[at], got.at[at], sems.at[2 * at + 1]).wait()

            def add(k, at=at):
                rows = part(k, SPAN // 11)
                total[at, rows] = low(kept[at, rows].astype(F32) + got[at, rows].astype(F32))

            each_loop(11, add)
            if together:
                out = outs[at // together].at[at % together]
                copies.append(pltpu.make_async_copy(total.at[at], out, out_sems.at[at]))
                copies[-1].start()
            for which, (mine, rows) in enumerate(pieces):
                if mine == at:
                    copies.append(pltpu.make_async_copy(total.at[at, rows], outs[which], out_sems.at[which]))
                    copies[-1].start()
        for copy in copies:
            copy.wait()

    spans = ((count, SPAN, ROW), BF16)
    arrays = [(HBM, low_kept), (ANY, low_got), (HBM, high_kept), (ANY, high_got)]
    if together:
        outs = [(ANY, ((together, SPAN, ROW), BF16))] * (count // together)
    else:
        outs = [(ANY, ((rows.stop - rows.start, ROW), BF16)) for _, rows in pieces]
    sums = call(
        kernel, "span_sums", [(SM, coords)] + arrays, outs, [spans] * 3 + [2 * count, max(count, len(pieces))], 56
    )
    return sums if together else [sums[len(sides) * at : len(sides) * (at + 1)] for at in range(count)]


def late_rows(late, above, below):
    gains = jnp.pad(late[0:8], ((above, below - 8), (0, 0)))
    return gains + jnp.pad(late[8:10], ((above + REL_AT, below - REL_AT - 2), (0, 0)))


def scatter_slow(state, back, shard_size, padded):
    late = back["late"]
    pieces = []
    for source, half in ((back, "low"), (state, "high")):
        for core in range(2):
            for at in range(8):
                z, x = at // 2, at % 2
                if core == 0:
                    span = source[half + "_kept"][4 * x + 3 - z]
                else:
                    span = source[half + ("_near", "_far")[x]][3 - z]
                d = len(pieces)
                pieces.append(span[: STARTS[d + 1] - STARTS[d] if d < PARTS - 1 else SPAN])
    rows = jnp.concatenate(pieces)
    first = ROW * BLOCK["small"][0]
    rows = low(rows.astype(F32) + late_rows(late, first, rows.shape[0] - first))
    flat = rows.reshape(-1)[: segment_bounds()[-1]]
    shard = lax.psum_scatter(flat, AXES, scatter_dimension=0, tiled=True)
    return jnp.pad(shard, (0, padded - shard_size)).astype(F32), lax.psum(late[0:8], AXES)


def scatter_grads(state, back, coords, me, shard_size, padded):
    if not fast_mesh():
        return scatter_slow(state, back, shard_size, padded)
    high = coords[0] == 1
    high_kept, low_kept = state["high_kept"], back["low_kept"]
    high_got = [over_core(state["high_near"]), over_core(state["high_far"])]
    low_far = over_core(back["low_far"])

    def chip_sum(own_half, x, places, sides):
        got = (low_far if x else low_near, high_got[x])
        return span_sums(coords, own_half, x, places, low_kept, got[0], high_kept, got[1], sides)

    for_y, for_x = chip_sum(False, 1, range(4), 2)
    from_x, from_y = over_x(for_x), over_y(for_y)
    low_near = over_core(after(back["low_near"], for_x, for_y))
    late = after(back["late"], for_x, for_y)
    late = late + over_core(late)
    late = late + over_z(late, 1)
    to_x = chip_sum(True, 1, range(4), SIDES)
    to_y = chip_sum(False, 0, range(4), SIDES)
    mine = chip_sum(True, 0, range(4), SIDES)
    late = late + over_z(after(late, mine[3][1], to_y[3][1], to_x[3][1]), 2)
    from_x, from_y, to_x, to_y, mine, late = lax.optimization_barrier((from_x, from_y, to_x, to_y, mine, late))
    late = late + over_x(late)
    late = late + over_y(late)
    running = [None, None]
    before = [(), ()]
    for at in range(4):
        for side, rows in enumerate(SIDES):
            send_x, send_y = to_x[at][side], to_y[at][side]
            if at < 2:
                send_x = low(added(send_x, from_y[at, rows]))
            else:
                send_y = low(added(send_y, from_x[at - 2, rows]))
            got_x, got_y = over_x(after(send_x, *before[side])), over_y(after(send_y, *before[side]))
            before[side] = (got_x, got_y)
            parts = [mine[at][side], got_x, got_y]
            if at:
                parts.append(round_z(running[side]))
            running[side] = added(*parts)
            if at < 3:
                running[side] = low(running[side])
    total = jnp.concatenate(running)
    first = ROW * BLOCK["small"][0] - STARTS[PARTS - 1]
    total = total + jnp.where(me == PARTS - 1, 1.0, 0.0) * late_rows(late, first, SPAN - first)
    flat = jnp.pad(total.reshape(-1), (0, max(0, TILE * ROW + padded - SPAN * ROW)))
    return lax.dynamic_slice(flat, (shard_offset(me, shard_size),), (padded,)), late[0:8]


def sum_everywhere(vector):
    if not fast_mesh():
        return lax.psum(vector, AXES)
    vector = vector + over_core(vector)
    vector = vector + over_x(vector)
    vector = vector + over_y(vector)
    vector = vector + over_z(vector, 1)
    return vector + over_z(vector, 2)


def most_segments(shard_size, devices):
    bounds = segment_bounds()
    most = 1
    for at in range(devices):
        low_end, high_end = at * shard_size, (at + 1) * shard_size
        most = max(most, sum(1 for b in bounds[1:-1] if low_end < b < high_end) + 1)
    return most


LANES = 128
CHUNK = 1024 * LANES
STRIP = 128 * LANES


def chunk_spans(segments, step):
    first, last = step * CHUNK, (step + 1) * CHUNK
    for at in range(segments.shape[0] - 2):
        start, end = segments[1 + at], segments[2 + at]
        whole = (start <= first) & (last <= end)
        some = (start < last) & (end > first) & jnp.logical_not(whole)
        yield at, whole, some, start - first, end - first


def strips(body, start=None):
    return lax.fori_loop(0, CHUNK // STRIP, lambda at, carry: body(part(at, STRIP), at * STRIP, carry), start)


def square(entries, strip):
    return entries[strip].reshape(STRIP // LANES, LANES)


def inside(place, start, end):
    row = lax.broadcasted_iota(jnp.int32, (STRIP // LANES, LANES), 0)
    place = place + row * LANES + lax.broadcasted_iota(jnp.int32, (STRIP // LANES, LANES), 1)
    return (place >= start) & (place < end)


def fold(values):
    return jnp.sum(values.reshape(-1, 8, LANES), axis=0)


def update_kernel(segments, params, first, second, grad, new_first, new_second, update, sums):
    step = pl.program_id(0)
    nothing = jnp.zeros((8, LANES), F32)

    @pl.when(step == 0)
    def _():
        sums[...] = nothing

    def move(strip, place, totals):
        grads = grad[strip]
        firsts = BETA_FIRST * first[strip] + (1.0 - BETA_FIRST) * grads
        seconds = BETA_SECOND * second[strip] + (1.0 - BETA_SECOND) * grads * grads
        new_first[strip] = firsts
        new_second[strip] = seconds
        first_hat = firsts * (1.0 / (1.0 - BETA_FIRST**STEP))
        second_hat = seconds * (1.0 / (1.0 - BETA_SECOND**STEP))
        weights = params[strip]
        change = first_hat / (jnp.sqrt(second_hat) + ADAM_EPS) + WEIGHT_DECAY * weights
        update[strip] = change
        squares = [(each_one * each_one).reshape(STRIP // LANES, LANES) for each_one in (weights, change)]
        return totals[0] + fold(squares[0]), totals[1] + fold(squares[1])

    totals = strips(move, (nothing, nothing))
    lane = lax.broadcasted_iota(jnp.int32, (1, LANES), 1)

    def add(at, totals):
        for row, total in enumerate(totals):
            total = jnp.sum(jnp.sum(total, axis=0, keepdims=True), axis=1, keepdims=True)
            sums[row : row + 1, :] += jnp.where(lane == segments[0] + at, total, 0.0)

    for at, whole, some, start, end in chunk_spans(segments, step):

        @pl.when(whole)
        def _(at=at):
            add(at, totals)

        @pl.when(some)
        def _(at=at, start=start, end=end):
            def squares(strip, place, totals):
                here = inside(place, start, end)
                own = [square(entries, strip) for entries in (params, update)]
                own = [fold(jnp.where(here, each_one * each_one, 0.0)) for each_one in own]
                return totals[0] + own[0], totals[1] + own[1]

            add(at, strips(squares, (nothing, nothing)))


def apply_kernel(segments, sums, params, update, new_params, *norms):
    step = pl.program_id(0)
    roots = jnp.sqrt(sums[0:2, :])
    trust = roots[0:1, :] / (roots[1:2, :] + ADAM_EPS)
    for out, row in zip(norms, (roots[0:1, :], roots[1:2, :], trust)):
        out[...] = row.reshape(LANES)[: out.shape[0]]
    lane = lax.broadcasted_iota(jnp.int32, (1, LANES), 1)
    for at, whole, some, start, end in chunk_spans(segments, step):

        scale = LEARN_RATE * jnp.sum(jnp.where(lane == segments[0] + at, trust, 0.0), axis=1, keepdims=True)
        scale = jnp.broadcast_to(scale, (1, LANES))

        def moved(strip, scale=scale):
            return square(params, strip) - scale * square(update, strip)

        @pl.when(whole)
        def _(moved=moved):
            def all_of(strip, place, carry):
                new_params[strip] = moved(strip).reshape(STRIP)
                return carry

            strips(all_of, 0)

        @pl.when(some)
        def _(moved=moved, start=start, end=end):
            def part_of(strip, place, carry):
                chosen = jnp.where(inside(place, start, end), moved(strip), square(new_params, strip))
                new_params[strip] = chosen.reshape(STRIP)
                return carry

            strips(part_of, 0)


def shards(frames, lengths, cotangent, params, first_moment, second_moment):
    shard_size = params.shape[0]
    devices = lax.axis_size("dp") * lax.axis_size("fsdp")
    me = lax.axis_index(AXES)
    if fast_mesh():
        dp, fsdp = lax.axis_index("dp"), lax.axis_index("fsdp")
        coords = jnp.stack([dp // 2, dp % 2, fsdp // 2, fsdp % 2]).astype(jnp.int32)
    else:
        coords = jnp.zeros((4,), jnp.int32)
    state = forward(coords, lengths, frames[0], cotangent[0], gather_shards(low(params), me))
    back = backward(coords, frames[0], state)
    steps = -(-shard_size // CHUNK)
    size = max(shard_size, CHUNK)
    grad_shard, gain_grads = scatter_grads(state, back, coords, me, shard_size, size)

    def filled(flat):
        return jnp.pad(flat, (0, size - shard_size)) if size > shard_size else flat

    bounds = segment_bounds()
    spans = most_segments(shard_size, devices)
    shard_low = me * shard_size
    first_segment = sum((shard_low >= b).astype(jnp.int32) for b in bounds[1:-1])
    table = jnp.asarray(bounds[1:] + [bounds[-1]] * spans, jnp.int32)
    ends = jnp.clip(lax.dynamic_slice(table, (first_segment,), (spans,)) - shard_low, 0, shard_size)
    segments = jnp.concatenate([first_segment[None], jnp.zeros((1,), jnp.int32), ends]).astype(jnp.int32)
    grid = pl.BlockSpec((CHUNK,), lambda step: (step,))
    whole = pl.BlockSpec((8, LANES), lambda step: (0, 0))
    flat_kind = jax.ShapeDtypeStruct((size,), F32)
    tile_kind = jax.ShapeDtypeStruct((8, LANES), F32)
    weights = filled(params)
    new_first, new_second, update, sums = pl.pallas_call(
        update_kernel,
        name="update",
        grid=(steps,),
        in_specs=[SM] + [grid] * 4,
        out_specs=[grid] * 3 + [whole],
        out_shape=[flat_kind] * 3 + [tile_kind],
    )(segments, weights, filled(first_moment), filled(second_moment), grad_shard)
    sums = sum_everywhere(sums)
    count = len(segment_shapes())
    new_params, *norms = pl.pallas_call(
        apply_kernel,
        name="apply",
        grid=(steps,),
        in_specs=[SM, whole, grid, grid],
        out_specs=[grid] + [pl.BlockSpec((count,), lambda step: (0,))] * 3,
        out_shape=[flat_kind] + [jax.ShapeDtypeStruct((count,), F32)] * 3,
    )(segments, sums, weights, update)
    return (
        state["out"].reshape(frames.shape),
        back["fgrad"].reshape(frames.shape),
        new_params[:shard_size],
        new_first[:shard_size],
        new_second[:shard_size],
        *norms,
        gain_grads.reshape(-1),
    )


def solution(mesh):
    placed = (
        P(("dp", "fsdp"), None, None),
        P(("dp", "fsdp")),
        P(("dp", "fsdp"), None, None),
        P(("dp", "fsdp")),
        P(("dp", "fsdp")),
        P(("dp", "fsdp")),
    )
    return jax.shard_map(
        shards,
        mesh=mesh,
        in_specs=placed,
        out_specs=(
            P(("dp", "fsdp"), None, None),
            P(("dp", "fsdp"), None, None),
            P(("dp", "fsdp")),
            P(("dp", "fsdp")),
            P(("dp", "fsdp")),
            P(),
            P(),
            P(),
            P(),
        ),
        check_vma=False,
    )
```

```python
import math
from types import SimpleNamespace

import jax
import jax.numpy as jnp
from jax import lax
from jax.experimental import pallas as pl
from jax.experimental.pallas import tpu as pltpu
from jax.sharding import PartitionSpec as P

STEP = 8
BETA_FIRST = 0.5
BETA_SECOND = 0.5
LEARN_RATE = 0.5
WEIGHT_DECAY = 0.01
ADAM_EPS = 1e-06
AXES = ("dp", "fsdp")


def segment_shapes():
    gate_width = CG // 2
    return [
        (D, FF),
        (FF, D),
        (D, 3 * D),
        (D, D),
        (D, CG),
        (gate_width, D),
        (2 * D, D),
        (D, FF),
        (FF, D),
        (5 * D + gate_width,),
        (KER, gate_width + 2 * D),
        (RELW, H),
    ]


D = 512
H = 8
HS = 64
FF = 2048
CG = 3072
KER = 31
RELW = 128
NORM_EPS = 1e-05
MASK_FILL = -1000000000.0
ROW = 512
HALF = ROW // 2
SLOTS = 160
KEYS = 256
PAD = 16
PADDED = SLOTS + 2 * PAD
GATE = CG // 2
BLOCK = {
    "ffa_in": (0, 4),
    "ffa_out": (4, 4),
    "qkv": (8, 3),
    "att_out": (11, 1),
    "cg_in": (12, 6),
    "cg_out": (18, 3),
    "merge": (21, 2),
    "ffb_in": (23, 4),
    "ffb_out": (27, 4),
    "small": (31, 1),
}
TAPS_AT = 8
REL_AT = 8 + 5 * KER
SMALL = 176
F32, BF16 = jnp.float32, jnp.bfloat16


def dot(left, right):
    return lax.dot_general(left, right, (((1,), (0,)), ((), ())), preferred_element_type=F32)


def dot_t(left, right):
    return lax.dot_general(left, right, (((1,), (1,)), ((), ())), preferred_element_type=F32)


def t_dot(left, right):
    return lax.dot_general(left, right, (((0,), (0,)), ((), ())), preferred_element_type=F32)


def low(values):
    return values.astype(BF16)


def each(count, body):
    for at in range(count):
        body(at)


def each_loop(count, body, together=1):
    def step(at, carry):
        for inner in range(together):
            body(at * together + inner)
        return carry

    lax.fori_loop(0, count // together, step, 0)


def part(at, size):
    if isinstance(at, int):
        return slice(at * size, at * size + size)
    return pl.ds(pl.multiple_of(at * size, size), size)


def rows_of(name):
    first, count = BLOCK[name]
    return slice(ROW * first, ROW * (first + count))


def lane_mean(values, width):
    return jnp.sum(values, axis=-1, keepdims=True) * (1.0 / width)


def normed(values):
    centered = values - lane_mean(values, values.shape[-1])
    scale = lax.rsqrt(lane_mean(centered * centered, values.shape[-1]) + NORM_EPS)
    return centered * scale, scale


def valid_rows(length):
    return (lax.broadcasted_iota(jnp.int32, (SLOTS, 1), 0) < length).astype(F32)


def fold_rows(values):
    return jnp.sum(values, axis=0, keepdims=True)


def norm_rows(source, gain, target):
    for k in range(2):
        hat, _ = normed(source[part(k, 80), :].astype(F32))
        target[part(k, 80), :] = low(hat * gain)


def norm_rows_back(values, gain, grad, add):
    total = jnp.zeros((1, values.shape[1]), F32)
    for k in range(2):
        rows = part(k, 80)
        hat, scale = normed(values[rows, :].astype(F32))
        mine = grad[rows, :]
        total = total + fold_rows(mine * hat)
        inner = mine * gain
        width = values.shape[1]
        moved = lane_mean(inner, width) + hat * lane_mean(inner * hat, width)
        add(rows, scale * (inner - moved))
    return total


TOTAL_ROWS = 16037
PARTS = 32
TILE = 16
SPAN = 528
STARTS = [TILE * (TOTAL_ROWS * d // (PARTS * TILE)) for d in range(PARTS + 1)]
FIRST_PARTS = max(d for d in range(PARTS) if STARTS[d] < ROW * sum(BLOCK["ffa_out"]))
SHORTEST = min(high - first for first, high in zip(STARTS, STARTS[1:]))


def start_of(d):
    return ((TOTAL_ROWS * d) >> 9) * TILE


def gathered_layout():
    layout = []
    for core in range(2):
        layout += [[(core, 0, 0, back, 0, SPAN, 0)] for back in range(4)]
        for y, x, first, last in ((0, 1, 0, HALF), (1, 0, HALF, SPAN)):
            whole = [(core, y, x, back, 0, SPAN, 0) for back in range(4)]
            diagonal = [(core, 1, 1, back, first, last) for back in range(4)]
            layout += [[whole[0]], [whole[1]]]
            layout += [[whole[2], (*diagonal[0], SPAN)], [whole[3], (*diagonal[1], SPAN)]]
            layout += [[(*diagonal[2], 0), (*diagonal[3], last - first)]]
    return layout


LAYOUT = gathered_layout()


def source_part(coords, piece):
    y, c, z, x = coords[0], coords[1], coords[2], coords[3]
    yy, cc, xx, zz = y ^ piece[1], c ^ piece[0], x ^ piece[2], (z + 4 - piece[3]) & 3
    return ((yy * 2 + cc) * 4 + zz) * 2 + xx


class Loads:
    def __init__(self, coords, sources, target, seams, sems):
        self.target, self.seams, self.sems = target, seams, sems
        self.here, self.joined = set(), set()
        seams[0, 0] = jnp.zeros((TILE, ROW), BF16)
        seams[PARTS, 1] = jnp.zeros((TILE, ROW), BF16)

        for soon in (True, False):
            for pieces, source in zip(LAYOUT, sources):
                for piece in pieces:
                    d = source_part(coords, piece)
                    first_ones = (d <= FIRST_PARTS) | (d == PARTS - 1)

                    @pl.when(first_ones if soon else jnp.logical_not(first_ones))
                    def _(piece=piece, source=source, d=d):
                        self.start(piece, source, d)

    def start(self, piece, source, d):
        def rows(at, size):
            return pl.ds(pl.multiple_of(at, TILE), size)

        first, last, offset = piece[4:]
        offset = offset - first
        start = start_of(d)
        length = start_of(d + 1) - start
        inner, outer = max(first, TILE), min(last, SHORTEST)
        sem = self.sems.at[d]
        pltpu.make_async_copy(
            source.at[offset + inner : offset + outer], self.target.at[rows(start + inner, outer - inner)], sem
        ).start()
        if first == 0:
            pltpu.make_async_copy(source.at[offset : offset + TILE], self.seams.at[d, 1], sem).start()
        if last == SPAN:

            @pl.when(length > SHORTEST)
            def _():
                pltpu.make_async_copy(
                    source.at[offset + SHORTEST : offset + SHORTEST + TILE],
                    self.target.at[rows(start + SHORTEST, TILE)],
                    sem,
                ).start()

            pltpu.make_async_copy(source.at[rows(offset + length, TILE)], self.seams.at[d + 1, 0], sem).start()

    def wait_part(self, d):
        if d in self.here or not 0 <= d < PARTS:
            return
        self.here.add(d)
        size = STARTS[d + 1] - STARTS[d] + TILE
        pltpu.make_async_copy(self.target.at[0:size], self.target.at[0:size], self.sems.at[d]).wait()

    def wait(self, name):
        rows = rows_of(name)
        last = min(rows.stop, STARTS[-1] + TILE)
        for d in range(PARTS + 1):
            if STARTS[d] < last and STARTS[d] + TILE > rows.start and d not in self.joined:
                self.wait_part(d - 1)
                self.wait_part(d)
                self.joined.add(d)
                self.target[STARTS[d] : STARTS[d] + TILE, :] = self.seams[d, 0] + self.seams[d, 1]
            if d < PARTS and STARTS[d] + TILE < last and STARTS[d + 1] > rows.start:
                self.wait_part(d)


class Emits:
    def __init__(self, coords, halves, sems):
        self.coords, self.halves, self.sems = coords, halves, sems
        self.pending = []

    def put(self, d, values, rows):
        core, z, x = (d // 8) % 2, (d // 2) % 4, d % 2
        kept, sent = self.halves[d // 16]
        far_x = self.coords[3] ^ x
        place = (self.coords[2] + 3 - z) & 3
        sem = self.sems.at[len(self.pending)]

        @pl.when(self.coords[1] == core)
        def _():
            pltpu.make_async_copy(values, kept.at[4 * far_x + place, rows], sem).start()

        @pl.when((self.coords[1] != core) & (far_x == 0))
        def _():
            pltpu.make_async_copy(values, sent[0].at[place, rows], sem).start()

        @pl.when((self.coords[1] != core) & (far_x == 1))
        def _():
            pltpu.make_async_copy(values, sent[1].at[place, rows], sem).start()

        self.pending.append(pltpu.make_async_copy(values, kept.at[0, rows], sem))

    def put_tensor(self, name, values):
        rows = rows_of(name)
        for d in range(PARTS):
            first, last = max(rows.start, STARTS[d]), min(rows.stop, STARTS[d] + SPAN)
            if first < last:
                self.put(d, values.at[first - rows.start : last - rows.start], slice(first - STARTS[d], last - STARTS[d]))

    def wait(self):
        for copy in self.pending:
            copy.wait()


def split_columns(raw, target, wide, stage):
    def chunk(k):
        rows = part(k, 128 * wide)
        for lane in range(4):
            stage[lane, 0 : 128 * wide, :] = raw[rows, lane * 128 : lane * 128 + 128].astype(F32)
        for c in range(wide):
            for lane in range(4):
                place = ROW * c + lane * 128
                target[part(k, 128), place : place + 128] = low(stage[lane, pl.ds(c, 128, stride=wide), :])

    each_loop(4, chunk)


def weight_columns(left, grads, wide, stage, left_t, target):
    left_t[...] = left[...].T

    def chunk(j):
        value = dot(left_t[...], grads[:, part(j, 256)])
        c, pair = j // 2, (j % 2) * 2
        for half in range(2):
            stage[pair + half, pl.ds(c, ROW, stride=wide), :] = value[:, 128 * half : 128 * half + 128]

    each(2 * wide, chunk)

    def lower(k):
        rows = part(k, ROW)
        for lane in range(4):
            target[rows, lane * 128 : lane * 128 + 128] = low(stage[lane, rows, :])

    each(wide, lower)


def weight_rows(left, grads, count, left_t, target):
    def chunk(k):
        left_t[...] = left[:, part(k, ROW)].T
        for at in range(2):
            target[part(k, ROW), 256 * at : 256 * at + 256] = low(dot(left_t[...], grads[:, 256 * at : 256 * at + 256]))

    each(count, chunk)


def feed_forward(inputs, gain, w_in, w_out, nrm, act, slope, result):
    norm_rows(inputs, gain, nrm)

    def up(j):
        at = part(j, 256)
        hidden = dot(nrm[...], w_in[:, at])
        sig = jax.nn.sigmoid(hidden)
        active = hidden * sig
        act[:, at] = low(active)
        slope[:, at] = low(sig + active * (1.0 - sig))

    each(FF // 256, up)

    def down(j):
        at = part(j, 256)
        result[:, at] = inputs[:, at].astype(F32) + 0.5 * dot(act[...], w_out[:, at])

    each(2, down)


def feed_back(dout, w_in, w_out, nrm, act, slope, dhid, dnrm, stage, left_t, g_in, g_out, emits, name):
    def up(j):
        at = part(j, 256)
        grad = dot_t(dout[...], w_out[at, :])
        dhid[:, at] = low(grad * slope[:, at].astype(F32))

    each(FF // 256, up)
    weight_rows(act, dout, 4, left_t, g_out)
    emits.put_tensor(name + "_out", g_out)

    def down(j):
        at = part(j, 256)
        dnrm[:, at] = dot_t(dhid[:, 0:FF], w_in[at, :])

    each(2, down)
    weight_columns(nrm, dhid, 4, stage, left_t, g_in)
    emits.put_tensor(name + "_in", g_in)


def bucket_map():
    entry = lax.broadcasted_iota(jnp.int32, (2 * ROW, ROW), 0) // H
    far = lax.broadcasted_iota(jnp.int32, (2 * ROW, ROW), 1)
    far = jnp.where(far >= ROW // 2, far - ROW, far)
    bucket = jnp.clip(far, -(RELW // 2), RELW // 2 - 1) + RELW // 2
    return (entry == bucket).astype(F32)


def own_entries(flat):
    entry = lax.broadcasted_iota(jnp.int32, (H, 2 * ROW), 1)
    head = lax.broadcasted_iota(jnp.int32, (H, 2 * ROW), 0)
    return jnp.where(lax.rem(entry, H) == head, flat, 0.0)


def tap_row(small, tap, row, lane):
    return small[lane, pl.ds(TAPS_AT + 5 * tap + row, 1), :]


def shifted_sum(padded, at, factor):
    total = None
    for low_part in range(8):
        slab = padded[low_part : low_part + SLOTS + 24, at]
        inner = None
        for high_part in range(4):
            offset = 8 * high_part + low_part
            if offset:
                term = factor(offset) * slab[8 * high_part : 8 * high_part + SLOTS]
                inner = term if inner is None else inner + term
        total = inner if total is None else total + inner
    return total


def convolve(padded, small, first_row, width, finish):

    def chunk(j):
        at = part(j, 128)
        row, lane = first_row + j // 4, j % 4
        finish(j, at, shifted_sum(padded, at, lambda offset: tap_row(small, offset - 1, row, lane)))

    each_loop(width // 128, chunk)


def convolve_back(grads, padded, small, first_row, width, sgrad, finish):

    def chunk(j):
        at = part(j, 128)
        row, lane = first_row + j // 4, j % 4
        finish(j, at, shifted_sum(grads, at, lambda offset: tap_row(small, KER - offset, row, lane)))
        own = grads[PAD : PAD + SLOTS, at]
        for low_part in range(8):
            slab = padded[low_part : low_part + SLOTS + 24, at]
            for high_part in range(4):
                offset = 8 * high_part + low_part
                if offset:
                    tile = slab[8 * high_part : 8 * high_part + SLOTS]
                    sgrad[lane, pl.ds(TAPS_AT + 5 * (offset - 1) + row, 1), :] = fold_rows(own * tile)

    each_loop(width // 128, chunk)


def clear_margins(padded):
    padded[0:PAD, :] = jnp.zeros((PAD, padded.shape[1]), F32)
    padded[PAD + SLOTS : PADDED, :] = jnp.zeros((PAD, padded.shape[1]), F32)


def gelu_parts(hidden):
    bell = jnp.exp(-0.5 * hidden * hidden)
    spread = 1.0 + (0.3275911 * 2.0**-0.5) * jnp.abs(hidden)
    near = pl.reciprocal(spread, approx=True)
    near = near * (2.0 - spread * near)
    tail = jnp.full_like(near, 0.5 * 1.061405429)
    for factor in (-1.453152027, 1.421413741, -0.284496736, 0.254829592):
        tail = tail * near + 0.5 * factor
    tail = tail * near * bell
    below = jnp.where(hidden >= 0.0, 1.0 - tail, tail)
    return hidden * below, below + hidden * bell * ((2.0 * math.pi) ** -0.5)


def attention_forward(r, length):
    norm_rows(r.x1, r.small[1:2, :], r.nrm_t)
    r.qkv[SLOTS:KEYS, :] = jnp.zeros((KEYS - SLOTS, 3 * D), BF16)
    flat = jnp.concatenate([r.small[REL_AT : REL_AT + 1, :], r.small[REL_AT + 1 : REL_AT + 2, :]], axis=1)
    r.bias[...] = dot(low(own_entries(jnp.broadcast_to(flat, (H, 2 * ROW)))), low(bucket_map()))

    def project(j):
        at = part(j, 256)
        r.qkv[0:SLOTS, at] = low(dot(r.nrm_t[...], r.w_qkv[:, at]))

    each(3 * D // 256, project)
    valid = lax.broadcasted_iota(jnp.int32, (1, KEYS), 1) < length
    first_half = lax.broadcasted_iota(jnp.int32, (1, 128), 1) < HS

    def heads(pair):
        queries = r.qkv[0:SLOTS, part(pair, 128)]
        keys = r.qkv[:, part(pair + 4, 128)]
        values = r.qkv[:, part(pair + 8, 128)]
        outs = []
        for odd in range(2):
            head = 2 * pair + odd
            half = first_half if odd == 0 else jnp.logical_not(first_half)
            mine = jnp.where(half, queries, jnp.zeros_like(queries))
            spread = jnp.broadcast_to(r.bias[pl.ds(head, 1), :], (SLOTS, ROW))
            spread = pltpu.roll(spread, 0, 1, stride=1, stride_axis=0)[:, 0:KEYS]
            scores = jnp.where(valid, dot_t(mine, keys) * HS ** (-0.5) + spread, MASK_FILL)
            shifted = jnp.exp(scores - jnp.max(scores, axis=-1, keepdims=True))
            chances = low(shifted / jnp.sum(shifted, axis=-1, keepdims=True))
            r.probs[head] = chances
            outs.append(dot(chances, values))
        r.ctx[:, part(pair, 128)] = low(jnp.where(first_half, outs[0], outs[1]))

    each(H // 2, heads)

    def project_out(j):
        at = part(j, 256)
        r.cat[:, at] = dot(r.ctx[...], r.w[rows_of("att_out"), at])

    each(2, project_out)


def gating_forward(r, length):
    norm_rows(r.x1, r.small[2:3, :], r.nrm_c)

    def up(j):
        at = part(j, 256)
        r.hid[...] = dot(r.nrm_c[...], r.w_cg[:, at])
        for k in range(5):
            rows = part(k, 32)
            active, slope = gelu_parts(r.hid[rows, :])
            r.ug[rows, at] = active
            r.slope_c[rows, at] = low(slope)

    each_loop(CG // 256, up, 4)
    tiles = [slice(GATE + 128 * j, GATE + 128 * j + 128) for j in range(GATE // 128)]
    total = jnp.zeros((SLOTS, 128), F32)
    for at in tiles:
        total = total + r.ug[:, at]
    mean = lane_mean(total, GATE)
    total = jnp.zeros((SLOTS, 128), F32)
    for at in tiles:
        centered = r.ug[:, at] - mean
        total = total + centered * centered
    scale = lax.rsqrt(lane_mean(total, GATE) + NORM_EPS)
    r.gmean[...] = jnp.broadcast_to(mean, (SLOTS, 128))
    r.gscale[...] = jnp.broadcast_to(scale, (SLOTS, 128))
    scale = scale * valid_rows(length)
    for j, at in enumerate(tiles):
        gain = r.small[5 + j // 4 : 6 + j // 4, part(j % 4, 128)]
        r.gpad[PAD : PAD + SLOTS, part(j, 128)] = (r.ug[:, at] - mean) * scale * gain

    def finish(j, at, value):
        r.cv[:, at] = low(value)
        r.gated[:, at] = low(r.ug[:, at] * value)

    convolve(r.gpad, r.tiles, 0, GATE, finish)

    def down(j):
        r.cat[:, part(j + 2, 256)] = dot(r.gated[...], r.w[rows_of("cg_out"), part(j, 256)])

    each(2, down)


def merge_forward(r, length):
    valid = valid_rows(length)
    for j in range(8):
        at = part(j, 128)
        r.mpad[PAD : PAD + SLOTS, at] = r.cat[:, at] * valid

    def finish(j, at, value):
        r.mixed[:, at] = low(r.cat[:, at] + value)

    convolve(r.mpad, r.tiles, 3, 2 * D, finish)

    def merge(j):
        at = part(j, 256)
        r.x2[:, at] = r.x1[:, at] + dot(r.mixed[...], r.w[rows_of("merge"), at])

    each(2, merge)


def final_norm(r, length):
    gain = r.small[4:5, :]
    valid = valid_rows(length)
    total = jnp.zeros((1, D), F32)
    for k in range(2):
        rows = part(k, 80)
        hat, scale = normed(r.x3[rows, :])
        r.out[rows, :] = low(hat * gain * valid[80 * k : 80 * k + 80])
        mine = r.cot[rows, :].astype(F32) * valid[80 * k : 80 * k + 80]
        total = total + fold_rows(mine * hat)
        inner = mine * gain
        back = scale * (inner - (lane_mean(inner, D) + hat * lane_mean(inner * hat, D)))
        r.dx[rows, :] = back
        r.dout[rows, :] = low(0.5 * back)
    r.gains[4:5, :] = total


def merge_back(r, length, emits):
    for k in range(2):
        r.dout[part(k, 80), :] = low(r.dx[part(k, 80), :])
    w_merge = r.w.at[rows_of("merge")]

    def merge(j):
        at = part(j, 256)
        r.dpad[PAD : PAD + SLOTS, at] = dot_t(r.dout[...], w_merge[at, :])

    each(2 * D // 256, merge)
    weight_rows(r.mixed, r.dout, 2, r.left_t, w_merge)
    emits.put_tensor("merge", w_merge)

    def finish(j, at, value):
        r.djoin[:, at] = low(r.dpad[PAD : PAD + SLOTS, at] + value * valid_rows(length))

    convolve_back(r.dpad, r.mpad, r.tiles, 3, 2 * D, r.tgrad, finish)


def gating_back(r, length, emits):
    w_co = r.w.at[rows_of("cg_out")]

    def gate(j):
        at = part(j, 256)
        value = dot_t(r.djoin[:, D:], w_co[at, :])
        r.dhid[:, at] = low(value * r.cv[:, at].astype(F32) * r.slope_c[:, at].astype(F32))
        r.dpad[PAD : PAD + SLOTS, at] = value * r.ug[:, at]

    each(GATE // 256, gate)
    r.dout[...] = r.djoin[:, D:]
    weight_rows(r.gated, r.dout, 3, r.left_t, w_co)
    emits.put_tensor("cg_out", w_co)

    def finish(j, at, value):
        r.dgate[:, at] = value * valid_rows(length)

    convolve_back(r.dpad, r.gpad, r.tiles, 0, GATE, r.tgrad, finish)
    tiles = GATE // 128
    for quarter in range(4):
        rows = part(quarter, SLOTS // 4)
        mean, scale = r.gmean[rows, :], r.gscale[rows, :]
        total, total_hat = jnp.zeros_like(mean), jnp.zeros_like(mean)

        def parts(j, rows=rows, mean=mean, scale=scale):
            row, lane = 5 + j // 4, part(j % 4, 128)
            hat = (r.ug[rows, part(j + tiles, 128)] - mean) * scale
            grad = r.dgate[rows, part(j, 128)]
            return hat, grad, grad * r.small[row : row + 1, lane]

        for j in range(tiles):
            hat, grad, inner = parts(j)
            products = jnp.sum((grad * hat).reshape(-1, 8, 128), axis=0)
            r.gate_sums[part(j, 8), :] = products if quarter == 0 else r.gate_sums[part(j, 8), :] + products
            total = total + inner
            total_hat = total_hat + inner * hat
        total = jnp.broadcast_to(lane_mean(total, GATE), total.shape)
        total_hat = jnp.broadcast_to(lane_mean(total_hat, GATE), total.shape)
        for j in range(tiles):
            hat, _, inner = parts(j)
            far = part(j + tiles, 128)
            r.dgate[rows, part(j, 128)] = scale * (inner - total - hat * total_hat)
    for j in range(tiles):
        far = part(j + tiles, 128)
        r.dhid[:, far] = low(r.dgate[:, part(j, 128)] * r.slope_c[:, far].astype(F32))
        r.tgrad[j % 4, 5 + j // 4 : 6 + j // 4, :] = fold_rows(r.gate_sums[part(j, 8), :])

    def down(j):
        at = part(j, 256)
        r.dnrm[:, at] = dot_t(r.dhid[...], r.w_cg[at, :])

    each(2, down)
    g_cg = r.w.at[rows_of("cg_in")]
    weight_columns(r.nrm_c, r.dhid, 6, r.stage, r.left_t, g_cg)
    emits.put_tensor("cg_in", g_cg)

    def add(rows, back):
        r.dx[rows, :] += back

    r.gains[2:3, :] = norm_rows_back(r.x1, r.small[2:3, :], r.dnrm, add)


def forward_kernel(names, coords, length_ref, frames, cot, *refs):
    sources, refs = refs[: len(LAYOUT)], refs[len(LAYOUT) :]
    r = SimpleNamespace(**dict(zip(names, refs)))
    r.cot = cot
    length = length_ref[0]
    loads = Loads(coords, sources, r.w, r.seams, r.load_sems)
    kept = []

    def keep(source, target):
        copy = pltpu.make_async_copy(source, target, r.keep_sems.at[len(kept)])
        copy.start()
        kept.append(copy)

    for padded in (r.gpad, r.mpad, r.dpad):
        clear_margins(padded)
    r.tgrad[...] = jnp.zeros_like(r.tgrad)
    r.gains[...] = jnp.zeros_like(r.gains)
    loads.wait("small")
    r.small[...] = r.w[ROW * 31 : ROW * 31 + SMALL, :].astype(F32)
    for lane in range(4):
        r.tiles[lane] = r.small[:, part(lane, 128)]
    loads.wait("ffa_in")
    split_columns(r.w.at[rows_of("ffa_in")], r.w_ffa_in, 4, r.stage)
    keep(r.w_ffa_in, r.keep_ffa_in)
    loads.wait("ffa_out")
    keep(r.w.at[rows_of("ffa_out")], r.keep_ffa_out)
    feed_forward(frames, r.small[0:1, :], r.w_ffa_in, r.w.at[rows_of("ffa_out")], r.nrm, r.act, r.slope, r.x1)
    keep(r.nrm, r.keep_nrm)
    keep(r.act, r.keep_act)
    keep(r.slope, r.keep_slope)
    keep(r.x1, r.keep_x1)
    loads.wait("qkv")
    split_columns(r.w.at[rows_of("qkv")], r.w_qkv, 3, r.stage)
    keep(r.w_qkv, r.keep_qkv)
    loads.wait("att_out")
    keep(r.w.at[rows_of("att_out")], r.keep_att)
    attention_forward(r, length)
    keep(r.nrm_t, r.keep_nrm_t)
    keep(r.qkv, r.keep_heads)
    keep(r.probs, r.keep_probs)
    keep(r.ctx, r.keep_ctx)
    loads.wait("cg_in")
    split_columns(r.w.at[rows_of("cg_in")], r.w_cg, 6, r.stage)
    loads.wait("cg_out")
    gating_forward(r, length)
    loads.wait("merge")
    merge_forward(r, length)
    loads.wait("ffb_in")
    split_columns(r.w.at[rows_of("ffb_in")], r.w_ffb_in, 4, r.stage)
    loads.wait("ffb_out")
    w_out = r.w.at[rows_of("ffb_out")]
    feed_forward(r.x2, r.small[3:4, :], r.w_ffb_in, w_out, r.nrm_b, r.act_b, r.slope_b, r.x3)
    final_norm(r, length)
    emits = Emits(
        coords,
        ((r.low_kept, (r.low_near, r.low_far)), (r.high_kept, (r.high_near, r.high_far))),
        r.emit_sems,
    )
    feed_back(
        r.dout, r.w_ffb_in, w_out, r.nrm_b, r.act_b, r.slope_b, r.dhid, r.dnrm, r.stage, r.left_t,
        r.w.at[rows_of("ffb_in")], w_out, emits, "ffb",
    )

    def add(rows, back):
        r.dx[rows, :] += back

    r.gains[3:4, :] = norm_rows_back(r.x2, r.small[3:4, :], r.dnrm, add)
    merge_back(r, length, emits)
    keep(r.djoin, r.keep_djoin)
    gating_back(r, length, emits)
    keep(r.dx, r.keep_dx)
    for lane in range(4):
        at = part(lane, 128)
        r.gains[5:8, at] = r.tgrad[lane, 5:8, :]
        r.w[ROW * 31 : ROW * 31 + SMALL, at] = low(r.tgrad[lane])
    r.w[ROW * 31 : ROW * 31 + 16, :] = low(
        jnp.concatenate(
            [
                jnp.zeros((8, ROW), F32),
                jnp.concatenate([r.tgrad[lane, 8:16, :] for lane in range(4)], axis=1),
            ],
            axis=0,
        )
    )
    r.w[ROW * 31 + SMALL : ROW * 32, :] = jnp.zeros((ROW - SMALL, ROW), BF16)
    emits.put_tensor("small", r.w.at[rows_of("small")])
    for copy in kept:
        copy.wait()
    emits.wait()


def attention_back(r, emits):
    def project(j):
        at = part(j, 256)
        r.dctx[:, at] = low(dot_t(r.datt[...], r.w_att[at, :]))

    each(2, project)
    weight_rows(r.ctx, r.datt, 1, r.left_t, r.w_att)
    emits.put_tensor("att_out", r.w_att)
    first_half = lax.broadcasted_iota(jnp.int32, (1, 128), 1) < HS
    at_row = lax.broadcasted_iota(jnp.int32, (SLOTS, SLOTS), 0)
    at_column = lax.broadcasted_iota(jnp.int32, (SLOTS, SLOTS), 1)
    flip = low((at_row + at_column == SLOTS - 1).astype(F32))

    def heads(pair):
        queries = r.qkv[0:SLOTS, part(pair, 128)]
        keys = r.qkv[:, part(pair + 4, 128)]
        values = r.qkv[:, part(pair + 8, 128)]
        context = r.dctx[:, part(pair, 128)]
        q_parts, k_parts, v_parts = [], [], []
        for odd in range(2):
            head = 2 * pair + odd
            half = first_half if odd == 0 else jnp.logical_not(first_half)
            chances = r.probs[head]
            v_parts.append(t_dot(chances, context)[0:SLOTS])
            wide_chances = chances.astype(F32)
            chance_grad = dot_t(jnp.where(half, context, jnp.zeros_like(context)), values)
            inner = jnp.sum(wide_chances * chance_grad, axis=-1, keepdims=True)
            score_grad = low(wide_chances * (chance_grad - inner))
            q_parts.append(dot(score_grad, keys))
            k_parts.append(t_dot(score_grad, queries)[0:SLOTS])
            wide = jnp.concatenate([dot(flip, score_grad), jnp.zeros((SLOTS, ROW - KEYS), F32)], axis=1)
            wide = pltpu.roll(wide, ROW - SLOTS + 1, 1, stride=1, stride_axis=0)
            r.sums[pl.ds(head, 1), :] = fold_rows(wide)
        scale = HS ** (-0.5)
        r.dhid[:, part(pair, 128)] = low(jnp.where(first_half, q_parts[0], q_parts[1]) * scale)
        r.dhid[:, part(pair + 4, 128)] = low(jnp.where(first_half, k_parts[0], k_parts[1]) * scale)
        r.dhid[:, part(pair + 8, 128)] = low(jnp.where(first_half, v_parts[0], v_parts[1]))

    each(H // 2, heads)

    def down(j):
        at = part(j, 256)
        r.dnrm[:, at] = dot_t(r.dhid[:, 0 : 3 * D], r.w_qkv[at, :])

    each(2, down)

    def add(rows, back):
        r.dx[rows, :] += back
        r.dout[rows, :] = low(0.5 * r.dx[rows, :])

    r.late[1:2, :] = norm_rows_back(r.x1, r.gain_rows[1:2, :], r.dnrm, add)


def attention_weights_back(r, emits):
    weight_columns(r.nrm_t, r.dhid, 3, r.stage, r.left_t, r.g_qkv)
    emits.put_tensor("qkv", r.g_qkv)
    by_entry = lax.dot_general(
        r.sums[...],
        bucket_map(),
        (((1,), (1,)), ((), ())),
        precision=lax.Precision.HIGHEST,
        preferred_element_type=F32,
    )
    flat = fold_rows(own_entries(by_entry))
    r.late[8:9, :] = flat[:, 0:ROW]
    r.late[9:10, :] = flat[:, ROW:]


def backward_kernel(names, coords, frames, gains, gain_rows, *refs):
    r = SimpleNamespace(**dict(zip(names, refs)))
    r.gain_rows = gain_rows
    waits = {}
    for at, (name, source, target) in enumerate(
        (
            ("att", r.in_att, r.w_att),
            ("djoin", r.in_djoin.at[:, 0:D], r.datt),
            ("ctx", r.in_ctx, r.ctx),
            ("heads", r.in_heads, r.qkv),
            ("probs", r.in_probs, r.probs),
            ("qkv", r.in_qkv, r.w_qkv),
            ("x1", r.in_x1, r.x1),
            ("dx", r.in_dx, r.dx),
            ("nrm_t", r.in_nrm_t, r.nrm_t),
            ("ffa_out", r.in_ffa_out, r.w_ffa_out),
            ("slope", r.in_slope, r.slope),
            ("act", r.in_act, r.act),
            ("ffa_in", r.in_ffa_in, r.w_ffa_in),
            ("nrm", r.in_nrm, r.nrm),
        )
    ):
        waits[name] = pltpu.make_async_copy(source, target, r.load_sems.at[at])
        waits[name].start()
    r.late[...] = jnp.zeros_like(r.late)
    emits = Emits(coords, ((r.low_kept, (r.low_near, r.low_far)),), r.emit_sems)
    for name in ("att", "djoin", "ctx", "heads", "probs", "qkv", "x1", "dx"):
        waits[name].wait()
    attention_back(r, emits)
    waits["nrm_t"].wait()
    attention_weights_back(r, emits)
    for name in ("ffa_out", "slope", "act", "ffa_in", "nrm"):
        waits[name].wait()
    feed_back(
        r.dout, r.w_ffa_in, r.w_ffa_out, r.nrm, r.act, r.slope, r.dhid, r.dnrm, r.stage, r.left_t, r.g_ffa_in,
        r.w_ffa_out, emits, "ffa",
    )

    def add(rows, back):
        r.fgrad[rows, :] = low(r.dx[rows, :] + back)

    r.late[0:1, :] = norm_rows_back(frames, gain_rows[0:1, :], r.dnrm, add)
    r.late[2:8, :] = gains[2:8, :]
    emits.wait()


VM = pl.BlockSpec(memory_space=pltpu.VMEM)
SM = pl.BlockSpec(memory_space=pltpu.SMEM)
ANY = pl.BlockSpec(memory_space=pl.ANY)
WIDE, THIN = ((SLOTS, D), F32), ((SLOTS, D), BF16)
FULL = ((SLOTS, FF), BF16)
KEPT, SENT = ((8, SPAN, ROW), BF16), ((4, SPAN, ROW), BF16)

FORWARD_OUT = {
    "out": (VM, THIN),
    "gains": (VM, ((8, ROW), F32)),
    "small": (VM, ((SMALL, ROW), F32)),
    "high_kept": (ANY, KEPT),
    "high_near": (ANY, SENT),
    "high_far": (ANY, SENT),
    "low_kept": (ANY, KEPT),
    "low_near": (ANY, SENT),
    "low_far": (ANY, SENT),
    "keep_ffa_in": (ANY, ((D, FF), BF16)),
    "keep_ffa_out": (ANY, ((FF, D), BF16)),
    "keep_qkv": (ANY, ((D, 3 * D), BF16)),
    "keep_att": (ANY, ((D, D), BF16)),
    "keep_nrm": (ANY, THIN),
    "keep_act": (ANY, FULL),
    "keep_slope": (ANY, FULL),
    "keep_x1": (ANY, WIDE),
    "keep_nrm_t": (ANY, THIN),
    "keep_heads": (ANY, ((KEYS, 3 * D), BF16)),
    "keep_probs": (ANY, ((H, SLOTS, KEYS), BF16)),
    "keep_ctx": (ANY, THIN),
    "keep_djoin": (ANY, ((SLOTS, 2 * D), BF16)),
    "keep_dx": (ANY, WIDE),
}
FORWARD_SCRATCH = {
    "w": ((32 * ROW, ROW), BF16),
    "w_ffa_in": ((D, FF), BF16),
    "w_qkv": ((D, 3 * D), BF16),
    "w_cg": ((D, CG), BF16),
    "w_ffb_in": ((D, FF), BF16),
    "stage": ((4, 6 * ROW, 128), F32),
    "left_t": ((ROW, SLOTS), BF16),
    "tiles": ((4, SMALL, 128), F32),
    "tgrad": ((4, SMALL, 128), F32),
    "bias": ((H, ROW), F32),
    "nrm": THIN,
    "act": FULL,
    "slope": FULL,
    "nrm_t": THIN,
    "qkv": ((KEYS, 3 * D), BF16),
    "probs": ((H, SLOTS, KEYS), BF16),
    "ctx": THIN,
    "nrm_c": THIN,
    "hid": ((SLOTS, 256), F32),
    "ug": ((SLOTS, CG), F32),
    "slope_c": ((SLOTS, CG), BF16),
    "gmean": ((SLOTS, 128), F32),
    "gscale": ((SLOTS, 128), F32),
    "gate_sums": ((8 * GATE // 128, 128), F32),
    "gpad": ((PADDED, GATE), F32),
    "cv": ((SLOTS, GATE), BF16),
    "gated": ((SLOTS, GATE), BF16),
    "cat": ((SLOTS, 2 * D), F32),
    "mpad": ((PADDED, 2 * D), F32),
    "mixed": ((SLOTS, 2 * D), BF16),
    "nrm_b": THIN,
    "act_b": FULL,
    "slope_b": FULL,
    "dpad": ((PADDED, GATE), F32),
    "djoin": ((SLOTS, 2 * D), BF16),
    "dgate": ((SLOTS, GATE), F32),
    "dhid": ((SLOTS, CG), BF16),
    "dnrm": WIDE,
    "dout": THIN,
    "dx": WIDE,
    "x1": WIDE,
    "x2": WIDE,
    "x3": WIDE,
    "seams": ((PARTS + 1, 2, TILE, ROW), BF16),
    "load_sems": PARTS,
    "keep_sems": 16,
    "emit_sems": 40,
}
BACKWARD_IN = (
    "ffa_in", "ffa_out", "qkv", "att", "nrm", "act", "slope", "x1", "nrm_t", "heads", "probs", "ctx", "djoin", "dx",
)
PASSED = ("low_kept", "low_near", "low_far")
BACKWARD_OUT = {
    "fgrad": (VM, THIN),
    "late": (VM, ((16, ROW), F32)),
    "low_kept": (ANY, KEPT),
    "low_near": (ANY, SENT),
    "low_far": (ANY, SENT),
}
BACKWARD_SCRATCH = {
    "w_ffa_in": ((D, FF), BF16),
    "w_ffa_out": ((FF, D), BF16),
    "w_qkv": ((D, 3 * D), BF16),
    "w_att": ((D, D), BF16),
    "g_ffa_in": ((FF, D), BF16),
    "g_qkv": ((3 * D, D), BF16),
    "stage": ((4, 4 * ROW, 128), F32),
    "left_t": ((ROW, SLOTS), BF16),
    "sums": ((H, ROW), F32),
    "nrm": THIN,
    "act": FULL,
    "slope": FULL,
    "nrm_t": THIN,
    "qkv": ((KEYS, 3 * D), BF16),
    "probs": ((H, SLOTS, KEYS), BF16),
    "ctx": THIN,
    "datt": THIN,
    "dctx": THIN,
    "dhid": FULL,
    "dnrm": WIDE,
    "dout": THIN,
    "dx": WIDE,
    "x1": WIDE,
    "load_sems": 14,
    "emit_sems": 24,
}


def call(kernel, name, ins, outs, scratch, limit, aliases=None):
    return pl.pallas_call(
        kernel,
        name=name,
        in_specs=[space for space, _ in ins],
        out_specs=[space for space, _ in outs],
        out_shape=[jax.ShapeDtypeStruct(*kind) for _, kind in outs],
        scratch_shapes=[
            pltpu.SemaphoreType.DMA((each_one,)) if isinstance(each_one, int) else pltpu.VMEM(*each_one)
            for each_one in scratch
        ],
        input_output_aliases=aliases or {},
        compiler_params=pltpu.CompilerParams(vmem_limit_bytes=limit * 2**20),
    )(*[array for _, array in ins])


def forward(coords, length, frames, cot, blocks):
    def kernel(*refs):
        forward_kernel([*FORWARD_OUT, *FORWARD_SCRATCH], *refs)

    outs = call(
        kernel,
        "forward",
        [(SM, coords), (SM, length), (VM, frames), (VM, cot)] + [(ANY, block) for block in blocks],
        list(FORWARD_OUT.values()),
        list(FORWARD_SCRATCH.values()),
        58,
    )
    return dict(zip(FORWARD_OUT, outs))


def backward(coords, frames, state):
    def kernel(*refs):
        names = ["in_" + name for name in BACKWARD_IN + PASSED]
        backward_kernel([*names, *BACKWARD_OUT, *BACKWARD_SCRATCH], *refs)

    ins = [(SM, coords), (VM, frames), (VM, state["gains"]), (VM, state["small"])]
    ins += [(ANY, state["keep_" + name]) for name in BACKWARD_IN]
    ins += [(ANY, state[name]) for name in PASSED]
    outs = call(
        kernel,
        "backward",
        ins,
        list(BACKWARD_OUT.values()),
        list(BACKWARD_SCRATCH.values()),
        58,
        {len(ins) - 3 + at: 2 + at for at in range(3)},
    )
    return dict(zip(BACKWARD_OUT, outs))


def segment_bounds():
    bounds = [0]
    for extent in segment_shapes():
        bounds.append(bounds[-1] + math.prod(extent))
    return bounds


def fast_mesh():
    return lax.axis_size("dp") == 4 and lax.axis_size("fsdp") == 8


def over_x(value):
    return lax.ppermute(value, "fsdp", [(i, i ^ 1) for i in range(8)])


def over_y(value):
    return lax.ppermute(value, "dp", [(i, i ^ 2) for i in range(4)])


def over_core(value):
    return lax.ppermute(value, "dp", [(i, i ^ 1) for i in range(4)])


def round_z(value):
    return lax.ppermute(value, "fsdp", [(i, (i + 2) % 8) for i in range(8)])


def over_z(value, step):
    return lax.ppermute(value, "fsdp", [(i, i ^ (2 * step)) for i in range(8)])


def after(value, *others):
    return lax.optimization_barrier((value, *others))[0]


def shard_offset(me, shard_size):
    return me * shard_size - start_of(me) * ROW


def gather_shards(shard, me):
    shard_size = shard.shape[0]
    if not fast_mesh():
        whole = lax.all_gather(shard, AXES, axis=0, tiled=True)
        whole = jnp.pad(whole, (0, (STARTS[-1] + SPAN) * ROW - whole.shape[0])).reshape(-1, ROW)
        spans = [whole[start : start + SPAN] for start in STARTS[:-1]]
        spans = spans[:1] + [jnp.concatenate([jnp.zeros((TILE, ROW), BF16), span[TILE:]]) for span in spans[1:]]
        return [
            jnp.concatenate([spans[source_part((0, 0, 0, 0), piece)][piece[4] : piece[5]] for piece in pieces])
            for pieces in LAYOUT
        ]
    most = TILE * ROW
    padded = jnp.pad(shard, (most, SPAN * ROW - shard_size))
    span = lax.dynamic_slice(padded, (most - shard_offset(me, shard_size),), (SPAN * ROW,)).reshape(SPAN, ROW)
    own, by_x, by_y = [span], [], []
    for back in range(4):
        if back < 3:
            own.append(round_z(own[back]))
        if back < 2:
            by_x.append(over_x(own[back]))
            by_y.append(over_y(own[back]))
            own[back + 1], by_x[back], by_y[back] = lax.optimization_barrier((own[back + 1], by_x[back], by_y[back]))
        else:
            by_x.append(over_x(jnp.concatenate([own[back], by_y[back - 2][:HALF]])))
            by_y.append(over_y(jnp.concatenate([own[back], by_x[back - 2][HALF:SPAN]])))
    by_x.append(over_x(jnp.concatenate([by_y[2][:HALF], by_y[3][:HALF]])))
    by_y.append(over_y(jnp.concatenate([by_x[2][HALF:SPAN], by_x[3][HALF:SPAN]])))
    late_ones = (by_x[3], by_y[3])
    far_own = [over_core(each_one) for each_one in own[:2]] + [over_core(after(each_one, *late_ones)) for each_one in own[2:]]
    far = [far_own]
    for way in (by_x, by_y):
        far.append([over_core(way[0]), over_core(way[1]), over_core(after(way[2], *late_ones))])
        far[-1] += [over_core(way[at]) for at in (3, 4)]
    return own + by_x + by_y + far[0] + far[1] + far[2]


def added(*parts):
    total = parts[0].astype(F32)
    for each_one in parts[1:]:
        total = total + each_one.astype(F32)
    return total


SIDES = (slice(0, HALF), slice(HALF, SPAN))


HBM = pl.BlockSpec(memory_space=pltpu.HBM)


def span_sums(coords, own_half, x, places, low_kept, low_got, high_kept, high_got, sides):
    count = len(places)
    together = sides if isinstance(sides, int) else 0
    pieces = [(at, rows) for at in range(count) for rows in (() if together else sides)]

    def kernel(coords, low_kept, low_got, high_kept, high_got, *refs):
        outs, (kept, got, total, sems, out_sems) = refs[:-5], refs[-5:]
        high = coords[0] == int(own_half)
        for source, other, wanted in ((low_kept, low_got, jnp.logical_not(high)), (high_kept, high_got, high)):

            @pl.when(wanted)
            def _(source=source, other=other):
                for at, place in enumerate(places):
                    pltpu.make_async_copy(source.at[4 * x + place], kept.at[at], sems.at[2 * at]).start()
                    pltpu.make_async_copy(other.at[place], got.at[at], sems.at[2 * at + 1]).start()

        copies = []
        for at in range(count):
            pltpu.make_async_copy(low_kept.at[at], kept.at[at], sems.at[2 * at]).wait()
            pltpu.make_async_copy(low_got.at[at], got.at[at], sems.at[2 * at + 1]).wait()

            def add(k, at=at):
                rows = part(k, SPAN // 11)
                total[at, rows] = low(kept[at, rows].astype(F32) + got[at, rows].astype(F32))

            each_loop(11, add)
            if together:
                out = outs[at // together].at[at % together]
                copies.append(pltpu.make_async_copy(total.at[at], out, out_sems.at[at]))
                copies[-1].start()
            for which, (mine, rows) in enumerate(pieces):
                if mine == at:
                    copies.append(pltpu.make_async_copy(total.at[at, rows], outs[which], out_sems.at[which]))
                    copies[-1].start()
        for copy in copies:
            copy.wait()

    spans = ((count, SPAN, ROW), BF16)
    arrays = [(HBM, low_kept), (ANY, low_got), (HBM, high_kept), (ANY, high_got)]
    if together:
        outs = [(ANY, ((together, SPAN, ROW), BF16))] * (count // together)
    else:
        outs = [(ANY, ((rows.stop - rows.start, ROW), BF16)) for _, rows in pieces]
    sums = call(
        kernel, "span_sums", [(SM, coords)] + arrays, outs, [spans] * 3 + [2 * count, max(count, len(pieces))], 56
    )
    return sums if together else [sums[len(sides) * at : len(sides) * (at + 1)] for at in range(count)]


def late_rows(late, above, below):
    gains = jnp.pad(late[0:8], ((above, below - 8), (0, 0)))
    return gains + jnp.pad(late[8:10], ((above + REL_AT, below - REL_AT - 2), (0, 0)))


def scatter_slow(state, back, shard_size, padded):
    late = back["late"]
    pieces = []
    for source, half in ((back, "low"), (state, "high")):
        for core in range(2):
            for at in range(8):
                z, x = at // 2, at % 2
                if core == 0:
                    span = source[half + "_kept"][4 * x + 3 - z]
                else:
                    span = source[half + ("_near", "_far")[x]][3 - z]
                d = len(pieces)
                pieces.append(span[: STARTS[d + 1] - STARTS[d] if d < PARTS - 1 else SPAN])
    rows = jnp.concatenate(pieces)
    first = ROW * BLOCK["small"][0]
    rows = low(rows.astype(F32) + late_rows(late, first, rows.shape[0] - first))
    flat = rows.reshape(-1)[: segment_bounds()[-1]]
    shard = lax.psum_scatter(flat, AXES, scatter_dimension=0, tiled=True)
    return jnp.pad(shard, (0, padded - shard_size)).astype(F32), lax.psum(late[0:8], AXES)


def scatter_grads(state, back, coords, me, shard_size, padded):
    if not fast_mesh():
        return scatter_slow(state, back, shard_size, padded)
    high = coords[0] == 1
    high_kept, low_kept = state["high_kept"], back["low_kept"]
    high_got = [over_core(state["high_near"]), over_core(state["high_far"])]
    low_far = over_core(back["low_far"])

    def chip_sum(own_half, x, places, sides):
        got = (low_far if x else low_near, high_got[x])
        return span_sums(coords, own_half, x, places, low_kept, got[0], high_kept, got[1], sides)

    for_y, for_x = chip_sum(False, 1, range(4), 2)
    from_x, from_y = over_x(for_x), over_y(for_y)
    low_near = over_core(after(back["low_near"], for_x, for_y))
    late = after(back["late"], for_x, for_y)
    late = late + over_core(late)
    late = late + over_z(late, 1)
    to_x = chip_sum(True, 1, range(4), SIDES)
    to_y = chip_sum(False, 0, range(4), SIDES)
    mine = chip_sum(True, 0, range(4), SIDES)
    late = late + over_z(after(late, mine[3][1], to_y[3][1], to_x[3][1]), 2)
    from_y, to_x, to_y, mine, late = lax.optimization_barrier((from_y, to_x, to_y, mine, late))
    late = late + over_x(late)
    late = late + over_y(late)
    running = [None, None]
    before = [(), ()]
    for at in range(4):
        for side, rows in enumerate(SIDES):
            send_x, send_y = to_x[at][side], to_y[at][side]
            if at < 2:
                send_x = low(added(send_x, from_y[at, rows]))
            else:
                send_y = low(added(send_y, from_x[at - 2, rows]))
            got_x, got_y = over_x(after(send_x, *before[side])), over_y(after(send_y, *before[side]))
            before[side] = (got_x, got_y)
            parts = [mine[at][side], got_x, got_y]
            if at:
                parts.append(round_z(running[side]))
            running[side] = added(*parts)
            if at < 3:
                running[side] = low(running[side])
    total = jnp.concatenate(running)
    first = ROW * BLOCK["small"][0] - STARTS[PARTS - 1]
    total = total + jnp.where(me == PARTS - 1, 1.0, 0.0) * late_rows(late, first, SPAN - first)
    flat = jnp.pad(total.reshape(-1), (0, max(0, TILE * ROW + padded - SPAN * ROW)))
    return lax.dynamic_slice(flat, (shard_offset(me, shard_size),), (padded,)), late[0:8]


def sum_everywhere(vector):
    if not fast_mesh():
        return lax.psum(vector, AXES)
    vector = vector + over_core(vector)
    vector = vector + over_x(vector)
    vector = vector + over_y(vector)
    vector = vector + over_z(vector, 1)
    return vector + over_z(vector, 2)


def most_segments(shard_size, devices):
    bounds = segment_bounds()
    most = 1
    for at in range(devices):
        low_end, high_end = at * shard_size, (at + 1) * shard_size
        most = max(most, sum(1 for b in bounds[1:-1] if low_end < b < high_end) + 1)
    return most


LANES = 128
CHUNK = 1024 * LANES
STRIP = 128 * LANES


def chunk_spans(segments, step):
    first, last = step * CHUNK, (step + 1) * CHUNK
    for at in range(segments.shape[0] - 2):
        start, end = segments[1 + at], segments[2 + at]
        whole = (start <= first) & (last <= end)
        some = (start < last) & (end > first) & jnp.logical_not(whole)
        yield at, whole, some, start - first, end - first


def strips(body, start=None):
    return lax.fori_loop(0, CHUNK // STRIP, lambda at, carry: body(part(at, STRIP), at * STRIP, carry), start)


def square(entries, strip):
    return entries[strip].reshape(STRIP // LANES, LANES)


def inside(place, start, end):
    row = lax.broadcasted_iota(jnp.int32, (STRIP // LANES, LANES), 0)
    place = place + row * LANES + lax.broadcasted_iota(jnp.int32, (STRIP // LANES, LANES), 1)
    return (place >= start) & (place < end)


def fold(values):
    return jnp.sum(values.reshape(-1, 8, LANES), axis=0)


def update_kernel(segments, params, first, second, grad, new_first, new_second, update, sums):
    step = pl.program_id(0)
    nothing = jnp.zeros((8, LANES), F32)

    @pl.when(step == 0)
    def _():
        sums[...] = nothing

    def move(strip, place, totals):
        grads = grad[strip]
        firsts = BETA_FIRST * first[strip] + (1.0 - BETA_FIRST) * grads
        seconds = BETA_SECOND * second[strip] + (1.0 - BETA_SECOND) * grads * grads
        new_first[strip] = firsts
        new_second[strip] = seconds
        first_hat = firsts * (1.0 / (1.0 - BETA_FIRST**STEP))
        second_hat = seconds * (1.0 / (1.0 - BETA_SECOND**STEP))
        weights = params[strip]
        change = first_hat / (jnp.sqrt(second_hat) + ADAM_EPS) + WEIGHT_DECAY * weights
        update[strip] = change
        squares = [(each_one * each_one).reshape(STRIP // LANES, LANES) for each_one in (weights, change)]
        return totals[0] + fold(squares[0]), totals[1] + fold(squares[1])

    totals = strips(move, (nothing, nothing))
    lane = lax.broadcasted_iota(jnp.int32, (1, LANES), 1)

    def add(at, totals):
        for row, total in enumerate(totals):
            total = jnp.sum(jnp.sum(total, axis=0, keepdims=True), axis=1, keepdims=True)
            sums[row : row + 1, :] += jnp.where(lane == segments[0] + at, total, 0.0)

    for at, whole, some, start, end in chunk_spans(segments, step):

        @pl.when(whole)
        def _(at=at):
            add(at, totals)

        @pl.when(some)
        def _(at=at, start=start, end=end):
            def squares(strip, place, totals):
                here = inside(place, start, end)
                own = [square(entries, strip) for entries in (params, update)]
                own = [fold(jnp.where(here, each_one * each_one, 0.0)) for each_one in own]
                return totals[0] + own[0], totals[1] + own[1]

            add(at, strips(squares, (nothing, nothing)))


def apply_kernel(segments, sums, params, update, new_params, *norms):
    step = pl.program_id(0)
    roots = jnp.sqrt(sums[0:2, :])
    trust = roots[0:1, :] / (roots[1:2, :] + ADAM_EPS)
    for out, row in zip(norms, (roots[0:1, :], roots[1:2, :], trust)):
        out[...] = row.reshape(LANES)[: out.shape[0]]
    lane = lax.broadcasted_iota(jnp.int32, (1, LANES), 1)
    for at, whole, some, start, end in chunk_spans(segments, step):

        scale = LEARN_RATE * jnp.sum(jnp.where(lane == segments[0] + at, trust, 0.0), axis=1, keepdims=True)
        scale = jnp.broadcast_to(scale, (1, LANES))

        def moved(strip, scale=scale):
            return square(params, strip) - scale * square(update, strip)

        @pl.when(whole)
        def _(moved=moved):
            def all_of(strip, place, carry):
                new_params[strip] = moved(strip).reshape(STRIP)
                return carry

            strips(all_of, 0)

        @pl.when(some)
        def _(moved=moved, start=start, end=end):
            def part_of(strip, place, carry):
                chosen = jnp.where(inside(place, start, end), moved(strip), square(new_params, strip))
                new_params[strip] = chosen.reshape(STRIP)
                return carry

            strips(part_of, 0)


def shards(frames, lengths, cotangent, params, first_moment, second_moment):
    shard_size = params.shape[0]
    devices = lax.axis_size("dp") * lax.axis_size("fsdp")
    me = lax.axis_index(AXES)
    if fast_mesh():
        dp, fsdp = lax.axis_index("dp"), lax.axis_index("fsdp")
        coords = jnp.stack([dp // 2, dp % 2, fsdp // 2, fsdp % 2]).astype(jnp.int32)
    else:
        coords = jnp.zeros((4,), jnp.int32)
    state = forward(coords, lengths, frames[0], cotangent[0], gather_shards(low(params), me))
    back = backward(coords, frames[0], state)
    steps = -(-shard_size // CHUNK)
    size = max(shard_size, CHUNK)
    grad_shard, gain_grads = scatter_grads(state, back, coords, me, shard_size, size)

    def filled(flat):
        return jnp.pad(flat, (0, size - shard_size)) if size > shard_size else flat

    bounds = segment_bounds()
    spans = most_segments(shard_size, devices)
    shard_low = me * shard_size
    first_segment = sum((shard_low >= b).astype(jnp.int32) for b in bounds[1:-1])
    table = jnp.asarray(bounds[1:] + [bounds[-1]] * spans, jnp.int32)
    ends = jnp.clip(lax.dynamic_slice(table, (first_segment,), (spans,)) - shard_low, 0, shard_size)
    segments = jnp.concatenate([first_segment[None], jnp.zeros((1,), jnp.int32), ends]).astype(jnp.int32)
    grid = pl.BlockSpec((CHUNK,), lambda step: (step,))
    whole = pl.BlockSpec((8, LANES), lambda step: (0, 0))
    flat_kind = jax.ShapeDtypeStruct((size,), F32)
    tile_kind = jax.ShapeDtypeStruct((8, LANES), F32)
    weights = filled(params)
    new_first, new_second, update, sums = pl.pallas_call(
        update_kernel,
        name="update",
        grid=(steps,),
        in_specs=[SM] + [grid] * 4,
        out_specs=[grid] * 3 + [whole],
        out_shape=[flat_kind] * 3 + [tile_kind],
    )(segments, weights, filled(first_moment), filled(second_moment), grad_shard)
    sums = sum_everywhere(sums)
    count = len(segment_shapes())
    new_params, *norms = pl.pallas_call(
        apply_kernel,
        name="apply",
        grid=(steps,),
        in_specs=[SM, whole, grid, grid],
        out_specs=[grid] + [pl.BlockSpec((count,), lambda step: (0,))] * 3,
        out_shape=[flat_kind] + [jax.ShapeDtypeStruct((count,), F32)] * 3,
    )(segments, sums, weights, update)
    return (
        state["out"].reshape(frames.shape),
        back["fgrad"].reshape(frames.shape),
        new_params[:shard_size],
        new_first[:shard_size],
        new_second[:shard_size],
        *norms,
        gain_grads.reshape(-1),
    )


def solution(mesh):
    placed = (
        P(("dp", "fsdp"), None, None),
        P(("dp", "fsdp")),
        P(("dp", "fsdp"), None, None),
        P(("dp", "fsdp")),
        P(("dp", "fsdp")),
        P(("dp", "fsdp")),
    )
    return jax.shard_map(
        shards,
        mesh=mesh,
        in_specs=placed,
        out_specs=(
            P(("dp", "fsdp"), None, None),
            P(("dp", "fsdp"), None, None),
            P(("dp", "fsdp")),
            P(("dp", "fsdp")),
            P(("dp", "fsdp")),
            P(),
            P(),
            P(),
            P(),
        ),
        check_vma=False,
    )
```
